32 devices in a mesh: groups: 2 (over y), wide: 8 (over z, x), tp: 2 (over core).
Axes of the slice: x: 2, y: 2, z: 4, core: 2. Of those that a mesh axis runs over, the one named last changes fastest.
Arguments:
- pre_codes: bfloat16 [64, 4, 4, 2, 512], P(('groups', 'wide'), None, 'tp'), parts along dimension 0, may hold values from -6 to 6
- pre_scales: bfloat16 [64, 4, 4, 2, 4], P(('groups', 'wide'), None, 'tp'), parts along dimension 0, may hold values from 0.099609375 to 1
- req_dest: int32 [64], P(('groups', 'wide')), parts along dimension 0, may hold values from 0 to 7, as said below
- req_blocks: int32 [64], P(('groups', 'wide')), parts along dimension 0, may hold values from 1 to 4, as said below
- res_codes: bfloat16 [128, 64, 2, 512], P(('groups', 'wide'), None, None, 'tp'), parts along dimension 0, may hold values from -6 to 6
- res_scales: bfloat16 [128, 64, 2, 4], P(('groups', 'wide'), None, None, 'tp'), parts along dimension 0, may hold values from 0.099609375 to 1
- res_len: int32 [128], P(('groups', 'wide')), parts along dimension 0, may hold values from 1 to 64, as said below
- res_query: bfloat16 [128, 2, 8192], P(('groups', 'wide'), None, 'tp'), parts along dimension 0, may hold values from -128 to 128
- res_new: bfloat16 [128, 2, 2, 512], P(('groups', 'wide'), None, None, 'tp'), parts along dimension 0, may hold values from -6 to 6
- arr_query: bfloat16 [96, 2, 8192], P(('groups', 'wide'), None, 'tp'), parts along dimension 0, may hold values from -128 to 128
- arr_new: bfloat16 [96, 2, 2, 512], P(('groups', 'wide'), None, None, 'tp'), parts along dimension 0, may hold values from -6 to 6
Outputs:
- res_out: bfloat16 [128, 2, 8192], P(('groups', 'wide'), None, 'tp'), parts along dimension 0
- arr_out: bfloat16 [96, 2, 8192], P(('groups', 'wide'), None, 'tp'), parts along dimension 0
The draws below stay inside these ranges and needn't reach their ends.
There are 2 independent parts, one for each index of `groups`. The reference program is written for one: setup_inputs(seed, part) draws one part's arguments, and reference() takes and returns one part's arrays. A program takes and returns all parts, laid end to end along the dimension named above; each array names one. Nothing has to cross between parts.
Inputs may be any that keep to these rules, and one draw needn't show every extreme that they name: `req_dest`: each prefill instance sends at most one request to one decode instance; each decode instance receives at least 2 and at most 6 requests, and some decode instance receives 6 in every draw. For every even r, request r of each prefill instance goes to the instance a fixed distance away along the axis, the same distance for all prefill instances, and request r + 1 to the instance at one of two further such distances. `req_blocks`: some request holds 4 blocks in every draw. `res_len`: some resident request has 64 tokens in every draw.
All inputs are finite; a program needn't handle non-finite values.
Results may differ from the reference program's by a relative error of at most 0.0032.
Values may be sent and summed in bfloat16 or wider, within the bound.
No kernel may reach another device: no remote copies, remote signals or barrier semaphores. Data moves between devices by JAX's collectives and lax.ppermute only.
A program may use at most 64 MiB of HBM per device.

```python
import math
import jax
import jax.numpy as jnp
from jax import lax

KVH = 4
HD = 128
HQ = 64
BLK = 4
MAXB = 4
PR = 4
AR = 6
R = 8
LRES = 64
REQ_ALL = 32
RES_ALL = 64
N_WIDE = 8


def routing(key):
    subkeys = jax.random.split(key, 5)
    pair_count = PR // 2
    offsets = jax.random.permutation(subkeys[0], N_WIDE)[:3 * pair_count].astype(jnp.int32)
    first_offsets = offsets[:pair_count]
    second_offsets = offsets[pair_count:2 * pair_count]
    third_offsets = offsets[2 * pair_count:]
    picked = jax.random.randint(subkeys[1], (N_WIDE, pair_count), 0, 2)
    busiest = jax.random.randint(subkeys[2], (), 0, N_WIDE)
    senders = jnp.arange(N_WIDE, dtype=jnp.int32)[:, None]
    force_second = senders == (busiest - second_offsets[None, :]) % N_WIDE
    force_third = senders == (busiest - third_offsets[None, :]) % N_WIDE
    picked = jnp.where(force_second, 0, jnp.where(force_third, 1, picked))
    even_dest = (senders + first_offsets[None, :]) % N_WIDE
    odd_offset = jnp.where(picked == 0, second_offsets[None, :], third_offsets[None, :])
    odd_dest = (senders + odd_offset) % N_WIDE
    destination = jnp.stack([even_dest, odd_dest], axis=-1).reshape(N_WIDE * PR)
    blocks = jax.random.randint(subkeys[3], (N_WIDE * PR,), 1, MAXB + 1)
    longest = jax.random.randint(subkeys[4], (), 0, N_WIDE * PR)
    blocks = jnp.where(jnp.arange(N_WIDE * PR) == longest, MAXB, blocks)
    return (destination.astype(jnp.int32), blocks.astype(jnp.int32))


def draw_req_dest(key, part):
    destination, blocks = routing(key)
    return destination


def draw_req_blocks(key, part):
    destination, blocks = routing(key)
    return blocks


def draw_res_len(key, part):
    key = jax.random.fold_in(key, 31)
    subkeys = jax.random.split(key, 2)
    lengths = jax.random.randint(subkeys[0], (N_WIDE * R,), 1, LRES + 1)
    longest = jax.random.randint(subkeys[1], (), 0, N_WIDE * R)
    return jnp.where(jnp.arange(N_WIDE * R) == longest, LRES, lengths).astype(jnp.int32)


def fresh_pair(key, row_count):
    subkeys = jax.random.split(key, 1)
    fresh_base = jnp.clip(1.5 * jax.random.normal(subkeys[0], (row_count, 2, 2, KVH * HD), jnp.float32), -6.0, 6.0)
    return fresh_base


def draw_res_new(key, part):
    fresh_base = fresh_pair(key, N_WIDE * R)
    return fresh_base.astype(jnp.bfloat16)


def draw_res_query(key, part):
    key = jax.random.fold_in(key, 43)
    query = jnp.clip(jax.random.normal(key, (N_WIDE * R, 2, HQ * HD), jnp.float32), -6.0, 6.0)
    return query.astype(jnp.bfloat16)


def draw_arr_new(key, part):
    fresh_base = fresh_pair(jax.random.fold_in(key, 77), N_WIDE * AR)
    return fresh_base.astype(jnp.bfloat16)


def draw_arr_query(key, part):
    key = jax.random.fold_in(key, 47)
    query = jnp.clip(jax.random.normal(key, (N_WIDE * AR, 2, HQ * HD), jnp.float32), -6.0, 6.0)
    return query.astype(jnp.bfloat16)


def block_scale(key, dims, cuts, smallest, high):
    gain = 1.0
    for axis_at, parts in cuts:
        heights = jax.random.uniform(jax.random.fold_in(jax.random.fold_in(key, 6), axis_at), (parts,), jnp.float32, smallest / len(cuts), high / len(cuts))
        gain = gain * jnp.repeat(jnp.exp(heights), dims[axis_at] // parts).reshape((-1,) + (1,) * (len(dims) - 1 - axis_at))
    return gain


def normal_values(stream_key, dims, width, most, pieces=(), kind=jnp.bfloat16):
    gain = block_scale(stream_key, dims, pieces, -0.22, 0.18) if pieces else 1.0
    result = jax.random.normal(stream_key, dims, jnp.float32) * width * gain
    return jnp.minimum(jnp.maximum(result, -most), most).astype(kind)


def setup_inputs(seed: int = 0, part: int = 0) -> dict:
    arg_keys = jax.random.split(jax.random.key(seed), 12)
    part_splits = jax.random.split(jax.random.fold_in(arg_keys[11], part), 12)
    pre_codes = normal_values(part_splits[0], (REQ_ALL, MAXB, BLK, 2, KVH * HD), 1.0, 6.0, ((0, 8), (2, 2)))
    pre_scales = jnp.clip(jnp.exp(math.log(1.0) - 2.306499 * jax.random.uniform(part_splits[1], (REQ_ALL, MAXB, BLK, 2, KVH), jnp.float32) ** block_scale(part_splits[1], (REQ_ALL, MAXB, BLK, 2, KVH), ((0, 8), (2, 2)), -0.2, 0.2)), 0.099609375, 1.0).astype(jnp.bfloat16)
    req_dest = draw_req_dest(jax.random.fold_in(jax.random.fold_in(arg_keys[11], part), 71), part)
    req_blocks = draw_req_blocks(jax.random.fold_in(jax.random.fold_in(arg_keys[11], part), 71), part)
    res_codes = normal_values(part_splits[4], (RES_ALL, LRES, 2, KVH * HD), 1.0, 6.0, ((0, 8), (3, 2)))
    res_scales = jnp.clip(jnp.exp(math.log(1.0) - 2.306499 * jax.random.uniform(part_splits[5], (RES_ALL, LRES, 2, KVH), jnp.float32) ** block_scale(part_splits[5], (RES_ALL, LRES, 2, KVH), ((0, 8), (3, 2)), -0.2, 0.2)), 0.099609375, 1.0).astype(jnp.bfloat16)
    res_len = draw_res_len(jax.random.fold_in(jax.random.fold_in(arg_keys[11], part), 71), part)
    res_query = draw_res_query(jax.random.fold_in(jax.random.fold_in(arg_keys[11], part), 71), part)
    res_new = draw_res_new(jax.random.fold_in(jax.random.fold_in(arg_keys[11], part), 71), part)
    arr_query = draw_arr_query(jax.random.fold_in(jax.random.fold_in(arg_keys[11], part), 71), part)
    arr_new = draw_arr_new(jax.random.fold_in(jax.random.fold_in(arg_keys[11], part), 71), part)
    return {"pre_codes": pre_codes, "pre_scales": pre_scales, "req_dest": req_dest, "req_blocks": req_blocks, "res_codes": res_codes, "res_scales": res_scales, "res_len": res_len, "res_query": res_query, "res_new": res_new, "arr_query": arr_query, "arr_new": arr_new}


def dequantize(quantized, scales):
    leading = quantized.shape[:-2]
    expanded = quantized.reshape(leading + (2, KVH, HD)).astype(jnp.float32)
    factors = scales.astype(jnp.float32)[..., None]
    return (expanded * factors).astype(jnp.bfloat16)

def attend(query, fresh_kv, cache, is_valid):
    slot_count = query.shape[0]
    score_scale = 1.0 / math.sqrt(HD)
    queries = query.reshape(slot_count, 2, KVH, HQ // KVH, HD).astype(jnp.float32)
    cache_keys = cache[:, :, 0].astype(jnp.float32)
    cache_values = cache[:, :, 1].astype(jnp.float32)
    new_keys = fresh_kv[:, :, 0].reshape(slot_count, 2, KVH, HD).astype(jnp.float32)
    new_values = fresh_kv[:, :, 1].reshape(slot_count, 2, KVH, HD).astype(jnp.float32)
    cache_scores = jnp.einsum('sekgd,stkd->sekgt', queries, cache_keys) * score_scale
    fresh_scores = jnp.einsum('sekgd,sfkd->sekgf', queries, new_keys) * score_scale
    step_index = jnp.arange(2)
    cache_mask = is_valid[:, None, None, None, :]
    fresh_mask = (step_index[None, :] <= step_index[:, None])[None, :, None, None, :]
    cache_scores = jnp.where(cache_mask, cache_scores, -jnp.inf)
    fresh_scores = jnp.where(fresh_mask, fresh_scores, -jnp.inf)
    row_top = jnp.maximum(lax.optimization_barrier(jnp.max(cache_scores, axis=-1)), lax.optimization_barrier(jnp.max(fresh_scores, axis=-1)))
    cache_weights = jnp.exp(cache_scores - row_top[..., None])
    fresh_weights = jnp.exp(fresh_scores - row_top[..., None])
    row_total = lax.optimization_barrier(jnp.sum(cache_weights, axis=-1)) + lax.optimization_barrier(jnp.sum(fresh_weights, axis=-1))
    cache_rounded = lax.optimization_barrier(cache_weights.astype(jnp.bfloat16)).astype(jnp.float32)
    fresh_rounded = lax.optimization_barrier(fresh_weights.astype(jnp.bfloat16)).astype(jnp.float32)
    mixed_sum = jnp.einsum('sekgt,stkd->sekgd', cache_rounded, cache_values)
    mixed_sum = mixed_sum + jnp.einsum('sekgf,sfkd->sekgd', fresh_rounded, new_values)
    return (mixed_sum / row_total[..., None]).reshape(slot_count, 2, HQ * HD).astype(jnp.bfloat16)

def arrivals(req_dest, req_blocks):
    request_total = req_dest.shape[0]
    sorted_order = jnp.argsort(req_dest * request_total + jnp.arange(request_total, dtype=jnp.int32), stable=True).astype(jnp.int32)
    sorted_dest = req_dest[sorted_order]
    counts = jnp.zeros((N_WIDE,), jnp.int32).at[req_dest].add(1)
    starts = jnp.cumsum(counts) - counts
    arrival_rank = jnp.arange(request_total, dtype=jnp.int32) - starts[sorted_dest]
    slot_place = sorted_dest * AR + arrival_rank
    request = jnp.zeros((N_WIDE * AR,), jnp.int32).at[slot_place].set(sorted_order)
    blocks = jnp.zeros((N_WIDE * AR,), jnp.int32).at[slot_place].set(req_blocks[sorted_order])
    return (request, blocks)

def reference(pre_codes, pre_scales, req_dest, req_blocks, res_codes, res_scales, res_len, res_query, res_new, arr_query, arr_new):
    resident = dequantize(res_codes, res_scales)
    res_valid = jnp.arange(LRES, dtype=jnp.int32)[None, :] < res_len[:, None]
    res_out = attend(res_query, res_new, resident, res_valid)
    request, blocks = arrivals(req_dest, req_blocks)
    arrived = dequantize(pre_codes[request], pre_scales[request])
    arrived = arrived.reshape((N_WIDE * AR, MAXB * BLK) + arrived.shape[3:])
    token_block = jnp.arange(MAXB * BLK, dtype=jnp.int32) // BLK
    arr_valid = token_block[None, :] < blocks[:, None]
    arr_out = attend(arr_query, arr_new, arrived, arr_valid)
    return (res_out, arr_out)
```

```python
import functools
import math

import jax
import jax.numpy as jnp
from jax import lax
from jax.experimental import pallas as pl
from jax.experimental.pallas import tpu as pltpu
from jax.sharding import PartitionSpec as P

KVH = 4
HD = 128
HQ = 64
GROUP = HQ // KVH
STEPS = 2

NEGATIVE = -1e30
EMPTY = 1024.0
SCORE_SCALE = 1.0 / math.sqrt(HD)

BF16 = jnp.bfloat16
F32 = jnp.float32


def iota(shape, axis):
    return lax.broadcasted_iota(jnp.int32, shape, axis)


def dot_nt(a, b):
    return lax.dot_general(a, b, (((1,), (1,)), ((), ())), preferred_element_type=F32)


def dot_nn(a, b):
    return lax.dot_general(a, b, (((1,), (0,)), ((), ())), preferred_element_type=F32)


def whole(memory_space=pltpu.VMEM):
    return pl.BlockSpec(memory_space=memory_space)


def pack_kernel(tp, block_rows, dest_ref, blocks_ref, codes_ref, scales_ref, send_ref):
    requests, tokens, heads = codes_ref.shape[:3]
    rows = 2 * tokens
    per_core = heads // tp
    send_ref[...] = jnp.full(send_ref.shape, EMPTY, BF16)
    row_block = iota((rows, HD), 0) // block_rows

    def place(r):
        there = dest_ref[r]
        held = row_block < blocks_ref[r]
        scales = scales_ref[r].astype(F32)
        for j in range(heads):
            codes = codes_ref[r, :, j].astype(F32).reshape(rows, HD)
            values = codes * scales[:, j : j + 1]
            values = jnp.where(held, values, EMPTY).astype(BF16)
            send_ref[there * tp + j // per_core, j % per_core] = values

    if requests <= 8:
        for r in range(requests):
            place(r)
    else:
        lax.fori_loop(0, requests, lambda r, c: (place(r), c)[1], 0)


def resident_kernel(len_ref, codes_ref, scales_ref, query_ref, new_ref, out_ref):
    slots, rows = codes_ref.shape[:2]
    heads = scales_ref.shape[2]
    tokens = rows // (2 * heads)
    queries = query_ref.shape[1]
    new_rows = new_ref.shape[1]

    from_scale = iota((rows, rows), 1)
    to_row = iota((rows, rows), 0)
    source = ((to_row % 2) * heads + (to_row // 2) % heads) * tokens + to_row // (2 * heads)
    spread = jnp.where(from_scale == source, 1.0, 0.0).astype(BF16)
    flat = jnp.concatenate(
        [scales_ref[:, p, h] for p in range(2) for h in range(heads)], axis=1
    )
    columns = dot_nt(spread, flat)

    col = iota((queries, rows), 1)
    row_head = iota((queries, rows), 0) // (queries // heads)
    is_key = (col % 2 == 0) & ((col // 2) % heads == row_head)
    col_token = jnp.where(is_key, col // (2 * heads), tokens)

    new_col = iota((queries, new_rows), 1)
    new_head = iota((queries, new_rows), 0) // (queries // heads)
    new_step = iota((queries, new_rows), 0) % STEPS
    new_ok = (
        (new_col % 2 == 0)
        & ((new_col // 2) % heads == new_head)
        & (new_col // (2 * heads) <= new_step)
    )

    for s in range(slots):
        cache = (codes_ref[s].astype(F32) * columns[:, s : s + 1]).astype(BF16)
        query = query_ref[s]
        new = new_ref[s]
        scores = jnp.where(
            col_token < len_ref[s], dot_nt(query, cache) * SCORE_SCALE, NEGATIVE
        )
        new_scores = jnp.where(new_ok, dot_nt(query, new) * SCORE_SCALE, NEGATIVE)
        top = jnp.maximum(
            jnp.max(scores, axis=1, keepdims=True), jnp.max(new_scores, axis=1, keepdims=True)
        )
        weights = jnp.exp(scores - top)
        new_weights = jnp.exp(new_scores - top)
        total = jnp.sum(weights, axis=1, keepdims=True) + jnp.sum(
            new_weights, axis=1, keepdims=True
        )
        weights = pltpu.roll(weights, 1, 1).astype(BF16)
        new_weights = jnp.concatenate(
            [jnp.zeros((queries, 1), F32), new_weights[:, : new_rows - 1]], axis=1
        ).astype(BF16)
        mixed = dot_nn(weights, cache) + dot_nn(new_weights, new)
        out_ref[s] = (mixed / total).astype(BF16)


def arrival_kernel(tp, got_ref, query_ref, new_ref, out_ref):
    chunks, heads, chunk_rows = got_ref.shape[:3]
    slots, _, per_head = query_ref.shape[:3]
    rows = slots * per_head
    columns = chunks * chunk_rows
    sender_rows = tp * chunk_rows
    piece = min(columns, 256)

    caches = [got_ref[:, h].reshape(columns, HD) for h in range(heads)]
    ones = jnp.ones((8, HD), BF16)
    sums = dot_nt(ones, caches[0])
    col = iota((8, columns), 1)
    held = sums < EMPTY
    first = jnp.where(held & (col % sender_rows == 0), 1.0, 0.0).astype(BF16)
    before = jnp.where(
        iota((piece, piece), 0) // sender_rows < iota((piece, piece), 1) // sender_rows, 1.0, 0.0
    ).astype(BF16)
    base = jnp.zeros((8, 1), F32)
    ranks = []
    for p in range(0, columns, piece):
        part = first[:, p : p + piece]
        ranks.append(dot_nn(part, before) + base)
        if p + piece < columns:
            base = base + jnp.sum(part.astype(F32), axis=1, keepdims=True)
    rank = ranks[0] if len(ranks) == 1 else jnp.concatenate(ranks, axis=1)
    slot_of = jnp.where(held & (col % 2 == 0), rank, -1.0)[:1]
    first_slot = (pl.program_id(0) * slots).astype(F32)

    new_rows = new_ref.shape[0] * new_ref.shape[1] // heads
    row_slot = iota((rows, new_rows), 0) // per_head
    row_step = iota((rows, new_rows), 0) % STEPS
    new_col = iota((rows, new_rows), 1)
    new_ok = (
        (new_col % 2 == 0)
        & (new_col // (2 * STEPS) == row_slot)
        & ((new_col // 2) % STEPS <= row_step)
    )
    slot_rows = (iota((rows, 1), 0) // per_head).astype(F32) + first_slot
    mask = slot_of == slot_rows

    for h in range(heads):
        query = query_ref[:, h].reshape(rows, HD)
        new = jnp.concatenate(
            [
                new_ref[a, 2 * (f * heads + h) : 2 * (f * heads + h) + 2]
                for a in range(slots)
                for f in range(STEPS)
            ],
            axis=0,
        )
        cache = caches[h]
        scores = jnp.where(mask, dot_nt(query, cache) * SCORE_SCALE, NEGATIVE)
        new_scores = jnp.where(new_ok, dot_nt(query, new) * SCORE_SCALE, NEGATIVE)
        top = jnp.maximum(
            jnp.max(scores, axis=1, keepdims=True), jnp.max(new_scores, axis=1, keepdims=True)
        )
        weights = jnp.exp(scores - top)
        new_weights = jnp.exp(new_scores - top)
        total = jnp.sum(weights, axis=1, keepdims=True) + jnp.sum(
            new_weights, axis=1, keepdims=True
        )
        weights = pltpu.roll(weights, 1, 1).astype(BF16)
        new_weights = jnp.concatenate(
            [jnp.zeros((rows, 1), F32), new_weights[:, : new_rows - 1]], axis=1
        ).astype(BF16)
        mixed = dot_nn(weights, cache) + dot_nn(new_weights, new)
        out_ref[:, h] = (mixed / total).astype(BF16).reshape(slots, per_head, HD)


def pack(pre_codes, pre_scales, req_dest, req_blocks, peers, tp):
    requests, blocks, block_tokens = pre_codes.shape[:3]
    tokens = blocks * block_tokens
    codes = pre_codes.reshape(requests, tokens, 2, KVH, HD).transpose(0, 1, 3, 2, 4)
    scales = pre_scales.reshape(requests, tokens * 2, KVH)
    out = jax.ShapeDtypeStruct((peers * tp, KVH // tp, tokens * 2, HD), BF16)
    return pl.pallas_call(
        functools.partial(pack_kernel, tp, 2 * block_tokens),
        out_shape=out,
        in_specs=[whole(pltpu.SMEM), whole(pltpu.SMEM), whole(), whole()],
        out_specs=whole(),
        name="pack",
    )(req_dest, req_blocks, codes, scales)


def query_rows(query):
    slots, steps, width = query.shape
    return query.reshape(slots, steps, width // HD, HD).transpose(0, 2, 1, 3)


def new_rows_of(new):
    slots, steps, pair, width = new.shape
    heads = width // HD
    return (
        new.reshape(slots, steps, pair, heads, HD)
        .transpose(0, 1, 3, 2, 4)
        .reshape(slots, steps * heads * pair, HD)
    )


def from_rows(out, shape):
    slots, steps, width = shape
    return out.reshape(slots, width // HD, steps, HD).transpose(0, 2, 1, 3).reshape(shape)


def resident(res_codes, res_scales, res_len, res_query, res_new):
    slots, tokens, _, width = res_codes.shape
    heads = width // HD
    codes = (
        res_codes.reshape(slots, tokens, 2, heads, HD)
        .transpose(0, 1, 3, 2, 4)
        .reshape(slots, tokens * heads * 2, HD)
    )
    scales = res_scales.transpose(0, 2, 3, 1)
    query = query_rows(res_query).reshape(slots, heads * GROUP * STEPS, HD)
    work = slots * heads * GROUP * STEPS * tokens * heads * 2
    out = pl.pallas_call(
        resident_kernel,
        out_shape=jax.ShapeDtypeStruct(query.shape, BF16),
        in_specs=[whole(pltpu.SMEM)] + [whole()] * 4,
        out_specs=whole(),
        cost_estimate=pl.CostEstimate(
            flops=4 * work * HD, bytes_accessed=2 * res_codes.size + 4 * query.size, transcendentals=work
        ),
        name="resident",
    )(res_len, codes, scales, query, new_rows_of(res_new))
    return from_rows(out, res_query.shape)


def arrivals(got, arr_query, arr_new, tp):
    slots, steps, width = arr_query.shape
    heads = width // (HD * GROUP)
    query = query_rows(arr_query).reshape(slots, heads, GROUP * steps, HD)
    new = new_rows_of(arr_new)
    size = max(n for n in range(1, 7) if slots % n == 0)
    out = pl.pallas_call(
        functools.partial(arrival_kernel, tp),
        out_shape=jax.ShapeDtypeStruct(query.shape, BF16),
        grid=(slots // size,),
        in_specs=[
            pl.BlockSpec(got.shape, lambda i: (0, 0, 0, 0)),
            pl.BlockSpec((size,) + query.shape[1:], lambda i: (i, 0, 0, 0)),
            pl.BlockSpec((size,) + new.shape[1:], lambda i: (i, 0, 0)),
        ],
        out_specs=pl.BlockSpec((size,) + query.shape[1:], lambda i: (i, 0, 0, 0)),
        compiler_params=pltpu.CompilerParams(vmem_limit_bytes=48 * 2**20),
        name="arrivals",
    )(got, query, new)
    return from_rows(out, arr_query.shape)


def shards(
    pre_codes,
    pre_scales,
    req_dest,
    req_blocks,
    res_codes,
    res_scales,
    res_len,
    res_query,
    res_new,
    arr_query,
    arr_new,
):
    peers = lax.axis_size("wide")
    tp = lax.axis_size("tp")
    send = pack(pre_codes, pre_scales, req_dest, req_blocks, peers, tp)
    got = lax.all_to_all(send, ("wide", "tp"), split_axis=0, concat_axis=0, tiled=True)
    res_out = resident(res_codes, res_scales, res_len, res_query, res_new)
    arr_out = arrivals(got, arr_query, arr_new, tp)
    return (res_out, arr_out)


def solution(mesh):
    in_specs = (
        P(("groups", "wide"), None, "tp", None, None),
        P(("groups", "wide"), None, "tp", None, None),
        P(("groups", "wide")),
        P(("groups", "wide")),
        P(("groups", "wide"), None, None, "tp"),
        P(("groups", "wide"), None, None, "tp"),
        P(("groups", "wide")),
        P(("groups", "wide"), None, "tp"),
        P(("groups", "wide"), None, None, "tp"),
        P(("groups", "wide"), None, "tp"),
        P(("groups", "wide"), None, None, "tp"),
    )
    out_specs = (P(("groups", "wide"), None, "tp"), P(("groups", "wide"), None, "tp"))
    return jax.shard_map(shards, mesh=mesh, in_specs=in_specs, out_specs=out_specs, check_vma=False)
```

```python
import functools
import math

import jax
import jax.numpy as jnp
from jax import lax
from jax.experimental import pallas as pl
from jax.experimental.pallas import tpu as pltpu
from jax.sharding import PartitionSpec as P

KVH = 4
HD = 128
HQ = 64
GROUP = HQ // KVH
STEPS = 2

NEGATIVE = -1e30
EMPTY = 1024.0
SCORE_SCALE = 1.0 / math.sqrt(HD)

BF16 = jnp.bfloat16
F32 = jnp.float32


def iota(shape, axis):
    return lax.broadcasted_iota(jnp.int32, shape, axis)


def dot_nt(a, b):
    return lax.dot_general(a, b, (((1,), (1,)), ((), ())), preferred_element_type=F32)


def dot_nn(a, b):
    return lax.dot_general(a, b, (((1,), (0,)), ((), ())), preferred_element_type=F32)


def whole(memory_space=pltpu.VMEM):
    return pl.BlockSpec(memory_space=memory_space)


def pack_kernel(peers, tp, block_rows, dest_ref, blocks_ref, codes_ref, scales_ref, *refs):
    requests, tokens, heads = codes_ref.shape[:3]
    rows = 2 * tokens
    per_core = heads // tp
    apart = len(refs) > 1
    send_ref = refs[-1]
    send_ref[...] = jnp.full(send_ref.shape, EMPTY, BF16)
    row_block = iota((rows, HD), 0) // block_rows
    here = lax.axis_index("wide") if apart else 0
    core = lax.axis_index("tp") if apart else 0

    def place(r):
        there = lax.rem(dest_ref[r] - here + peers, peers)
        held = row_block < blocks_ref[r]
        scales = scales_ref[r].astype(F32)
        for j in range(heads):
            codes = codes_ref[r, :, j].astype(F32).reshape(rows, HD)
            values = codes * scales[:, j : j + 1]
            values = jnp.where(held, values, EMPTY).astype(BF16)
            to_core = lax.rem(j // per_core - core + tp, tp)
            send_ref[there * tp + to_core, j % per_core] = values

    if requests <= 8:
        for r in range(requests):
            place(r)
    else:
        lax.fori_loop(0, requests, lambda r, c: (place(r), c)[1], 0)
    if apart:
        for k, ref in enumerate(refs[:-1]):
            ref[...] = send_ref[k]


def resident_kernel(len_ref, codes_ref, scales_ref, query_ref, new_ref, out_ref):
    slots, rows = codes_ref.shape[:2]
    heads = scales_ref.shape[2]
    tokens = rows // (2 * heads)
    queries = query_ref.shape[1]
    new_rows = new_ref.shape[1]

    from_scale = iota((rows, rows), 1)
    to_row = iota((rows, rows), 0)
    source = ((to_row % 2) * heads + (to_row // 2) % heads) * tokens + to_row // (2 * heads)
    spread = jnp.where(from_scale == source, 1.0, 0.0).astype(BF16)
    flat = jnp.concatenate(
        [scales_ref[:, p, h] for p in range(2) for h in range(heads)], axis=1
    )
    columns = dot_nt(spread, flat)

    col = iota((queries, rows), 1)
    row_head = iota((queries, rows), 0) // (queries // heads)
    is_key = (col % 2 == 0) & ((col // 2) % heads == row_head)
    col_token = jnp.where(is_key, col // (2 * heads), tokens)

    new_col = iota((queries, new_rows), 1)
    new_head = iota((queries, new_rows), 0) // (queries // heads)
    new_step = iota((queries, new_rows), 0) % STEPS
    new_ok = (
        (new_col % 2 == 0)
        & ((new_col // 2) % heads == new_head)
        & (new_col // (2 * heads) <= new_step)
    )

    for s in range(slots):
        cache = (codes_ref[s].astype(F32) * columns[:, s : s + 1]).astype(BF16)
        query = query_ref[s]
        new = new_ref[s]
        scores = jnp.where(
            col_token < len_ref[s], dot_nt(query, cache) * SCORE_SCALE, NEGATIVE
        )
        new_scores = jnp.where(new_ok, dot_nt(query, new) * SCORE_SCALE, NEGATIVE)
        top = jnp.maximum(
            jnp.max(scores, axis=1, keepdims=True), jnp.max(new_scores, axis=1, keepdims=True)
        )
        weights = jnp.exp(scores - top)
        new_weights = jnp.exp(new_scores - top)
        total = jnp.sum(weights, axis=1, keepdims=True) + jnp.sum(
            new_weights, axis=1, keepdims=True
        )
        weights = pltpu.roll(weights, 1, 1).astype(BF16)
        new_weights = jnp.concatenate(
            [jnp.zeros((queries, 1), F32), new_weights[:, : new_rows - 1]], axis=1
        ).astype(BF16)
        mixed = dot_nn(weights, cache) + dot_nn(new_weights, new)
        out_ref[s] = (mixed / total).astype(BF16)


def arrival_kernel(peers, tp, query_ref, new_ref, *refs):
    got_refs, out_ref = refs[:-1], refs[-1]
    apart = len(got_refs) > 1
    slots, heads, per_head = query_ref.shape[:3]
    chunk_rows = got_refs[0].shape[-2]
    rows = slots * per_head
    columns = peers * tp * chunk_rows
    sender_rows = tp * chunk_rows
    piece = min(columns, 256)

    if apart:
        caches = [jnp.concatenate([ref[h] for ref in got_refs], axis=0) for h in range(heads)]
        here = lax.axis_index("wide")
    else:
        caches = [got_refs[0][:, h].reshape(columns, HD) for h in range(heads)]

    def sender(index):
        return lax.rem(here - index + peers, peers) if apart else index

    ones = jnp.ones((8, HD), BF16)
    sums = dot_nt(ones, caches[0])
    col = iota((8, columns), 1)
    held = sums < EMPTY
    first = jnp.where(held & (col % sender_rows == 0), 1.0, 0.0).astype(BF16)
    before = jnp.where(
        sender(iota((piece, piece), 0) // sender_rows)
        < sender(iota((piece, piece), 1) // sender_rows),
        1.0,
        0.0,
    ).astype(BF16)
    base = jnp.zeros((8, 1), F32)
    ranks = []
    for p in range(0, columns, piece):
        part = first[:, p : p + piece]
        ranks.append(dot_nn(part, before) + base)
        if p + piece < columns:
            base = base + jnp.sum(part.astype(F32), axis=1, keepdims=True)
    rank = ranks[0] if len(ranks) == 1 else jnp.concatenate(ranks, axis=1)
    slot_of = jnp.where(held & (col % 2 == 0), rank, -1.0)[:1]
    first_slot = (pl.program_id(0) * slots).astype(F32)

    new_rows = new_ref.shape[0] * new_ref.shape[1] // heads
    row_slot = iota((rows, new_rows), 0) // per_head
    row_step = iota((rows, new_rows), 0) % STEPS
    new_col = iota((rows, new_rows), 1)
    new_ok = (
        (new_col % 2 == 0)
        & (new_col // (2 * STEPS) == row_slot)
        & ((new_col // 2) % STEPS <= row_step)
    )
    slot_rows = (iota((rows, 1), 0) // per_head).astype(F32) + first_slot
    mask = slot_of == slot_rows

    for h in range(heads):
        query = query_ref[:, h].reshape(rows, HD)
        new = jnp.concatenate(
            [
                new_ref[a, 2 * (f * heads + h) : 2 * (f * heads + h) + 2]
                for a in range(slots)
                for f in range(STEPS)
            ],
            axis=0,
        )
        cache = caches[h]
        scores = jnp.where(mask, dot_nt(query, cache) * SCORE_SCALE, NEGATIVE)
        new_scores = jnp.where(new_ok, dot_nt(query, new) * SCORE_SCALE, NEGATIVE)
        top = jnp.maximum(
            jnp.max(scores, axis=1, keepdims=True), jnp.max(new_scores, axis=1, keepdims=True)
        )
        weights = jnp.exp(scores - top)
        new_weights = jnp.exp(new_scores - top)
        total = jnp.sum(weights, axis=1, keepdims=True) + jnp.sum(
            new_weights, axis=1, keepdims=True
        )
        weights = pltpu.roll(weights, 1, 1).astype(BF16)
        new_weights = jnp.concatenate(
            [jnp.zeros((rows, 1), F32), new_weights[:, : new_rows - 1]], axis=1
        ).astype(BF16)
        mixed = dot_nn(weights, cache) + dot_nn(new_weights, new)
        out_ref[:, h] = (mixed / total).astype(BF16).reshape(slots, per_head, HD)


def pack(pre_codes, pre_scales, req_dest, req_blocks, peers, tp, apart):
    requests, blocks, block_tokens = pre_codes.shape[:3]
    tokens = blocks * block_tokens
    codes = pre_codes.reshape(requests, tokens, 2, KVH, HD).transpose(0, 1, 3, 2, 4)
    scales = pre_scales.reshape(requests, tokens * 2, KVH)
    chunk = (KVH // tp, tokens * 2, HD)
    send = (peers * tp,) + chunk
    return pl.pallas_call(
        functools.partial(pack_kernel, peers, tp, 2 * block_tokens),
        out_shape=[jax.ShapeDtypeStruct(chunk, BF16)] * (peers * tp)
        if apart
        else [jax.ShapeDtypeStruct(send, BF16)],
        in_specs=[whole(pltpu.SMEM), whole(pltpu.SMEM), whole(), whole()],
        out_specs=[whole()] * (peers * tp if apart else 1),
        scratch_shapes=[pltpu.VMEM(send, BF16)] if apart else [],
        name="pack",
    )(req_dest, req_blocks, codes, scales)


def exchange(chunks, peers, tp):
    if len(chunks) == 1:
        return [lax.all_to_all(chunks[0], ("wide", "tp"), split_axis=0, concat_axis=0, tiled=True)]
    got = [chunks[0]]
    for k in range(1, peers * tp):
        ahead, across = divmod(k, tp)
        pairs = [
            (w * tp + t, (w + ahead) % peers * tp + (t + across) % tp)
            for w in range(peers)
            for t in range(tp)
        ]
        got.append(lax.ppermute(chunks[k], ("wide", "tp"), pairs))
    return got


def query_rows(query):
    slots, steps, width = query.shape
    return query.reshape(slots, steps, width // HD, HD).transpose(0, 2, 1, 3)


def new_rows_of(new):
    slots, steps, pair, width = new.shape
    heads = width // HD
    return (
        new.reshape(slots, steps, pair, heads, HD)
        .transpose(0, 1, 3, 2, 4)
        .reshape(slots, steps * heads * pair, HD)
    )


def from_rows(out, shape):
    slots, steps, width = shape
    return out.reshape(slots, width // HD, steps, HD).transpose(0, 2, 1, 3).reshape(shape)


def resident(res_codes, res_scales, res_len, res_query, res_new):
    slots, tokens, _, width = res_codes.shape
    heads = width // HD
    codes = (
        res_codes.reshape(slots, tokens, 2, heads, HD)
        .transpose(0, 1, 3, 2, 4)
        .reshape(slots, tokens * heads * 2, HD)
    )
    scales = res_scales.transpose(0, 2, 3, 1)
    query = query_rows(res_query).reshape(slots, heads * GROUP * STEPS, HD)
    work = slots * heads * GROUP * STEPS * tokens * heads * 2
    out = pl.pallas_call(
        resident_kernel,
        out_shape=jax.ShapeDtypeStruct(query.shape, BF16),
        in_specs=[whole(pltpu.SMEM)] + [whole()] * 4,
        out_specs=whole(),
        cost_estimate=pl.CostEstimate(
            flops=4 * work * HD, bytes_accessed=2 * res_codes.size + 4 * query.size, transcendentals=work
        ),
        name="resident",
    )(res_len, codes, scales, query, new_rows_of(res_new))
    return from_rows(out, res_query.shape)


def arrivals(got, arr_query, arr_new, peers, tp):
    slots, steps, width = arr_query.shape
    heads = width // (HD * GROUP)
    query = query_rows(arr_query).reshape(slots, heads, GROUP * steps, HD)
    new = new_rows_of(arr_new)
    size = max(n for n in range(1, 7) if slots % n == 0)

    def fixed(ref):
        return pl.BlockSpec(ref.shape, lambda i: (0,) * ref.ndim)

    def by_slot(ref):
        return pl.BlockSpec((size,) + ref.shape[1:], lambda i: (i,) + (0,) * (ref.ndim - 1))

    out = pl.pallas_call(
        functools.partial(arrival_kernel, peers, tp),
        out_shape=jax.ShapeDtypeStruct(query.shape, BF16),
        grid=(slots // size,),
        in_specs=[by_slot(query), by_slot(new)] + [fixed(g) for g in got],
        out_specs=by_slot(query),
        compiler_params=pltpu.CompilerParams(vmem_limit_bytes=48 * 2**20),
        name="arrivals",
    )(query, new, *got)
    return from_rows(out, arr_query.shape)


def shards(
    pre_codes,
    pre_scales,
    req_dest,
    req_blocks,
    res_codes,
    res_scales,
    res_len,
    res_query,
    res_new,
    arr_query,
    arr_new,
):
    peers = lax.axis_size("wide")
    tp = lax.axis_size("tp")
    chunks = pack(pre_codes, pre_scales, req_dest, req_blocks, peers, tp, peers * tp <= 16)
    got = exchange(chunks, peers, tp)
    res_out = resident(res_codes, res_scales, res_len, res_query, res_new)
    arr_out = arrivals(got, arr_query, arr_new, peers, tp)
    return (res_out, arr_out)


def solution(mesh):
    in_specs = (
        P(("groups", "wide"), None, "tp", None, None),
        P(("groups", "wide"), None, "tp", None, None),
        P(("groups", "wide")),
        P(("groups", "wide")),
        P(("groups", "wide"), None, None, "tp"),
        P(("groups", "wide"), None, None, "tp"),
        P(("groups", "wide")),
        P(("groups", "wide"), None, "tp"),
        P(("groups", "wide"), None, None, "tp"),
        P(("groups", "wide"), None, "tp"),
        P(("groups", "wide"), None, None, "tp"),
    )
    out_specs = (P(("groups", "wide"), None, "tp"), P(("groups", "wide"), None, "tp"))
    return jax.shard_map(shards, mesh=mesh, in_specs=in_specs, out_specs=out_specs, check_vma=False)
```

```python
import functools
import math

import jax
import jax.numpy as jnp
from jax import lax
from jax.experimental import pallas as pl
from jax.experimental.pallas import tpu as pltpu
from jax.sharding import PartitionSpec as P

KVH = 4
HD = 128
HQ = 64
GROUP = HQ // KVH
STEPS = 2

NEGATIVE = -1e30
EMPTY = 1024.0
SCORE_SCALE = 1.0 / math.sqrt(HD)

SWAPS = 4

BF16 = jnp.bfloat16
F32 = jnp.float32


def iota(shape, axis):
    return lax.broadcasted_iota(jnp.int32, shape, axis)


def dot_nt(a, b):
    return lax.dot_general(a, b, (((1,), (1,)), ((), ())), preferred_element_type=F32)


def dot_nn(a, b):
    return lax.dot_general(a, b, (((1,), (0,)), ((), ())), preferred_element_type=F32)


def whole(memory_space=pltpu.VMEM):
    return pl.BlockSpec(memory_space=memory_space)


def pack_kernel(tp, block_rows, dest_ref, blocks_ref, codes_ref, scales_ref, *refs):
    requests, tokens, heads = codes_ref.shape[:3]
    rows = 2 * tokens
    per_core = heads // tp
    apart = len(refs) > 1
    send_ref = refs[-1]
    send_ref[...] = jnp.full(send_ref.shape, EMPTY, BF16)
    row_block = iota((rows, HD), 0) // block_rows
    here = lax.axis_index("wide") * tp + lax.axis_index("tp") if apart else 0

    def place(r):
        held = row_block < blocks_ref[r]
        scales = scales_ref[r].astype(F32)
        for j in range(heads):
            codes = codes_ref[r, :, j].astype(F32).reshape(rows, HD)
            values = codes * scales[:, j : j + 1]
            values = jnp.where(held, values, EMPTY).astype(BF16)
            there = dest_ref[r] * tp + j // per_core
            if apart:
                there = jnp.bitwise_xor(there, here)
                there = (there % SWAPS) * SWAPS + there // SWAPS
            send_ref[there, j % per_core] = values

    if requests <= 8:
        for r in range(requests):
            place(r)
    else:
        lax.fori_loop(0, requests, lambda r, c: (place(r), c)[1], 0)
    if apart:
        for k, ref in enumerate(refs[:-1]):
            ref[...] = send_ref[k * SWAPS : (k + 1) * SWAPS]


def resident_kernel(first, len_ref, codes_ref, scales_ref, query_ref, new_ref, *refs):
    out_ref = refs[-1]
    slots, rows = codes_ref.shape[:2]
    heads = scales_ref.shape[2]
    tokens = rows // (2 * heads)
    queries = query_ref.shape[1]
    new_rows = new_ref.shape[1]

    from_scale = iota((rows, rows), 1)
    to_row = iota((rows, rows), 0)
    source = ((to_row % 2) * heads + (to_row // 2) % heads) * tokens + to_row // (2 * heads)
    spread = jnp.where(from_scale == source, 1.0, 0.0).astype(BF16)
    flat = jnp.concatenate(
        [scales_ref[:, p, h] for p in range(2) for h in range(heads)], axis=1
    )
    columns = dot_nt(spread, flat)

    col = iota((queries, rows), 1)
    row_head = iota((queries, rows), 0) // (queries // heads)
    is_key = (col % 2 == 0) & ((col // 2) % heads == row_head)
    col_token = jnp.where(is_key, col // (2 * heads), tokens)

    new_col = iota((queries, new_rows), 1)
    new_head = iota((queries, new_rows), 0) // (queries // heads)
    new_step = iota((queries, new_rows), 0) % STEPS
    new_ok = (
        (new_col % 2 == 0)
        & ((new_col // 2) % heads == new_head)
        & (new_col // (2 * heads) <= new_step)
    )

    for s in range(slots):
        cache = (codes_ref[s].astype(F32) * columns[:, s : s + 1]).astype(BF16)
        query = query_ref[s]
        new = new_ref[s]
        scores = jnp.where(
            col_token < len_ref[first + s], dot_nt(query, cache) * SCORE_SCALE, NEGATIVE
        )
        new_scores = jnp.where(new_ok, dot_nt(query, new) * SCORE_SCALE, NEGATIVE)
        top = jnp.maximum(
            jnp.max(scores, axis=1, keepdims=True), jnp.max(new_scores, axis=1, keepdims=True)
        )
        weights = jnp.exp(scores - top)
        new_weights = jnp.exp(new_scores - top)
        total = jnp.sum(weights, axis=1, keepdims=True) + jnp.sum(
            new_weights, axis=1, keepdims=True
        )
        weights = pltpu.roll(weights, 1, 1).astype(BF16)
        new_weights = jnp.concatenate(
            [jnp.zeros((queries, 1), F32), new_weights[:, : new_rows - 1]], axis=1
        ).astype(BF16)
        mixed = dot_nn(weights, cache) + dot_nn(new_weights, new)
        out_ref[s] = (mixed / total).astype(BF16)


def arrival_kernel(peers, tp, query_ref, new_ref, *refs):
    got_refs, out_ref = refs[:-1], refs[-1]
    apart = len(got_refs) > 1
    slots, heads, per_head = query_ref.shape[:3]
    chunk_rows = got_refs[0].shape[-2]
    rows = slots * per_head
    columns = peers * tp * chunk_rows
    sender_rows = tp * chunk_rows
    piece = min(columns, 256)

    if apart:
        chunks = [ref[0] for ref in got_refs[:SWAPS]]
        chunks += [ref[k] for ref in got_refs[SWAPS:] for k in range(SWAPS)]
        caches = [jnp.concatenate([chunk[h] for chunk in chunks], axis=0) for h in range(heads)]
        here = lax.axis_index("wide")
    else:
        caches = [got_refs[0][:, h].reshape(columns, HD) for h in range(heads)]

    def sender(index):
        return jnp.bitwise_xor(index, here) if apart else index

    ones = jnp.ones((8, HD), BF16)
    sums = dot_nt(ones, caches[0])
    col = iota((8, columns), 1)
    held = sums < EMPTY
    first = jnp.where(held & (col % sender_rows == 0), 1.0, 0.0).astype(BF16)
    before = jnp.where(
        sender(iota((piece, piece), 0) // sender_rows)
        < sender(iota((piece, piece), 1) // sender_rows),
        1.0,
        0.0,
    ).astype(BF16)
    base = jnp.zeros((8, 1), F32)
    ranks = []
    for p in range(0, columns, piece):
        part = first[:, p : p + piece]
        ranks.append(dot_nn(part, before) + base)
        if p + piece < columns:
            base = base + jnp.sum(part.astype(F32), axis=1, keepdims=True)
    rank = ranks[0] if len(ranks) == 1 else jnp.concatenate(ranks, axis=1)
    slot_of = jnp.where(held & (col % 2 == 0), rank, -1.0)[:1]
    first_slot = (pl.program_id(0) * slots).astype(F32)

    new_rows = new_ref.shape[0] * new_ref.shape[1] // heads
    row_slot = iota((rows, new_rows), 0) // per_head
    row_step = iota((rows, new_rows), 0) % STEPS
    new_col = iota((rows, new_rows), 1)
    new_ok = (
        (new_col % 2 == 0)
        & (new_col // (2 * STEPS) == row_slot)
        & ((new_col // 2) % STEPS <= row_step)
    )
    slot_rows = (iota((rows, 1), 0) // per_head).astype(F32) + first_slot
    mask = slot_of == slot_rows

    for h in range(heads):
        query = query_ref[:, h].reshape(rows, HD)
        new = jnp.concatenate(
            [
                new_ref[a, 2 * (f * heads + h) : 2 * (f * heads + h) + 2]
                for a in range(slots)
                for f in range(STEPS)
            ],
            axis=0,
        )
        cache = caches[h]
        scores = jnp.where(mask, dot_nt(query, cache) * SCORE_SCALE, NEGATIVE)
        new_scores = jnp.where(new_ok, dot_nt(query, new) * SCORE_SCALE, NEGATIVE)
        top = jnp.maximum(
            jnp.max(scores, axis=1, keepdims=True), jnp.max(new_scores, axis=1, keepdims=True)
        )
        weights = jnp.exp(scores - top)
        new_weights = jnp.exp(new_scores - top)
        total = jnp.sum(weights, axis=1, keepdims=True) + jnp.sum(
            new_weights, axis=1, keepdims=True
        )
        weights = pltpu.roll(weights, 1, 1).astype(BF16)
        new_weights = jnp.concatenate(
            [jnp.zeros((rows, 1), F32), new_weights[:, : new_rows - 1]], axis=1
        ).astype(BF16)
        mixed = dot_nn(weights, cache) + dot_nn(new_weights, new)
        out_ref[:, h] = (mixed / total).astype(BF16).reshape(slots, per_head, HD)


def pack(pre_codes, pre_scales, req_dest, req_blocks, peers, tp, apart):
    requests, blocks, block_tokens = pre_codes.shape[:3]
    tokens = blocks * block_tokens
    codes = pre_codes.reshape(requests, tokens, 2, KVH, HD).transpose(0, 1, 3, 2, 4)
    scales = pre_scales.reshape(requests, tokens * 2, KVH)
    chunk = (KVH // tp, tokens * 2, HD)
    send = (peers * tp,) + chunk
    return pl.pallas_call(
        functools.partial(pack_kernel, tp, 2 * block_tokens),
        out_shape=[jax.ShapeDtypeStruct((SWAPS,) + chunk, BF16)] * SWAPS
        if apart
        else [jax.ShapeDtypeStruct(send, BF16)],
        in_specs=[whole(pltpu.SMEM), whole(pltpu.SMEM), whole(), whole()],
        out_specs=[whole()] * (SWAPS if apart else 1),
        scratch_shapes=[pltpu.VMEM(send, BF16)] if apart else [],
        compiler_params=pltpu.CompilerParams(vmem_limit_bytes=16 * 2**20),
        name="pack",
    )(req_dest, req_blocks, codes, scales)


def swap(x, bits, peers, tp):
    pairs = [(i, i ^ bits) for i in range(peers * tp)]
    return lax.ppermute(x, ("wide", "tp"), pairs)


def exchange_low(chunks, peers, tp):
    return [chunks[0]] + [swap(chunks[k], k, peers, tp) for k in range(1, SWAPS)]


def exchange_high(chunks, peers, tp):
    got = list(chunks)
    for k in range(1, SWAPS):
        part = jnp.stack([chunk[k] for chunk in chunks])
        got.append(swap(part, k * SWAPS, peers, tp))
    return got


def query_rows(query):
    slots, steps, width = query.shape
    return query.reshape(slots, steps, width // HD, HD).transpose(0, 2, 1, 3)


def new_rows_of(new):
    slots, steps, pair, width = new.shape
    heads = width // HD
    return (
        new.reshape(slots, steps, pair, heads, HD)
        .transpose(0, 1, 3, 2, 4)
        .reshape(slots, steps * heads * pair, HD)
    )


def from_rows(out, shape):
    slots, steps, width = shape
    return out.reshape(slots, width // HD, steps, HD).transpose(0, 2, 1, 3).reshape(shape)


def resident(res_codes, res_scales, res_len, res_query, res_new, piece, pieces, before):
    slots, tokens, _, width = res_codes.shape
    heads = width // HD
    codes = (
        res_codes.reshape(slots, tokens, 2, heads, HD)
        .transpose(0, 1, 3, 2, 4)
        .reshape(slots, tokens * heads * 2, HD)
    )
    scales = res_scales.transpose(0, 2, 3, 1)
    query = query_rows(res_query).reshape(slots, heads * GROUP * STEPS, HD)
    new = new_rows_of(res_new)
    size = slots // pieces
    work = size * heads * GROUP * STEPS * tokens * heads * 2

    def part(ref):
        return pl.BlockSpec(
            (size,) + ref.shape[1:], lambda i: (piece,) + (0,) * (ref.ndim - 1)
        )

    ins = [codes, scales, query, new]
    out = pl.pallas_call(
        functools.partial(resident_kernel, piece * size),
        out_shape=jax.ShapeDtypeStruct(query.shape, BF16),
        grid=(1,),
        in_specs=[whole(pltpu.SMEM)] + [part(x) for x in ins] + [whole(pl.ANY)] * len(before),
        out_specs=part(query),
        input_output_aliases={5: 0} if before else {},
        cost_estimate=pl.CostEstimate(
            flops=4 * work * HD,
            bytes_accessed=2 * (codes.size + 2 * query.size) // pieces,
            transcendentals=work,
        ),
        compiler_params=pltpu.CompilerParams(vmem_limit_bytes=16 * 2**20),
        name="resident",
    )(res_len, *ins, *before)
    return out


def arrivals(got, arr_query, arr_new, peers, tp):
    slots, steps, width = arr_query.shape
    heads = width // (HD * GROUP)
    query = query_rows(arr_query).reshape(slots, heads, GROUP * steps, HD)
    new = new_rows_of(arr_new)
    size = max(n for n in range(1, 7) if slots % n == 0)

    def fixed(ref):
        return pl.BlockSpec(ref.shape, lambda i: (0,) * ref.ndim)

    def by_slot(ref):
        return pl.BlockSpec((size,) + ref.shape[1:], lambda i: (i,) + (0,) * (ref.ndim - 1))

    out = pl.pallas_call(
        functools.partial(arrival_kernel, peers, tp),
        out_shape=jax.ShapeDtypeStruct(query.shape, BF16),
        grid=(slots // size,),
        in_specs=[by_slot(query), by_slot(new)] + [fixed(g) for g in got],
        out_specs=by_slot(query),
        compiler_params=pltpu.CompilerParams(
            vmem_limit_bytes=(16 if peers * tp <= 16 else 48) * 2**20
        ),
        name="arrivals",
    )(query, new, *got)
    return from_rows(out, arr_query.shape)


def shards(
    pre_codes,
    pre_scales,
    req_dest,
    req_blocks,
    res_codes,
    res_scales,
    res_len,
    res_query,
    res_new,
    arr_query,
    arr_new,
):
    peers = lax.axis_size("wide")
    tp = lax.axis_size("tp")
    apart = peers * tp == SWAPS * SWAPS and tp < SWAPS
    res = (res_codes, res_scales, res_len, res_query, res_new)
    chunks = pack(pre_codes, pre_scales, req_dest, req_blocks, peers, tp, apart)
    if apart:
        near = exchange_low(chunks, peers, tp)
        out = resident(*res, 0, 2, [])
        got = exchange_high(near, peers, tp)
        out = resident(*res, 1, 2, [out])
    else:
        got = [lax.all_to_all(chunks[0], ("wide", "tp"), split_axis=0, concat_axis=0, tiled=True)]
        out = resident(*res, 0, 1, [])
    res_out = from_rows(out, res_query.shape)
    arr_out = arrivals(got, arr_query, arr_new, peers, tp)
    return (res_out, arr_out)


def solution(mesh):
    in_specs = (
        P(("groups", "wide"), None, "tp", None, None),
        P(("groups", "wide"), None, "tp", None, None),
        P(("groups", "wide")),
        P(("groups", "wide")),
        P(("groups", "wide"), None, None, "tp"),
        P(("groups", "wide"), None, None, "tp"),
        P(("groups", "wide")),
        P(("groups", "wide"), None, "tp"),
        P(("groups", "wide"), None, None, "tp"),
        P(("groups", "wide"), None, "tp"),
        P(("groups", "wide"), None, None, "tp"),
    )
    out_specs = (P(("groups", "wide"), None, "tp"), P(("groups", "wide"), None, "tp"))
    return jax.shard_map(shards, mesh=mesh, in_specs=in_specs, out_specs=out_specs, check_vma=False)
```

```python
import functools
import math

import jax
import jax.numpy as jnp
from jax import lax
from jax.experimental import pallas as pl
from jax.experimental.pallas import tpu as pltpu
from jax.sharding import PartitionSpec as P

KVH = 4
HD = 128
HQ = 64
GROUP = HQ // KVH
STEPS = 2

NEGATIVE = -1e30
EMPTY = 1024.0
SCORE_SCALE = 1.0 / math.sqrt(HD)

BF16 = jnp.bfloat16
F32 = jnp.float32


def iota(shape, axis):
    return lax.broadcasted_iota(jnp.int32, shape, axis)


def over(x, n):
    return jnp.right_shift(x, n.bit_length() - 1) if n & (n - 1) == 0 else x // n


def mod(x, n):
    return jnp.bitwise_and(x, n - 1) if n & (n - 1) == 0 else x % n


def dot_nt(a, b):
    return lax.dot_general(a, b, (((1,), (1,)), ((), ())), preferred_element_type=F32)


def dot_nn(a, b):
    return lax.dot_general(a, b, (((1,), (0,)), ((), ())), preferred_element_type=F32)


def top_of(*parts):
    return functools.reduce(jnp.maximum, [jnp.max(p, axis=1, keepdims=True) for p in parts])


def sum_of(*parts):
    return functools.reduce(jnp.add, [jnp.sum(p, axis=1, keepdims=True) for p in parts])


def to_values(weights):
    width = weights.shape[1]
    if width % HD:
        zero = jnp.zeros((weights.shape[0], 1), F32)
        return jnp.concatenate([zero, weights[:, : width - 1]], axis=1).astype(BF16)
    tiles = [pltpu.roll(weights[:, c : c + HD], 1, 1) for c in range(0, width, HD)]
    return jnp.concatenate(tiles, axis=1).astype(BF16)


def pack_kernel(
    tp, block_rows, dest_hbm, blocks_hbm, codes_hbm, scales_hbm, send_ref,
    dest_ref, blocks_ref, codes_ref, scales_ref, sems,
):
    pairs = [
        (codes_hbm, codes_ref), (scales_hbm, scales_ref),
        (dest_hbm, dest_ref), (blocks_hbm, blocks_ref),
    ]
    copies = [pltpu.make_async_copy(a, b, sems.at[i]) for i, (a, b) in enumerate(pairs)]
    for copy in copies:
        copy.start()
    requests, tokens, heads = codes_ref.shape[:3]
    rows = 2 * tokens
    per_core = heads // tp
    last = send_ref.shape[0] - 1
    send_ref[...] = jnp.full(send_ref.shape, EMPTY, BF16)
    row_block = over(iota((rows, HD), 0), block_rows)
    for copy in copies:
        copy.wait()

    def place(r):
        there = last - dest_ref[r] * tp
        held = row_block < blocks_ref[r]
        scales = scales_ref[r].astype(F32)
        for j in range(heads):
            codes = codes_ref[r, :, j].astype(F32).reshape(rows, HD)
            values = codes * scales[:, j : j + 1]
            values = jnp.where(held, values, EMPTY).astype(BF16)
            send_ref[there - j // per_core, j % per_core] = values

    if requests <= 8:
        for r in range(requests):
            place(r)
    else:
        lax.fori_loop(0, requests, lambda r, c: (place(r), c)[1], 0)


def resident_kernel(len_ref, codes_ref, scales_ref, query_ref, new_ref, out_ref):
    slots, rows = codes_ref.shape[:2]
    heads = scales_ref.shape[2]
    tokens = rows // (2 * heads)
    queries = query_ref.shape[1]
    new_rows = new_ref.shape[1]

    row = iota((rows, HD), 0)
    source = (mod(row, 2) * heads + mod(over(row, 2), heads)) * tokens + over(row, 2 * heads)
    lane = iota((rows, HD), 1)
    spread = jnp.concatenate(
        [jnp.where(source == lane + c, 1.0, 0.0).astype(BF16) for c in range(0, rows, HD)],
        axis=1,
    )
    flat = jnp.concatenate(
        [scales_ref[:, p, h] for p in range(2) for h in range(heads)], axis=1
    )
    columns = dot_nt(spread, flat).astype(BF16)

    col = iota((queries, rows), 1)
    row_head = over(iota((queries, rows), 0), queries // heads)
    is_key = (mod(col, 2) == 0) & (mod(over(col, 2), heads) == row_head)
    col_token = jnp.where(is_key, over(col, 2 * heads), tokens)

    new_col = iota((queries, new_rows), 1)
    new_row = iota((queries, new_rows), 0)
    new_ok = (
        (mod(new_col, 2) == 0)
        & (mod(over(new_col, 2), heads) == over(new_row, queries // heads))
        & (over(new_col, 2 * heads) <= mod(new_row, STEPS))
    )

    every = range(slots)
    caches = [codes_ref[s] * columns[:, s : s + 1] for s in every]
    scores = [dot_nt(query_ref[s], caches[s]) for s in every]
    new_scores = [dot_nt(query_ref[s], new_ref[s]) for s in every]
    scores = [jnp.where(col_token < len_ref[s], scores[s] * SCORE_SCALE, NEGATIVE) for s in every]
    new_scores = [jnp.where(new_ok, new_scores[s] * SCORE_SCALE, NEGATIVE) for s in every]
    top = [top_of(scores[s], new_scores[s]) for s in every]
    weights = [jnp.exp(scores[s] - top[s]) for s in every]
    new_weights = [jnp.exp(new_scores[s] - top[s]) for s in every]
    total = [sum_of(weights[s], new_weights[s]) for s in every]
    mixed = [
        dot_nn(to_values(weights[s]), caches[s]) + dot_nn(to_values(new_weights[s]), new_ref[s])
        for s in every
    ]
    for s in every:
        out_ref[s] = (mixed[s] / total[s]).astype(BF16)


def arrival_kernel(tp, got_ref, query_ref, new_ref, out_ref):
    chunks, heads, chunk_rows = got_ref.shape[:3]
    slots, _, per_head = query_ref.shape[:3]
    rows = slots * per_head
    columns = chunks * chunk_rows
    sender_rows = tp * chunk_rows
    piece = min(columns, 256)

    caches = [got_ref[:, h].reshape(columns, HD) for h in range(heads)]
    queries = [query_ref[:, h].reshape(rows, HD) for h in range(heads)]
    new = new_ref[...].reshape(slots * new_ref.shape[1], HD)
    sums = dot_nt(jnp.ones((8, HD), BF16), caches[0])
    scores = [dot_nt(queries[h], caches[h]) for h in range(heads)]
    new_scores = [dot_nt(queries[h], new) for h in range(heads)]

    col = iota((8, columns), 1)
    held = sums < EMPTY
    first = jnp.where(held & (mod(col, sender_rows) == 0), 1.0, 0.0).astype(BF16)
    before = jnp.where(
        over(iota((piece, piece), 0), sender_rows) > over(iota((piece, piece), 1), sender_rows),
        1.0,
        0.0,
    ).astype(BF16)
    base = jnp.zeros((8, 1), F32)
    ranks = []
    for p in reversed(range(0, columns, piece)):
        part = first[:, p : p + piece]
        ranks.insert(0, dot_nn(part, before) + base)
        if p:
            base = base + jnp.sum(part.astype(F32), axis=1, keepdims=True)
    rank = ranks[0] if len(ranks) == 1 else jnp.concatenate(ranks, axis=1)
    slot_of = jnp.where(held & (mod(col, 2) == 0), rank, -1.0)[:1]
    first_slot = (pl.program_id(0) * slots).astype(F32)
    mine = [slot_of == first_slot + a for a in range(slots)]

    new_col = iota((rows, new.shape[0]), 1)
    new_row = iota((rows, new.shape[0]), 0)
    new_here = (
        (mod(new_col, 2) == 0)
        & (over(new_col, 2 * heads * STEPS) == over(new_row, per_head))
        & (mod(over(new_col, 2 * heads), STEPS) <= mod(new_row, STEPS))
    )
    new_head = jnp.where(new_here, mod(over(new_col, 2), heads), heads)

    every = range(heads)
    scores = [
        jnp.concatenate(
            [
                jnp.where(mine[a], scores[h][a * per_head : (a + 1) * per_head] * SCORE_SCALE, NEGATIVE)
                for a in range(slots)
            ],
            axis=0,
        )
        for h in every
    ]
    new_scores = [jnp.where(new_head == h, new_scores[h] * SCORE_SCALE, NEGATIVE) for h in every]
    top = [top_of(scores[h], new_scores[h]) for h in every]
    weights = [jnp.exp(scores[h] - top[h]) for h in every]
    new_weights = [jnp.exp(new_scores[h] - top[h]) for h in every]
    total = [sum_of(weights[h], new_weights[h]) for h in every]
    mixed = [
        dot_nn(to_values(weights[h]), caches[h]) + dot_nn(to_values(new_weights[h]), new)
        for h in every
    ]
    for h in every:
        out_ref[:, h] = (mixed[h] / total[h]).astype(BF16).reshape(slots, per_head, HD)


def whole(memory_space=pltpu.VMEM):
    return pl.BlockSpec(memory_space=memory_space)


def in_hbm(x):
    return pltpu.with_memory_space_constraint(x, pltpu.HBM)


def limit(mib):
    return pltpu.CompilerParams(vmem_limit_bytes=mib * 2**20)


def pack(pre_codes, pre_scales, req_dest, req_blocks, peers, tp):
    requests, blocks, block_tokens = pre_codes.shape[:3]
    tokens = blocks * block_tokens
    codes = pre_codes.reshape(requests, tokens, 2, KVH, HD).transpose(0, 1, 3, 2, 4)
    scales = pre_scales.reshape(requests, tokens * 2, KVH)
    return pl.pallas_call(
        functools.partial(pack_kernel, tp, 2 * block_tokens),
        out_shape=pltpu.VMEM((peers * tp, KVH // tp, tokens * 2, HD), BF16),
        in_specs=[whole(pltpu.HBM)] * 4,
        out_specs=whole(),
        scratch_shapes=[
            pltpu.SMEM(req_dest.shape, jnp.int32),
            pltpu.SMEM(req_blocks.shape, jnp.int32),
            pltpu.VMEM(codes.shape, BF16),
            pltpu.VMEM(scales.shape, BF16),
            pltpu.SemaphoreType.DMA((4,)),
        ],
        compiler_params=limit(16),
        name="pack",
    )(*[in_hbm(x) for x in (req_dest, req_blocks, codes, scales)])


def query_rows(query):
    slots, steps, width = query.shape
    return query.reshape(slots, steps, width // HD, HD).transpose(0, 2, 1, 3)


def new_rows_of(new):
    slots, steps, pair, width = new.shape
    heads = width // HD
    return (
        new.reshape(slots, steps, pair, heads, HD)
        .transpose(0, 1, 3, 2, 4)
        .reshape(slots, steps * heads * pair, HD)
    )


def from_rows(out, shape):
    slots, steps, width = shape
    return out.reshape(slots, width // HD, steps, HD).transpose(0, 2, 1, 3).reshape(shape)


def resident(res_codes, res_scales, res_len, res_query, res_new):
    slots, tokens, _, width = res_codes.shape
    heads = width // HD
    codes = (
        res_codes.reshape(slots, tokens, 2, heads, HD)
        .transpose(0, 1, 3, 2, 4)
        .reshape(slots, tokens * heads * 2, HD)
    )
    scales = res_scales.transpose(0, 2, 3, 1)
    query = query_rows(res_query).reshape(slots, heads * GROUP * STEPS, HD)
    work = slots * heads * GROUP * STEPS * tokens * heads * 2
    out = pl.pallas_call(
        resident_kernel,
        out_shape=jax.ShapeDtypeStruct(query.shape, BF16),
        in_specs=[whole(pltpu.SMEM)] + [whole()] * 4,
        out_specs=whole(),
        cost_estimate=pl.CostEstimate(
            flops=4 * work * HD,
            bytes_accessed=2 * (codes.size + 2 * query.size),
            transcendentals=work,
        ),
        compiler_params=limit(16),
        name="resident",
    )(in_hbm(res_len), codes, scales, query, new_rows_of(res_new))
    return from_rows(out, res_query.shape)


def arrivals(got, arr_query, arr_new, tp):
    slots, steps, width = arr_query.shape
    heads = width // (HD * GROUP)
    query = query_rows(arr_query).reshape(slots, heads, GROUP * steps, HD)
    new = new_rows_of(arr_new)
    size = max(n for n in range(1, 7) if slots % n == 0)
    small = got.size <= 2**18
    out = pl.pallas_call(
        functools.partial(arrival_kernel, tp),
        out_shape=jax.ShapeDtypeStruct(query.shape, BF16),
        grid=(slots // size,),
        in_specs=[
            pl.BlockSpec(got.shape, lambda i: (0, 0, 0, 0)),
            pl.BlockSpec((size,) + query.shape[1:], lambda i: (i, 0, 0, 0)),
            pl.BlockSpec((size,) + new.shape[1:], lambda i: (i, 0, 0)),
        ],
        out_specs=pl.BlockSpec((size,) + query.shape[1:], lambda i: (i, 0, 0, 0)),
        compiler_params=limit(16 if small else 48),
        name="arrivals",
    )(got, query, new)
    return from_rows(out, arr_query.shape)


def shards(
    pre_codes,
    pre_scales,
    req_dest,
    req_blocks,
    res_codes,
    res_scales,
    res_len,
    res_query,
    res_new,
    arr_query,
    arr_new,
):
    peers = lax.axis_size("wide")
    tp = lax.axis_size("tp")
    send = pack(pre_codes, pre_scales, req_dest, req_blocks, peers, tp)
    got = lax.all_to_all(
        send,
        ("wide", "tp"),
        split_axis=0,
        concat_axis=0,
        tiled=True,
        axis_index_groups=[list(reversed(range(peers * tp)))],
    )
    res_out = resident(res_codes, res_scales, res_len, res_query, res_new)
    arr_out = arrivals(got, arr_query, arr_new, tp)
    return (res_out, arr_out)


def solution(mesh):
    in_specs = (
        P(("groups", "wide"), None, "tp", None, None),
        P(("groups", "wide"), None, "tp", None, None),
        P(("groups", "wide")),
        P(("groups", "wide")),
        P(("groups", "wide"), None, None, "tp"),
        P(("groups", "wide"), None, None, "tp"),
        P(("groups", "wide")),
        P(("groups", "wide"), None, "tp"),
        P(("groups", "wide"), None, None, "tp"),
        P(("groups", "wide"), None, "tp"),
        P(("groups", "wide"), None, None, "tp"),
    )
    out_specs = (P(("groups", "wide"), None, "tp"), P(("groups", "wide"), None, "tp"))
    return jax.shard_map(shards, mesh=mesh, in_specs=in_specs, out_specs=out_specs, check_vma=False)
```

```python
import functools
import math

import jax
import jax.numpy as jnp
from jax import lax
from jax.experimental import pallas as pl
from jax.experimental.pallas import tpu as pltpu
from jax.sharding import PartitionSpec as P

KVH = 4
HD = 128
HQ = 64
GROUP = HQ // KVH
STEPS = 2

NEGATIVE = -1e30
EMPTY = 1024.0
SCORE_SCALE = 1.0 / math.sqrt(HD)

BF16 = jnp.bfloat16
F32 = jnp.float32


def iota(shape, axis):
    return lax.broadcasted_iota(jnp.int32, shape, axis)


def over(x, n):
    return jnp.right_shift(x, n.bit_length() - 1) if n & (n - 1) == 0 else x // n


def mod(x, n):
    return jnp.bitwise_and(x, n - 1) if n & (n - 1) == 0 else x % n


def dot_nt(a, b):
    return lax.dot_general(a, b, (((1,), (1,)), ((), ())), preferred_element_type=F32)


def dot_nn(a, b):
    return lax.dot_general(a, b, (((1,), (0,)), ((), ())), preferred_element_type=F32)


def top_of(*parts):
    return functools.reduce(jnp.maximum, [jnp.max(p, axis=1, keepdims=True) for p in parts])


def sum_of(*parts):
    return functools.reduce(jnp.add, [jnp.sum(p, axis=1, keepdims=True) for p in parts])


def to_values(weights):
    tiles = [pltpu.roll(weights[:, c : c + HD], 1, 1) for c in range(0, weights.shape[1], HD)]
    return jnp.concatenate(tiles, axis=1).astype(BF16)


def values_up(rows):
    return pltpu.roll(rows.astype(F32), rows.shape[0] - 1, 0).astype(BF16)


def pack_kernel(
    tp, heads, block_rows, dest_hbm, blocks_hbm, codes_hbm, scales_hbm, cache_hbm,
    send_ref, cache_ref, dest_ref, blocks_ref, codes_ref, scales_ref, sems,
):
    pairs = [
        (codes_hbm, codes_ref), (scales_hbm, scales_ref),
        (dest_hbm, dest_ref), (blocks_hbm, blocks_ref), (cache_hbm, cache_ref),
    ]
    copies = [pltpu.make_async_copy(a, b, sems.at[i]) for i, (a, b) in enumerate(pairs)]
    for copy in copies:
        copy.start()
    requests, all_rows = codes_ref.shape[:2]
    rows = all_rows // heads
    per_core = heads // tp
    last = send_ref.shape[0] - 1
    send_ref[...] = jnp.full(send_ref.shape, EMPTY, BF16)
    row_block = over(iota((rows, HD), 0), block_rows)
    to_row = iota((all_rows, all_rows), 0)
    from_row = iota((all_rows, all_rows), 1)
    source = over(mod(to_row, rows), 2) * (2 * heads) + over(to_row, rows) * 2 + mod(to_row, 2)
    by_head = jnp.where(from_row == source, 1.0, 0.0).astype(BF16)
    for copy in copies[:-1]:
        copy.wait()

    def place(r):
        there = last - dest_ref[r] * tp
        held = row_block < blocks_ref[r]
        codes = dot_nn(by_head, codes_ref[r])
        scales = scales_ref[r].astype(F32)
        for j in range(heads):
            values = codes[j * rows : (j + 1) * rows] * scales[:, j : j + 1]
            values = jnp.where(held, values, EMPTY).astype(BF16)
            send_ref[there - j // per_core, j % per_core] = values

    if requests <= 8:
        for r in range(requests):
            place(r)
    else:
        lax.fori_loop(0, requests, lambda r, c: (place(r), c)[1], 0)
    copies[-1].wait()


def resident_kernel(len_ref, codes_ref, scales_ref, query_ref, new_ref, out_ref):
    slots, rows = codes_ref.shape[:2]
    heads = scales_ref.shape[2]
    tokens = rows // (2 * heads)
    queries = query_ref.shape[1]
    new_rows = new_ref.shape[0]

    row = iota((rows, HD), 0)
    source = (mod(row, 2) * heads + mod(over(row, 2), heads)) * tokens + over(row, 2 * heads)
    lane = iota((rows, HD), 1)
    spread = jnp.concatenate(
        [jnp.where(source == lane + c, 1.0, 0.0).astype(BF16) for c in range(0, rows, HD)],
        axis=1,
    )
    flat = jnp.concatenate(
        [scales_ref[:, p, h] for p in range(2) for h in range(heads)], axis=1
    )
    columns = dot_nt(spread, flat).astype(BF16)

    col = iota((queries, rows), 1)
    row_head = over(iota((queries, rows), 0), queries // heads)
    is_key = (mod(col, 2) == 0) & (mod(over(col, 2), heads) == row_head)
    col_token = jnp.where(is_key, over(col, 2 * heads), tokens)

    new_col = iota((queries, new_rows), 1)
    new_row = iota((queries, new_rows), 0)
    new_ok = (
        (mod(new_col, 2) == 0)
        & (mod(over(new_col, 2), heads) == over(new_row, queries // heads))
        & (mod(over(new_col, 2 * heads), STEPS) <= mod(new_row, STEPS))
    )
    new_slot = jnp.where(new_ok, over(new_col, 2 * heads * STEPS), slots)

    every = range(slots)
    new = new_ref[...]
    new_all = dot_nt(query_ref[...].reshape(slots * queries, HD), new)
    caches = [codes_ref[s] * columns[:, s : s + 1] for s in every]
    scores = [dot_nt(query_ref[s], caches[s]) for s in every]
    scores = [jnp.where(col_token < len_ref[s], scores[s] * SCORE_SCALE, NEGATIVE) for s in every]
    new_scores = [
        jnp.where(new_slot == s, new_all[s * queries : (s + 1) * queries] * SCORE_SCALE, NEGATIVE)
        for s in every
    ]
    top = [top_of(scores[s], new_scores[s]) for s in every]
    weights = [jnp.exp(scores[s] - top[s]) for s in every]
    new_weights = [jnp.exp(new_scores[s] - top[s]) for s in every]
    total = [sum_of(weights[s], new_weights[s]) for s in every]
    new_mixed = dot_nn(jnp.concatenate(new_weights, axis=0).astype(BF16), values_up(new))
    mixed = [
        dot_nn(to_values(weights[s]), caches[s]) + new_mixed[s * queries : (s + 1) * queries]
        for s in every
    ]
    for s in every:
        out_ref[s] = (mixed[s] * (1.0 / total[s])).astype(BF16)


def arrival_kernel(
    tp, got_ref, query_ref, new_ref, done_ref, out_hbm, done_hbm, out_ref, sems
):
    step = pl.program_id(0)
    hand_on = pltpu.make_async_copy(done_ref, done_hbm, sems.at[0])
    pl.when(step == 0)(hand_on.start)

    chunks, heads, chunk_rows = got_ref.shape[:3]
    slots, _, per_head = query_ref.shape[:3]
    rows = slots * per_head
    columns = chunks * chunk_rows
    sender_rows = tp * chunk_rows
    piece = min(columns, 256)
    every = range(heads)

    caches = [got_ref[:, h].reshape(columns, HD) for h in every]
    queries = [query_ref[:, h].reshape(rows, HD) for h in every]
    new = new_ref[...]
    ones = jnp.ones((16, HD), BF16)
    scores = [dot_nt(jnp.concatenate([ones, queries[0]], axis=0), caches[0])]
    sums, scores[0] = scores[0][:8], scores[0][16:]
    scores += [dot_nt(queries[h], caches[h]) for h in every[1:]]
    new_all = dot_nt(jnp.concatenate(queries, axis=0), new)

    col = iota((8, columns), 1)
    held = sums < EMPTY
    first = jnp.where(held & (mod(col, sender_rows) == 0), 1.0, 0.0).astype(BF16)
    before = jnp.where(
        over(iota((piece, piece), 0), sender_rows) > over(iota((piece, piece), 1), sender_rows),
        1.0,
        0.0,
    ).astype(BF16)
    base = jnp.zeros((8, 1), F32)
    ranks = []
    for p in reversed(range(0, columns, piece)):
        part = first[:, p : p + piece]
        ranks.insert(0, dot_nn(part, before) + base)
        if p:
            base = base + jnp.sum(part.astype(F32), axis=1, keepdims=True)
    rank = ranks[0] if len(ranks) == 1 else jnp.concatenate(ranks, axis=1)
    slot_of = jnp.where(held & (mod(col, 2) == 0), rank, -1.0)[:1]
    first_slot = (step * slots).astype(F32)
    mine = [slot_of == first_slot + a for a in range(slots)]

    new_col = iota((rows, new.shape[0]), 1)
    new_row = iota((rows, new.shape[0]), 0)
    new_here = (
        (mod(new_col, 2) == 0)
        & (over(new_col, 2 * heads * STEPS) == over(new_row, per_head))
        & (mod(over(new_col, 2 * heads), STEPS) <= mod(new_row, STEPS))
    )
    new_head = jnp.where(new_here, mod(over(new_col, 2), heads), heads)

    scores = [
        jnp.concatenate(
            [
                jnp.where(mine[a], scores[h][a * per_head : (a + 1) * per_head] * SCORE_SCALE, NEGATIVE)
                for a in range(slots)
            ],
            axis=0,
        )
        for h in every
    ]
    new_scores = [
        jnp.where(new_head == h, new_all[h * rows : (h + 1) * rows] * SCORE_SCALE, NEGATIVE)
        for h in every
    ]
    top = [top_of(scores[h], new_scores[h]) for h in every]
    weights = [jnp.exp(scores[h] - top[h]) for h in every]
    new_weights = [jnp.exp(new_scores[h] - top[h]) for h in every]
    total = [sum_of(weights[h], new_weights[h]) for h in every]
    new_mixed = dot_nn(jnp.concatenate(new_weights, axis=0).astype(BF16), values_up(new))
    copies = []
    for h in every:
        mixed = dot_nn(to_values(weights[h]), caches[h]) + new_mixed[h * rows : (h + 1) * rows]
        out_ref[h] = (mixed * (1.0 / total[h])).astype(BF16).reshape(slots, per_head, HD)
        there = out_hbm.at[pl.ds(step * slots, slots), h]
        copies.append(pltpu.make_async_copy(out_ref.at[h], there, sems.at[1 + h]))
        copies[-1].start()
    for copy in copies:
        copy.wait()
    pl.when(step == pl.num_programs(0) - 1)(hand_on.wait)


def whole(memory_space=pltpu.VMEM):
    return pl.BlockSpec(memory_space=memory_space)


def in_hbm(x):
    return pltpu.with_memory_space_constraint(x, pltpu.HBM)


def limit(mib):
    return pltpu.CompilerParams(vmem_limit_bytes=mib * 2**20)


def pack(pre_codes, pre_scales, req_dest, req_blocks, cache, peers, tp):
    requests, blocks, block_tokens = pre_codes.shape[:3]
    tokens = blocks * block_tokens
    codes = (
        pre_codes.reshape(requests, tokens, 2, KVH, HD)
        .transpose(0, 1, 3, 2, 4)
        .reshape(requests, tokens * KVH * 2, HD)
    )
    scales = pre_scales.reshape(requests, tokens * 2, KVH)
    ins = [req_dest, req_blocks, codes, scales, cache]
    return pl.pallas_call(
        functools.partial(pack_kernel, tp, KVH, 2 * block_tokens),
        out_shape=[
            pltpu.VMEM((peers * tp, KVH // tp, tokens * 2, HD), BF16),
            pltpu.VMEM(cache.shape, BF16),
        ],
        in_specs=[whole(pltpu.HBM)] * len(ins),
        out_specs=[whole()] * 2,
        scratch_shapes=[
            pltpu.SMEM(req_dest.shape, jnp.int32),
            pltpu.SMEM(req_blocks.shape, jnp.int32),
            pltpu.VMEM(codes.shape, BF16),
            pltpu.VMEM(scales.shape, BF16),
            pltpu.SemaphoreType.DMA((len(ins),)),
        ],
        compiler_params=limit(16),
        name="pack",
    )(*[in_hbm(x) for x in ins])


def cache_rows(codes):
    slots, tokens, _, width = codes.shape
    heads = width // HD
    return (
        codes.reshape(slots, tokens, 2, heads, HD)
        .transpose(0, 1, 3, 2, 4)
        .reshape(slots, tokens * heads * 2, HD)
    )


def query_rows(query):
    slots, steps, width = query.shape
    return query.reshape(slots, steps, width // HD, HD).transpose(0, 2, 1, 3)


def new_rows_of(new):
    slots, steps, pair, width = new.shape
    heads = width // HD
    return (
        new.reshape(slots, steps, pair, heads, HD)
        .transpose(0, 1, 3, 2, 4)
        .reshape(slots * steps * heads * pair, HD)
    )


def from_rows(out, shape):
    slots, steps, width = shape
    return out.reshape(slots, width // HD, steps, HD).transpose(0, 2, 1, 3).reshape(shape)


def resident(codes, res_scales, res_len, res_query, res_new):
    slots, rows = codes.shape[:2]
    heads = res_scales.shape[-1]
    scales = res_scales.transpose(0, 2, 3, 1)
    query = query_rows(res_query).reshape(slots, heads * GROUP * STEPS, HD)
    work = query.shape[0] * query.shape[1] * rows
    return pl.pallas_call(
        resident_kernel,
        out_shape=pltpu.VMEM(query.shape, BF16),
        in_specs=[whole(pltpu.SMEM)] + [whole()] * 4,
        out_specs=whole(),
        cost_estimate=pl.CostEstimate(
            flops=4 * work * HD,
            bytes_accessed=2 * (codes.size + 2 * query.size),
            transcendentals=work,
        ),
        compiler_params=limit(16),
        name="resident",
    )(in_hbm(res_len), codes, scales, query, new_rows_of(res_new))


def arrivals(got, arr_query, arr_new, done, tp):
    slots, steps, width = arr_query.shape
    heads = width // (HD * GROUP)
    query = query_rows(arr_query).reshape(slots, heads, GROUP * steps, HD)
    new = new_rows_of(arr_new)
    size = max(n for n in range(1, 7) if slots % n == 0)
    small = got.size <= 2**18
    return pl.pallas_call(
        functools.partial(arrival_kernel, tp),
        out_shape=[
            jax.ShapeDtypeStruct(query.shape, BF16),
            jax.ShapeDtypeStruct(done.shape, BF16),
        ],
        grid=(slots // size,),
        in_specs=[
            pl.BlockSpec(got.shape, lambda i: (0, 0, 0, 0)),
            pl.BlockSpec((size,) + query.shape[1:], lambda i: (i, 0, 0, 0)),
            pl.BlockSpec((new.shape[0] // slots * size, HD), lambda i: (i, 0)),
            whole(),
        ],
        out_specs=[whole(pltpu.HBM)] * 2,
        scratch_shapes=[
            pltpu.VMEM((heads, size) + query.shape[2:], BF16),
            pltpu.SemaphoreType.DMA((1 + heads,)),
        ],
        compiler_params=limit(16 if small else 48),
        name="arrivals",
    )(got, query, new, done)


def shards(
    pre_codes,
    pre_scales,
    req_dest,
    req_blocks,
    res_codes,
    res_scales,
    res_len,
    res_query,
    res_new,
    arr_query,
    arr_new,
):
    peers = lax.axis_size("wide")
    tp = lax.axis_size("tp")
    send, cache = pack(
        pre_codes, pre_scales, req_dest, req_blocks, cache_rows(res_codes), peers, tp
    )
    got = lax.all_to_all(
        send,
        ("wide", "tp"),
        split_axis=0,
        concat_axis=0,
        tiled=True,
        axis_index_groups=[list(reversed(range(peers * tp)))],
    )
    done = resident(cache, res_scales, res_len, res_query, res_new)
    arr_out, res_out = arrivals(got, arr_query, arr_new, done, tp)
    return (from_rows(res_out, res_query.shape), from_rows(arr_out, arr_query.shape))


def solution(mesh):
    in_specs = (
        P(("groups", "wide"), None, "tp", None, None),
        P(("groups", "wide"), None, "tp", None, None),
        P(("groups", "wide")),
        P(("groups", "wide")),
        P(("groups", "wide"), None, None, "tp"),
        P(("groups", "wide"), None, None, "tp"),
        P(("groups", "wide")),
        P(("groups", "wide"), None, "tp"),
        P(("groups", "wide"), None, None, "tp"),
        P(("groups", "wide"), None, "tp"),
        P(("groups", "wide"), None, None, "tp"),
    )
    out_specs = (P(("groups", "wide"), None, "tp"), P(("groups", "wide"), None, "tp"))
    return jax.shard_map(shards, mesh=mesh, in_specs=in_specs, out_specs=out_specs, check_vma=False)
```

```python
import functools
import math

import jax
import jax.numpy as jnp
from jax import lax
from jax.experimental import pallas as pl
from jax.experimental.pallas import tpu as pltpu
from jax.sharding import PartitionSpec as P

KVH = 4
HD = 128
HQ = 64
GROUP = HQ // KVH
STEPS = 2

NEGATIVE = -1e30
EMPTY = 1024.0
SCORE_SCALE = 1.0 / math.sqrt(HD)

BF16 = jnp.bfloat16
F32 = jnp.float32


def iota(shape, axis):
    return lax.broadcasted_iota(jnp.int32, shape, axis)


def over(x, n):
    return jnp.right_shift(x, n.bit_length() - 1) if n & (n - 1) == 0 else x // n


def mod(x, n):
    return jnp.bitwise_and(x, n - 1) if n & (n - 1) == 0 else x % n


def dot_nt(a, b):
    return lax.dot_general(a, b, (((1,), (1,)), ((), ())), preferred_element_type=F32)


def dot_nn(a, b):
    return lax.dot_general(a, b, (((1,), (0,)), ((), ())), preferred_element_type=F32)


def top_of(*parts):
    return functools.reduce(jnp.maximum, [jnp.max(p, axis=1, keepdims=True) for p in parts])


def sum_of(*parts):
    return functools.reduce(jnp.add, [jnp.sum(p, axis=1, keepdims=True) for p in parts])


def to_values(weights):
    tiles = [pltpu.roll(weights[:, c : c + HD], 1, 1) for c in range(0, weights.shape[1], HD)]
    return jnp.concatenate(tiles, axis=1).astype(BF16)


def values_up(rows):
    return pltpu.roll(rows.astype(F32), rows.shape[0] - 1, 0).astype(BF16)


def pack_kernel(
    tp, heads, block_rows, dest_hbm, blocks_hbm, codes_hbm, scales_hbm, send_ref,
    dest_ref, blocks_ref, codes_ref, scales_ref, sems,
):
    pairs = [
        (codes_hbm, codes_ref), (scales_hbm, scales_ref),
        (dest_hbm, dest_ref), (blocks_hbm, blocks_ref),
    ]
    copies = [pltpu.make_async_copy(a, b, sems.at[i]) for i, (a, b) in enumerate(pairs)]
    for copy in copies:
        copy.start()
    requests, all_rows = codes_ref.shape[:2]
    rows = all_rows // heads
    per_core = heads // tp
    peers = send_ref.shape[0] // tp
    send_ref[...] = jnp.full(send_ref.shape, EMPTY, BF16)
    row_block = over(iota((rows, HD), 0), block_rows)
    to_row = iota((all_rows, all_rows), 0)
    from_row = iota((all_rows, all_rows), 1)
    source = over(mod(to_row, rows), 2) * (2 * heads) + over(to_row, rows) * 2 + mod(to_row, 2)
    by_head = jnp.where(from_row == source, 1.0, 0.0).astype(BF16)
    for copy in copies:
        copy.wait()

    def place(r):
        there = lax.rem(dest_ref[r] + (peers - peers // 2), peers) * tp
        held = row_block < blocks_ref[r]
        codes = dot_nn(by_head, codes_ref[r])
        scales = scales_ref[r].astype(F32)
        for j in range(heads):
            values = codes[j * rows : (j + 1) * rows] * scales[:, j : j + 1]
            values = jnp.where(held, values, EMPTY).astype(BF16)
            send_ref[there + j // per_core, j % per_core] = values

    if requests <= 8:
        for r in range(requests):
            place(r)
    else:
        lax.fori_loop(0, requests, lambda r, c: (place(r), c)[1], 0)


def resident_kernel(len_ref, codes_ref, scales_ref, query_ref, new_ref, out_ref):
    slots, rows = codes_ref.shape[:2]
    heads = scales_ref.shape[2]
    tokens = rows // (2 * heads)
    queries = query_ref.shape[1]
    new_rows = new_ref.shape[0]

    row = iota((rows, HD), 0)
    source = (mod(row, 2) * heads + mod(over(row, 2), heads)) * tokens + over(row, 2 * heads)
    lane = iota((rows, HD), 1)
    spread = jnp.concatenate(
        [jnp.where(source == lane + c, 1.0, 0.0).astype(BF16) for c in range(0, rows, HD)],
        axis=1,
    )
    flat = jnp.concatenate(
        [scales_ref[:, p, h] for p in range(2) for h in range(heads)], axis=1
    )
    columns = dot_nt(spread, flat).astype(BF16)

    col = iota((queries, rows), 1)
    row_head = over(iota((queries, rows), 0), queries // heads)
    is_key = (mod(col, 2) == 0) & (mod(over(col, 2), heads) == row_head)
    col_token = jnp.where(is_key, over(col, 2 * heads), tokens)

    new_col = iota((queries, new_rows), 1)
    new_row = iota((queries, new_rows), 0)
    new_ok = (
        (mod(new_col, 2) == 0)
        & (mod(over(new_col, 2), heads) == over(new_row, queries // heads))
        & (mod(over(new_col, 2 * heads), STEPS) <= mod(new_row, STEPS))
    )
    new_slot = jnp.where(new_ok, over(new_col, 2 * heads * STEPS), slots)

    every = range(slots)
    new = new_ref[...]
    new_all = dot_nt(query_ref[...].reshape(slots * queries, HD), new)
    caches = [codes_ref[s] * columns[:, s : s + 1] for s in every]
    scores = [dot_nt(query_ref[s], caches[s]) for s in every]
    scores = [jnp.where(col_token < len_ref[s], scores[s] * SCORE_SCALE, NEGATIVE) for s in every]
    new_scores = [
        jnp.where(new_slot == s, new_all[s * queries : (s + 1) * queries] * SCORE_SCALE, NEGATIVE)
        for s in every
    ]
    top = [top_of(scores[s], new_scores[s]) for s in every]
    weights = [jnp.exp(scores[s] - top[s]) for s in every]
    new_weights = [jnp.exp(new_scores[s] - top[s]) for s in every]
    total = [sum_of(weights[s], new_weights[s]) for s in every]
    new_mixed = dot_nn(jnp.concatenate(new_weights, axis=0).astype(BF16), values_up(new))
    mixed = [
        dot_nn(to_values(weights[s]), caches[s]) + new_mixed[s * queries : (s + 1) * queries]
        for s in every
    ]
    for s in every:
        out_ref[s] = (mixed[s] * (1.0 / total[s])).astype(BF16)


def arrival_kernel(
    tp, got_ref, query_ref, new_ref, done_ref, out_hbm, done_hbm, out_ref, sems
):
    step = pl.program_id(0)
    hand_on = pltpu.make_async_copy(done_ref, done_hbm, sems.at[0])
    pl.when(step == 0)(hand_on.start)

    chunks, heads, chunk_rows = got_ref.shape[:3]
    slots, _, per_head = query_ref.shape[:3]
    rows = slots * per_head
    columns = chunks * chunk_rows
    sender_rows = tp * chunk_rows
    piece = min(columns, 256)
    every = range(heads)

    caches = [got_ref[:, h].reshape(columns, HD) for h in every]
    queries = [query_ref[:, h].reshape(rows, HD) for h in every]
    new = new_ref[...]
    ones = jnp.ones((16, HD), BF16)
    scores = [dot_nt(jnp.concatenate([ones, queries[0]], axis=0), caches[0])]
    sums, scores[0] = scores[0][:8], scores[0][16:]
    scores += [dot_nt(queries[h], caches[h]) for h in every[1:]]
    new_all = dot_nt(jnp.concatenate(queries, axis=0), new)

    col = iota((8, columns), 1)
    held = sums < EMPTY
    first = jnp.where(held & (mod(col, sender_rows) == 0), 1.0, 0.0).astype(BF16)
    starts = list(range(0, columns, piece))
    half = len(starts) // 2

    def sender(index):
        at = over(index, sender_rows)
        return at if half else mod(at + chunks // tp // 2, chunks // tp)

    before = jnp.where(
        sender(iota((piece, piece), 0)) < sender(iota((piece, piece), 1)), 1.0, 0.0
    ).astype(BF16)
    base = jnp.zeros((8, 1), F32)
    ranks = {}
    for p in starts[half:] + starts[:half]:
        part = first[:, p : p + piece]
        ranks[p] = dot_nn(part, before) + base
        if half:
            base = base + jnp.sum(part.astype(F32), axis=1, keepdims=True)
    rank = jnp.concatenate([ranks[p] for p in starts], axis=1)
    slot_of = jnp.where(held & (mod(col, 2) == 0), rank, -1.0)[:1]
    first_slot = (step * slots).astype(F32)
    mine = [slot_of == first_slot + a for a in range(slots)]

    new_col = iota((rows, new.shape[0]), 1)
    new_row = iota((rows, new.shape[0]), 0)
    new_here = (
        (mod(new_col, 2) == 0)
        & (over(new_col, 2 * heads * STEPS) == over(new_row, per_head))
        & (mod(over(new_col, 2 * heads), STEPS) <= mod(new_row, STEPS))
    )
    new_head = jnp.where(new_here, mod(over(new_col, 2), heads), heads)

    scores = [
        jnp.concatenate(
            [
                jnp.where(mine[a], scores[h][a * per_head : (a + 1) * per_head] * SCORE_SCALE, NEGATIVE)
                for a in range(slots)
            ],
            axis=0,
        )
        for h in every
    ]
    new_scores = [
        jnp.where(new_head == h, new_all[h * rows : (h + 1) * rows] * SCORE_SCALE, NEGATIVE)
        for h in every
    ]
    top = [top_of(scores[h], new_scores[h]) for h in every]
    weights = [jnp.exp(scores[h] - top[h]) for h in every]
    new_weights = [jnp.exp(new_scores[h] - top[h]) for h in every]
    total = [sum_of(weights[h], new_weights[h]) for h in every]
    new_mixed = dot_nn(jnp.concatenate(new_weights, axis=0).astype(BF16), values_up(new))
    copies = []
    for h in every:
        mixed = dot_nn(to_values(weights[h]), caches[h]) + new_mixed[h * rows : (h + 1) * rows]
        out_ref[h] = (mixed * (1.0 / total[h])).astype(BF16).reshape(slots, per_head, HD)
        there = out_hbm.at[pl.ds(step * slots, slots), h]
        copies.append(pltpu.make_async_copy(out_ref.at[h], there, sems.at[1 + h]))
        copies[-1].start()
    for copy in copies:
        copy.wait()
    pl.when(step == pl.num_programs(0) - 1)(hand_on.wait)


def whole(memory_space=pltpu.VMEM):
    return pl.BlockSpec(memory_space=memory_space)


def in_hbm(x):
    return pltpu.with_memory_space_constraint(x, pltpu.HBM)


def limit(mib):
    return pltpu.CompilerParams(vmem_limit_bytes=mib * 2**20)


def pack(pre_codes, pre_scales, req_dest, req_blocks, peers, tp):
    requests, blocks, block_tokens = pre_codes.shape[:3]
    tokens = blocks * block_tokens
    codes = (
        pre_codes.reshape(requests, tokens, 2, KVH, HD)
        .transpose(0, 1, 3, 2, 4)
        .reshape(requests, tokens * KVH * 2, HD)
    )
    scales = pre_scales.reshape(requests, tokens * 2, KVH)
    ins = [req_dest, req_blocks, codes, scales]
    return pl.pallas_call(
        functools.partial(pack_kernel, tp, KVH, 2 * block_tokens),
        out_shape=pltpu.VMEM((peers * tp, KVH // tp, tokens * 2, HD), BF16),
        in_specs=[whole(pltpu.HBM)] * len(ins),
        out_specs=whole(),
        scratch_shapes=[
            pltpu.SMEM(req_dest.shape, jnp.int32),
            pltpu.SMEM(req_blocks.shape, jnp.int32),
            pltpu.VMEM(codes.shape, BF16),
            pltpu.VMEM(scales.shape, BF16),
            pltpu.SemaphoreType.DMA((len(ins),)),
        ],
        compiler_params=limit(16),
        name="pack",
    )(*[in_hbm(x) for x in ins])


def cache_rows(codes):
    slots, tokens, _, width = codes.shape
    heads = width // HD
    return (
        codes.reshape(slots, tokens, 2, heads, HD)
        .transpose(0, 1, 3, 2, 4)
        .reshape(slots, tokens * heads * 2, HD)
    )


def query_rows(query):
    slots, steps, width = query.shape
    return query.reshape(slots, steps, width // HD, HD).transpose(0, 2, 1, 3)


def new_rows_of(new):
    slots, steps, pair, width = new.shape
    heads = width // HD
    return (
        new.reshape(slots, steps, pair, heads, HD)
        .transpose(0, 1, 3, 2, 4)
        .reshape(slots * steps * heads * pair, HD)
    )


def from_rows(out, shape):
    slots, steps, width = shape
    return out.reshape(slots, width // HD, steps, HD).transpose(0, 2, 1, 3).reshape(shape)


def resident(codes, res_scales, res_len, res_query, res_new):
    slots, rows = codes.shape[:2]
    heads = res_scales.shape[-1]
    scales = res_scales.transpose(0, 2, 3, 1)
    query = query_rows(res_query).reshape(slots, heads * GROUP * STEPS, HD)
    work = query.shape[0] * query.shape[1] * rows
    return pl.pallas_call(
        resident_kernel,
        out_shape=pltpu.VMEM(query.shape, BF16),
        in_specs=[whole(pltpu.SMEM)] + [whole()] * 4,
        out_specs=whole(),
        cost_estimate=pl.CostEstimate(
            flops=4 * work * HD,
            bytes_accessed=2 * (codes.size + 2 * query.size),
            transcendentals=work,
        ),
        compiler_params=limit(16),
        name="resident",
    )(in_hbm(res_len), codes, scales, query, new_rows_of(res_new))


def arrivals(got, arr_query, arr_new, done, tp):
    slots, steps, width = arr_query.shape
    heads = width // (HD * GROUP)
    query = query_rows(arr_query).reshape(slots, heads, GROUP * steps, HD)
    new = new_rows_of(arr_new)
    size = max(n for n in range(1, 7) if slots % n == 0)
    small = got.size <= 2**18
    return pl.pallas_call(
        functools.partial(arrival_kernel, tp),
        out_shape=[
            jax.ShapeDtypeStruct(query.shape, BF16),
            jax.ShapeDtypeStruct(done.shape, BF16),
        ],
        grid=(slots // size,),
        in_specs=[
            pl.BlockSpec(got.shape, lambda i: (0, 0, 0, 0)),
            pl.BlockSpec((size,) + query.shape[1:], lambda i: (i, 0, 0, 0)),
            pl.BlockSpec((new.shape[0] // slots * size, HD), lambda i: (i, 0)),
            whole(),
        ],
        out_specs=[whole(pltpu.HBM)] * 2,
        scratch_shapes=[
            pltpu.VMEM((heads, size) + query.shape[2:], BF16),
            pltpu.SemaphoreType.DMA((1 + heads,)),
        ],
        compiler_params=limit(16 if small else 48),
        name="arrivals",
    )(got, query, new, done)


def shards(
    pre_codes,
    pre_scales,
    req_dest,
    req_blocks,
    res_codes,
    res_scales,
    res_len,
    res_query,
    res_new,
    arr_query,
    arr_new,
):
    peers = lax.axis_size("wide")
    tp = lax.axis_size("tp")
    send = pack(pre_codes, pre_scales, req_dest, req_blocks, peers, tp)
    got = lax.all_to_all(
        send,
        ("wide", "tp"),
        split_axis=0,
        concat_axis=0,
        tiled=True,
        axis_index_groups=[[(i + peers // 2 * tp) % (peers * tp) for i in range(peers * tp)]],
    )
    done = resident(cache_rows(res_codes), res_scales, res_len, res_query, res_new)
    arr_out, res_out = arrivals(got, arr_query, arr_new, done, tp)
    return (from_rows(res_out, res_query.shape), from_rows(arr_out, arr_query.shape))


def solution(mesh):
    in_specs = (
        P(("groups", "wide"), None, "tp", None, None),
        P(("groups", "wide"), None, "tp", None, None),
        P(("groups", "wide")),
        P(("groups", "wide")),
        P(("groups", "wide"), None, None, "tp"),
        P(("groups", "wide"), None, None, "tp"),
        P(("groups", "wide")),
        P(("groups", "wide"), None, "tp"),
        P(("groups", "wide"), None, None, "tp"),
        P(("groups", "wide"), None, "tp"),
        P(("groups", "wide"), None, None, "tp"),
    )
    out_specs = (P(("groups", "wide"), None, "tp"), P(("groups", "wide"), None, "tp"))
    return jax.shard_map(shards, mesh=mesh, in_specs=in_specs, out_specs=out_specs, check_vma=False)
```

```python
import functools
import math

import jax
import jax.numpy as jnp
from jax import lax
from jax.experimental import pallas as pl
from jax.experimental.pallas import tpu as pltpu
from jax.sharding import PartitionSpec as P

KVH = 4
HD = 128
HQ = 64
GROUP = HQ // KVH
STEPS = 2

NEGATIVE = -1e30
EMPTY = 1024.0
SCORE_SCALE = 1.0 / math.sqrt(HD)

BF16 = jnp.bfloat16
F32 = jnp.float32


def iota(shape, axis):
    return lax.broadcasted_iota(jnp.int32, shape, axis)


def over(x, n):
    return jnp.right_shift(x, n.bit_length() - 1) if n & (n - 1) == 0 else x // n


def mod(x, n):
    return jnp.bitwise_and(x, n - 1) if n & (n - 1) == 0 else x % n


def dot_nt(a, b):
    return lax.dot_general(a, b, (((1,), (1,)), ((), ())), preferred_element_type=F32)


def dot_nn(a, b):
    return lax.dot_general(a, b, (((1,), (0,)), ((), ())), preferred_element_type=F32)


def top_of(*parts):
    return functools.reduce(jnp.maximum, [jnp.max(p, axis=1, keepdims=True) for p in parts])


def sum_of(*parts):
    return functools.reduce(jnp.add, [jnp.sum(p, axis=1, keepdims=True) for p in parts])


def to_values(weights):
    tiles = [pltpu.roll(weights[:, c : c + HD], 1, 1) for c in range(0, weights.shape[1], HD)]
    return jnp.concatenate(tiles, axis=1).astype(BF16)


def values_up(rows):
    return pltpu.roll(rows.astype(F32), rows.shape[0] - 1, 0).astype(BF16)


def pack_kernel(
    tp, heads, block_rows, dest_hbm, blocks_hbm, codes_hbm, scales_hbm, send_ref,
    dest_ref, blocks_ref, codes_ref, scales_ref, sems,
):
    pairs = [
        (codes_hbm, codes_ref), (scales_hbm, scales_ref),
        (dest_hbm, dest_ref), (blocks_hbm, blocks_ref),
    ]
    copies = [pltpu.make_async_copy(a, b, sems.at[i]) for i, (a, b) in enumerate(pairs)]
    for copy in copies:
        copy.start()
    requests, all_rows = codes_ref.shape[:2]
    rows = all_rows // heads
    per_core = heads // tp
    peers = send_ref.shape[0] // tp
    send_ref[...] = jnp.full(send_ref.shape, EMPTY, BF16)
    row_block = over(iota((rows, HD), 0), block_rows)
    to_row = iota((all_rows, all_rows), 0)
    from_row = iota((all_rows, all_rows), 1)
    source = over(mod(to_row, rows), 2) * (2 * heads) + over(to_row, rows) * 2 + mod(to_row, 2)
    by_head = jnp.where(from_row == source, 1.0, 0.0).astype(BF16)
    for copy in copies:
        copy.wait()

    def place(r):
        there = lax.rem(dest_ref[r] + (peers - peers // 2), peers) * tp
        held = row_block < blocks_ref[r]
        codes = dot_nn(by_head, codes_ref[r])
        scales = scales_ref[r].astype(F32)
        for j in range(heads):
            values = codes[j * rows : (j + 1) * rows] * scales[:, j : j + 1]
            values = jnp.where(held, values, EMPTY).astype(BF16)
            send_ref[there + j // per_core, j % per_core] = values

    if requests <= 8:
        for r in range(requests):
            place(r)
    else:
        lax.fori_loop(0, requests, lambda r, c: (place(r), c)[1], 0)


def spread_kernel(
    tp, heads, block_rows, dest_hbm, blocks_hbm, codes_hbm, scales_hbm, own_hbm, other_ref,
    dest_ref, blocks_ref, codes_ref, scales_ref, own_ref, sems,
):
    pairs = [
        (codes_hbm, codes_ref), (scales_hbm, scales_ref),
        (dest_hbm, dest_ref), (blocks_hbm, blocks_ref),
    ]
    copies = [pltpu.make_async_copy(a, b, sems.at[i]) for i, (a, b) in enumerate(pairs)]
    for copy in copies:
        copy.start()
    requests, all_rows = codes_ref.shape[:2]
    rows = all_rows // heads
    per_core = heads // tp
    core = lax.axis_index("tp")
    row_block = over(iota((rows, HD), 0), block_rows)
    to_row = iota((all_rows, all_rows), 0)
    from_row = iota((all_rows, all_rows), 1)
    at_core = mod(over(to_row, rows * per_core) + core, tp) * per_core
    head = at_core + mod(over(to_row, rows), per_core)
    source = over(mod(to_row, rows), 2) * (2 * heads) + head * 2 + mod(to_row, 2)
    by_head = jnp.where(from_row == source, 1.0, 0.0).astype(BF16)
    tag_row = iota((16, HD), 0)
    for copy in copies:
        copy.wait()
    tags = jnp.full((16, HD), -1.0, F32)
    for r in range(requests):
        tags = jnp.where(tag_row == r, dest_ref[r].astype(F32), tags)
        held = row_block < blocks_ref[r]
        codes = dot_nn(by_head, codes_ref[r])
        scales = scales_ref[r].astype(F32)
        swapped = jnp.concatenate([scales[:, per_core:], scales[:, :per_core]], axis=1)
        scales = jnp.where(core == 0, scales, swapped)
        for j in range(heads):
            values = codes[j * rows : (j + 1) * rows] * scales[:, j : j + 1]
            values = jnp.where(held, values, EMPTY).astype(BF16)
            to = own_ref if j < per_core else other_ref
            at = ((j % per_core) * requests + r) * rows
            to[at : at + rows] = values
    at = per_core * requests * rows
    own_ref[at : at + 16] = tags.astype(BF16)
    other_ref[at : at + 16] = tags.astype(BF16)
    out = pltpu.make_async_copy(own_ref, own_hbm, sems.at[0])
    out.start()
    out.wait()


def gathered_kernel(
    requests, heads, own_ref, other_ref, query_ref, new_ref, done_ref, out_hbm, done_hbm,
    out_ref, sems,
):
    hand_on = pltpu.make_async_copy(done_ref, done_hbm, sems.at[0])
    hand_on.start()
    senders, height = own_ref.shape[:2]
    slots, _, per_head = query_ref.shape[:3]
    rows = slots * per_head
    every = range(heads)
    span = (height - 16) // heads
    columns = senders * span
    here = lax.axis_index("wide").astype(F32)

    tags = own_ref[:, heads * span :].reshape(senders * 16, HD)
    lane = iota((16, HD), 1)
    pick = jnp.where(lane == 0, 1.0, 0.0).astype(BF16)
    dest = dot_nt(pick, tags)
    match = jnp.where(dest == here, 1.0, 0.0)
    n = senders * 16
    before = jnp.where(iota((n, n), 0) < iota((n, n), 1), 1.0, 0.0).astype(BF16)
    rank = dot_nn(match.astype(BF16), before)
    place = jnp.where(match > 0, rank + 1, 0.0).astype(BF16)
    unit = span // requests
    col = iota((n, columns), 1)
    tag = iota((n, columns), 0)
    expand = jnp.where(
        tag == over(col, span) * 16 + mod(over(col, unit), requests), 1.0, 0.0
    ).astype(BF16)
    slot_of = dot_nn(place, expand)[:8] - 1

    parts = [ref[:, h * span : (h + 1) * span].reshape(columns, HD) for h in every for ref in (own_ref, other_ref)]
    queries = [query_ref[:, h].reshape(rows, HD) for h in every]
    new = new_ref[...]
    ones = jnp.ones((16, HD), BF16)
    caches = [jnp.concatenate([parts[2 * h], parts[2 * h + 1]], axis=0) for h in every]
    scores = [dot_nt(jnp.concatenate([ones, queries[0]], axis=0), caches[0])]
    sums, scores[0] = scores[0][:8], scores[0][16:]
    scores += [dot_nt(queries[h], caches[h]) for h in every[1:]]
    new_all = dot_nt(jnp.concatenate(queries, axis=0), new)
    key = mod(iota((8, 2 * columns), 1), 2) == 0
    slot_of = jnp.concatenate([slot_of, slot_of], axis=1)
    slot_of = jnp.where((sums < EMPTY) & key, slot_of, -1.0)[:1]
    mine = [slot_of == a for a in range(slots)]

    new_col = iota((rows, new.shape[0]), 1)
    new_row = iota((rows, new.shape[0]), 0)
    new_here = (
        (mod(new_col, 2) == 0)
        & (over(new_col, 2 * heads * STEPS) == over(new_row, per_head))
        & (mod(over(new_col, 2 * heads), STEPS) <= mod(new_row, STEPS))
    )
    new_head = jnp.where(new_here, mod(over(new_col, 2), heads), heads)
    scores = [
        jnp.concatenate(
            [
                jnp.where(mine[a], scores[h][a * per_head : (a + 1) * per_head] * SCORE_SCALE, NEGATIVE)
                for a in range(slots)
            ],
            axis=0,
        )
        for h in every
    ]
    new_scores = [
        jnp.where(new_head == h, new_all[h * rows : (h + 1) * rows] * SCORE_SCALE, NEGATIVE)
        for h in every
    ]
    top = [top_of(scores[h], new_scores[h]) for h in every]
    weights = [jnp.exp(scores[h] - top[h]) for h in every]
    new_weights = [jnp.exp(new_scores[h] - top[h]) for h in every]
    total = [sum_of(weights[h], new_weights[h]) for h in every]
    new_mixed = dot_nn(jnp.concatenate(new_weights, axis=0).astype(BF16), values_up(new))
    copies = []
    for h in every:
        mixed = dot_nn(to_values(weights[h]), caches[h]) + new_mixed[h * rows : (h + 1) * rows]
        out_ref[h] = (mixed * (1.0 / total[h])).astype(BF16).reshape(slots, per_head, HD)
        copies.append(pltpu.make_async_copy(out_ref.at[h], out_hbm.at[:, h], sems.at[1 + h]))
        copies[-1].start()
    for copy in copies:
        copy.wait()
    hand_on.wait()


def resident_kernel(len_ref, codes_ref, scales_ref, query_ref, new_ref, out_ref):
    slots, rows = codes_ref.shape[:2]
    heads = scales_ref.shape[2]
    tokens = rows // (2 * heads)
    queries = query_ref.shape[1]
    new_rows = new_ref.shape[0]

    row = iota((rows, HD), 0)
    source = (mod(row, 2) * heads + mod(over(row, 2), heads)) * tokens + over(row, 2 * heads)
    lane = iota((rows, HD), 1)
    spread = jnp.concatenate(
        [jnp.where(source == lane + c, 1.0, 0.0).astype(BF16) for c in range(0, rows, HD)],
        axis=1,
    )
    flat = jnp.concatenate(
        [scales_ref[:, p, h] for p in range(2) for h in range(heads)], axis=1
    )
    columns = dot_nt(spread, flat).astype(BF16)

    col = iota((queries, rows), 1)
    row_head = over(iota((queries, rows), 0), queries // heads)
    is_key = (mod(col, 2) == 0) & (mod(over(col, 2), heads) == row_head)
    col_token = jnp.where(is_key, over(col, 2 * heads), tokens)

    new_col = iota((queries, new_rows), 1)
    new_row = iota((queries, new_rows), 0)
    new_ok = (
        (mod(new_col, 2) == 0)
        & (mod(over(new_col, 2), heads) == over(new_row, queries // heads))
        & (mod(over(new_col, 2 * heads), STEPS) <= mod(new_row, STEPS))
    )
    new_slot = jnp.where(new_ok, over(new_col, 2 * heads * STEPS), slots)

    every = range(slots)
    new = new_ref[...]
    new_all = dot_nt(query_ref[...].reshape(slots * queries, HD), new)
    caches = [codes_ref[s] * columns[:, s : s + 1] for s in every]
    scores = [dot_nt(query_ref[s], caches[s]) for s in every]
    scores = [jnp.where(col_token < len_ref[s], scores[s] * SCORE_SCALE, NEGATIVE) for s in every]
    new_scores = [
        jnp.where(new_slot == s, new_all[s * queries : (s + 1) * queries] * SCORE_SCALE, NEGATIVE)
        for s in every
    ]
    top = [top_of(scores[s], new_scores[s]) for s in every]
    weights = [jnp.exp(scores[s] - top[s]) for s in every]
    new_weights = [jnp.exp(new_scores[s] - top[s]) for s in every]
    total = [sum_of(weights[s], new_weights[s]) for s in every]
    new_mixed = dot_nn(jnp.concatenate(new_weights, axis=0).astype(BF16), values_up(new))
    mixed = [
        dot_nn(to_values(weights[s]), caches[s]) + new_mixed[s * queries : (s + 1) * queries]
        for s in every
    ]
    for s in every:
        out_ref[s] = (mixed[s] * (1.0 / total[s])).astype(BF16)


def arrival_kernel(
    tp, got_ref, query_ref, new_ref, done_ref, out_hbm, done_hbm, out_ref, sems
):
    step = pl.program_id(0)
    hand_on = pltpu.make_async_copy(done_ref, done_hbm, sems.at[0])
    pl.when(step == 0)(hand_on.start)

    chunks, heads, chunk_rows = got_ref.shape[:3]
    slots, _, per_head = query_ref.shape[:3]
    rows = slots * per_head
    columns = chunks * chunk_rows
    sender_rows = tp * chunk_rows
    piece = min(columns, 256)
    every = range(heads)

    caches = [got_ref[:, h].reshape(columns, HD) for h in every]
    queries = [query_ref[:, h].reshape(rows, HD) for h in every]
    new = new_ref[...]
    ones = jnp.ones((16, HD), BF16)
    scores = [dot_nt(jnp.concatenate([ones, queries[0]], axis=0), caches[0])]
    sums, scores[0] = scores[0][:8], scores[0][16:]
    scores += [dot_nt(queries[h], caches[h]) for h in every[1:]]
    new_all = dot_nt(jnp.concatenate(queries, axis=0), new)

    col = iota((8, columns), 1)
    held = sums < EMPTY
    first = jnp.where(held & (mod(col, sender_rows) == 0), 1.0, 0.0).astype(BF16)
    starts = list(range(0, columns, piece))
    half = len(starts) // 2

    def sender(index):
        at = over(index, sender_rows)
        return at if half else mod(at + chunks // tp // 2, chunks // tp)

    before = jnp.where(
        sender(iota((piece, piece), 0)) < sender(iota((piece, piece), 1)), 1.0, 0.0
    ).astype(BF16)
    base = jnp.zeros((8, 1), F32)
    ranks = {}
    for p in starts[half:] + starts[:half]:
        part = first[:, p : p + piece]
        ranks[p] = dot_nn(part, before) + base
        if half:
            base = base + jnp.sum(part.astype(F32), axis=1, keepdims=True)
    rank = jnp.concatenate([ranks[p] for p in starts], axis=1)
    slot_of = jnp.where(held & (mod(col, 2) == 0), rank, -1.0)[:1]
    first_slot = (step * slots).astype(F32)
    mine = [slot_of == first_slot + a for a in range(slots)]

    new_col = iota((rows, new.shape[0]), 1)
    new_row = iota((rows, new.shape[0]), 0)
    new_here = (
        (mod(new_col, 2) == 0)
        & (over(new_col, 2 * heads * STEPS) == over(new_row, per_head))
        & (mod(over(new_col, 2 * heads), STEPS) <= mod(new_row, STEPS))
    )
    new_head = jnp.where(new_here, mod(over(new_col, 2), heads), heads)

    scores = [
        jnp.concatenate(
            [
                jnp.where(mine[a], scores[h][a * per_head : (a + 1) * per_head] * SCORE_SCALE, NEGATIVE)
                for a in range(slots)
            ],
            axis=0,
        )
        for h in every
    ]
    new_scores = [
        jnp.where(new_head == h, new_all[h * rows : (h + 1) * rows] * SCORE_SCALE, NEGATIVE)
        for h in every
    ]
    top = [top_of(scores[h], new_scores[h]) for h in every]
    weights = [jnp.exp(scores[h] - top[h]) for h in every]
    new_weights = [jnp.exp(new_scores[h] - top[h]) for h in every]
    total = [sum_of(weights[h], new_weights[h]) for h in every]
    new_mixed = dot_nn(jnp.concatenate(new_weights, axis=0).astype(BF16), values_up(new))
    copies = []
    for h in every:
        mixed = dot_nn(to_values(weights[h]), caches[h]) + new_mixed[h * rows : (h + 1) * rows]
        out_ref[h] = (mixed * (1.0 / total[h])).astype(BF16).reshape(slots, per_head, HD)
        there = out_hbm.at[pl.ds(step * slots, slots), h]
        copies.append(pltpu.make_async_copy(out_ref.at[h], there, sems.at[1 + h]))
        copies[-1].start()
    for copy in copies:
        copy.wait()
    pl.when(step == pl.num_programs(0) - 1)(hand_on.wait)


def whole(memory_space=pltpu.VMEM):
    return pl.BlockSpec(memory_space=memory_space)


def in_hbm(x):
    return pltpu.with_memory_space_constraint(x, pltpu.HBM)


def limit(mib):
    return pltpu.CompilerParams(vmem_limit_bytes=mib * 2**20)


def pack(pre_codes, pre_scales, req_dest, req_blocks, peers, tp):
    requests, blocks, block_tokens = pre_codes.shape[:3]
    tokens = blocks * block_tokens
    codes = (
        pre_codes.reshape(requests, tokens, 2, KVH, HD)
        .transpose(0, 1, 3, 2, 4)
        .reshape(requests, tokens * KVH * 2, HD)
    )
    scales = pre_scales.reshape(requests, tokens * 2, KVH)
    ins = [req_dest, req_blocks, codes, scales]
    return pl.pallas_call(
        functools.partial(pack_kernel, tp, KVH, 2 * block_tokens),
        out_shape=pltpu.VMEM((peers * tp, KVH // tp, tokens * 2, HD), BF16),
        in_specs=[whole(pltpu.HBM)] * len(ins),
        out_specs=whole(),
        scratch_shapes=[
            pltpu.SMEM(req_dest.shape, jnp.int32),
            pltpu.SMEM(req_blocks.shape, jnp.int32),
            pltpu.VMEM(codes.shape, BF16),
            pltpu.VMEM(scales.shape, BF16),
            pltpu.SemaphoreType.DMA((len(ins),)),
        ],
        compiler_params=limit(16),
        name="pack",
    )(*[in_hbm(x) for x in ins])


def spread(pre_codes, pre_scales, req_dest, req_blocks, tp):
    requests, blocks, block_tokens = pre_codes.shape[:3]
    tokens = blocks * block_tokens
    codes = (
        pre_codes.reshape(requests, tokens, 2, KVH, HD)
        .transpose(0, 1, 3, 2, 4)
        .reshape(requests, tokens * KVH * 2, HD)
    )
    scales = pre_scales.reshape(requests, tokens * 2, KVH)
    ins = [req_dest, req_blocks, codes, scales]
    shape = (KVH // tp * requests * tokens * 2 + 16, HD)
    return pl.pallas_call(
        functools.partial(spread_kernel, tp, KVH, 2 * block_tokens),
        out_shape=[pltpu.HBM(shape, BF16), pltpu.VMEM(shape, BF16)],
        in_specs=[whole(pltpu.HBM)] * len(ins),
        out_specs=[whole(pltpu.HBM), whole()],
        scratch_shapes=[
            pltpu.SMEM(req_dest.shape, jnp.int32),
            pltpu.SMEM(req_blocks.shape, jnp.int32),
            pltpu.VMEM(codes.shape, BF16),
            pltpu.VMEM(scales.shape, BF16),
            pltpu.VMEM(shape, BF16),
            pltpu.SemaphoreType.DMA((len(ins),)),
        ],
        compiler_params=limit(16),
        name="spread",
    )(*[in_hbm(x) for x in ins])


def gathered(own, other, requests, arr_query, arr_new, done):
    slots, steps, width = arr_query.shape
    heads = width // (HD * GROUP)
    query = query_rows(arr_query).reshape(slots, heads, GROUP * steps, HD)
    new = new_rows_of(arr_new)
    return pl.pallas_call(
        functools.partial(gathered_kernel, requests, heads),
        out_shape=[
            jax.ShapeDtypeStruct(query.shape, BF16),
            jax.ShapeDtypeStruct(done.shape, BF16),
        ],
        in_specs=[whole()] * 5,
        out_specs=[whole(pltpu.HBM)] * 2,
        scratch_shapes=[
            pltpu.VMEM((heads, slots) + query.shape[2:], BF16),
            pltpu.SemaphoreType.DMA((1 + heads,)),
        ],
        compiler_params=limit(24),
        name="gathered",
    )(in_hbm(own), in_hbm(other), query, new, done)


def cache_rows(codes):
    slots, tokens, _, width = codes.shape
    heads = width // HD
    return (
        codes.reshape(slots, tokens, 2, heads, HD)
        .transpose(0, 1, 3, 2, 4)
        .reshape(slots, tokens * heads * 2, HD)
    )


def query_rows(query):
    slots, steps, width = query.shape
    return query.reshape(slots, steps, width // HD, HD).transpose(0, 2, 1, 3)


def new_rows_of(new):
    slots, steps, pair, width = new.shape
    heads = width // HD
    return (
        new.reshape(slots, steps, pair, heads, HD)
        .transpose(0, 1, 3, 2, 4)
        .reshape(slots * steps * heads * pair, HD)
    )


def from_rows(out, shape):
    slots, steps, width = shape
    return out.reshape(slots, width // HD, steps, HD).transpose(0, 2, 1, 3).reshape(shape)


def resident(codes, res_scales, res_len, res_query, res_new):
    slots, rows = codes.shape[:2]
    heads = res_scales.shape[-1]
    scales = res_scales.transpose(0, 2, 3, 1)
    query = query_rows(res_query).reshape(slots, heads * GROUP * STEPS, HD)
    work = query.shape[0] * query.shape[1] * rows
    return pl.pallas_call(
        resident_kernel,
        out_shape=pltpu.VMEM(query.shape, BF16),
        in_specs=[whole(pltpu.SMEM)] + [whole()] * 4,
        out_specs=whole(),
        cost_estimate=pl.CostEstimate(
            flops=4 * work * HD,
            bytes_accessed=2 * (codes.size + 2 * query.size),
            transcendentals=work,
        ),
        compiler_params=limit(16),
        name="resident",
    )(in_hbm(res_len), codes, scales, query, new_rows_of(res_new))


def arrivals(got, arr_query, arr_new, done, tp):
    slots, steps, width = arr_query.shape
    heads = width // (HD * GROUP)
    query = query_rows(arr_query).reshape(slots, heads, GROUP * steps, HD)
    new = new_rows_of(arr_new)
    size = max(n for n in range(1, 7) if slots % n == 0)
    small = got.size <= 2**18
    return pl.pallas_call(
        functools.partial(arrival_kernel, tp),
        out_shape=[
            jax.ShapeDtypeStruct(query.shape, BF16),
            jax.ShapeDtypeStruct(done.shape, BF16),
        ],
        grid=(slots // size,),
        in_specs=[
            pl.BlockSpec(got.shape, lambda i: (0, 0, 0, 0)),
            pl.BlockSpec((size,) + query.shape[1:], lambda i: (i, 0, 0, 0)),
            pl.BlockSpec((new.shape[0] // slots * size, HD), lambda i: (i, 0)),
            whole(),
        ],
        out_specs=[whole(pltpu.HBM)] * 2,
        scratch_shapes=[
            pltpu.VMEM((heads, size) + query.shape[2:], BF16),
            pltpu.SemaphoreType.DMA((1 + heads,)),
        ],
        compiler_params=limit(16 if small else 48),
        name="arrivals",
    )(got, query, new, done)


def shards(
    pre_codes,
    pre_scales,
    req_dest,
    req_blocks,
    res_codes,
    res_scales,
    res_len,
    res_query,
    res_new,
    arr_query,
    arr_new,
):
    peers = lax.axis_size("wide")
    tp = lax.axis_size("tp")
    res = (cache_rows(res_codes), res_scales, res_len, res_query, res_new)
    if peers <= 8:
        own, other = spread(pre_codes, pre_scales, req_dest, req_blocks, tp)
        own = lax.all_gather(own, "wide")
        other = lax.ppermute(other, "tp", [(t, tp - 1 - t) for t in range(tp)])
        other = lax.all_gather(other, "wide")
        done = resident(*res)
        arr_out, res_out = gathered(own, other, req_dest.shape[0], arr_query, arr_new, done)
    else:
        send = pack(pre_codes, pre_scales, req_dest, req_blocks, peers, tp)
        got = lax.all_to_all(
            send,
            ("wide", "tp"),
            split_axis=0,
            concat_axis=0,
            tiled=True,
            axis_index_groups=[[(i + peers // 2 * tp) % (peers * tp) for i in range(peers * tp)]],
        )
        done = resident(*res)
        arr_out, res_out = arrivals(got, arr_query, arr_new, done, tp)
    return (from_rows(res_out, res_query.shape), from_rows(arr_out, arr_query.shape))


def solution(mesh):
    in_specs = (
        P(("groups", "wide"), None, "tp", None, None),
        P(("groups", "wide"), None, "tp", None, None),
        P(("groups", "wide")),
        P(("groups", "wide")),
        P(("groups", "wide"), None, None, "tp"),
        P(("groups", "wide"), None, None, "tp"),
        P(("groups", "wide")),
        P(("groups", "wide"), None, "tp"),
        P(("groups", "wide"), None, None, "tp"),
        P(("groups", "wide"), None, "tp"),
        P(("groups", "wide"), None, None, "tp"),
    )
    out_specs = (P(("groups", "wide"), None, "tp"), P(("groups", "wide"), None, "tp"))
    return jax.shard_map(shards, mesh=mesh, in_specs=in_specs, out_specs=out_specs, check_vma=False)
```

```python
import functools
import math

import jax
import jax.numpy as jnp
from jax import lax
from jax.experimental import pallas as pl
from jax.experimental.pallas import tpu as pltpu
from jax.sharding import PartitionSpec as P

KVH = 4
HD = 128
HQ = 64
GROUP = HQ // KVH
STEPS = 2

NEGATIVE = -1e30
EMPTY = 1024.0
SCORE_SCALE = 1.0 / math.sqrt(HD)

BF16 = jnp.bfloat16
F32 = jnp.float32


def iota(shape, axis):
    return lax.broadcasted_iota(jnp.int32, shape, axis)


def over(x, n):
    return jnp.right_shift(x, n.bit_length() - 1) if n & (n - 1) == 0 else x // n


def mod(x, n):
    return jnp.bitwise_and(x, n - 1) if n & (n - 1) == 0 else x % n


def place_of(instance, peers, middle):
    if middle is None:
        return instance
    place = jnp.where(instance > middle, peers - instance, peers - 1 - instance)
    return jnp.where(instance == middle, 0, place)


def instance_at(place, peers, middle):
    if middle is None:
        return place
    instance = jnp.where(place < peers - middle, peers - place, peers - 1 - place)
    return jnp.where(place == 0, middle, instance)


def dot_nt(a, b):
    return lax.dot_general(a, b, (((1,), (1,)), ((), ())), preferred_element_type=F32)


def dot_nn(a, b):
    return lax.dot_general(a, b, (((1,), (0,)), ((), ())), preferred_element_type=F32)


def top_of(*parts):
    return functools.reduce(jnp.maximum, [jnp.max(p, axis=1, keepdims=True) for p in parts])


def sum_of(*parts):
    return functools.reduce(jnp.add, [jnp.sum(p, axis=1, keepdims=True) for p in parts])


def to_values(weights):
    tiles = [pltpu.roll(weights[:, c : c + HD], 1, 1) for c in range(0, weights.shape[1], HD)]
    return jnp.concatenate(tiles, axis=1).astype(BF16)


def values_up(rows):
    return pltpu.roll(rows.astype(F32), rows.shape[0] - 1, 0).astype(BF16)


def pack_kernel(
    tp, middle, heads, block_rows, dest_hbm, blocks_hbm, codes_hbm, scales_hbm, send_ref,
    dest_ref, blocks_ref, codes_ref, scales_ref, sems,
):
    requests, all_rows = codes_ref.shape[:2]
    few = requests <= 8
    pairs = [(dest_hbm, dest_ref), (blocks_hbm, blocks_ref), (scales_hbm, scales_ref)]
    if few:
        pairs += [(codes_hbm.at[r], codes_ref.at[r]) for r in range(requests)]
    else:
        pairs += [(codes_hbm, codes_ref)]
    copies = [pltpu.make_async_copy(a, b, sems.at[i]) for i, (a, b) in enumerate(pairs)]
    for copy in copies:
        copy.start()
    rows = all_rows // heads
    per_core = heads // tp
    peers = send_ref.shape[0] // tp
    send_ref[...] = jnp.full(send_ref.shape, EMPTY, BF16)
    row_block = over(iota((rows, HD), 0), block_rows)
    to_row = iota((all_rows, all_rows), 0)
    from_row = iota((all_rows, all_rows), 1)
    source = over(mod(to_row, rows), 2) * (2 * heads) + over(to_row, rows) * 2 + mod(to_row, 2)
    by_head = jnp.where(from_row == source, 1.0, 0.0).astype(BF16)
    for copy in copies[:3]:
        copy.wait()

    def place(r):
        there = place_of(dest_ref[r], peers, middle) * tp + tp - 1
        held = row_block < blocks_ref[r]
        codes = dot_nn(by_head, codes_ref[r])
        scales = scales_ref[r].astype(F32)
        for j in range(heads):
            values = codes[j * rows : (j + 1) * rows] * scales[:, j : j + 1]
            values = jnp.where(held, values, EMPTY).astype(BF16)
            send_ref[there - j // per_core, j % per_core] = values

    if few:
        for r in range(requests):
            copies[3 + r].wait()
            place(r)
    else:
        copies[3].wait()
        lax.fori_loop(0, requests, lambda r, c: (place(r), c)[1], 0)


def resident_kernel(len_ref, codes_ref, scales_ref, query_ref, new_ref, out_ref):
    slots, rows = codes_ref.shape[:2]
    heads = scales_ref.shape[2]
    tokens = rows // (2 * heads)
    queries = query_ref.shape[1]
    new_rows = new_ref.shape[0]

    row = iota((rows, HD), 0)
    source = (mod(row, 2) * heads + mod(over(row, 2), heads)) * tokens + over(row, 2 * heads)
    lane = iota((rows, HD), 1)
    spread = jnp.concatenate(
        [jnp.where(source == lane + c, 1.0, 0.0).astype(BF16) for c in range(0, rows, HD)],
        axis=1,
    )
    flat = jnp.concatenate(
        [scales_ref[:, p, h] for p in range(2) for h in range(heads)], axis=1
    )
    columns = dot_nt(spread, flat).astype(BF16)

    col = iota((queries, rows), 1)
    row_head = over(iota((queries, rows), 0), queries // heads)
    is_key = (mod(col, 2) == 0) & (mod(over(col, 2), heads) == row_head)
    col_token = jnp.where(is_key, over(col, 2 * heads), tokens)

    new_col = iota((queries, new_rows), 1)
    new_row = iota((queries, new_rows), 0)
    new_ok = (
        (mod(new_col, 2) == 0)
        & (mod(over(new_col, 2), heads) == over(new_row, queries // heads))
        & (mod(over(new_col, 2 * heads), STEPS) <= mod(new_row, STEPS))
    )
    new_slot = jnp.where(new_ok, over(new_col, 2 * heads * STEPS), slots)

    every = range(slots)
    new = new_ref[...]
    new_all = dot_nt(query_ref[...].reshape(slots * queries, HD), new)
    caches = [codes_ref[s] * columns[:, s : s + 1] for s in every]
    scores = [dot_nt(query_ref[s], caches[s]) for s in every]
    scores = [jnp.where(col_token < len_ref[s], scores[s] * SCORE_SCALE, NEGATIVE) for s in every]
    new_scores = [
        jnp.where(new_slot == s, new_all[s * queries : (s + 1) * queries] * SCORE_SCALE, NEGATIVE)
        for s in every
    ]
    top = [top_of(scores[s], new_scores[s]) for s in every]
    weights = [jnp.exp(scores[s] - top[s]) for s in every]
    new_weights = [jnp.exp(new_scores[s] - top[s]) for s in every]
    total = [sum_of(weights[s], new_weights[s]) for s in every]
    new_mixed = dot_nn(jnp.concatenate(new_weights, axis=0).astype(BF16), values_up(new))
    mixed = [
        dot_nn(to_values(weights[s]), caches[s]) + new_mixed[s * queries : (s + 1) * queries]
        for s in every
    ]
    for s in every:
        out_ref[s] = (mixed[s] * (1.0 / total[s])).astype(BF16)


def arrival_kernel(
    tp, middle, got_ref, query_ref, new_ref, done_ref, out_hbm, done_hbm, out_ref, sems
):
    step = pl.program_id(0)
    hand_on = pltpu.make_async_copy(done_ref, done_hbm, sems.at[0])
    pl.when(step == 0)(hand_on.start)

    chunks, heads, chunk_rows = got_ref.shape[:3]
    slots, _, per_head = query_ref.shape[:3]
    rows = slots * per_head
    columns = chunks * chunk_rows
    sender_rows = tp * chunk_rows
    piece = min(columns, 256)
    every = range(heads)

    caches = [got_ref[:, h].reshape(columns, HD) for h in every]
    queries = [query_ref[:, h].reshape(rows, HD) for h in every]
    new = new_ref[...]
    ones = jnp.ones((16, HD), BF16)
    scores = [dot_nt(jnp.concatenate([ones, queries[0]], axis=0), caches[0])]
    sums, scores[0] = scores[0][:8], scores[0][16:]
    scores += [dot_nt(queries[h], caches[h]) for h in every[1:]]
    new_all = dot_nt(jnp.concatenate(queries, axis=0), new)

    col = iota((8, columns), 1)
    held = sums < EMPTY
    first = jnp.where(held & (mod(col, sender_rows) == 0), 1.0, 0.0).astype(BF16)
    def sender(index):
        return instance_at(over(index, sender_rows), chunks // tp, middle)

    before = jnp.where(
        sender(iota((piece, piece), 0)) < sender(iota((piece, piece), 1)), 1.0, 0.0
    ).astype(BF16)
    base = jnp.zeros((8, 1), F32)
    ranks = []
    for p in range(0, columns, piece):
        part = first[:, p : p + piece]
        ranks.append(dot_nn(part, before) + base)
        if p + piece < columns:
            base = base + jnp.sum(part.astype(F32), axis=1, keepdims=True)
    rank = jnp.concatenate(ranks, axis=1)
    slot_of = jnp.where(held & (mod(col, 2) == 0), rank, -1.0)[:1]
    first_slot = (step * slots).astype(F32)
    mine = [slot_of == first_slot + a for a in range(slots)]

    new_col = iota((rows, new.shape[0]), 1)
    new_row = iota((rows, new.shape[0]), 0)
    new_here = (
        (mod(new_col, 2) == 0)
        & (over(new_col, 2 * heads * STEPS) == over(new_row, per_head))
        & (mod(over(new_col, 2 * heads), STEPS) <= mod(new_row, STEPS))
    )
    new_head = jnp.where(new_here, mod(over(new_col, 2), heads), heads)

    scores = [
        jnp.concatenate(
            [
                jnp.where(mine[a], scores[h][a * per_head : (a + 1) * per_head] * SCORE_SCALE, NEGATIVE)
                for a in range(slots)
            ],
            axis=0,
        )
        for h in every
    ]
    new_scores = [
        jnp.where(new_head == h, new_all[h * rows : (h + 1) * rows] * SCORE_SCALE, NEGATIVE)
        for h in every
    ]
    top = [top_of(scores[h], new_scores[h]) for h in every]
    weights = [jnp.exp(scores[h] - top[h]) for h in every]
    new_weights = [jnp.exp(new_scores[h] - top[h]) for h in every]
    total = [sum_of(weights[h], new_weights[h]) for h in every]
    new_mixed = dot_nn(jnp.concatenate(new_weights, axis=0).astype(BF16), values_up(new))
    copies = []
    for h in every:
        mixed = dot_nn(to_values(weights[h]), caches[h]) + new_mixed[h * rows : (h + 1) * rows]
        out_ref[h] = (mixed * (1.0 / total[h])).astype(BF16).reshape(slots, per_head, HD)
        there = out_hbm.at[pl.ds(step * slots, slots), h]
        copies.append(pltpu.make_async_copy(out_ref.at[h], there, sems.at[1 + h]))
        copies[-1].start()
    for copy in copies:
        copy.wait()
    pl.when(step == pl.num_programs(0) - 1)(hand_on.wait)


def whole(memory_space=pltpu.VMEM):
    return pl.BlockSpec(memory_space=memory_space)


def in_hbm(x):
    return pltpu.with_memory_space_constraint(x, pltpu.HBM)


def limit(mib):
    return pltpu.CompilerParams(vmem_limit_bytes=mib * 2**20)


def pack(pre_codes, pre_scales, req_dest, req_blocks, peers, tp, middle):
    requests, blocks, block_tokens = pre_codes.shape[:3]
    tokens = blocks * block_tokens
    codes = (
        pre_codes.reshape(requests, tokens, 2, KVH, HD)
        .transpose(0, 1, 3, 2, 4)
        .reshape(requests, tokens * KVH * 2, HD)
    )
    scales = pre_scales.reshape(requests, tokens * 2, KVH)
    ins = [req_dest, req_blocks, codes, scales]
    return pl.pallas_call(
        functools.partial(pack_kernel, tp, middle, KVH, 2 * block_tokens),
        out_shape=pltpu.VMEM((peers * tp, KVH // tp, tokens * 2, HD), BF16),
        in_specs=[whole(pltpu.HBM)] * len(ins),
        out_specs=whole(),
        scratch_shapes=[
            pltpu.SMEM(req_dest.shape, jnp.int32),
            pltpu.SMEM(req_blocks.shape, jnp.int32),
            pltpu.VMEM(codes.shape, BF16),
            pltpu.VMEM(scales.shape, BF16),
            pltpu.SemaphoreType.DMA((3 + (requests if requests <= 8 else 1),)),
        ],
        compiler_params=limit(16),
        name="pack",
    )(*[in_hbm(x) for x in ins])


def cache_rows(codes):
    slots, tokens, _, width = codes.shape
    heads = width // HD
    return (
        codes.reshape(slots, tokens, 2, heads, HD)
        .transpose(0, 1, 3, 2, 4)
        .reshape(slots, tokens * heads * 2, HD)
    )


def query_rows(query):
    slots, steps, width = query.shape
    return query.reshape(slots, steps, width // HD, HD).transpose(0, 2, 1, 3)


def new_rows_of(new):
    slots, steps, pair, width = new.shape
    heads = width // HD
    return (
        new.reshape(slots, steps, pair, heads, HD)
        .transpose(0, 1, 3, 2, 4)
        .reshape(slots * steps * heads * pair, HD)
    )


def from_rows(out, shape):
    slots, steps, width = shape
    return out.reshape(slots, width // HD, steps, HD).transpose(0, 2, 1, 3).reshape(shape)


def resident(codes, res_scales, res_len, res_query, res_new):
    slots, rows = codes.shape[:2]
    heads = res_scales.shape[-1]
    scales = res_scales.transpose(0, 2, 3, 1)
    query = query_rows(res_query).reshape(slots, heads * GROUP * STEPS, HD)
    work = query.shape[0] * query.shape[1] * rows
    return pl.pallas_call(
        resident_kernel,
        out_shape=pltpu.VMEM(query.shape, BF16),
        in_specs=[whole(pltpu.SMEM)] + [whole()] * 4,
        out_specs=whole(),
        cost_estimate=pl.CostEstimate(
            flops=4 * work * HD,
            bytes_accessed=2 * (codes.size + 2 * query.size),
            transcendentals=work,
        ),
        compiler_params=limit(16),
        name="resident",
    )(in_hbm(res_len), codes, scales, query, new_rows_of(res_new))


def arrivals(got, arr_query, arr_new, done, tp, middle):
    slots, steps, width = arr_query.shape
    heads = width // (HD * GROUP)
    query = query_rows(arr_query).reshape(slots, heads, GROUP * steps, HD)
    new = new_rows_of(arr_new)
    size = max(n for n in range(1, 7) if slots % n == 0)
    small = got.size <= 2**18
    return pl.pallas_call(
        functools.partial(arrival_kernel, tp, middle),
        out_shape=[
            jax.ShapeDtypeStruct(query.shape, BF16),
            jax.ShapeDtypeStruct(done.shape, BF16),
        ],
        grid=(slots // size,),
        in_specs=[
            pl.BlockSpec(got.shape, lambda i: (0, 0, 0, 0)),
            pl.BlockSpec((size,) + query.shape[1:], lambda i: (i, 0, 0, 0)),
            pl.BlockSpec((new.shape[0] // slots * size, HD), lambda i: (i, 0)),
            whole(),
        ],
        out_specs=[whole(pltpu.HBM)] * 2,
        scratch_shapes=[
            pltpu.VMEM((heads, size) + query.shape[2:], BF16),
            pltpu.SemaphoreType.DMA((1 + heads,)),
        ],
        compiler_params=limit(16 if small else 48),
        name="arrivals",
    )(got, query, new, done)


def shards(
    pre_codes,
    pre_scales,
    req_dest,
    req_blocks,
    res_codes,
    res_scales,
    res_len,
    res_query,
    res_new,
    arr_query,
    arr_new,
):
    peers = lax.axis_size("wide")
    tp = lax.axis_size("tp")
    middle = peers // 2 - 1 if peers <= 8 else None
    order = [peers // 2 - 1] + [w for w in reversed(range(peers)) if w != peers // 2 - 1]
    order = list(range(peers)) if middle is None else order
    send = pack(pre_codes, pre_scales, req_dest, req_blocks, peers, tp, middle)
    got = lax.all_to_all(
        send,
        ("wide", "tp"),
        split_axis=0,
        concat_axis=0,
        tiled=True,
        axis_index_groups=[[w * tp + t for w in order for t in reversed(range(tp))]],
    )
    done = resident(cache_rows(res_codes), res_scales, res_len, res_query, res_new)
    arr_out, res_out = arrivals(got, arr_query, arr_new, done, tp, middle)
    return (from_rows(res_out, res_query.shape), from_rows(arr_out, arr_query.shape))


def solution(mesh):
    in_specs = (
        P(("groups", "wide"), None, "tp", None, None),
        P(("groups", "wide"), None, "tp", None, None),
        P(("groups", "wide")),
        P(("groups", "wide")),
        P(("groups", "wide"), None, None, "tp"),
        P(("groups", "wide"), None, None, "tp"),
        P(("groups", "wide")),
        P(("groups", "wide"), None, "tp"),
        P(("groups", "wide"), None, None, "tp"),
        P(("groups", "wide"), None, "tp"),
        P(("groups", "wide"), None, None, "tp"),
    )
    out_specs = (P(("groups", "wide"), None, "tp"), P(("groups", "wide"), None, "tp"))
    return jax.shard_map(shards, mesh=mesh, in_specs=in_specs, out_specs=out_specs, check_vma=False)
```

```python
import functools
import math

import jax
import jax.numpy as jnp
from jax import lax
from jax.experimental import pallas as pl
from jax.experimental.pallas import tpu as pltpu
from jax.sharding import PartitionSpec as P

KVH = 4
HD = 128
HQ = 64
GROUP = HQ // KVH
STEPS = 2

NEGATIVE = -1e30
EMPTY = 1024.0
SCORE_SCALE = 1.0 / math.sqrt(HD)

BF16 = jnp.bfloat16
F32 = jnp.float32


def iota(shape, axis):
    return lax.broadcasted_iota(jnp.int32, shape, axis)


def over(x, n):
    return jnp.right_shift(x, n.bit_length() - 1) if n & (n - 1) == 0 else x // n


def mod(x, n):
    return jnp.bitwise_and(x, n - 1) if n & (n - 1) == 0 else x % n


def place_of(instance, peers, middle):
    if middle is None:
        return instance
    place = jnp.where(instance > middle, peers - instance, peers - 1 - instance)
    return jnp.where(instance == middle, 0, place)


def instance_at(place, peers, middle):
    if middle is None:
        return place
    instance = jnp.where(place < peers - middle, peers - place, peers - 1 - place)
    return jnp.where(place == 0, middle, instance)


def dot_nt(a, b):
    return lax.dot_general(a, b, (((1,), (1,)), ((), ())), preferred_element_type=F32)


def dot_nn(a, b):
    return lax.dot_general(a, b, (((1,), (0,)), ((), ())), preferred_element_type=F32)


def top_of(*parts):
    return functools.reduce(jnp.maximum, [jnp.max(p, axis=1, keepdims=True) for p in parts])


def sum_of(*parts):
    return functools.reduce(jnp.add, [jnp.sum(p, axis=1, keepdims=True) for p in parts])


def to_values(weights):
    tiles = [pltpu.roll(weights[:, c : c + HD], 1, 1) for c in range(0, weights.shape[1], HD)]
    return jnp.concatenate(tiles, axis=1).astype(BF16)


def values_up(rows):
    return pltpu.roll(rows.astype(F32), rows.shape[0] - 1, 0).astype(BF16)


def pack_kernel(
    tp, middle, heads, block_rows, dest_hbm, blocks_hbm, codes_hbm, scales_hbm, send_ref,
    dest_ref, blocks_ref, codes_ref, scales_ref, sems,
):
    requests, all_rows = codes_ref.shape[:2]
    pairs = [
        (codes_hbm, codes_ref), (scales_hbm, scales_ref),
        (dest_hbm, dest_ref), (blocks_hbm, blocks_ref),
    ]
    copies = [pltpu.make_async_copy(a, b, sems.at[i]) for i, (a, b) in enumerate(pairs)]
    for copy in copies:
        copy.start()
    rows = all_rows // heads
    per_core = heads // tp
    peers = send_ref.shape[0] // tp
    send_ref[...] = jnp.full(send_ref.shape, EMPTY, BF16)
    row_block = over(iota((rows, HD), 0), block_rows)
    to_row = iota((all_rows, all_rows), 0)
    from_row = iota((all_rows, all_rows), 1)
    source = over(mod(to_row, rows), 2) * (2 * heads) + over(to_row, rows) * 2 + mod(to_row, 2)
    by_head = jnp.where(from_row == source, 1.0, 0.0).astype(BF16)
    for copy in copies:
        copy.wait()

    def place(r):
        there = place_of(dest_ref[r], peers, middle) * tp + tp - 1
        held = row_block < blocks_ref[r]
        codes = dot_nn(by_head, codes_ref[r])
        scales = scales_ref[r].astype(F32)
        for j in range(heads):
            values = codes[j * rows : (j + 1) * rows] * scales[:, j : j + 1]
            values = jnp.where(held, values, EMPTY).astype(BF16)
            send_ref[there - j // per_core, j % per_core] = values

    if requests <= 8:
        for r in range(requests):
            place(r)
    else:
        lax.fori_loop(0, requests, lambda r, c: (place(r), c)[1], 0)


def resident_kernel(len_ref, codes_ref, scales_ref, query_ref, new_ref, out_ref):
    slots, rows = codes_ref.shape[:2]
    heads = scales_ref.shape[2]
    tokens = rows // (2 * heads)
    queries = query_ref.shape[1]
    new_rows = new_ref.shape[0]

    row = iota((rows, HD), 0)
    source = (mod(row, 2) * heads + mod(over(row, 2), heads)) * tokens + over(row, 2 * heads)
    lane = iota((rows, HD), 1)
    spread = jnp.concatenate(
        [jnp.where(source == lane + c, 1.0, 0.0).astype(BF16) for c in range(0, rows, HD)],
        axis=1,
    )
    flat = jnp.concatenate(
        [scales_ref[:, p, h] for p in range(2) for h in range(heads)], axis=1
    )
    columns = dot_nt(spread, flat).astype(BF16)

    col = iota((queries, rows), 1)
    row_head = over(iota((queries, rows), 0), queries // heads)
    is_key = (mod(col, 2) == 0) & (mod(over(col, 2), heads) == row_head)
    col_token = jnp.where(is_key, over(col, 2 * heads), tokens)

    new_col = iota((queries, new_rows), 1)
    new_row = iota((queries, new_rows), 0)
    new_ok = (
        (mod(new_col, 2) == 0)
        & (mod(over(new_col, 2), heads) == over(new_row, queries // heads))
        & (mod(over(new_col, 2 * heads), STEPS) <= mod(new_row, STEPS))
    )
    new_slot = jnp.where(new_ok, over(new_col, 2 * heads * STEPS), slots)

    every = range(slots)
    new = new_ref[...]
    new_all = dot_nt(query_ref[...].reshape(slots * queries, HD), new)
    caches = [codes_ref[s] * columns[:, s : s + 1] for s in every]
    scores = [dot_nt(query_ref[s], caches[s]) for s in every]
    scores = [jnp.where(col_token < len_ref[s], scores[s] * SCORE_SCALE, NEGATIVE) for s in every]
    new_scores = [
        jnp.where(new_slot == s, new_all[s * queries : (s + 1) * queries] * SCORE_SCALE, NEGATIVE)
        for s in every
    ]
    top = [top_of(scores[s], new_scores[s]) for s in every]
    weights = [jnp.exp(scores[s] - top[s]) for s in every]
    new_weights = [jnp.exp(new_scores[s] - top[s]) for s in every]
    total = [sum_of(weights[s], new_weights[s]) for s in every]
    new_mixed = dot_nn(jnp.concatenate(new_weights, axis=0).astype(BF16), values_up(new))
    mixed = [
        dot_nn(to_values(weights[s]), caches[s]) + new_mixed[s * queries : (s + 1) * queries]
        for s in every
    ]
    for s in every:
        out_ref[s] = (mixed[s] * (1.0 / total[s])).astype(BF16)


def arrival_kernel(
    tp, middle, got_ref, query_ref, new_ref, done_ref, out_hbm, done_hbm, out_ref, sems
):
    step = pl.program_id(0)
    hand_on = pltpu.make_async_copy(done_ref, done_hbm, sems.at[0])
    pl.when(step == 0)(hand_on.start)

    chunks, heads, chunk_rows = got_ref.shape[:3]
    slots, _, per_head = query_ref.shape[:3]
    rows = slots * per_head
    columns = chunks * chunk_rows
    sender_rows = tp * chunk_rows
    piece = min(columns, 256)
    every = range(heads)

    caches = [got_ref[:, h].reshape(columns, HD) for h in every]
    queries = [query_ref[:, h].reshape(rows, HD) for h in every]
    new = new_ref[...]
    ones = jnp.ones((16, HD), BF16)
    scores = [dot_nt(jnp.concatenate([ones, queries[0]], axis=0), caches[0])]
    sums, scores[0] = scores[0][:8], scores[0][16:]
    scores += [dot_nt(queries[h], caches[h]) for h in every[1:]]
    new_all = dot_nt(jnp.concatenate(queries, axis=0), new)

    col = iota((8, columns), 1)
    held = sums < EMPTY
    first = jnp.where(held & (mod(col, sender_rows) == 0), 1.0, 0.0).astype(BF16)
    def sender(index):
        return instance_at(over(index, sender_rows), chunks // tp, middle)

    before = jnp.where(
        sender(iota((piece, piece), 0)) < sender(iota((piece, piece), 1)), 1.0, 0.0
    ).astype(BF16)
    base = jnp.zeros((8, 1), F32)
    ranks = []
    for p in range(0, columns, piece):
        part = first[:, p : p + piece]
        ranks.append(dot_nn(part, before) + base)
        if p + piece < columns:
            base = base + jnp.sum(part.astype(F32), axis=1, keepdims=True)
    rank = jnp.concatenate(ranks, axis=1)
    slot_of = jnp.where(held & (mod(col, 2) == 0), rank, -1.0)[:1]
    first_slot = (step * slots).astype(F32)
    mine = [slot_of == first_slot + a for a in range(slots)]

    new_col = iota((rows, new.shape[0]), 1)
    new_row = iota((rows, new.shape[0]), 0)
    new_here = (
        (mod(new_col, 2) == 0)
        & (over(new_col, 2 * heads * STEPS) == over(new_row, per_head))
        & (mod(over(new_col, 2 * heads), STEPS) <= mod(new_row, STEPS))
    )
    new_head = jnp.where(new_here, mod(over(new_col, 2), heads), heads)

    scores = [
        jnp.concatenate(
            [
                jnp.where(mine[a], scores[h][a * per_head : (a + 1) * per_head] * SCORE_SCALE, NEGATIVE)
                for a in range(slots)
            ],
            axis=0,
        )
        for h in every
    ]
    new_scores = [
        jnp.where(new_head == h, new_all[h * rows : (h + 1) * rows] * SCORE_SCALE, NEGATIVE)
        for h in every
    ]
    top = [top_of(scores[h], new_scores[h]) for h in every]
    weights = [jnp.exp(scores[h] - top[h]) for h in every]
    new_weights = [jnp.exp(new_scores[h] - top[h]) for h in every]
    total = [sum_of(weights[h], new_weights[h]) for h in every]
    new_mixed = dot_nn(jnp.concatenate(new_weights, axis=0).astype(BF16), values_up(new))
    copies = []
    for h in every:
        mixed = dot_nn(to_values(weights[h]), caches[h]) + new_mixed[h * rows : (h + 1) * rows]
        out_ref[h] = (mixed * (1.0 / total[h])).astype(BF16).reshape(slots, per_head, HD)
        there = out_hbm.at[pl.ds(step * slots, slots), h]
        copies.append(pltpu.make_async_copy(out_ref.at[h], there, sems.at[1 + h]))
        copies[-1].start()
    for copy in copies:
        copy.wait()
    pl.when(step == pl.num_programs(0) - 1)(hand_on.wait)


def whole(memory_space=pltpu.VMEM):
    return pl.BlockSpec(memory_space=memory_space)


def in_hbm(x):
    return pltpu.with_memory_space_constraint(x, pltpu.HBM)


def limit(mib):
    return pltpu.CompilerParams(vmem_limit_bytes=mib * 2**20)


def pack(pre_codes, pre_scales, req_dest, req_blocks, peers, tp, middle):
    requests, blocks, block_tokens = pre_codes.shape[:3]
    tokens = blocks * block_tokens
    codes = (
        pre_codes.reshape(requests, tokens, 2, KVH, HD)
        .transpose(0, 1, 3, 2, 4)
        .reshape(requests, tokens * KVH * 2, HD)
    )
    scales = pre_scales.reshape(requests, tokens * 2, KVH)
    ins = [req_dest, req_blocks, codes, scales]
    return pl.pallas_call(
        functools.partial(pack_kernel, tp, middle, KVH, 2 * block_tokens),
        out_shape=pltpu.VMEM((peers * tp, KVH // tp, tokens * 2, HD), BF16),
        in_specs=[whole(pltpu.HBM)] * len(ins),
        out_specs=whole(),
        scratch_shapes=[
            pltpu.SMEM(req_dest.shape, jnp.int32),
            pltpu.SMEM(req_blocks.shape, jnp.int32),
            pltpu.VMEM(codes.shape, BF16),
            pltpu.VMEM(scales.shape, BF16),
            pltpu.SemaphoreType.DMA((len(ins),)),
        ],
        compiler_params=limit(16),
        name="pack",
    )(*[in_hbm(x) for x in ins])


def cache_rows(codes):
    slots, tokens, _, width = codes.shape
    heads = width // HD
    return (
        codes.reshape(slots, tokens, 2, heads, HD)
        .transpose(0, 1, 3, 2, 4)
        .reshape(slots, tokens * heads * 2, HD)
    )


def query_rows(query):
    slots, steps, width = query.shape
    return query.reshape(slots, steps, width // HD, HD).transpose(0, 2, 1, 3)


def new_rows_of(new):
    slots, steps, pair, width = new.shape
    heads = width // HD
    return (
        new.reshape(slots, steps, pair, heads, HD)
        .transpose(0, 1, 3, 2, 4)
        .reshape(slots * steps * heads * pair, HD)
    )


def from_rows(out, shape):
    slots, steps, width = shape
    return out.reshape(slots, width // HD, steps, HD).transpose(0, 2, 1, 3).reshape(shape)


def resident(codes, res_scales, res_len, res_query, res_new):
    slots, rows = codes.shape[:2]
    heads = res_scales.shape[-1]
    scales = res_scales.transpose(0, 2, 3, 1)
    query = query_rows(res_query).reshape(slots, heads * GROUP * STEPS, HD)
    work = query.shape[0] * query.shape[1] * rows
    return pl.pallas_call(
        resident_kernel,
        out_shape=pltpu.VMEM(query.shape, BF16),
        in_specs=[whole(pltpu.SMEM)] + [whole()] * 4,
        out_specs=whole(),
        cost_estimate=pl.CostEstimate(
            flops=4 * work * HD,
            bytes_accessed=2 * (codes.size + 2 * query.size),
            transcendentals=work,
        ),
        compiler_params=limit(16),
        name="resident",
    )(in_hbm(res_len), codes, scales, query, new_rows_of(res_new))


def arrivals(got, arr_query, arr_new, done, tp, middle):
    slots, steps, width = arr_query.shape
    heads = width // (HD * GROUP)
    query = query_rows(arr_query).reshape(slots, heads, GROUP * steps, HD)
    new = new_rows_of(arr_new)
    size = max(n for n in range(1, 7) if slots % n == 0)
    small = got.size <= 2**18
    return pl.pallas_call(
        functools.partial(arrival_kernel, tp, middle),
        out_shape=[
            jax.ShapeDtypeStruct(query.shape, BF16),
            jax.ShapeDtypeStruct(done.shape, BF16),
        ],
        grid=(slots // size,),
        in_specs=[
            pl.BlockSpec(got.shape, lambda i: (0, 0, 0, 0)),
            pl.BlockSpec((size,) + query.shape[1:], lambda i: (i, 0, 0, 0)),
            pl.BlockSpec((new.shape[0] // slots * size, HD), lambda i: (i, 0)),
            whole(),
        ],
        out_specs=[whole(pltpu.HBM)] * 2,
        scratch_shapes=[
            pltpu.VMEM((heads, size) + query.shape[2:], BF16),
            pltpu.SemaphoreType.DMA((1 + heads,)),
        ],
        compiler_params=limit(16 if small else 48),
        name="arrivals",
    )(got, query, new, done)


def shards(
    pre_codes,
    pre_scales,
    req_dest,
    req_blocks,
    res_codes,
    res_scales,
    res_len,
    res_query,
    res_new,
    arr_query,
    arr_new,
):
    peers = lax.axis_size("wide")
    tp = lax.axis_size("tp")
    middle = peers // 2 + 1 if peers <= 8 else None
    order = list(range(peers))
    if middle is not None:
        order = [middle] + [w for w in reversed(order) if w != middle]
    send = pack(pre_codes, pre_scales, req_dest, req_blocks, peers, tp, middle)
    got = lax.all_to_all(
        send,
        ("wide", "tp"),
        split_axis=0,
        concat_axis=0,
        tiled=True,
        axis_index_groups=[[w * tp + t for w in order for t in reversed(range(tp))]],
    )
    done = resident(cache_rows(res_codes), res_scales, res_len, res_query, res_new)
    arr_out, res_out = arrivals(got, arr_query, arr_new, done, tp, middle)
    return (from_rows(res_out, res_query.shape), from_rows(arr_out, arr_query.shape))


def solution(mesh):
    in_specs = (
        P(("groups", "wide"), None, "tp", None, None),
        P(("groups", "wide"), None, "tp", None, None),
        P(("groups", "wide")),
        P(("groups", "wide")),
        P(("groups", "wide"), None, None, "tp"),
        P(("groups", "wide"), None, None, "tp"),
        P(("groups", "wide")),
        P(("groups", "wide"), None, "tp"),
        P(("groups", "wide"), None, None, "tp"),
        P(("groups", "wide"), None, "tp"),
        P(("groups", "wide"), None, None, "tp"),
    )
    out_specs = (P(("groups", "wide"), None, "tp"), P(("groups", "wide"), None, "tp"))
    return jax.shard_map(shards, mesh=mesh, in_specs=in_specs, out_specs=out_specs, check_vma=False)
```

```python
import functools
import math

import jax
import jax.numpy as jnp
from jax import lax
from jax.experimental import pallas as pl
from jax.experimental.pallas import tpu as pltpu
from jax.sharding import PartitionSpec as P

KVH = 4
HD = 128
HQ = 64
GROUP = HQ // KVH
STEPS = 2

NEGATIVE = -1e30
EMPTY = 1024.0
SCORE_SCALE = 1.0 / math.sqrt(HD)

BF16 = jnp.bfloat16
F32 = jnp.float32


def iota(shape, axis):
    return lax.broadcasted_iota(jnp.int32, shape, axis)


def over(x, n):
    return jnp.right_shift(x, n.bit_length() - 1) if n & (n - 1) == 0 else x // n


def mod(x, n):
    return jnp.bitwise_and(x, n - 1) if n & (n - 1) == 0 else x % n


def dot_nt(a, b):
    return lax.dot_general(a, b, (((1,), (1,)), ((), ())), preferred_element_type=F32)


def dot_nn(a, b):
    return lax.dot_general(a, b, (((1,), (0,)), ((), ())), preferred_element_type=F32)


def top_of(*parts):
    return functools.reduce(jnp.maximum, [jnp.max(p, axis=1, keepdims=True) for p in parts])


def sum_of(*parts):
    return functools.reduce(jnp.add, [jnp.sum(p, axis=1, keepdims=True) for p in parts])


def to_values(weights):
    tiles = [pltpu.roll(weights[:, c : c + HD], 1, 1) for c in range(0, weights.shape[1], HD)]
    return jnp.concatenate(tiles, axis=1).astype(BF16)


def values_up(rows):
    return pltpu.roll(rows.astype(F32), rows.shape[0] - 1, 0).astype(BF16)


def pack_kernel(
    tp, order, heads, block_rows, dest_ref, blocks_ref, codes_ref, scales_ref, send_ref
):
    requests, all_rows = codes_ref.shape[:2]
    rows = all_rows // heads
    per_core = heads // tp
    send_ref[...] = jnp.full(send_ref.shape, EMPTY, BF16)
    row_block = over(iota((rows, HD), 0), block_rows)
    to_row = iota((all_rows, all_rows), 0)
    from_row = iota((all_rows, all_rows), 1)
    source = over(mod(to_row, rows), 2) * (2 * heads) + over(to_row, rows) * 2 + mod(to_row, 2)
    by_head = jnp.where(from_row == source, 1.0, 0.0).astype(BF16)

    def place(r):
        there = dest_ref[r]
        if order is not None:
            spots = [jnp.where(there == w, p, 0) for p, w in enumerate(order)]
            there = functools.reduce(jnp.add, spots)
        there = there * tp + tp - 1
        held = row_block < blocks_ref[r]
        codes = dot_nn(by_head, codes_ref[r])
        scales = scales_ref[r].astype(F32)
        for j in range(heads):
            values = codes[j * rows : (j + 1) * rows] * scales[:, j : j + 1]
            values = jnp.where(held, values, EMPTY).astype(BF16)
            send_ref[there - j // per_core, j % per_core] = values

    if requests <= 8:
        for r in range(requests):
            place(r)
    else:
        lax.fori_loop(0, requests, lambda r, c: (place(r), c)[1], 0)


def sent_before(size, per_sender, order):
    def sender(index):
        at = over(index, per_sender)
        if order is None:
            return at
        return functools.reduce(jnp.add, [jnp.where(at == p, w, 0) for p, w in enumerate(order)])

    row = sender(iota((size, HD), 0))
    col = sender(iota((8, size), 1))[:1]
    tiles = [jnp.where(row < col[:, c : c + HD], 1.0, 0.0) for c in range(0, size, HD)]
    return jnp.concatenate(tiles, axis=1).astype(BF16)


def resident_kernel(
    per_sender, order, len_ref, codes_ref, scales_ref, query_ref, new_ref, out_ref, before_ref
):
    before_ref[...] = sent_before(before_ref.shape[0], per_sender, order)
    slots, rows = codes_ref.shape[:2]
    heads = scales_ref.shape[2]
    tokens = rows // (2 * heads)
    queries = query_ref.shape[1]
    new_rows = new_ref.shape[0]

    row = iota((rows, HD), 0)
    source = (mod(row, 2) * heads + mod(over(row, 2), heads)) * tokens + over(row, 2 * heads)
    lane = iota((rows, HD), 1)
    spread = jnp.concatenate(
        [jnp.where(source == lane + c, 1.0, 0.0).astype(BF16) for c in range(0, rows, HD)],
        axis=1,
    )
    flat = jnp.concatenate(
        [scales_ref[:, p, h] for p in range(2) for h in range(heads)], axis=1
    )
    columns = dot_nt(spread, flat).astype(BF16)

    col = iota((queries, rows), 1)
    row_head = over(iota((queries, rows), 0), queries // heads)
    is_key = (mod(col, 2) == 0) & (mod(over(col, 2), heads) == row_head)
    col_token = jnp.where(is_key, over(col, 2 * heads), tokens)

    new_col = iota((queries, new_rows), 1)
    new_row = iota((queries, new_rows), 0)
    new_ok = (
        (mod(new_col, 2) == 0)
        & (mod(over(new_col, 2), heads) == over(new_row, queries // heads))
        & (mod(over(new_col, 2 * heads), STEPS) <= mod(new_row, STEPS))
    )
    new_slot = jnp.where(new_ok, over(new_col, 2 * heads * STEPS), slots)

    every = range(slots)
    new = new_ref[...]
    new_all = dot_nt(query_ref[...].reshape(slots * queries, HD), new)
    caches = [codes_ref[s] * columns[:, s : s + 1] for s in every]
    scores = [dot_nt(query_ref[s], caches[s]) for s in every]
    scores = [jnp.where(col_token < len_ref[s], scores[s] * SCORE_SCALE, NEGATIVE) for s in every]
    new_scores = [
        jnp.where(new_slot == s, new_all[s * queries : (s + 1) * queries] * SCORE_SCALE, NEGATIVE)
        for s in every
    ]
    top = [top_of(scores[s], new_scores[s]) for s in every]
    weights = [jnp.exp(scores[s] - top[s]) for s in every]
    new_weights = [jnp.exp(new_scores[s] - top[s]) for s in every]
    total = [sum_of(weights[s], new_weights[s]) for s in every]
    new_mixed = dot_nn(jnp.concatenate(new_weights, axis=0).astype(BF16), values_up(new))
    mixed = [
        dot_nn(to_values(weights[s]), caches[s]) + new_mixed[s * queries : (s + 1) * queries]
        for s in every
    ]
    for s in every:
        out_ref[s] = (mixed[s] * (1.0 / total[s])).astype(BF16)


def arrival_kernel(
    tp, got_ref, query_ref, new_ref, done_ref, before_ref, out_hbm, done_hbm, out_ref, sems
):
    step = pl.program_id(0)
    hand_on = pltpu.make_async_copy(done_ref, done_hbm, sems.at[0])
    pl.when(step == 0)(hand_on.start)

    chunks, heads, chunk_rows = got_ref.shape[:3]
    slots, _, per_head = query_ref.shape[:3]
    rows = slots * per_head
    columns = chunks * chunk_rows
    sender_rows = tp * chunk_rows
    piece = before_ref.shape[0]
    every = range(heads)

    caches = [got_ref[:, h].reshape(columns, HD) for h in every]
    queries = [query_ref[:, h].reshape(rows, HD) for h in every]
    new = new_ref[...]
    ones = jnp.ones((16, HD), BF16)
    scores = [dot_nt(jnp.concatenate([ones, queries[0]], axis=0), caches[0])]
    sums, scores[0] = scores[0][:8], scores[0][16:]
    scores += [dot_nt(queries[h], caches[h]) for h in every[1:]]
    new_all = dot_nt(jnp.concatenate(queries, axis=0), new)

    col = iota((8, columns), 1)
    held = sums < EMPTY
    first = jnp.where(held & (mod(col, sender_rows) == 0), 1.0, 0.0).astype(BF16)
    base = jnp.zeros((8, 1), F32)
    ranks = []
    for p in range(0, columns, piece):
        part = first[:, p : p + piece]
        ranks.append(dot_nn(part, before_ref[...]) + base)
        if p + piece < columns:
            base = base + jnp.sum(part.astype(F32), axis=1, keepdims=True)
    rank = jnp.concatenate(ranks, axis=1)
    slot_of = jnp.where(held & (mod(col, 2) == 0), rank, -1.0)[:1]
    first_slot = (step * slots).astype(F32)
    mine = [slot_of == first_slot + a for a in range(slots)]

    new_col = iota((rows, new.shape[0]), 1)
    new_row = iota((rows, new.shape[0]), 0)
    new_here = (
        (mod(new_col, 2) == 0)
        & (over(new_col, 2 * heads * STEPS) == over(new_row, per_head))
        & (mod(over(new_col, 2 * heads), STEPS) <= mod(new_row, STEPS))
    )
    new_head = jnp.where(new_here, mod(over(new_col, 2), heads), heads)

    scores = [
        jnp.concatenate(
            [
                jnp.where(mine[a], scores[h][a * per_head : (a + 1) * per_head] * SCORE_SCALE, NEGATIVE)
                for a in range(slots)
            ],
            axis=0,
        )
        for h in every
    ]
    new_scores = [
        jnp.where(new_head == h, new_all[h * rows : (h + 1) * rows] * SCORE_SCALE, NEGATIVE)
        for h in every
    ]
    top = [top_of(scores[h], new_scores[h]) for h in every]
    weights = [jnp.exp(scores[h] - top[h]) for h in every]
    new_weights = [jnp.exp(new_scores[h] - top[h]) for h in every]
    total = [sum_of(weights[h], new_weights[h]) for h in every]
    new_mixed = dot_nn(jnp.concatenate(new_weights, axis=0).astype(BF16), values_up(new))
    copies = []
    for h in every:
        mixed = dot_nn(to_values(weights[h]), caches[h]) + new_mixed[h * rows : (h + 1) * rows]
        out_ref[h] = (mixed * (1.0 / total[h])).astype(BF16).reshape(slots, per_head, HD)
        there = out_hbm.at[pl.ds(step * slots, slots), h]
        copies.append(pltpu.make_async_copy(out_ref.at[h], there, sems.at[1 + h]))
        copies[-1].start()
    for copy in copies:
        copy.wait()
    pl.when(step == pl.num_programs(0) - 1)(hand_on.wait)


def whole(memory_space=pltpu.VMEM):
    return pl.BlockSpec(memory_space=memory_space)


def in_hbm(x):
    return pltpu.with_memory_space_constraint(x, pltpu.HBM)


def limit(mib):
    return pltpu.CompilerParams(vmem_limit_bytes=mib * 2**20)


def pack(pre_codes, pre_scales, req_dest, req_blocks, peers, tp, order):
    requests, blocks, block_tokens = pre_codes.shape[:3]
    tokens = blocks * block_tokens
    codes = (
        pre_codes.reshape(requests, tokens, 2, KVH, HD)
        .transpose(0, 1, 3, 2, 4)
        .reshape(requests, tokens * KVH * 2, HD)
    )
    scales = pre_scales.reshape(requests, tokens * 2, KVH)
    ins = [req_dest, req_blocks, codes, scales]
    return pl.pallas_call(
        functools.partial(pack_kernel, tp, order, KVH, 2 * block_tokens),
        out_shape=pltpu.VMEM((peers * tp, KVH // tp, tokens * 2, HD), BF16),
        in_specs=[whole(pltpu.SMEM)] * 2 + [whole()] * 2,
        out_specs=whole(),
        compiler_params=limit(16),
        name="pack",
    )(*[in_hbm(x) for x in ins])


def cache_rows(codes):
    slots, tokens, _, width = codes.shape
    heads = width // HD
    return (
        codes.reshape(slots, tokens, 2, heads, HD)
        .transpose(0, 1, 3, 2, 4)
        .reshape(slots, tokens * heads * 2, HD)
    )


def query_rows(query):
    slots, steps, width = query.shape
    return query.reshape(slots, steps, width // HD, HD).transpose(0, 2, 1, 3)


def new_rows_of(new):
    slots, steps, pair, width = new.shape
    heads = width // HD
    return (
        new.reshape(slots, steps, pair, heads, HD)
        .transpose(0, 1, 3, 2, 4)
        .reshape(slots * steps * heads * pair, HD)
    )


def from_rows(out, shape):
    slots, steps, width = shape
    return out.reshape(slots, width // HD, steps, HD).transpose(0, 2, 1, 3).reshape(shape)


def resident(codes, res_scales, res_len, res_query, res_new, got, tp, order):
    slots, rows = codes.shape[:2]
    heads = res_scales.shape[-1]
    scales = res_scales.transpose(0, 2, 3, 1)
    query = query_rows(res_query).reshape(slots, heads * GROUP * STEPS, HD)
    work = query.shape[0] * query.shape[1] * rows
    piece = min(got.shape[0] * got.shape[2], 256)
    return pl.pallas_call(
        functools.partial(resident_kernel, tp * got.shape[2], order),
        out_shape=[pltpu.VMEM(query.shape, BF16), pltpu.VMEM((piece, piece), BF16)],
        in_specs=[whole(pltpu.SMEM)] + [whole()] * 4,
        out_specs=[whole()] * 2,
        cost_estimate=pl.CostEstimate(
            flops=4 * work * HD,
            bytes_accessed=2 * (codes.size + 2 * query.size),
            transcendentals=work,
        ),
        compiler_params=limit(16),
        name="resident",
    )(in_hbm(res_len), codes, scales, query, new_rows_of(res_new))


def arrivals(got, arr_query, arr_new, done, before, tp):
    slots, steps, width = arr_query.shape
    heads = width // (HD * GROUP)
    query = query_rows(arr_query).reshape(slots, heads, GROUP * steps, HD)
    new = new_rows_of(arr_new)
    size = max(n for n in range(1, 7) if slots % n == 0)
    small = got.size <= 2**18
    return pl.pallas_call(
        functools.partial(arrival_kernel, tp),
        out_shape=[
            jax.ShapeDtypeStruct(query.shape, BF16),
            jax.ShapeDtypeStruct(done.shape, BF16),
        ],
        grid=(slots // size,),
        in_specs=[
            pl.BlockSpec(got.shape, lambda i: (0, 0, 0, 0)),
            pl.BlockSpec((size,) + query.shape[1:], lambda i: (i, 0, 0, 0)),
            pl.BlockSpec((new.shape[0] // slots * size, HD), lambda i: (i, 0)),
            whole(),
            whole(),
        ],
        out_specs=[whole(pltpu.HBM)] * 2,
        scratch_shapes=[
            pltpu.VMEM((heads, size) + query.shape[2:], BF16),
            pltpu.SemaphoreType.DMA((1 + heads,)),
        ],
        compiler_params=limit(16 if small else 48),
        name="arrivals",
    )(got, query, new, done, before)


def shards(
    pre_codes,
    pre_scales,
    req_dest,
    req_blocks,
    res_codes,
    res_scales,
    res_len,
    res_query,
    res_new,
    arr_query,
    arr_new,
):
    peers = lax.axis_size("wide")
    tp = lax.axis_size("tp")
    order = [5, 1, 2, 3, 4, 6, 7, 0] if peers == 8 else None
    send = pack(pre_codes, pre_scales, req_dest, req_blocks, peers, tp, order)
    got = lax.all_to_all(
        send,
        ("wide", "tp"),
        split_axis=0,
        concat_axis=0,
        tiled=True,
        axis_index_groups=[
            [w * tp + t for w in order or range(peers) for t in reversed(range(tp))]
        ],
    )
    done, before = resident(
        cache_rows(res_codes), res_scales, res_len, res_query, res_new, send, tp, order
    )
    arr_out, res_out = arrivals(got, arr_query, arr_new, done, before, tp)
    return (from_rows(res_out, res_query.shape), from_rows(arr_out, arr_query.shape))


def solution(mesh):
    in_specs = (
        P(("groups", "wide"), None, "tp", None, None),
        P(("groups", "wide"), None, "tp", None, None),
        P(("groups", "wide")),
        P(("groups", "wide")),
        P(("groups", "wide"), None, None, "tp"),
        P(("groups", "wide"), None, None, "tp"),
        P(("groups", "wide")),
        P(("groups", "wide"), None, "tp"),
        P(("groups", "wide"), None, None, "tp"),
        P(("groups", "wide"), None, "tp"),
        P(("groups", "wide"), None, None, "tp"),
    )
    out_specs = (P(("groups", "wide"), None, "tp"), P(("groups", "wide"), None, "tp"))
    return jax.shard_map(shards, mesh=mesh, in_specs=in_specs, out_specs=out_specs, check_vma=False)
```

```python
import functools
import math

import jax
import jax.numpy as jnp
from jax import lax
from jax.experimental import pallas as pl
from jax.experimental.pallas import tpu as pltpu
from jax.sharding import PartitionSpec as P

KVH = 4
HD = 128
HQ = 64
GROUP = HQ // KVH
STEPS = 2

NEGATIVE = -1e30
EMPTY = 1024.0
SCORE_SCALE = 1.0 / math.sqrt(HD)

BF16 = jnp.bfloat16
F32 = jnp.float32


def iota(shape, axis):
    return lax.broadcasted_iota(jnp.int32, shape, axis)


def over(x, n):
    return jnp.right_shift(x, n.bit_length() - 1) if n & (n - 1) == 0 else x // n


def mod(x, n):
    return jnp.bitwise_and(x, n - 1) if n & (n - 1) == 0 else x % n


def dot_nt(a, b):
    return lax.dot_general(a, b, (((1,), (1,)), ((), ())), preferred_element_type=F32)


def dot_nn(a, b):
    return lax.dot_general(a, b, (((1,), (0,)), ((), ())), preferred_element_type=F32)


def tiles_of(*parts):
    return [p[:, c : c + HD] for p in parts for c in range(0, p.shape[1], HD)]


def top_of(*parts):
    return jnp.max(functools.reduce(jnp.maximum, tiles_of(*parts)), axis=1, keepdims=True)


def sum_of(*parts):
    return jnp.sum(functools.reduce(jnp.add, tiles_of(*parts)), axis=1, keepdims=True)


def to_values(weights):
    tiles = [pltpu.roll(weights[:, c : c + HD], 1, 1) for c in range(0, weights.shape[1], HD)]
    return jnp.concatenate(tiles, axis=1).astype(BF16)


def new_tile(new):
    rows = new.shape[0]
    filled = jnp.concatenate([new, jnp.zeros((HD - rows, HD), BF16)], axis=0)
    return filled, pltpu.roll(filled.astype(F32), HD - 1, 0).astype(BF16)


def new_slots(rows, heads):
    col = iota((rows, HD), 1)
    row = iota((rows, HD), 0)
    ok = (
        (mod(col, 2) == 0)
        & (mod(over(col, 2), heads) == over(row, rows // heads))
        & (mod(over(col, 2 * heads), STEPS) <= mod(row, STEPS))
    )
    return jnp.where(ok, over(col, 2 * heads * STEPS), -1)


def pack_kernel(
    tp, order, heads, block_rows, dest_ref, blocks_ref, codes_ref, scales_ref, send_ref
):
    requests, all_rows = codes_ref.shape[:2]
    rows = all_rows // heads
    per_core = heads // tp
    send_ref[...] = jnp.full(send_ref.shape, EMPTY, BF16)
    row_block = over(iota((rows, HD), 0), block_rows)
    to_row = iota((all_rows, all_rows), 0)
    from_row = iota((all_rows, all_rows), 1)
    source = over(mod(to_row, rows), 2) * (2 * heads) + over(to_row, rows) * 2 + mod(to_row, 2)
    by_head = jnp.where(from_row == source, 1.0, 0.0).astype(BF16)

    def place(r):
        there = dest_ref[r]
        if order is not None:
            spots = [jnp.where(there == w, p, 0) for p, w in enumerate(order)]
            there = functools.reduce(jnp.add, spots)
        there = there * tp + tp - 1
        held = row_block < blocks_ref[r]
        codes = dot_nn(by_head, codes_ref[r])
        scales = scales_ref[r].astype(F32)
        for j in range(heads):
            values = codes[j * rows : (j + 1) * rows] * scales[:, j : j + 1]
            values = jnp.where(held, values, EMPTY).astype(BF16)
            send_ref[there - j // per_core, j % per_core] = values

    if requests <= 8:
        for r in range(requests):
            place(r)
    else:
        lax.fori_loop(0, requests, lambda r, c: (place(r), c)[1], 0)


def sent_before(size, per_sender, order):
    def sender(index):
        at = over(index, per_sender)
        if order is None:
            return at
        return functools.reduce(jnp.add, [jnp.where(at == p, w, 0) for p, w in enumerate(order)])

    row = sender(iota((size, HD), 0))
    col = sender(iota((8, size), 1))[:1]
    tiles = [jnp.where(row < col[:, c : c + HD], 1.0, 0.0) for c in range(0, size, HD)]
    return jnp.concatenate(tiles, axis=1).astype(BF16)


def resident_kernel(
    per_sender, order, group, len_ref, codes_hbm, scales_ref, query_ref, new_ref, arr_query_ref,
    arr_new_ref, out_ref, before_ref, arr_scores_ref, arr_values_ref, codes_ref, sem,
):
    fetch = pltpu.make_async_copy(codes_hbm, codes_ref, sem)
    fetch.start()
    slots, rows = codes_ref.shape[:2]
    heads = scales_ref.shape[2]
    tokens = rows // (2 * heads)
    queries = query_ref.shape[1]
    every = range(slots)

    before_ref[...] = sent_before(before_ref.shape[0], per_sender, order)
    slot_of = new_slots(queries, heads)
    per_head = queries // heads
    arr_slots = arr_query_ref.shape[0]
    arr_rows = arr_new_ref.shape[0] // arr_slots * group

    def prepare(g):
        keys, values = new_tile(arr_new_ref[pl.ds(g * arr_rows, arr_rows)])
        arr_values_ref[g] = values
        at = pl.ds(g * group, group)
        scores = dot_nt(arr_query_ref[at].reshape(group * queries, HD), keys) * SCORE_SCALE
        for a in range(group):
            part = scores[a * queries : (a + 1) * queries]
            part = jnp.where(slot_of == a, part, NEGATIVE)
            for h in range(heads):
                arr_scores_ref[h, g * group + a] = part[h * per_head : (h + 1) * per_head]

    if arr_slots == group:
        prepare(0)
    else:
        lax.fori_loop(0, arr_slots // group, lambda g, c: (prepare(g), c)[1], 0)

    row = iota((rows, HD), 0)
    source = (mod(row, 2) * heads + mod(over(row, 2), heads)) * tokens + over(row, 2 * heads)
    lane = iota((rows, HD), 1)
    spread = jnp.concatenate(
        [jnp.where(source == lane + c, 1.0, 0.0).astype(BF16) for c in range(0, rows, HD)],
        axis=1,
    )
    flat = jnp.concatenate(
        [scales_ref[:, p, h] for p in range(2) for h in range(heads)], axis=1
    )
    columns = dot_nt(spread, flat).astype(BF16)

    col = iota((queries, rows), 1)
    row_head = over(iota((queries, rows), 0), per_head)
    is_key = (mod(col, 2) == 0) & (mod(over(col, 2), heads) == row_head)
    col_token = jnp.where(is_key, over(col, 2 * heads), tokens)

    keys, values = new_tile(new_ref[...])
    new_all = dot_nt(query_ref[...].reshape(slots * queries, HD), keys) * SCORE_SCALE
    new_scores = [
        jnp.where(slot_of == s, new_all[s * queries : (s + 1) * queries], NEGATIVE) for s in every
    ]
    fetch.wait()
    caches = [codes_ref[s] * columns[:, s : s + 1] for s in every]
    scores = [dot_nt(query_ref[s], caches[s]) for s in every]
    scores = [jnp.where(col_token < len_ref[s], scores[s] * SCORE_SCALE, NEGATIVE) for s in every]
    top = [top_of(scores[s], new_scores[s]) for s in every]
    weights = [jnp.exp(scores[s] - top[s]) for s in every]
    new_weights = [jnp.exp(new_scores[s] - top[s]) for s in every]
    total = [sum_of(weights[s], new_weights[s]) for s in every]
    new_mixed = dot_nn(jnp.concatenate(new_weights, axis=0).astype(BF16), values)
    mixed = [
        dot_nn(to_values(weights[s]), caches[s]) + new_mixed[s * queries : (s + 1) * queries]
        for s in every
    ]
    for s in every:
        out_ref[s] = (mixed[s] * (1.0 / total[s])).astype(BF16)


def arrival_kernel(
    tp, got_ref, query_ref, new_scores_ref, new_values_ref, before_ref, out_ref
):
    chunks, heads, chunk_rows = got_ref.shape[:3]
    slots, _, per_head = query_ref.shape[:3]
    rows = slots * per_head
    columns = chunks * chunk_rows
    sender_rows = tp * chunk_rows
    piece = before_ref.shape[0]
    every = range(heads)

    caches = [got_ref[:, h].reshape(columns, HD) for h in every]
    queries = [query_ref[:, h].reshape(rows, HD) for h in every]
    ones = jnp.ones((16, HD), BF16)
    scores = [dot_nt(jnp.concatenate([ones, queries[0]], axis=0), caches[0])]
    sums, scores[0] = scores[0][:8], scores[0][16:]
    scores += [dot_nt(queries[h], caches[h]) for h in every[1:]]

    col = iota((8, columns), 1)
    held = sums < EMPTY
    first = jnp.where(held & (mod(col, sender_rows) == 0), 1.0, 0.0).astype(BF16)
    base = jnp.zeros((8, 1), F32)
    ranks = []
    for p in range(0, columns, piece):
        part = first[:, p : p + piece]
        ranks.append(dot_nn(part, before_ref[...]) + base)
        if p + piece < columns:
            base = base + jnp.sum(part.astype(F32), axis=1, keepdims=True)
    rank = jnp.concatenate(ranks, axis=1)
    slot_of = jnp.where(held & (mod(col, 2) == 0), rank, -1.0)[:1]
    first_slot = (pl.program_id(0) * slots).astype(F32)
    mine = [slot_of == first_slot + a for a in range(slots)]

    scores = [
        jnp.concatenate(
            [
                jnp.where(mine[a], scores[h][a * per_head : (a + 1) * per_head] * SCORE_SCALE, NEGATIVE)
                for a in range(slots)
            ],
            axis=0,
        )
        for h in every
    ]
    new_scores = [new_scores_ref[h].reshape(rows, HD) for h in every]
    top = [top_of(scores[h], new_scores[h]) for h in every]
    weights = [jnp.exp(scores[h] - top[h]) for h in every]
    new_weights = [jnp.exp(new_scores[h] - top[h]) for h in every]
    total = [sum_of(weights[h], new_weights[h]) for h in every]
    for h in every:
        mixed = dot_nn(to_values(weights[h]), caches[h])
        mixed = mixed + dot_nn(new_weights[h].astype(BF16), new_values_ref[0])
        out_ref[:, h] = (mixed * (1.0 / total[h])).astype(BF16).reshape(slots, per_head, HD)


def whole(memory_space=pltpu.VMEM):
    return pl.BlockSpec(memory_space=memory_space)


def in_hbm(x):
    return pltpu.with_memory_space_constraint(x, pltpu.HBM)


def limit(mib):
    return pltpu.CompilerParams(vmem_limit_bytes=mib * 2**20)


def pack(pre_codes, pre_scales, req_dest, req_blocks, peers, tp, order):
    requests, blocks, block_tokens = pre_codes.shape[:3]
    tokens = blocks * block_tokens
    codes = (
        pre_codes.reshape(requests, tokens, 2, KVH, HD)
        .transpose(0, 1, 3, 2, 4)
        .reshape(requests, tokens * KVH * 2, HD)
    )
    scales = pre_scales.reshape(requests, tokens * 2, KVH)
    ins = [req_dest, req_blocks, codes, scales]
    return pl.pallas_call(
        functools.partial(pack_kernel, tp, order, KVH, 2 * block_tokens),
        out_shape=pltpu.VMEM((peers * tp, KVH // tp, tokens * 2, HD), BF16),
        in_specs=[whole(pltpu.SMEM)] * 2 + [whole()] * 2,
        out_specs=whole(),
        compiler_params=limit(16),
        name="pack",
    )(*[in_hbm(x) for x in ins])


def cache_rows(codes):
    slots, tokens, _, width = codes.shape
    heads = width // HD
    return (
        codes.reshape(slots, tokens, 2, heads, HD)
        .transpose(0, 1, 3, 2, 4)
        .reshape(slots, tokens * heads * 2, HD)
    )


def query_rows(query):
    slots, steps, width = query.shape
    return query.reshape(slots, steps, width // HD, HD).transpose(0, 2, 1, 3)


def new_rows_of(new):
    slots, steps, pair, width = new.shape
    heads = width // HD
    return (
        new.reshape(slots, steps, pair, heads, HD)
        .transpose(0, 1, 3, 2, 4)
        .reshape(slots * steps * heads * pair, HD)
    )


def from_rows(out, shape):
    slots, steps, width = shape
    return out.reshape(slots, width // HD, steps, HD).transpose(0, 2, 1, 3).reshape(shape)


def resident(res, arr_query, arr_new, chunk_rows, peers, tp, order):
    res_codes, res_scales, res_len, res_query, res_new = res
    codes = cache_rows(res_codes)
    slots, rows = codes.shape[:2]
    heads = res_scales.shape[-1]
    scales = res_scales.transpose(0, 2, 3, 1)
    query = query_rows(res_query).reshape(slots, heads * GROUP * STEPS, HD)
    arr_slots = arr_query.shape[0]
    group = max(n for n in range(1, 7) if arr_slots % n == 0)
    arr_rows = query_rows(arr_query).reshape((arr_slots,) + query.shape[1:])
    work = query.shape[0] * query.shape[1] * rows
    piece = min(peers * tp * chunk_rows, 256)
    return pl.pallas_call(
        functools.partial(resident_kernel, tp * chunk_rows, order, group),
        out_shape=[
            jax.ShapeDtypeStruct(query.shape, BF16),
            pltpu.VMEM((piece, piece), BF16),
            pltpu.VMEM((heads, arr_slots, GROUP * STEPS, HD), F32),
            pltpu.VMEM((arr_slots // group, HD, HD), BF16),
        ],
        in_specs=[whole(pltpu.SMEM), whole(pltpu.HBM)] + [whole()] * 5,
        out_specs=[whole()] * 4,
        scratch_shapes=[pltpu.VMEM(codes.shape, BF16), pltpu.SemaphoreType.DMA],
        cost_estimate=pl.CostEstimate(
            flops=4 * work * HD,
            bytes_accessed=2 * (codes.size + 2 * query.size),
            transcendentals=work,
        ),
        compiler_params=limit(24),
        name="resident",
    )(
        in_hbm(res_len), in_hbm(codes), scales, query, new_rows_of(res_new), arr_rows,
        new_rows_of(arr_new),
    )


def arrivals(got, arr_query, before, new_scores, new_values, tp):
    slots, steps, width = arr_query.shape
    heads = width // (HD * GROUP)
    query = query_rows(arr_query).reshape(slots, heads, GROUP * steps, HD)
    groups = new_values.shape[0]
    size = slots // groups
    small = got.size <= 2**18
    return pl.pallas_call(
        functools.partial(arrival_kernel, tp),
        out_shape=jax.ShapeDtypeStruct(query.shape, BF16),
        grid=(groups,),
        in_specs=[
            pl.BlockSpec(got.shape, lambda i: (0, 0, 0, 0)),
            pl.BlockSpec((size,) + query.shape[1:], lambda i: (i, 0, 0, 0)),
            pl.BlockSpec((heads, size) + new_scores.shape[2:], lambda i: (0, i, 0, 0)),
            pl.BlockSpec((1, HD, HD), lambda i: (i, 0, 0)),
            pl.BlockSpec(before.shape, lambda i: (0, 0)),
        ],
        out_specs=pl.BlockSpec((size,) + query.shape[1:], lambda i: (i, 0, 0, 0)),
        compiler_params=limit(16 if small else 48),
        name="arrivals",
    )(got, query, new_scores, new_values, before)


def shards(
    pre_codes,
    pre_scales,
    req_dest,
    req_blocks,
    res_codes,
    res_scales,
    res_len,
    res_query,
    res_new,
    arr_query,
    arr_new,
):
    peers = lax.axis_size("wide")
    tp = lax.axis_size("tp")
    order = [5, 7, 6, 4, 3, 2, 1, 0] if peers == 8 else None
    send = pack(pre_codes, pre_scales, req_dest, req_blocks, peers, tp, order)
    got = lax.all_to_all(
        send,
        ("wide", "tp"),
        split_axis=0,
        concat_axis=0,
        tiled=True,
        axis_index_groups=[
            [w * tp + t for w in order or range(peers) for t in reversed(range(tp))]
        ],
    )
    res = (res_codes, res_scales, res_len, res_query, res_new)
    res_out, *prepared = resident(res, arr_query, arr_new, send.shape[2], peers, tp, order)
    arr_out = arrivals(got, arr_query, *prepared, tp)
    return (from_rows(res_out, res_query.shape), from_rows(arr_out, arr_query.shape))


def solution(mesh):
    in_specs = (
        P(("groups", "wide"), None, "tp", None, None),
        P(("groups", "wide"), None, "tp", None, None),
        P(("groups", "wide")),
        P(("groups", "wide")),
        P(("groups", "wide"), None, None, "tp"),
        P(("groups", "wide"), None, None, "tp"),
        P(("groups", "wide")),
        P(("groups", "wide"), None, "tp"),
        P(("groups", "wide"), None, None, "tp"),
        P(("groups", "wide"), None, "tp"),
        P(("groups", "wide"), None, None, "tp"),
    )
    out_specs = (P(("groups", "wide"), None, "tp"), P(("groups", "wide"), None, "tp"))
    return jax.shard_map(shards, mesh=mesh, in_specs=in_specs, out_specs=out_specs, check_vma=False)
```

```python
import functools
import math

import jax
import jax.numpy as jnp
from jax import lax
from jax.experimental import pallas as pl
from jax.experimental.pallas import tpu as pltpu
from jax.sharding import PartitionSpec as P

KVH = 4
HD = 128
HQ = 64
GROUP = HQ // KVH
STEPS = 2

NEGATIVE = -1e30
EMPTY = 1024.0
SCORE_SCALE = 1.0 / math.sqrt(HD)

BF16 = jnp.bfloat16
F32 = jnp.float32


def iota(shape, axis):
    return lax.broadcasted_iota(jnp.int32, shape, axis)


def over(x, n):
    return jnp.right_shift(x, n.bit_length() - 1) if n & (n - 1) == 0 else x // n


def mod(x, n):
    return jnp.bitwise_and(x, n - 1) if n & (n - 1) == 0 else x % n


def dot_nt(a, b):
    return lax.dot_general(a, b, (((1,), (1,)), ((), ())), preferred_element_type=F32)


def dot_nn(a, b):
    return lax.dot_general(a, b, (((1,), (0,)), ((), ())), preferred_element_type=F32)


def top_of(*parts):
    return functools.reduce(jnp.maximum, [jnp.max(p, axis=1, keepdims=True) for p in parts])


def sum_of(*parts):
    return functools.reduce(jnp.add, [jnp.sum(p, axis=1, keepdims=True) for p in parts])


def to_values(weights):
    tiles = [pltpu.roll(weights[:, c : c + HD], 1, 1) for c in range(0, weights.shape[1], HD)]
    return jnp.concatenate(tiles, axis=1).astype(BF16)


def values_up(rows):
    return pltpu.roll(rows.astype(F32), rows.shape[0] - 1, 0).astype(BF16)


def pack_kernel(
    tp, order, heads, block_rows, dest_ref, blocks_ref, codes_ref, scales_ref, send_ref
):
    requests, all_rows = codes_ref.shape[:2]
    rows = all_rows // heads
    per_core = heads // tp
    send_ref[...] = jnp.full(send_ref.shape, EMPTY, BF16)
    row_block = over(iota((rows, HD), 0), block_rows)
    to_row = iota((all_rows, all_rows), 0)
    from_row = iota((all_rows, all_rows), 1)
    source = over(mod(to_row, rows), 2) * (2 * heads) + over(to_row, rows) * 2 + mod(to_row, 2)
    by_head = jnp.where(from_row == source, 1.0, 0.0).astype(BF16)

    def place(r):
        there = dest_ref[r]
        if order is not None:
            spots = [jnp.where(there == w, p, 0) for p, w in enumerate(order)]
            there = functools.reduce(jnp.add, spots)
        there = there * tp + tp - 1
        held = row_block < blocks_ref[r]
        codes = dot_nn(by_head, codes_ref[r])
        scales = scales_ref[r].astype(F32)
        for j in range(heads):
            values = codes[j * rows : (j + 1) * rows] * scales[:, j : j + 1]
            values = jnp.where(held, values, EMPTY).astype(BF16)
            send_ref[there - j // per_core, j % per_core] = values

    if requests <= 8:
        for r in range(requests):
            place(r)
    else:
        lax.fori_loop(0, requests, lambda r, c: (place(r), c)[1], 0)


def sent_before(size, per_sender, order):
    def sender(index):
        at = over(index, per_sender)
        if order is None:
            return at
        return functools.reduce(jnp.add, [jnp.where(at == p, w, 0) for p, w in enumerate(order)])

    row = sender(iota((size, HD), 0))
    col = sender(iota((8, size), 1))[:1]
    tiles = [jnp.where(row < col[:, c : c + HD], 1.0, 0.0) for c in range(0, size, HD)]
    return jnp.concatenate(tiles, axis=1).astype(BF16)


def resident_kernel(
    per_sender, order, len_ref, codes_ref, scales_ref, query_ref, new_ref, out_ref, before_ref
):
    before_ref[...] = sent_before(before_ref.shape[0], per_sender, order)
    slots, rows = codes_ref.shape[:2]
    heads = scales_ref.shape[2]
    tokens = rows // (2 * heads)
    queries = query_ref.shape[1]
    new_rows = new_ref.shape[0]

    row = iota((rows, HD), 0)
    source = (mod(row, 2) * heads + mod(over(row, 2), heads)) * tokens + over(row, 2 * heads)
    lane = iota((rows, HD), 1)
    spread = jnp.concatenate(
        [jnp.where(source == lane + c, 1.0, 0.0).astype(BF16) for c in range(0, rows, HD)],
        axis=1,
    )
    flat = jnp.concatenate(
        [scales_ref[:, p, h] for p in range(2) for h in range(heads)], axis=1
    )
    columns = dot_nt(spread, flat).astype(BF16)

    col = iota((queries, rows), 1)
    row_head = over(iota((queries, rows), 0), queries // heads)
    is_key = (mod(col, 2) == 0) & (mod(over(col, 2), heads) == row_head)
    col_token = jnp.where(is_key, over(col, 2 * heads), tokens)

    new_col = iota((queries, new_rows), 1)
    new_row = iota((queries, new_rows), 0)
    new_ok = (
        (mod(new_col, 2) == 0)
        & (mod(over(new_col, 2), heads) == over(new_row, queries // heads))
        & (mod(over(new_col, 2 * heads), STEPS) <= mod(new_row, STEPS))
    )
    new_slot = jnp.where(new_ok, over(new_col, 2 * heads * STEPS), slots)

    every = range(slots)
    new = new_ref[...]
    new_all = dot_nt(query_ref[...].reshape(slots * queries, HD), new)
    caches = [codes_ref[s] * columns[:, s : s + 1] for s in every]
    scores = [dot_nt(query_ref[s], caches[s]) for s in every]
    scores = [jnp.where(col_token < len_ref[s], scores[s] * SCORE_SCALE, NEGATIVE) for s in every]
    new_scores = [
        jnp.where(new_slot == s, new_all[s * queries : (s + 1) * queries] * SCORE_SCALE, NEGATIVE)
        for s in every
    ]
    top = [top_of(scores[s], new_scores[s]) for s in every]
    weights = [jnp.exp(scores[s] - top[s]) for s in every]
    new_weights = [jnp.exp(new_scores[s] - top[s]) for s in every]
    total = [sum_of(weights[s], new_weights[s]) for s in every]
    new_mixed = dot_nn(jnp.concatenate(new_weights, axis=0).astype(BF16), values_up(new))
    mixed = [
        dot_nn(to_values(weights[s]), caches[s]) + new_mixed[s * queries : (s + 1) * queries]
        for s in every
    ]
    for s in every:
        out_ref[s] = (mixed[s] * (1.0 / total[s])).astype(BF16)


def arrival_kernel(
    tp, groups, got_ref, query_ref, new_ref, done_ref, before_ref, out_ref, done_hbm, sem
):
    step = pl.program_id(0) if groups > 1 else 0
    hand_on = pltpu.make_async_copy(done_ref, done_hbm, sem)
    if groups > 1:
        pl.when(step == 0)(hand_on.start)
    else:
        hand_on.start()

    chunks, heads, chunk_rows = got_ref.shape[:3]
    slots, _, per_head = query_ref.shape[:3]
    rows = slots * per_head
    columns = chunks * chunk_rows
    sender_rows = tp * chunk_rows
    piece = before_ref.shape[0]
    every = range(heads)

    caches = [got_ref[:, h].reshape(columns, HD) for h in every]
    queries = [query_ref[:, h].reshape(rows, HD) for h in every]
    new = new_ref[...]
    ones = jnp.ones((16, HD), BF16)
    scores = [dot_nt(jnp.concatenate([ones, queries[0]], axis=0), caches[0])]
    sums, scores[0] = scores[0][:8], scores[0][16:]
    scores += [dot_nt(queries[h], caches[h]) for h in every[1:]]
    new_all = dot_nt(jnp.concatenate(queries, axis=0), new)

    col = iota((8, columns), 1)
    held = sums < EMPTY
    first = jnp.where(held & (mod(col, sender_rows) == 0), 1.0, 0.0).astype(BF16)
    base = jnp.zeros((8, 1), F32)
    ranks = []
    for p in range(0, columns, piece):
        part = first[:, p : p + piece]
        ranks.append(dot_nn(part, before_ref[...]) + base)
        if p + piece < columns:
            base = base + jnp.sum(part.astype(F32), axis=1, keepdims=True)
    rank = jnp.concatenate(ranks, axis=1)
    slot_of = jnp.where(held & (mod(col, 2) == 0), rank, -1.0)[:1]
    first_slot = jnp.float32(step * slots)
    mine = [slot_of == first_slot + a for a in range(slots)]

    new_col = iota((rows, new.shape[0]), 1)
    new_row = iota((rows, new.shape[0]), 0)
    new_here = (
        (mod(new_col, 2) == 0)
        & (over(new_col, 2 * heads * STEPS) == over(new_row, per_head))
        & (mod(over(new_col, 2 * heads), STEPS) <= mod(new_row, STEPS))
    )
    new_head = jnp.where(new_here, mod(over(new_col, 2), heads), heads)

    scores = [
        jnp.concatenate(
            [
                jnp.where(mine[a], scores[h][a * per_head : (a + 1) * per_head] * SCORE_SCALE, NEGATIVE)
                for a in range(slots)
            ],
            axis=0,
        )
        for h in every
    ]
    new_scores = [
        jnp.where(new_head == h, new_all[h * rows : (h + 1) * rows] * SCORE_SCALE, NEGATIVE)
        for h in every
    ]
    top = [top_of(scores[h], new_scores[h]) for h in every]
    weights = [jnp.exp(scores[h] - top[h]) for h in every]
    new_weights = [jnp.exp(new_scores[h] - top[h]) for h in every]
    total = [sum_of(weights[h], new_weights[h]) for h in every]
    new_mixed = dot_nn(jnp.concatenate(new_weights, axis=0).astype(BF16), values_up(new))
    for h in every:
        mixed = dot_nn(to_values(weights[h]), caches[h]) + new_mixed[h * rows : (h + 1) * rows]
        out_ref[:, h] = (mixed * (1.0 / total[h])).astype(BF16).reshape(slots, per_head, HD)
    if groups > 1:
        pl.when(step == groups - 1)(hand_on.wait)
    else:
        hand_on.wait()


def whole(memory_space=pltpu.VMEM):
    return pl.BlockSpec(memory_space=memory_space)


def in_hbm(x):
    return pltpu.with_memory_space_constraint(x, pltpu.HBM)


def limit(mib):
    return pltpu.CompilerParams(vmem_limit_bytes=mib * 2**20)


def pack(pre_codes, pre_scales, req_dest, req_blocks, peers, tp, order):
    requests, blocks, block_tokens = pre_codes.shape[:3]
    tokens = blocks * block_tokens
    codes = (
        pre_codes.reshape(requests, tokens, 2, KVH, HD)
        .transpose(0, 1, 3, 2, 4)
        .reshape(requests, tokens * KVH * 2, HD)
    )
    scales = pre_scales.reshape(requests, tokens * 2, KVH)
    ins = [req_dest, req_blocks, codes, scales]
    return pl.pallas_call(
        functools.partial(pack_kernel, tp, order, KVH, 2 * block_tokens),
        out_shape=pltpu.VMEM((peers * tp, KVH // tp, tokens * 2, HD), BF16),
        in_specs=[whole(pltpu.SMEM)] * 2 + [whole()] * 2,
        out_specs=whole(),
        compiler_params=limit(16),
        name="pack",
    )(*[in_hbm(x) for x in ins])


def cache_rows(codes):
    slots, tokens, _, width = codes.shape
    heads = width // HD
    return (
        codes.reshape(slots, tokens, 2, heads, HD)
        .transpose(0, 1, 3, 2, 4)
        .reshape(slots, tokens * heads * 2, HD)
    )


def query_rows(query):
    slots, steps, width = query.shape
    return query.reshape(slots, steps, width // HD, HD).transpose(0, 2, 1, 3)


def new_rows_of(new):
    slots, steps, pair, width = new.shape
    heads = width // HD
    return (
        new.reshape(slots, steps, pair, heads, HD)
        .transpose(0, 1, 3, 2, 4)
        .reshape(slots * steps * heads * pair, HD)
    )


def from_rows(out, shape):
    slots, steps, width = shape
    return out.reshape(slots, width // HD, steps, HD).transpose(0, 2, 1, 3).reshape(shape)


def resident(codes, res_scales, res_len, res_query, res_new, got, tp, order):
    slots, rows = codes.shape[:2]
    heads = res_scales.shape[-1]
    scales = res_scales.transpose(0, 2, 3, 1)
    query = query_rows(res_query).reshape(slots, heads * GROUP * STEPS, HD)
    work = query.shape[0] * query.shape[1] * rows
    piece = min(got.shape[0] * got.shape[2], 256)
    return pl.pallas_call(
        functools.partial(resident_kernel, tp * got.shape[2], order),
        out_shape=[pltpu.VMEM(query.shape, BF16), pltpu.VMEM((piece, piece), BF16)],
        in_specs=[whole(pltpu.SMEM)] + [whole()] * 4,
        out_specs=[whole()] * 2,
        cost_estimate=pl.CostEstimate(
            flops=4 * work * HD,
            bytes_accessed=2 * (codes.size + 2 * query.size),
            transcendentals=work,
        ),
        compiler_params=limit(16),
        name="resident",
    )(in_hbm(res_len), codes, scales, query, new_rows_of(res_new))


def arrivals(got, arr_query, arr_new, done, before, tp):
    slots, steps, width = arr_query.shape
    heads = width // (HD * GROUP)
    query = query_rows(arr_query).reshape(slots, heads, GROUP * steps, HD)
    new = new_rows_of(arr_new)
    size = max(n for n in range(1, 7) if slots % n == 0)
    groups = slots // size
    small = got.size <= 2**18

    def part(ref, rows):
        if groups == 1:
            return whole()
        return pl.BlockSpec((rows,) + ref.shape[1:], lambda i: (i,) + (0,) * (ref.ndim - 1))

    return pl.pallas_call(
        functools.partial(arrival_kernel, tp, groups),
        out_shape=[
            jax.ShapeDtypeStruct(query.shape, BF16),
            jax.ShapeDtypeStruct(done.shape, BF16),
        ],
        grid=(groups,) if groups > 1 else (),
        in_specs=[
            whole(),
            part(query, size),
            part(new, new.shape[0] // groups),
            whole(),
            whole(),
        ],
        out_specs=[part(query, size), whole(pltpu.HBM)],
        scratch_shapes=[pltpu.SemaphoreType.DMA],
        compiler_params=limit(16 if small else 48),
        name="arrivals",
    )(got, query, new, done, before)


def shards(
    pre_codes,
    pre_scales,
    req_dest,
    req_blocks,
    res_codes,
    res_scales,
    res_len,
    res_query,
    res_new,
    arr_query,
    arr_new,
):
    peers = lax.axis_size("wide")
    tp = lax.axis_size("tp")
    order = [5, 7, 6, 4, 3, 2, 1, 0] if peers == 8 else None
    send = pack(pre_codes, pre_scales, req_dest, req_blocks, peers, tp, order)
    got = lax.all_to_all(
        send,
        ("wide", "tp"),
        split_axis=0,
        concat_axis=0,
        tiled=True,
        axis_index_groups=[
            [w * tp + t for w in order or range(peers) for t in reversed(range(tp))]
        ],
    )
    done, before = resident(
        cache_rows(res_codes), res_scales, res_len, res_query, res_new, send, tp, order
    )
    arr_out, res_out = arrivals(got, arr_query, arr_new, done, before, tp)
    return (from_rows(res_out, res_query.shape), from_rows(arr_out, arr_query.shape))


def solution(mesh):
    in_specs = (
        P(("groups", "wide"), None, "tp", None, None),
        P(("groups", "wide"), None, "tp", None, None),
        P(("groups", "wide")),
        P(("groups", "wide")),
        P(("groups", "wide"), None, None, "tp"),
        P(("groups", "wide"), None, None, "tp"),
        P(("groups", "wide")),
        P(("groups", "wide"), None, "tp"),
        P(("groups", "wide"), None, None, "tp"),
        P(("groups", "wide"), None, "tp"),
        P(("groups", "wide"), None, None, "tp"),
    )
    out_specs = (P(("groups", "wide"), None, "tp"), P(("groups", "wide"), None, "tp"))
    return jax.shard_map(shards, mesh=mesh, in_specs=in_specs, out_specs=out_specs, check_vma=False)
```

```python
import functools
import math

import jax
import jax.numpy as jnp
from jax import lax
from jax.experimental import pallas as pl
from jax.experimental.pallas import tpu as pltpu
from jax.sharding import PartitionSpec as P

KVH = 4
HD = 128
HQ = 64
GROUP = HQ // KVH
STEPS = 2

NEGATIVE = -1e30
EMPTY = 1024.0
SCORE_SCALE = 1.0 / math.sqrt(HD)

BF16 = jnp.bfloat16
F32 = jnp.float32


def iota(shape, axis):
    return lax.broadcasted_iota(jnp.int32, shape, axis)


def over(x, n):
    return jnp.right_shift(x, n.bit_length() - 1) if n & (n - 1) == 0 else x // n


def mod(x, n):
    return jnp.bitwise_and(x, n - 1) if n & (n - 1) == 0 else x % n


def dot_nt(a, b):
    return lax.dot_general(a, b, (((1,), (1,)), ((), ())), preferred_element_type=F32)


def dot_nn(a, b):
    return lax.dot_general(a, b, (((1,), (0,)), ((), ())), preferred_element_type=F32)


def top_of(*parts):
    return functools.reduce(jnp.maximum, [jnp.max(p, axis=1, keepdims=True) for p in parts])


def sum_of(*parts):
    return functools.reduce(jnp.add, [jnp.sum(p, axis=1, keepdims=True) for p in parts])


def to_values(weights):
    tiles = [pltpu.roll(weights[:, c : c + HD], 1, 1) for c in range(0, weights.shape[1], HD)]
    return jnp.concatenate(tiles, axis=1).astype(BF16)


def values_up(rows):
    return pltpu.roll(rows.astype(F32), rows.shape[0] - 1, 0).astype(BF16)


def pack_kernel(
    tp, order, heads, block_rows, dest_ref, blocks_ref, codes_ref, scales_ref, send_ref
):
    requests, all_rows = codes_ref.shape[:2]
    rows = all_rows // heads
    per_core = heads // tp
    send_ref[...] = jnp.full(send_ref.shape, EMPTY, BF16)
    row_block = over(iota((rows, HD), 0), block_rows)
    to_row = iota((all_rows, all_rows), 0)
    from_row = iota((all_rows, all_rows), 1)
    source = over(mod(to_row, rows), 2) * (2 * heads) + over(to_row, rows) * 2 + mod(to_row, 2)
    by_head = jnp.where(from_row == source, 1.0, 0.0).astype(BF16)

    def place(r):
        there = dest_ref[r]
        if order is not None:
            spots = [jnp.where(there == w, p, 0) for p, w in enumerate(order)]
            there = functools.reduce(jnp.add, spots)
        there = there * tp + tp - 1
        held = row_block < blocks_ref[r]
        codes = dot_nn(by_head, codes_ref[r])
        scales = scales_ref[r].astype(F32)
        for j in range(heads):
            values = codes[j * rows : (j + 1) * rows] * scales[:, j : j + 1]
            values = jnp.where(held, values, EMPTY).astype(BF16)
            send_ref[there - j // per_core, j % per_core] = values

    if requests <= 8:
        for r in range(requests):
            place(r)
    else:
        lax.fori_loop(0, requests, lambda r, c: (place(r), c)[1], 0)


def resident_kernel(len_ref, codes_ref, scales_ref, query_ref, new_ref, out_ref):
    slots, rows = codes_ref.shape[:2]
    heads = scales_ref.shape[2]
    tokens = rows // (2 * heads)
    queries = query_ref.shape[1]
    new_rows = new_ref.shape[0]

    row = iota((rows, HD), 0)
    source = (mod(row, 2) * heads + mod(over(row, 2), heads)) * tokens + over(row, 2 * heads)
    lane = iota((rows, HD), 1)
    spread = jnp.concatenate(
        [jnp.where(source == lane + c, 1.0, 0.0).astype(BF16) for c in range(0, rows, HD)],
        axis=1,
    )
    flat = jnp.concatenate(
        [scales_ref[:, p, h] for p in range(2) for h in range(heads)], axis=1
    )
    columns = dot_nt(spread, flat).astype(BF16)

    col = iota((queries, rows), 1)
    row_head = over(iota((queries, rows), 0), queries // heads)
    is_key = (mod(col, 2) == 0) & (mod(over(col, 2), heads) == row_head)
    col_token = jnp.where(is_key, over(col, 2 * heads), tokens)

    new_col = iota((queries, new_rows), 1)
    new_row = iota((queries, new_rows), 0)
    new_ok = (
        (mod(new_col, 2) == 0)
        & (mod(over(new_col, 2), heads) == over(new_row, queries // heads))
        & (mod(over(new_col, 2 * heads), STEPS) <= mod(new_row, STEPS))
    )
    new_slot = jnp.where(new_ok, over(new_col, 2 * heads * STEPS), slots)

    every = range(slots)
    new = new_ref[...]
    new_all = dot_nt(query_ref[...].reshape(slots * queries, HD), new)
    caches = [codes_ref[s] * columns[:, s : s + 1] for s in every]
    scores = [dot_nt(query_ref[s], caches[s]) for s in every]
    scores = [jnp.where(col_token < len_ref[s], scores[s] * SCORE_SCALE, NEGATIVE) for s in every]
    new_scores = [
        jnp.where(new_slot == s, new_all[s * queries : (s + 1) * queries] * SCORE_SCALE, NEGATIVE)
        for s in every
    ]
    top = [top_of(scores[s], new_scores[s]) for s in every]
    weights = [jnp.exp(scores[s] - top[s]) for s in every]
    new_weights = [jnp.exp(new_scores[s] - top[s]) for s in every]
    total = [sum_of(weights[s], new_weights[s]) for s in every]
    new_mixed = dot_nn(jnp.concatenate(new_weights, axis=0).astype(BF16), values_up(new))
    mixed = [
        dot_nn(to_values(weights[s]), caches[s]) + new_mixed[s * queries : (s + 1) * queries]
        for s in every
    ]
    for s in every:
        out_ref[s] = (mixed[s] * (1.0 / total[s])).astype(BF16)


def slots_by_rows(got_ref, tp, order, block_rows):
    chunks, _, chunk_rows = got_ref.shape[:3]
    sender_rows = tp * chunk_rows
    blocks = chunk_rows // block_rows
    rows = [got_ref[p * tp, 0].astype(F32) for p in range(chunks // tp)]
    here = [jnp.where(x[:1] < EMPTY, 1.0, 0.0) for x in rows]
    ranks = [
        sum([here[q] for q, v in enumerate(order) if v < w], jnp.zeros((1, HD), F32))
        for w in order
    ]
    lane = iota((1, HD), 1)
    block = over(lane, sender_rows) * blocks + over(mod(lane, chunk_rows), block_rows)
    block = jnp.where(mod(lane, 2) == 0, block, -1)
    per_tile = HD // sender_rows
    tiles = []
    for start in range(0, len(rows), per_tile):
        tile = jnp.full((1, HD), -1.0, F32)
        for i in range(per_tile):
            x, rank = rows[start + i], ranks[start + i]
            for b in range(blocks):
                at = b * block_rows
                value = jnp.where(x[at : at + 1] < EMPTY, rank, -1.0)
                tile = jnp.where(block == i * blocks + b, value, tile)
        tiles.append(tile)
    return jnp.concatenate(tiles, axis=1)


def slots_by_matmul(got_ref, tp):
    chunks, _, chunk_rows = got_ref.shape[:3]
    columns = chunks * chunk_rows
    sender_rows = tp * chunk_rows
    piece = min(columns, 256)
    sums = dot_nt(jnp.ones((16, HD), BF16), got_ref[:, 0].reshape(columns, HD))[:8]
    col = iota((8, columns), 1)
    held = sums < EMPTY
    first = jnp.where(held & (mod(col, sender_rows) == 0), 1.0, 0.0).astype(BF16)
    row = over(iota((piece, piece), 0), sender_rows)
    before = jnp.where(row < over(iota((piece, piece), 1), sender_rows), 1.0, 0.0).astype(BF16)
    base = jnp.zeros((8, 1), F32)
    ranks = []
    for p in range(0, columns, piece):
        part = first[:, p : p + piece]
        ranks.append(dot_nn(part, before) + base)
        base = base + jnp.sum(part.astype(F32), axis=1, keepdims=True)
    rank = jnp.concatenate(ranks, axis=1)
    return jnp.where(held & (mod(col, 2) == 0), rank, -1.0)[:1]


def arrival_kernel(
    tp, groups, order, block_rows, got_ref, query_ref, new_ref, done_ref, out_ref, done_hbm, sem
):
    step = pl.program_id(0) if groups > 1 else 0
    hand_on = pltpu.make_async_copy(done_ref, done_hbm, sem)
    if groups > 1:
        pl.when(step == 0)(hand_on.start)
    else:
        hand_on.start()

    chunks, heads, chunk_rows = got_ref.shape[:3]
    slots, _, per_head = query_ref.shape[:3]
    rows = slots * per_head
    columns = chunks * chunk_rows
    every = range(heads)

    caches = [got_ref[:, h].reshape(columns, HD) for h in every]
    queries = [query_ref[:, h].reshape(rows, HD) for h in every]
    new = new_ref[...]
    scores = [dot_nt(queries[h], caches[h]) for h in every]
    new_all = dot_nt(jnp.concatenate(queries, axis=0), new)
    if order is None:
        slot_of = slots_by_matmul(got_ref, tp)
    else:
        slot_of = slots_by_rows(got_ref, tp, order, block_rows)
    first_slot = jnp.float32(step * slots)
    mine = [slot_of == first_slot + a for a in range(slots)]

    new_col = iota((rows, new.shape[0]), 1)
    new_row = iota((rows, new.shape[0]), 0)
    new_here = (
        (mod(new_col, 2) == 0)
        & (over(new_col, 2 * heads * STEPS) == over(new_row, per_head))
        & (mod(over(new_col, 2 * heads), STEPS) <= mod(new_row, STEPS))
    )
    new_head = jnp.where(new_here, mod(over(new_col, 2), heads), heads)

    scores = [
        jnp.concatenate(
            [
                jnp.where(mine[a], scores[h][a * per_head : (a + 1) * per_head] * SCORE_SCALE, NEGATIVE)
                for a in range(slots)
            ],
            axis=0,
        )
        for h in every
    ]
    new_scores = [
        jnp.where(new_head == h, new_all[h * rows : (h + 1) * rows] * SCORE_SCALE, NEGATIVE)
        for h in every
    ]
    top = [top_of(scores[h], new_scores[h]) for h in every]
    weights = [jnp.exp(scores[h] - top[h]) for h in every]
    new_weights = [jnp.exp(new_scores[h] - top[h]) for h in every]
    total = [sum_of(weights[h], new_weights[h]) for h in every]
    new_mixed = dot_nn(jnp.concatenate(new_weights, axis=0).astype(BF16), values_up(new))
    for h in every:
        mixed = dot_nn(to_values(weights[h]), caches[h]) + new_mixed[h * rows : (h + 1) * rows]
        out_ref[:, h] = (mixed * (1.0 / total[h])).astype(BF16).reshape(slots, per_head, HD)
    if groups > 1:
        pl.when(step == groups - 1)(hand_on.wait)
    else:
        hand_on.wait()


def whole(memory_space=pltpu.VMEM):
    return pl.BlockSpec(memory_space=memory_space)


def in_hbm(x):
    return pltpu.with_memory_space_constraint(x, pltpu.HBM)


def limit(mib):
    return pltpu.CompilerParams(vmem_limit_bytes=mib * 2**20)


def pack(pre_codes, pre_scales, req_dest, req_blocks, peers, tp, order):
    requests, blocks, block_tokens = pre_codes.shape[:3]
    tokens = blocks * block_tokens
    codes = (
        pre_codes.reshape(requests, tokens, 2, KVH, HD)
        .transpose(0, 1, 3, 2, 4)
        .reshape(requests, tokens * KVH * 2, HD)
    )
    scales = pre_scales.reshape(requests, tokens * 2, KVH)
    ins = [req_dest, req_blocks, codes, scales]
    return pl.pallas_call(
        functools.partial(pack_kernel, tp, order, KVH, 2 * block_tokens),
        out_shape=pltpu.VMEM((peers * tp, KVH // tp, tokens * 2, HD), BF16),
        in_specs=[whole(pltpu.SMEM)] * 2 + [whole()] * 2,
        out_specs=whole(),
        compiler_params=limit(16),
        name="pack",
    )(*[in_hbm(x) for x in ins])


def cache_rows(codes):
    slots, tokens, _, width = codes.shape
    heads = width // HD
    return (
        codes.reshape(slots, tokens, 2, heads, HD)
        .transpose(0, 1, 3, 2, 4)
        .reshape(slots, tokens * heads * 2, HD)
    )


def query_rows(query):
    slots, steps, width = query.shape
    return query.reshape(slots, steps, width // HD, HD).transpose(0, 2, 1, 3)


def new_rows_of(new):
    slots, steps, pair, width = new.shape
    heads = width // HD
    return (
        new.reshape(slots, steps, pair, heads, HD)
        .transpose(0, 1, 3, 2, 4)
        .reshape(slots * steps * heads * pair, HD)
    )


def from_rows(out, shape):
    slots, steps, width = shape
    return out.reshape(slots, width // HD, steps, HD).transpose(0, 2, 1, 3).reshape(shape)


def resident(codes, res_scales, res_len, res_query, res_new):
    slots, rows = codes.shape[:2]
    heads = res_scales.shape[-1]
    scales = res_scales.transpose(0, 2, 3, 1)
    query = query_rows(res_query).reshape(slots, heads * GROUP * STEPS, HD)
    work = query.shape[0] * query.shape[1] * rows
    return pl.pallas_call(
        resident_kernel,
        out_shape=pltpu.VMEM(query.shape, BF16),
        in_specs=[whole(pltpu.SMEM)] + [whole()] * 4,
        out_specs=whole(),
        cost_estimate=pl.CostEstimate(
            flops=4 * work * HD,
            bytes_accessed=2 * (codes.size + 2 * query.size),
            transcendentals=work,
        ),
        compiler_params=limit(16),
        name="resident",
    )(in_hbm(res_len), codes, scales, query, new_rows_of(res_new))


def arrivals(got, arr_query, arr_new, done, tp, order, block_rows):
    slots, steps, width = arr_query.shape
    heads = width // (HD * GROUP)
    query = query_rows(arr_query).reshape(slots, heads, GROUP * steps, HD)
    new = new_rows_of(arr_new)
    size = max(n for n in range(1, 7) if slots % n == 0)
    groups = slots // size
    small = got.size <= 2**18

    def part(ref, rows):
        if groups == 1:
            return whole()
        return pl.BlockSpec((rows,) + ref.shape[1:], lambda i: (i,) + (0,) * (ref.ndim - 1))

    return pl.pallas_call(
        functools.partial(arrival_kernel, tp, groups, order, block_rows),
        out_shape=[
            jax.ShapeDtypeStruct(query.shape, BF16),
            jax.ShapeDtypeStruct(done.shape, BF16),
        ],
        grid=(groups,) if groups > 1 else (),
        in_specs=[
            whole(),
            part(query, size),
            part(new, new.shape[0] // groups),
            whole(),
        ],
        out_specs=[part(query, size), whole(pltpu.HBM)],
        scratch_shapes=[pltpu.SemaphoreType.DMA],
        compiler_params=limit(16 if small else 48),
        name="arrivals",
    )(got, query, new, done)


def shards(
    pre_codes,
    pre_scales,
    req_dest,
    req_blocks,
    res_codes,
    res_scales,
    res_len,
    res_query,
    res_new,
    arr_query,
    arr_new,
):
    peers = lax.axis_size("wide")
    tp = lax.axis_size("tp")
    order = [5, 7, 6, 4, 3, 2, 1, 0] if peers == 8 else None
    send = pack(pre_codes, pre_scales, req_dest, req_blocks, peers, tp, order)
    got = lax.all_to_all(
        send,
        ("wide", "tp"),
        split_axis=0,
        concat_axis=0,
        tiled=True,
        axis_index_groups=[
            [w * tp + t for w in order or range(peers) for t in reversed(range(tp))]
        ],
    )
    done = resident(cache_rows(res_codes), res_scales, res_len, res_query, res_new)
    block_rows = 2 * pre_codes.shape[2]
    arr_out, res_out = arrivals(got, arr_query, arr_new, done, tp, order, block_rows)
    return (from_rows(res_out, res_query.shape), from_rows(arr_out, arr_query.shape))


def solution(mesh):
    in_specs = (
        P(("groups", "wide"), None, "tp", None, None),
        P(("groups", "wide"), None, "tp", None, None),
        P(("groups", "wide")),
        P(("groups", "wide")),
        P(("groups", "wide"), None, None, "tp"),
        P(("groups", "wide"), None, None, "tp"),
        P(("groups", "wide")),
        P(("groups", "wide"), None, "tp"),
        P(("groups", "wide"), None, None, "tp"),
        P(("groups", "wide"), None, "tp"),
        P(("groups", "wide"), None, None, "tp"),
    )
    out_specs = (P(("groups", "wide"), None, "tp"), P(("groups", "wide"), None, "tp"))
    return jax.shard_map(shards, mesh=mesh, in_specs=in_specs, out_specs=out_specs, check_vma=False)
```

```python
import functools
import math

import jax
import jax.numpy as jnp
from jax import lax
from jax.experimental import pallas as pl
from jax.experimental.pallas import tpu as pltpu
from jax.sharding import PartitionSpec as P

KVH = 4
HD = 128
HQ = 64
GROUP = HQ // KVH
STEPS = 2

NEGATIVE = -1e30
EMPTY = 1024.0
SCORE_SCALE = 1.0 / math.sqrt(HD)

BF16 = jnp.bfloat16
F32 = jnp.float32


def iota(shape, axis):
    return lax.broadcasted_iota(jnp.int32, shape, axis)


def over(x, n):
    return jnp.right_shift(x, n.bit_length() - 1) if n & (n - 1) == 0 else x // n


def mod(x, n):
    return jnp.bitwise_and(x, n - 1) if n & (n - 1) == 0 else x % n


def dot_nt(a, b):
    return lax.dot_general(a, b, (((1,), (1,)), ((), ())), preferred_element_type=F32)


def dot_nn(a, b):
    return lax.dot_general(a, b, (((1,), (0,)), ((), ())), preferred_element_type=F32)


def top_of(*parts):
    return functools.reduce(jnp.maximum, [jnp.max(p, axis=1, keepdims=True) for p in parts])


def sum_of(*parts):
    return functools.reduce(jnp.add, [jnp.sum(p, axis=1, keepdims=True) for p in parts])


def to_values(weights):
    tiles = [pltpu.roll(weights[:, c : c + HD], 1, 1) for c in range(0, weights.shape[1], HD)]
    return jnp.concatenate(tiles, axis=1).astype(BF16)


def values_up(rows):
    return pltpu.roll(rows.astype(F32), rows.shape[0] - 1, 0).astype(BF16)


def pack_kernel(
    tp, order, heads, block_rows, dest_ref, blocks_ref, codes_ref, scales_ref, send_ref
):
    requests, all_rows = codes_ref.shape[:2]
    rows = all_rows // heads
    per_core = heads // tp
    send_ref[...] = jnp.full(send_ref.shape, EMPTY, BF16)
    row_block = over(iota((rows, HD), 0), block_rows)
    to_row = iota((all_rows, all_rows), 0)
    from_row = iota((all_rows, all_rows), 1)
    source = over(mod(to_row, rows), 2) * (2 * heads) + over(to_row, rows) * 2 + mod(to_row, 2)
    by_head = jnp.where(from_row == source, 1.0, 0.0).astype(BF16)

    def place(r):
        there = dest_ref[r]
        if order is not None:
            spots = [jnp.where(there == w, p, 0) for p, w in enumerate(order)]
            there = functools.reduce(jnp.add, spots)
        there = there * tp + tp - 1
        held = row_block < blocks_ref[r]
        codes = dot_nn(by_head, codes_ref[r])
        scales = scales_ref[r].astype(F32)
        for j in range(heads):
            values = codes[j * rows : (j + 1) * rows] * scales[:, j : j + 1]
            values = jnp.where(held, values, EMPTY).astype(BF16)
            send_ref[there - j // per_core, j % per_core] = values

    pl.loop(0, requests)(place)


def resident_kernel(len_ref, codes_ref, scales_ref, query_ref, new_ref, out_ref):
    slots, rows = codes_ref.shape[:2]
    heads = scales_ref.shape[2]
    tokens = rows // (2 * heads)
    queries = query_ref.shape[1]
    new_rows = new_ref.shape[0]

    row = iota((rows, HD), 0)
    source = (mod(row, 2) * heads + mod(over(row, 2), heads)) * tokens + over(row, 2 * heads)
    lane = iota((rows, HD), 1)
    spread = jnp.concatenate(
        [jnp.where(source == lane + c, 1.0, 0.0).astype(BF16) for c in range(0, rows, HD)],
        axis=1,
    )
    flat = jnp.concatenate(
        [scales_ref[:, p, h] for p in range(2) for h in range(heads)], axis=1
    )
    columns = dot_nt(spread, flat).astype(BF16)

    col = iota((queries, rows), 1)
    row_head = over(iota((queries, rows), 0), queries // heads)
    is_key = (mod(col, 2) == 0) & (mod(over(col, 2), heads) == row_head)
    col_token = jnp.where(is_key, over(col, 2 * heads), tokens)

    new_col = iota((queries, new_rows), 1)
    new_row = iota((queries, new_rows), 0)
    new_ok = (
        (mod(new_col, 2) == 0)
        & (mod(over(new_col, 2), heads) == over(new_row, queries // heads))
        & (mod(over(new_col, 2 * heads), STEPS) <= mod(new_row, STEPS))
    )
    new_slot = jnp.where(new_ok, over(new_col, 2 * heads * STEPS), slots)

    every = range(slots)
    new = new_ref[...]
    new_all = dot_nt(query_ref[...].reshape(slots * queries, HD), new)
    caches = [codes_ref[s] * columns[:, s : s + 1] for s in every]
    scores = [dot_nt(query_ref[s], caches[s]) for s in every]
    scores = [jnp.where(col_token < len_ref[s], scores[s] * SCORE_SCALE, NEGATIVE) for s in every]
    new_scores = [
        jnp.where(new_slot == s, new_all[s * queries : (s + 1) * queries] * SCORE_SCALE, NEGATIVE)
        for s in every
    ]
    top = [top_of(scores[s], new_scores[s]) for s in every]
    weights = [jnp.exp(scores[s] - top[s]) for s in every]
    new_weights = [jnp.exp(new_scores[s] - top[s]) for s in every]
    total = [sum_of(weights[s], new_weights[s]) for s in every]
    new_mixed = dot_nn(jnp.concatenate(new_weights, axis=0).astype(BF16), values_up(new))
    mixed = [
        dot_nn(to_values(weights[s]), caches[s]) + new_mixed[s * queries : (s + 1) * queries]
        for s in every
    ]
    for s in every:
        out_ref[s] = (mixed[s] * (1.0 / total[s])).astype(BF16)


def slots_by_rows(got_ref, tp, order, block_rows):
    chunks, _, chunk_rows = got_ref.shape[:3]
    sender_rows = tp * chunk_rows
    blocks = chunk_rows // block_rows
    rows = [got_ref[p * tp, 0].astype(F32) for p in range(chunks // tp)]
    here = [jnp.where(x[:1] < EMPTY, 1.0, 0.0) for x in rows]
    ranks = [
        sum([here[q] for q, v in enumerate(order) if v < w], jnp.zeros((1, HD), F32))
        for w in order
    ]
    lane = iota((1, HD), 1)
    block = over(lane, sender_rows) * blocks + over(mod(lane, chunk_rows), block_rows)
    block = jnp.where(mod(lane, 2) == 0, block, -1)
    per_tile = HD // sender_rows
    tiles = []
    for start in range(0, len(rows), per_tile):
        tile = jnp.full((1, HD), -1.0, F32)
        for i in range(per_tile):
            x, rank = rows[start + i], ranks[start + i]
            for b in range(blocks):
                at = b * block_rows
                value = jnp.where(x[at : at + 1] < EMPTY, rank, -1.0)
                tile = jnp.where(block == i * blocks + b, value, tile)
        tiles.append(tile)
    return jnp.concatenate(tiles, axis=1)


def slots_by_matmul(got_ref, tp):
    chunks, _, chunk_rows = got_ref.shape[:3]
    columns = chunks * chunk_rows
    sender_rows = tp * chunk_rows
    piece = min(columns, 256)
    sums = dot_nt(jnp.ones((16, HD), BF16), got_ref[:, 0].reshape(columns, HD))[:8]
    col = iota((8, columns), 1)
    held = sums < EMPTY
    first = jnp.where(held & (mod(col, sender_rows) == 0), 1.0, 0.0).astype(BF16)
    row = over(iota((piece, piece), 0), sender_rows)
    before = jnp.where(row < over(iota((piece, piece), 1), sender_rows), 1.0, 0.0).astype(BF16)
    base = jnp.zeros((8, 1), F32)
    ranks = []
    for p in range(0, columns, piece):
        part = first[:, p : p + piece]
        ranks.append(dot_nn(part, before) + base)
        base = base + jnp.sum(part.astype(F32), axis=1, keepdims=True)
    rank = jnp.concatenate(ranks, axis=1)
    return jnp.where(held & (mod(col, 2) == 0), rank, -1.0)[:1]


def arrival_kernel(
    tp, groups, order, block_rows, got_ref, query_ref, new_ref, done_ref, out_ref, done_hbm, sem
):
    step = pl.program_id(0) if groups > 1 else 0
    hand_on = pltpu.make_async_copy(done_ref, done_hbm, sem)
    if groups > 1:
        pl.when(step == 0)(hand_on.start)
    else:
        hand_on.start()

    chunks, heads, chunk_rows = got_ref.shape[:3]
    slots, _, per_head = query_ref.shape[:3]
    rows = slots * per_head
    columns = chunks * chunk_rows
    every = range(heads)

    new = new_ref[...]
    new_values = values_up(new)
    if order is None:
        slot_of = slots_by_matmul(got_ref, tp)
    else:
        slot_of = slots_by_rows(got_ref, tp, order, block_rows)
    first_slot = jnp.float32(step * slots)
    mine = [slot_of == first_slot + a for a in range(slots)]

    new_col = iota((rows, new.shape[0]), 1)
    new_row = iota((rows, new.shape[0]), 0)
    new_here = (
        (mod(new_col, 2) == 0)
        & (over(new_col, 2 * heads * STEPS) == over(new_row, per_head))
        & (mod(over(new_col, 2 * heads), STEPS) <= mod(new_row, STEPS))
    )
    new_head = jnp.where(new_here, mod(over(new_col, 2), heads), heads)

    def attend(h):
        cache = got_ref[:, h].reshape(columns, HD)
        query = query_ref[:, h].reshape(rows, HD)
        scores = dot_nt(query, cache) * SCORE_SCALE
        scores = jnp.concatenate(
            [
                jnp.where(mine[a], scores[a * per_head : (a + 1) * per_head], NEGATIVE)
                for a in range(slots)
            ],
            axis=0,
        )
        new_scores = jnp.where(new_head == h, dot_nt(query, new) * SCORE_SCALE, NEGATIVE)
        top = top_of(scores, new_scores)
        weights = jnp.exp(scores - top)
        new_weights = jnp.exp(new_scores - top)
        total = sum_of(weights, new_weights)
        mixed = dot_nn(to_values(weights), cache) + dot_nn(new_weights.astype(BF16), new_values)
        out_ref[:, h] = (mixed * (1.0 / total)).astype(BF16).reshape(slots, per_head, HD)

    pl.loop(0, heads)(attend)
    if groups > 1:
        pl.when(step == groups - 1)(hand_on.wait)
    else:
        hand_on.wait()


def whole(memory_space=pltpu.VMEM):
    return pl.BlockSpec(memory_space=memory_space)


def in_hbm(x):
    return pltpu.with_memory_space_constraint(x, pltpu.HBM)


def limit(mib):
    return pltpu.CompilerParams(vmem_limit_bytes=mib * 2**20)


def pack(pre_codes, pre_scales, req_dest, req_blocks, peers, tp, order):
    requests, blocks, block_tokens = pre_codes.shape[:3]
    tokens = blocks * block_tokens
    codes = (
        pre_codes.reshape(requests, tokens, 2, KVH, HD)
        .transpose(0, 1, 3, 2, 4)
        .reshape(requests, tokens * KVH * 2, HD)
    )
    scales = pre_scales.reshape(requests, tokens * 2, KVH)
    ins = [req_dest, req_blocks, codes, scales]
    return pl.pallas_call(
        functools.partial(pack_kernel, tp, order, KVH, 2 * block_tokens),
        out_shape=pltpu.VMEM((peers * tp, KVH // tp, tokens * 2, HD), BF16),
        in_specs=[whole(pltpu.SMEM)] * 2 + [whole()] * 2,
        out_specs=whole(),
        compiler_params=limit(16),
        name="pack",
    )(*[in_hbm(x) for x in ins])


def cache_rows(codes):
    slots, tokens, _, width = codes.shape
    heads = width // HD
    return (
        codes.reshape(slots, tokens, 2, heads, HD)
        .transpose(0, 1, 3, 2, 4)
        .reshape(slots, tokens * heads * 2, HD)
    )


def query_rows(query):
    slots, steps, width = query.shape
    return query.reshape(slots, steps, width // HD, HD).transpose(0, 2, 1, 3)


def new_rows_of(new):
    slots, steps, pair, width = new.shape
    heads = width // HD
    return (
        new.reshape(slots, steps, pair, heads, HD)
        .transpose(0, 1, 3, 2, 4)
        .reshape(slots * steps * heads * pair, HD)
    )


def from_rows(out, shape):
    slots, steps, width = shape
    return out.reshape(slots, width // HD, steps, HD).transpose(0, 2, 1, 3).reshape(shape)


def resident(codes, res_scales, res_len, res_query, res_new):
    slots, rows = codes.shape[:2]
    heads = res_scales.shape[-1]
    scales = res_scales.transpose(0, 2, 3, 1)
    query = query_rows(res_query).reshape(slots, heads * GROUP * STEPS, HD)
    work = query.shape[0] * query.shape[1] * rows
    return pl.pallas_call(
        resident_kernel,
        out_shape=pltpu.VMEM(query.shape, BF16),
        in_specs=[whole(pltpu.SMEM)] + [whole()] * 4,
        out_specs=whole(),
        cost_estimate=pl.CostEstimate(
            flops=4 * work * HD,
            bytes_accessed=2 * (codes.size + 2 * query.size),
            transcendentals=work,
        ),
        compiler_params=limit(16),
        name="resident",
    )(in_hbm(res_len), codes, scales, query, new_rows_of(res_new))


def arrivals(got, arr_query, arr_new, done, tp, order, block_rows):
    slots, steps, width = arr_query.shape
    heads = width // (HD * GROUP)
    query = query_rows(arr_query).reshape(slots, heads, GROUP * steps, HD)
    new = new_rows_of(arr_new)
    size = max(n for n in range(1, 7) if slots % n == 0)
    groups = slots // size
    small = got.size <= 2**18

    def part(ref, rows):
        if groups == 1:
            return whole()
        return pl.BlockSpec((rows,) + ref.shape[1:], lambda i: (i,) + (0,) * (ref.ndim - 1))

    return pl.pallas_call(
        functools.partial(arrival_kernel, tp, groups, order, block_rows),
        out_shape=[
            jax.ShapeDtypeStruct(query.shape, BF16),
            jax.ShapeDtypeStruct(done.shape, BF16),
        ],
        grid=(groups,) if groups > 1 else (),
        in_specs=[
            whole(),
            part(query, size),
            part(new, new.shape[0] // groups),
            whole(),
        ],
        out_specs=[part(query, size), whole(pltpu.HBM)],
        scratch_shapes=[pltpu.SemaphoreType.DMA],
        compiler_params=limit(16 if small else 48),
        name="arrivals",
    )(got, query, new, done)


def shards(
    pre_codes,
    pre_scales,
    req_dest,
    req_blocks,
    res_codes,
    res_scales,
    res_len,
    res_query,
    res_new,
    arr_query,
    arr_new,
):
    peers = lax.axis_size("wide")
    tp = lax.axis_size("tp")
    order = [5, 7, 6, 4, 3, 2, 1, 0] if peers == 8 else None
    send = pack(pre_codes, pre_scales, req_dest, req_blocks, peers, tp, order)
    got = lax.all_to_all(
        send,
        ("wide", "tp"),
        split_axis=0,
        concat_axis=0,
        tiled=True,
        axis_index_groups=[
            [w * tp + t for w in order or range(peers) for t in reversed(range(tp))]
        ],
    )
    done = resident(cache_rows(res_codes), res_scales, res_len, res_query, res_new)
    block_rows = 2 * pre_codes.shape[2]
    arr_out, res_out = arrivals(got, arr_query, arr_new, done, tp, order, block_rows)
    return (from_rows(res_out, res_query.shape), from_rows(arr_out, arr_query.shape))


def solution(mesh):
    in_specs = (
        P(("groups", "wide"), None, "tp", None, None),
        P(("groups", "wide"), None, "tp", None, None),
        P(("groups", "wide")),
        P(("groups", "wide")),
        P(("groups", "wide"), None, None, "tp"),
        P(("groups", "wide"), None, None, "tp"),
        P(("groups", "wide")),
        P(("groups", "wide"), None, "tp"),
        P(("groups", "wide"), None, None, "tp"),
        P(("groups", "wide"), None, "tp"),
        P(("groups", "wide"), None, None, "tp"),
    )
    out_specs = (P(("groups", "wide"), None, "tp"), P(("groups", "wide"), None, "tp"))
    return jax.shard_map(shards, mesh=mesh, in_specs=in_specs, out_specs=out_specs, check_vma=False)
```

```python
import functools
import math

import jax
import jax.numpy as jnp
from jax import lax
from jax.experimental import pallas as pl
from jax.experimental.pallas import tpu as pltpu
from jax.sharding import PartitionSpec as P

KVH = 4
HD = 128
HQ = 64
GROUP = HQ // KVH
STEPS = 2

NEGATIVE = -1e30
EMPTY = 1024.0
SCORE_SCALE = 1.0 / math.sqrt(HD)

PARTS = 4

BF16 = jnp.bfloat16
F32 = jnp.float32


def iota(shape, axis):
    return lax.broadcasted_iota(jnp.int32, shape, axis)


def over(x, n):
    return jnp.right_shift(x, n.bit_length() - 1) if n & (n - 1) == 0 else x // n


def mod(x, n):
    return jnp.bitwise_and(x, n - 1) if n & (n - 1) == 0 else x % n


def dot_nt(a, b):
    return lax.dot_general(a, b, (((1,), (1,)), ((), ())), preferred_element_type=F32)


def dot_nn(a, b):
    return lax.dot_general(a, b, (((1,), (0,)), ((), ())), preferred_element_type=F32)


def top_of(*parts):
    return functools.reduce(jnp.maximum, [jnp.max(p, axis=1, keepdims=True) for p in parts])


def sum_of(*parts):
    return functools.reduce(jnp.add, [jnp.sum(p, axis=1, keepdims=True) for p in parts])


def to_values(weights):
    tiles = [pltpu.roll(weights[:, c : c + HD], 1, 1) for c in range(0, weights.shape[1], HD)]
    return jnp.concatenate(tiles, axis=1).astype(BF16)


def values_up(rows):
    return pltpu.roll(rows.astype(F32), rows.shape[0] - 1, 0).astype(BF16)


def in_parts(source, target, sems):
    size = source.shape[0] // PARTS
    pieces = [pl.ds(i * size, size) for i in range(PARTS)]
    return [
        pltpu.make_async_copy(source.at[p], target.at[p], sems.at[i])
        for i, p in enumerate(pieces)
    ]


def hand_out(copies):
    for copy in copies:
        copy.start()
    for copy in copies:
        copy.wait()


def pack_kernel(
    tp, order, heads, block_rows, dest_ref, blocks_ref, codes_hbm, scales_ref, send_hbm,
    codes_ref, send_ref, sems,
):
    fetches = in_parts(codes_hbm, codes_ref, sems.at[0])
    for copy in fetches:
        copy.start()
    requests, all_rows = codes_ref.shape[:2]
    rows = all_rows // heads
    per_core = heads // tp
    send_ref[...] = jnp.full(send_ref.shape, EMPTY, BF16)
    row_block = over(iota((rows, HD), 0), block_rows)
    to_row = iota((all_rows, all_rows), 0)
    from_row = iota((all_rows, all_rows), 1)
    source = over(mod(to_row, rows), 2) * (2 * heads) + over(to_row, rows) * 2 + mod(to_row, 2)
    by_head = jnp.where(from_row == source, 1.0, 0.0).astype(BF16)
    for copy in fetches:
        copy.wait()

    def place(r):
        there = dest_ref[r]
        if order is not None:
            spots = [jnp.where(there == w, p, 0) for p, w in enumerate(order)]
            there = functools.reduce(jnp.add, spots)
        there = there * tp + tp - 1
        held = row_block < blocks_ref[r]
        codes = dot_nn(by_head, codes_ref[r])
        scales = scales_ref[r].astype(F32)
        for j in range(heads):
            values = codes[j * rows : (j + 1) * rows] * scales[:, j : j + 1]
            values = jnp.where(held, values, EMPTY).astype(BF16)
            send_ref[there - j // per_core, j % per_core] = values

    if requests <= 8:
        for r in range(requests):
            place(r)
    else:
        lax.fori_loop(0, requests, lambda r, c: (place(r), c)[1], 0)
    hand_out(in_parts(send_ref, send_hbm, sems.at[1]))


def resident_kernel(len_ref, codes_ref, scales_ref, query_ref, new_ref, out_ref):
    slots, rows = codes_ref.shape[:2]
    heads = scales_ref.shape[2]
    tokens = rows // (2 * heads)
    queries = query_ref.shape[1]
    new_rows = new_ref.shape[0]

    row = iota((rows, HD), 0)
    source = (mod(row, 2) * heads + mod(over(row, 2), heads)) * tokens + over(row, 2 * heads)
    lane = iota((rows, HD), 1)
    spread = jnp.concatenate(
        [jnp.where(source == lane + c, 1.0, 0.0).astype(BF16) for c in range(0, rows, HD)],
        axis=1,
    )
    flat = jnp.concatenate(
        [scales_ref[:, p, h] for p in range(2) for h in range(heads)], axis=1
    )
    columns = dot_nt(spread, flat).astype(BF16)

    col = iota((queries, rows), 1)
    row_head = over(iota((queries, rows), 0), queries // heads)
    is_key = (mod(col, 2) == 0) & (mod(over(col, 2), heads) == row_head)
    col_token = jnp.where(is_key, over(col, 2 * heads), tokens)

    new_col = iota((queries, new_rows), 1)
    new_row = iota((queries, new_rows), 0)
    new_ok = (
        (mod(new_col, 2) == 0)
        & (mod(over(new_col, 2), heads) == over(new_row, queries // heads))
        & (mod(over(new_col, 2 * heads), STEPS) <= mod(new_row, STEPS))
    )
    new_slot = jnp.where(new_ok, over(new_col, 2 * heads * STEPS), slots)

    every = range(slots)
    new = new_ref[...]
    new_all = dot_nt(query_ref[...].reshape(slots * queries, HD), new)
    caches = [codes_ref[s] * columns[:, s : s + 1] for s in every]
    scores = [dot_nt(query_ref[s], caches[s]) for s in every]
    scores = [jnp.where(col_token < len_ref[s], scores[s] * SCORE_SCALE, NEGATIVE) for s in every]
    new_scores = [
        jnp.where(new_slot == s, new_all[s * queries : (s + 1) * queries] * SCORE_SCALE, NEGATIVE)
        for s in every
    ]
    top = [top_of(scores[s], new_scores[s]) for s in every]
    weights = [jnp.exp(scores[s] - top[s]) for s in every]
    new_weights = [jnp.exp(new_scores[s] - top[s]) for s in every]
    total = [sum_of(weights[s], new_weights[s]) for s in every]
    new_mixed = dot_nn(jnp.concatenate(new_weights, axis=0).astype(BF16), values_up(new))
    mixed = [
        dot_nn(to_values(weights[s]), caches[s]) + new_mixed[s * queries : (s + 1) * queries]
        for s in every
    ]
    for s in every:
        out_ref[s] = (mixed[s] * (1.0 / total[s])).astype(BF16)


def slots_by_rows(got_ref, tp, order, block_rows):
    chunks, _, chunk_rows = got_ref.shape[:3]
    sender_rows = tp * chunk_rows
    blocks = chunk_rows // block_rows
    rows = [got_ref[p * tp, 0].astype(F32) for p in range(chunks // tp)]
    here = [jnp.where(x[:1] < EMPTY, 1.0, 0.0) for x in rows]
    ranks = [
        sum([here[q] for q, v in enumerate(order) if v < w], jnp.zeros((1, HD), F32))
        for w in order
    ]
    lane = iota((1, HD), 1)
    block = over(lane, sender_rows) * blocks + over(mod(lane, chunk_rows), block_rows)
    block = jnp.where(mod(lane, 2) == 0, block, -1)
    per_tile = HD // sender_rows
    tiles = []
    for start in range(0, len(rows), per_tile):
        tile = jnp.full((1, HD), -1.0, F32)
        for i in range(per_tile):
            x, rank = rows[start + i], ranks[start + i]
            for b in range(blocks):
                at = b * block_rows
                value = jnp.where(x[at : at + 1] < EMPTY, rank, -1.0)
                tile = jnp.where(block == i * blocks + b, value, tile)
        tiles.append(tile)
    return jnp.concatenate(tiles, axis=1)


def slots_by_matmul(got_ref, tp):
    chunks, _, chunk_rows = got_ref.shape[:3]
    columns = chunks * chunk_rows
    sender_rows = tp * chunk_rows
    piece = min(columns, 256)
    sums = dot_nt(jnp.ones((16, HD), BF16), got_ref[:, 0].reshape(columns, HD))[:8]
    col = iota((8, columns), 1)
    held = sums < EMPTY
    first = jnp.where(held & (mod(col, sender_rows) == 0), 1.0, 0.0).astype(BF16)
    row = over(iota((piece, piece), 0), sender_rows)
    before = jnp.where(row < over(iota((piece, piece), 1), sender_rows), 1.0, 0.0).astype(BF16)
    base = jnp.zeros((8, 1), F32)
    ranks = []
    for p in range(0, columns, piece):
        part = first[:, p : p + piece]
        ranks.append(dot_nn(part, before) + base)
        base = base + jnp.sum(part.astype(F32), axis=1, keepdims=True)
    rank = jnp.concatenate(ranks, axis=1)
    return jnp.where(held & (mod(col, 2) == 0), rank, -1.0)[:1]


def arrival_kernel(
    tp, groups, order, block_rows, got_ref, query_ref, new_ref, done_ref, out_hbm, done_hbm,
    out_ref, sems,
):
    step = pl.program_id(0) if groups > 1 else 0
    hand_on = pltpu.make_async_copy(done_ref, done_hbm, sems.at[0])
    if groups > 1:
        pl.when(step == 0)(hand_on.start)
    else:
        hand_on.start()

    chunks, heads, chunk_rows = got_ref.shape[:3]
    slots, _, per_head = query_ref.shape[:3]
    rows = slots * per_head
    columns = chunks * chunk_rows
    every = range(heads)

    caches = [got_ref[:, h].reshape(columns, HD) for h in every]
    queries = [query_ref[:, h].reshape(rows, HD) for h in every]
    new = new_ref[...]
    scores = [dot_nt(queries[h], caches[h]) for h in every]
    new_all = dot_nt(jnp.concatenate(queries, axis=0), new)
    if order is None:
        slot_of = slots_by_matmul(got_ref, tp)
    else:
        slot_of = slots_by_rows(got_ref, tp, order, block_rows)
    first_slot = jnp.float32(step * slots)
    mine = [slot_of == first_slot + a for a in range(slots)]

    new_col = iota((rows, new.shape[0]), 1)
    new_row = iota((rows, new.shape[0]), 0)
    new_here = (
        (mod(new_col, 2) == 0)
        & (over(new_col, 2 * heads * STEPS) == over(new_row, per_head))
        & (mod(over(new_col, 2 * heads), STEPS) <= mod(new_row, STEPS))
    )
    new_head = jnp.where(new_here, mod(over(new_col, 2), heads), heads)

    scores = [
        jnp.concatenate(
            [
                jnp.where(mine[a], scores[h][a * per_head : (a + 1) * per_head] * SCORE_SCALE, NEGATIVE)
                for a in range(slots)
            ],
            axis=0,
        )
        for h in every
    ]
    new_scores = [
        jnp.where(new_head == h, new_all[h * rows : (h + 1) * rows] * SCORE_SCALE, NEGATIVE)
        for h in every
    ]
    top = [top_of(scores[h], new_scores[h]) for h in every]
    weights = [jnp.exp(scores[h] - top[h]) for h in every]
    new_weights = [jnp.exp(new_scores[h] - top[h]) for h in every]
    total = [sum_of(weights[h], new_weights[h]) for h in every]
    new_mixed = dot_nn(jnp.concatenate(new_weights, axis=0).astype(BF16), values_up(new))
    for h in every:
        mixed = dot_nn(to_values(weights[h]), caches[h]) + new_mixed[h * rows : (h + 1) * rows]
        out_ref[:, h] = (mixed * (1.0 / total[h])).astype(BF16).reshape(slots, per_head, HD)
    pieces = [a for a in range(slots) if a % 2 == 0]
    copies = []
    for i, a in enumerate(pieces):
        size = min(2, slots - a)
        source = out_ref.at[pl.ds(a, size)]
        target = out_hbm.at[pl.ds(step * slots + a, size)]
        copies.append(pltpu.make_async_copy(source, target, sems.at[1 + i]))
    hand_out(copies)
    if groups > 1:
        pl.when(step == groups - 1)(hand_on.wait)
    else:
        hand_on.wait()


def whole(memory_space=pltpu.VMEM):
    return pl.BlockSpec(memory_space=memory_space)


def in_hbm(x):
    return pltpu.with_memory_space_constraint(x, pltpu.HBM)


def limit(mib):
    return pltpu.CompilerParams(vmem_limit_bytes=mib * 2**20)


def pack(pre_codes, pre_scales, req_dest, req_blocks, peers, tp, order):
    requests, blocks, block_tokens = pre_codes.shape[:3]
    tokens = blocks * block_tokens
    codes = (
        pre_codes.reshape(requests, tokens, 2, KVH, HD)
        .transpose(0, 1, 3, 2, 4)
        .reshape(requests, tokens * KVH * 2, HD)
    )
    scales = pre_scales.reshape(requests, tokens * 2, KVH)
    send = (peers * tp, KVH // tp, tokens * 2, HD)
    ins = [req_dest, req_blocks, codes, scales]
    return pl.pallas_call(
        functools.partial(pack_kernel, tp, order, KVH, 2 * block_tokens),
        out_shape=jax.ShapeDtypeStruct(send, BF16),
        in_specs=[whole(pltpu.SMEM)] * 2 + [whole(pltpu.HBM), whole()],
        out_specs=whole(pltpu.HBM),
        scratch_shapes=[
            pltpu.VMEM(codes.shape, BF16),
            pltpu.VMEM(send, BF16),
            pltpu.SemaphoreType.DMA((2, PARTS)),
        ],
        compiler_params=limit(16),
        name="pack",
    )(*[in_hbm(x) for x in ins])


def cache_rows(codes):
    slots, tokens, _, width = codes.shape
    heads = width // HD
    return (
        codes.reshape(slots, tokens, 2, heads, HD)
        .transpose(0, 1, 3, 2, 4)
        .reshape(slots, tokens * heads * 2, HD)
    )


def query_rows(query):
    slots, steps, width = query.shape
    return query.reshape(slots, steps, width // HD, HD).transpose(0, 2, 1, 3)


def new_rows_of(new):
    slots, steps, pair, width = new.shape
    heads = width // HD
    return (
        new.reshape(slots, steps, pair, heads, HD)
        .transpose(0, 1, 3, 2, 4)
        .reshape(slots * steps * heads * pair, HD)
    )


def from_rows(out, shape):
    slots, steps, width = shape
    return out.reshape(slots, width // HD, steps, HD).transpose(0, 2, 1, 3).reshape(shape)


def resident(codes, res_scales, res_len, res_query, res_new):
    slots, rows = codes.shape[:2]
    heads = res_scales.shape[-1]
    scales = res_scales.transpose(0, 2, 3, 1)
    query = query_rows(res_query).reshape(slots, heads * GROUP * STEPS, HD)
    work = query.shape[0] * query.shape[1] * rows
    return pl.pallas_call(
        resident_kernel,
        out_shape=pltpu.VMEM(query.shape, BF16),
        in_specs=[whole(pltpu.SMEM)] + [whole()] * 4,
        out_specs=whole(),
        cost_estimate=pl.CostEstimate(
            flops=4 * work * HD,
            bytes_accessed=2 * (codes.size + 2 * query.size),
            transcendentals=work,
        ),
        compiler_params=limit(16),
        name="resident",
    )(in_hbm(res_len), codes, scales, query, new_rows_of(res_new))


def arrivals(got, arr_query, arr_new, done, tp, order, block_rows):
    slots, steps, width = arr_query.shape
    heads = width // (HD * GROUP)
    query = query_rows(arr_query).reshape(slots, heads, GROUP * steps, HD)
    new = new_rows_of(arr_new)
    size = max(n for n in range(1, 7) if slots % n == 0)
    groups = slots // size
    small = got.size <= 2**18

    def part(ref, rows):
        if groups == 1:
            return whole()
        return pl.BlockSpec((rows,) + ref.shape[1:], lambda i: (i,) + (0,) * (ref.ndim - 1))

    return pl.pallas_call(
        functools.partial(arrival_kernel, tp, groups, order, block_rows),
        out_shape=[
            jax.ShapeDtypeStruct(query.shape, BF16),
            jax.ShapeDtypeStruct(done.shape, BF16),
        ],
        grid=(groups,) if groups > 1 else (),
        in_specs=[
            whole(),
            part(query, size),
            part(new, new.shape[0] // groups),
            whole(),
        ],
        out_specs=[whole(pltpu.HBM)] * 2,
        scratch_shapes=[
            pltpu.VMEM((size,) + query.shape[1:], BF16),
            pltpu.SemaphoreType.DMA((1 + (size + 1) // 2,)),
        ],
        compiler_params=limit(16 if small else 48),
        name="arrivals",
    )(got, query, new, done)


def shards(
    pre_codes,
    pre_scales,
    req_dest,
    req_blocks,
    res_codes,
    res_scales,
    res_len,
    res_query,
    res_new,
    arr_query,
    arr_new,
):
    peers = lax.axis_size("wide")
    tp = lax.axis_size("tp")
    order = [6, 7, 5, 4, 3, 2, 1, 0] if peers == 8 else None
    send = pack(pre_codes, pre_scales, req_dest, req_blocks, peers, tp, order)
    got = lax.all_to_all(
        send,
        ("wide", "tp"),
        split_axis=0,
        concat_axis=0,
        tiled=True,
        axis_index_groups=[
            [w * tp + t for w in order or range(peers) for t in reversed(range(tp))]
        ],
    )
    done = resident(cache_rows(res_codes), res_scales, res_len, res_query, res_new)
    block_rows = 2 * pre_codes.shape[2]
    arr_out, res_out = arrivals(got, arr_query, arr_new, done, tp, order, block_rows)
    return (from_rows(res_out, res_query.shape), from_rows(arr_out, arr_query.shape))


def solution(mesh):
    in_specs = (
        P(("groups", "wide"), None, "tp", None, None),
        P(("groups", "wide"), None, "tp", None, None),
        P(("groups", "wide")),
        P(("groups", "wide")),
        P(("groups", "wide"), None, None, "tp"),
        P(("groups", "wide"), None, None, "tp"),
        P(("groups", "wide")),
        P(("groups", "wide"), None, "tp"),
        P(("groups", "wide"), None, None, "tp"),
        P(("groups", "wide"), None, "tp"),
        P(("groups", "wide"), None, None, "tp"),
    )
    out_specs = (P(("groups", "wide"), None, "tp"), P(("groups", "wide"), None, "tp"))
    return jax.shard_map(shards, mesh=mesh, in_specs=in_specs, out_specs=out_specs, check_vma=False)
```

```python
import functools
import math

import jax
import jax.numpy as jnp
from jax import lax
from jax.experimental import pallas as pl
from jax.experimental.pallas import tpu as pltpu
from jax.sharding import PartitionSpec as P

KVH = 4
HD = 128
HQ = 64
GROUP = HQ // KVH
STEPS = 2

NEGATIVE = -1e30
EMPTY = 1024.0
SCORE_SCALE = 1.0 / math.sqrt(HD)

BF16 = jnp.bfloat16
F32 = jnp.float32


def iota(shape, axis):
    return lax.broadcasted_iota(jnp.int32, shape, axis)


def over(x, n):
    return jnp.right_shift(x, n.bit_length() - 1) if n & (n - 1) == 0 else x // n


def mod(x, n):
    return jnp.bitwise_and(x, n - 1) if n & (n - 1) == 0 else x % n


def dot_nt(a, b):
    return lax.dot_general(a, b, (((1,), (1,)), ((), ())), preferred_element_type=F32)


def dot_nn(a, b):
    return lax.dot_general(a, b, (((1,), (0,)), ((), ())), preferred_element_type=F32)


def top_of(*parts):
    return functools.reduce(jnp.maximum, [jnp.max(p, axis=1, keepdims=True) for p in parts])


def sum_of(*parts):
    return functools.reduce(jnp.add, [jnp.sum(p, axis=1, keepdims=True) for p in parts])


def to_values(weights):
    tiles = [pltpu.roll(weights[:, c : c + HD], 1, 1) for c in range(0, weights.shape[1], HD)]
    return jnp.concatenate(tiles, axis=1).astype(BF16)


def values_up(rows):
    return pltpu.roll(rows.astype(F32), rows.shape[0] - 1, 0).astype(BF16)


def pack_kernel(
    tp, order, heads, block_rows, dest_ref, blocks_ref, codes_ref, scales_ref, send_ref
):
    requests, all_rows = codes_ref.shape[:2]
    rows = all_rows // heads
    per_core = heads // tp
    send_ref[...] = jnp.full(send_ref.shape, EMPTY, BF16)
    row_block = over(iota((rows, HD), 0), block_rows)
    to_row = iota((all_rows, all_rows), 0)
    from_row = iota((all_rows, all_rows), 1)
    source = over(mod(to_row, rows), 2) * (2 * heads) + over(to_row, rows) * 2 + mod(to_row, 2)
    by_head = jnp.where(from_row == source, 1.0, 0.0).astype(BF16)

    def place(r):
        there = dest_ref[r]
        if order is not None:
            spots = [jnp.where(there == w, p, 0) for p, w in enumerate(order)]
            there = functools.reduce(jnp.add, spots)
        there = there * tp + tp - 1
        held = row_block < blocks_ref[r]
        codes = dot_nn(by_head, codes_ref[r])
        scales = scales_ref[r].astype(F32)
        for j in range(heads):
            values = codes[j * rows : (j + 1) * rows] * scales[:, j : j + 1]
            values = jnp.where(held, values, EMPTY).astype(BF16)
            send_ref[there - j // per_core, j % per_core] = values

    if requests <= 8:
        for r in range(requests):
            place(r)
    else:
        lax.fori_loop(0, requests, lambda r, c: (place(r), c)[1], 0)


def resident_kernel(len_ref, codes_ref, scales_ref, query_ref, new_ref, out_ref):
    slots, rows = codes_ref.shape[:2]
    heads = scales_ref.shape[2]
    tokens = rows // (2 * heads)
    queries = query_ref.shape[1]
    new_rows = new_ref.shape[0]

    row = iota((rows, HD), 0)
    source = (mod(row, 2) * heads + mod(over(row, 2), heads)) * tokens + over(row, 2 * heads)
    lane = iota((rows, HD), 1)
    spread = jnp.concatenate(
        [jnp.where(source == lane + c, 1.0, 0.0).astype(BF16) for c in range(0, rows, HD)],
        axis=1,
    )
    flat = jnp.concatenate(
        [scales_ref[:, p, h] for p in range(2) for h in range(heads)], axis=1
    )
    columns = dot_nt(spread, flat).astype(BF16)

    col = iota((queries, rows), 1)
    row_head = over(iota((queries, rows), 0), queries // heads)
    is_key = (mod(col, 2) == 0) & (mod(over(col, 2), heads) == row_head)
    col_token = jnp.where(is_key, over(col, 2 * heads), tokens)

    new_col = iota((queries, new_rows), 1)
    new_row = iota((queries, new_rows), 0)
    new_ok = (
        (mod(new_col, 2) == 0)
        & (mod(over(new_col, 2), heads) == over(new_row, queries // heads))
        & (mod(over(new_col, 2 * heads), STEPS) <= mod(new_row, STEPS))
    )
    new_slot = jnp.where(new_ok, over(new_col, 2 * heads * STEPS), slots)

    every = range(slots)
    new = new_ref[...]
    new_all = dot_nt(query_ref[...].reshape(slots * queries, HD), new)
    caches = [codes_ref[s] * columns[:, s : s + 1] for s in every]
    scores = [dot_nt(query_ref[s], caches[s]) for s in every]
    scores = [jnp.where(col_token < len_ref[s], scores[s] * SCORE_SCALE, NEGATIVE) for s in every]
    new_scores = [
        jnp.where(new_slot == s, new_all[s * queries : (s + 1) * queries] * SCORE_SCALE, NEGATIVE)
        for s in every
    ]
    top = [top_of(scores[s], new_scores[s]) for s in every]
    weights = [jnp.exp(scores[s] - top[s]) for s in every]
    new_weights = [jnp.exp(new_scores[s] - top[s]) for s in every]
    total = [sum_of(weights[s], new_weights[s]) for s in every]
    new_mixed = dot_nn(jnp.concatenate(new_weights, axis=0).astype(BF16), values_up(new))
    mixed = [
        dot_nn(to_values(weights[s]), caches[s]) + new_mixed[s * queries : (s + 1) * queries]
        for s in every
    ]
    for s in every:
        out_ref[s] = (mixed[s] * (1.0 / total[s])).astype(BF16)


def slots_by_rows(got_ref, tp, order, block_rows):
    chunks, _, chunk_rows = got_ref.shape[:3]
    sender_rows = tp * chunk_rows
    blocks = chunk_rows // block_rows
    rows = [got_ref[p * tp, 0].astype(F32) for p in range(chunks // tp)]
    here = [jnp.where(x[:1] < EMPTY, 1.0, 0.0) for x in rows]
    ranks = [
        sum([here[q] for q, v in enumerate(order) if v < w], jnp.zeros((1, HD), F32))
        for w in order
    ]
    lane = iota((1, HD), 1)
    block = over(lane, sender_rows) * blocks + over(mod(lane, chunk_rows), block_rows)
    block = jnp.where(mod(lane, 2) == 0, block, -1)
    per_tile = HD // sender_rows
    tiles = []
    for start in range(0, len(rows), per_tile):
        tile = jnp.full((1, HD), -1.0, F32)
        for i in range(per_tile):
            x, rank = rows[start + i], ranks[start + i]
            for b in range(blocks):
                at = b * block_rows
                value = jnp.where(x[at : at + 1] < EMPTY, rank, -1.0)
                tile = jnp.where(block == i * blocks + b, value, tile)
        tiles.append(tile)
    return jnp.concatenate(tiles, axis=1)


def slots_by_matmul(got_ref, tp):
    chunks, _, chunk_rows = got_ref.shape[:3]
    columns = chunks * chunk_rows
    sender_rows = tp * chunk_rows
    piece = min(columns, 256)
    sums = dot_nt(jnp.ones((16, HD), BF16), got_ref[:, 0].reshape(columns, HD))[:8]
    col = iota((8, columns), 1)
    held = sums < EMPTY
    first = jnp.where(held & (mod(col, sender_rows) == 0), 1.0, 0.0).astype(BF16)
    row = over(iota((piece, piece), 0), sender_rows)
    before = jnp.where(row < over(iota((piece, piece), 1), sender_rows), 1.0, 0.0).astype(BF16)
    base = jnp.zeros((8, 1), F32)
    ranks = []
    for p in range(0, columns, piece):
        part = first[:, p : p + piece]
        ranks.append(dot_nn(part, before) + base)
        base = base + jnp.sum(part.astype(F32), axis=1, keepdims=True)
    rank = jnp.concatenate(ranks, axis=1)
    return jnp.where(held & (mod(col, 2) == 0), rank, -1.0)[:1]


def arrival_kernel(
    tp, groups, order, block_rows, got_ref, query_ref, new_ref, done_ref, out_ref, done_hbm, sem
):
    step = pl.program_id(0) if groups > 1 else 0
    hand_on = pltpu.make_async_copy(done_ref, done_hbm, sem)
    if groups > 1:
        pl.when(step == 0)(hand_on.start)
    else:
        hand_on.start()

    chunks, heads, chunk_rows = got_ref.shape[:3]
    slots, _, per_head = query_ref.shape[:3]
    rows = slots * per_head
    columns = chunks * chunk_rows
    every = range(heads)

    caches = [got_ref[:, h].reshape(columns, HD) for h in every]
    queries = [query_ref[:, h].reshape(rows, HD) for h in every]
    new = new_ref[...]
    scores = [dot_nt(queries[h], caches[h]) for h in every]
    new_all = dot_nt(jnp.concatenate(queries, axis=0), new)
    if order is None:
        slot_of = slots_by_matmul(got_ref, tp)
    else:
        slot_of = slots_by_rows(got_ref, tp, order, block_rows)
    first_slot = jnp.float32(step * slots)
    mine = [slot_of == first_slot + a for a in range(slots)]

    new_col = iota((rows, new.shape[0]), 1)
    new_row = iota((rows, new.shape[0]), 0)
    new_here = (
        (mod(new_col, 2) == 0)
        & (over(new_col, 2 * heads * STEPS) == over(new_row, per_head))
        & (mod(over(new_col, 2 * heads), STEPS) <= mod(new_row, STEPS))
    )
    new_head = jnp.where(new_here, mod(over(new_col, 2), heads), heads)

    scores = [
        jnp.concatenate(
            [
                jnp.where(mine[a], scores[h][a * per_head : (a + 1) * per_head] * SCORE_SCALE, NEGATIVE)
                for a in range(slots)
            ],
            axis=0,
        )
        for h in every
    ]
    new_scores = [
        jnp.where(new_head == h, new_all[h * rows : (h + 1) * rows] * SCORE_SCALE, NEGATIVE)
        for h in every
    ]
    top = [top_of(scores[h], new_scores[h]) for h in every]
    weights = [jnp.exp(scores[h] - top[h]) for h in every]
    new_weights = [jnp.exp(new_scores[h] - top[h]) for h in every]
    total = [sum_of(weights[h], new_weights[h]) for h in every]
    new_mixed = dot_nn(jnp.concatenate(new_weights, axis=0).astype(BF16), values_up(new))
    for h in every:
        mixed = dot_nn(to_values(weights[h]), caches[h]) + new_mixed[h * rows : (h + 1) * rows]
        out_ref[:, h] = (mixed * (1.0 / total[h])).astype(BF16).reshape(slots, per_head, HD)
    if groups > 1:
        pl.when(step == groups - 1)(hand_on.wait)
    else:
        hand_on.wait()


def whole(memory_space=pltpu.VMEM):
    return pl.BlockSpec(memory_space=memory_space)


def in_hbm(x):
    return pltpu.with_memory_space_constraint(x, pltpu.HBM)


def limit(mib):
    return pltpu.CompilerParams(vmem_limit_bytes=mib * 2**20)


def pack(pre_codes, pre_scales, req_dest, req_blocks, peers, tp, order):
    requests, blocks, block_tokens = pre_codes.shape[:3]
    tokens = blocks * block_tokens
    codes = (
        pre_codes.reshape(requests, tokens, 2, KVH, HD)
        .transpose(0, 1, 3, 2, 4)
        .reshape(requests, tokens * KVH * 2, HD)
    )
    scales = pre_scales.reshape(requests, tokens * 2, KVH)
    ins = [req_dest, req_blocks, codes, scales]
    return pl.pallas_call(
        functools.partial(pack_kernel, tp, order, KVH, 2 * block_tokens),
        out_shape=pltpu.VMEM((peers * tp, KVH // tp, tokens * 2, HD), BF16),
        in_specs=[whole(pltpu.SMEM)] * 2 + [whole()] * 2,
        out_specs=whole(),
        compiler_params=limit(16),
        name="pack",
    )(*[in_hbm(x) for x in ins])


def cache_rows(codes):
    slots, tokens, _, width = codes.shape
    heads = width // HD
    return (
        codes.reshape(slots, tokens, 2, heads, HD)
        .transpose(0, 1, 3, 2, 4)
        .reshape(slots, tokens * heads * 2, HD)
    )


def query_rows(query):
    slots, steps, width = query.shape
    return query.reshape(slots, steps, width // HD, HD).transpose(0, 2, 1, 3)


def new_rows_of(new):
    slots, steps, pair, width = new.shape
    heads = width // HD
    return (
        new.reshape(slots, steps, pair, heads, HD)
        .transpose(0, 1, 3, 2, 4)
        .reshape(slots * steps * heads * pair, HD)
    )


def from_rows(out, shape):
    slots, steps, width = shape
    return out.reshape(slots, width // HD, steps, HD).transpose(0, 2, 1, 3).reshape(shape)


def resident(codes, res_scales, res_len, res_query, res_new):
    slots, rows = codes.shape[:2]
    heads = res_scales.shape[-1]
    scales = res_scales.transpose(0, 2, 3, 1)
    query = query_rows(res_query).reshape(slots, heads * GROUP * STEPS, HD)
    work = query.shape[0] * query.shape[1] * rows
    return pl.pallas_call(
        resident_kernel,
        out_shape=pltpu.VMEM(query.shape, BF16),
        in_specs=[whole(pltpu.SMEM)] + [whole()] * 4,
        out_specs=whole(),
        cost_estimate=pl.CostEstimate(
            flops=4 * work * HD,
            bytes_accessed=2 * (codes.size + 2 * query.size),
            transcendentals=work,
        ),
        compiler_params=limit(16),
        name="resident",
    )(in_hbm(res_len), codes, scales, query, new_rows_of(res_new))


def arrivals(got, arr_query, arr_new, done, tp, order, block_rows):
    slots, steps, width = arr_query.shape
    heads = width // (HD * GROUP)
    query = query_rows(arr_query).reshape(slots, heads, GROUP * steps, HD)
    new = new_rows_of(arr_new)
    size = max(n for n in range(1, 7) if slots % n == 0)
    groups = slots // size
    small = got.size <= 2**18

    def part(ref, rows):
        if groups == 1:
            return whole()
        return pl.BlockSpec((rows,) + ref.shape[1:], lambda i: (i,) + (0,) * (ref.ndim - 1))

    return pl.pallas_call(
        functools.partial(arrival_kernel, tp, groups, order, block_rows),
        out_shape=[
            jax.ShapeDtypeStruct(query.shape, BF16),
            jax.ShapeDtypeStruct(done.shape, BF16),
        ],
        grid=(groups,) if groups > 1 else (),
        in_specs=[
            whole(),
            part(query, size),
            part(new, new.shape[0] // groups),
            whole(),
        ],
        out_specs=[part(query, size), whole(pltpu.HBM)],
        scratch_shapes=[pltpu.SemaphoreType.DMA],
        compiler_params=limit(16 if small else 48),
        name="arrivals",
    )(got, query, new, done)


def shards(
    pre_codes,
    pre_scales,
    req_dest,
    req_blocks,
    res_codes,
    res_scales,
    res_len,
    res_query,
    res_new,
    arr_query,
    arr_new,
):
    peers = lax.axis_size("wide")
    tp = lax.axis_size("tp")
    order = [5, 4, 7, 6, 1, 0, 3, 2] if peers == 8 else None
    send = pack(pre_codes, pre_scales, req_dest, req_blocks, peers, tp, order)
    got = lax.all_to_all(
        send,
        ("wide", "tp"),
        split_axis=0,
        concat_axis=0,
        tiled=True,
        axis_index_groups=[
            [w * tp + t for w in order or range(peers) for t in reversed(range(tp))]
        ],
    )
    done = resident(cache_rows(res_codes), res_scales, res_len, res_query, res_new)
    block_rows = 2 * pre_codes.shape[2]
    arr_out, res_out = arrivals(got, arr_query, arr_new, done, tp, order, block_rows)
    return (from_rows(res_out, res_query.shape), from_rows(arr_out, arr_query.shape))


def solution(mesh):
    in_specs = (
        P(("groups", "wide"), None, "tp", None, None),
        P(("groups", "wide"), None, "tp", None, None),
        P(("groups", "wide")),
        P(("groups", "wide")),
        P(("groups", "wide"), None, None, "tp"),
        P(("groups", "wide"), None, None, "tp"),
        P(("groups", "wide")),
        P(("groups", "wide"), None, "tp"),
        P(("groups", "wide"), None, None, "tp"),
        P(("groups", "wide"), None, "tp"),
        P(("groups", "wide"), None, None, "tp"),
    )
    out_specs = (P(("groups", "wide"), None, "tp"), P(("groups", "wide"), None, "tp"))
    return jax.shard_map(shards, mesh=mesh, in_specs=in_specs, out_specs=out_specs, check_vma=False)
```

```python
import functools
import math

import jax
import jax.numpy as jnp
from jax import lax
from jax.experimental import pallas as pl
from jax.experimental.pallas import tpu as pltpu
from jax.sharding import PartitionSpec as P

KVH = 4
HD = 128
HQ = 64
GROUP = HQ // KVH
STEPS = 2

NEGATIVE = -1e30
EMPTY = 1024.0
SCORE_SCALE = 1.0 / math.sqrt(HD)

BF16 = jnp.bfloat16
F32 = jnp.float32


def iota(shape, axis):
    return lax.broadcasted_iota(jnp.int32, shape, axis)


def over(x, n):
    return jnp.right_shift(x, n.bit_length() - 1) if n & (n - 1) == 0 else x // n


def mod(x, n):
    return jnp.bitwise_and(x, n - 1) if n & (n - 1) == 0 else x % n


def dot_nt(a, b):
    return lax.dot_general(a, b, (((1,), (1,)), ((), ())), preferred_element_type=F32)


def dot_nn(a, b):
    return lax.dot_general(a, b, (((1,), (0,)), ((), ())), preferred_element_type=F32)


def top_of(*parts):
    return functools.reduce(jnp.maximum, [jnp.max(p, axis=1, keepdims=True) for p in parts])


def sum_of(*parts):
    return functools.reduce(jnp.add, [jnp.sum(p, axis=1, keepdims=True) for p in parts])


def to_values(weights):
    tiles = [pltpu.roll(weights[:, c : c + HD], 1, 1) for c in range(0, weights.shape[1], HD)]
    return jnp.concatenate(tiles, axis=1).astype(BF16)


def values_up(rows):
    return pltpu.roll(rows.astype(F32), rows.shape[0] - 1, 0).astype(BF16)


def pack_kernel(
    tp, order, heads, block_rows, dest_ref, blocks_ref, codes_ref, scales_ref, send_ref
):
    requests, all_rows = codes_ref.shape[:2]
    rows = all_rows // heads
    per_core = heads // tp
    send_ref[...] = jnp.full(send_ref.shape, EMPTY, BF16)
    row_block = over(iota((rows, HD), 0), block_rows)
    to_row = iota((all_rows, all_rows), 0)
    from_row = iota((all_rows, all_rows), 1)
    source = over(mod(to_row, rows), 2) * (2 * heads) + over(to_row, rows) * 2 + mod(to_row, 2)
    by_head = jnp.where(from_row == source, 1.0, 0.0).astype(BF16)

    def place(r):
        there = dest_ref[r]
        spots = [there * tp + t for t in range(tp)]
        if order is not None:
            for t in range(tp):
                at = {core // tp: p for p, core in enumerate(order) if core % tp == t}
                spots[t] = functools.reduce(
                    jnp.add, [jnp.where(there == w, p, 0) for w, p in at.items()]
                )
        held = row_block < blocks_ref[r]
        codes = dot_nn(by_head, codes_ref[r])
        scales = scales_ref[r].astype(F32)
        for j in range(heads):
            values = codes[j * rows : (j + 1) * rows] * scales[:, j : j + 1]
            values = jnp.where(held, values, EMPTY).astype(BF16)
            send_ref[spots[j // per_core], j % per_core] = values

    if requests <= 8:
        for r in range(requests):
            place(r)
    else:
        lax.fori_loop(0, requests, lambda r, c: (place(r), c)[1], 0)


def resident_kernel(len_ref, codes_ref, scales_ref, query_ref, new_ref, out_ref):
    slots, rows = codes_ref.shape[:2]
    heads = scales_ref.shape[2]
    tokens = rows // (2 * heads)
    queries = query_ref.shape[1]
    new_rows = new_ref.shape[0]

    row = iota((rows, HD), 0)
    source = (mod(row, 2) * heads + mod(over(row, 2), heads)) * tokens + over(row, 2 * heads)
    lane = iota((rows, HD), 1)
    spread = jnp.concatenate(
        [jnp.where(source == lane + c, 1.0, 0.0).astype(BF16) for c in range(0, rows, HD)],
        axis=1,
    )
    flat = jnp.concatenate(
        [scales_ref[:, p, h] for p in range(2) for h in range(heads)], axis=1
    )
    columns = dot_nt(spread, flat).astype(BF16)

    col = iota((queries, rows), 1)
    row_head = over(iota((queries, rows), 0), queries // heads)
    is_key = (mod(col, 2) == 0) & (mod(over(col, 2), heads) == row_head)
    col_token = jnp.where(is_key, over(col, 2 * heads), tokens)

    new_col = iota((queries, new_rows), 1)
    new_row = iota((queries, new_rows), 0)
    new_ok = (
        (mod(new_col, 2) == 0)
        & (mod(over(new_col, 2), heads) == over(new_row, queries // heads))
        & (mod(over(new_col, 2 * heads), STEPS) <= mod(new_row, STEPS))
    )
    new_slot = jnp.where(new_ok, over(new_col, 2 * heads * STEPS), slots)

    every = range(slots)
    new = new_ref[...]
    new_all = dot_nt(query_ref[...].reshape(slots * queries, HD), new)
    caches = [codes_ref[s] * columns[:, s : s + 1] for s in every]
    scores = [dot_nt(query_ref[s], caches[s]) for s in every]
    scores = [jnp.where(col_token < len_ref[s], scores[s] * SCORE_SCALE, NEGATIVE) for s in every]
    new_scores = [
        jnp.where(new_slot == s, new_all[s * queries : (s + 1) * queries] * SCORE_SCALE, NEGATIVE)
        for s in every
    ]
    top = [top_of(scores[s], new_scores[s]) for s in every]
    weights = [jnp.exp(scores[s] - top[s]) for s in every]
    new_weights = [jnp.exp(new_scores[s] - top[s]) for s in every]
    total = [sum_of(weights[s], new_weights[s]) for s in every]
    new_mixed = dot_nn(jnp.concatenate(new_weights, axis=0).astype(BF16), values_up(new))
    mixed = [
        dot_nn(to_values(weights[s]), caches[s]) + new_mixed[s * queries : (s + 1) * queries]
        for s in every
    ]
    for s in every:
        out_ref[s] = (mixed[s] * (1.0 / total[s])).astype(BF16)


def slots_by_rows(got_ref, tp, order, block_rows):
    chunk_rows = got_ref.shape[2]
    blocks = chunk_rows // block_rows
    rows = [got_ref[k, 0].astype(F32) for k in range(len(order))]
    here = {
        core // tp: jnp.where(x[:1] < EMPTY, 1.0, 0.0)
        for core, x in zip(order, rows)
        if core % tp == 0
    }
    ranks = {
        w: sum([here[v] for v in here if v < w], jnp.zeros((1, HD), F32)) for w in here
    }
    lane = iota((1, HD), 1)
    block = over(lane, block_rows)
    block = jnp.where(mod(lane, 2) == 0, block, -1)
    per_tile = HD // chunk_rows
    tiles = []
    for start in range(0, len(order), per_tile):
        tile = jnp.full((1, HD), -1.0, F32)
        for i in range(per_tile):
            x, rank = rows[start + i], ranks[order[start + i] // tp]
            for b in range(blocks):
                at = b * block_rows
                value = jnp.where(x[at : at + 1] < EMPTY, rank, -1.0)
                tile = jnp.where(block == i * blocks + b, value, tile)
        tiles.append(tile)
    return jnp.concatenate(tiles, axis=1)


def slots_by_matmul(got_ref, tp):
    chunks, _, chunk_rows = got_ref.shape[:3]
    columns = chunks * chunk_rows
    sender_rows = tp * chunk_rows
    piece = min(columns, 256)
    sums = dot_nt(jnp.ones((16, HD), BF16), got_ref[:, 0].reshape(columns, HD))[:8]
    col = iota((8, columns), 1)
    held = sums < EMPTY
    first = jnp.where(held & (mod(col, sender_rows) == 0), 1.0, 0.0).astype(BF16)
    row = over(iota((piece, piece), 0), sender_rows)
    before = jnp.where(row < over(iota((piece, piece), 1), sender_rows), 1.0, 0.0).astype(BF16)
    base = jnp.zeros((8, 1), F32)
    ranks = []
    for p in range(0, columns, piece):
        part = first[:, p : p + piece]
        ranks.append(dot_nn(part, before) + base)
        base = base + jnp.sum(part.astype(F32), axis=1, keepdims=True)
    rank = jnp.concatenate(ranks, axis=1)
    return jnp.where(held & (mod(col, 2) == 0), rank, -1.0)[:1]


def arrival_kernel(
    tp, groups, order, block_rows, got_ref, query_ref, new_ref, done_ref, out_ref, done_hbm, sem
):
    step = pl.program_id(0) if groups > 1 else 0
    hand_on = pltpu.make_async_copy(done_ref, done_hbm, sem)
    if groups > 1:
        pl.when(step == 0)(hand_on.start)
    else:
        hand_on.start()

    chunks, heads, chunk_rows = got_ref.shape[:3]
    slots, _, per_head = query_ref.shape[:3]
    rows = slots * per_head
    columns = chunks * chunk_rows
    every = range(heads)

    caches = [got_ref[:, h].reshape(columns, HD) for h in every]
    queries = [query_ref[:, h].reshape(rows, HD) for h in every]
    new = new_ref[...]
    scores = [dot_nt(queries[h], caches[h]) for h in every]
    new_all = dot_nt(jnp.concatenate(queries, axis=0), new)
    if order is None:
        slot_of = slots_by_matmul(got_ref, tp)
    else:
        slot_of = slots_by_rows(got_ref, tp, order, block_rows)
    first_slot = jnp.float32(step * slots)
    mine = [slot_of == first_slot + a for a in range(slots)]

    new_col = iota((rows, new.shape[0]), 1)
    new_row = iota((rows, new.shape[0]), 0)
    new_here = (
        (mod(new_col, 2) == 0)
        & (over(new_col, 2 * heads * STEPS) == over(new_row, per_head))
        & (mod(over(new_col, 2 * heads), STEPS) <= mod(new_row, STEPS))
    )
    new_head = jnp.where(new_here, mod(over(new_col, 2), heads), heads)

    scores = [
        jnp.concatenate(
            [
                jnp.where(mine[a], scores[h][a * per_head : (a + 1) * per_head] * SCORE_SCALE, NEGATIVE)
                for a in range(slots)
            ],
            axis=0,
        )
        for h in every
    ]
    new_scores = [
        jnp.where(new_head == h, new_all[h * rows : (h + 1) * rows] * SCORE_SCALE, NEGATIVE)
        for h in every
    ]
    top = [top_of(scores[h], new_scores[h]) for h in every]
    weights = [jnp.exp(scores[h] - top[h]) for h in every]
    new_weights = [jnp.exp(new_scores[h] - top[h]) for h in every]
    total = [sum_of(weights[h], new_weights[h]) for h in every]
    new_mixed = dot_nn(jnp.concatenate(new_weights, axis=0).astype(BF16), values_up(new))
    for h in every:
        mixed = dot_nn(to_values(weights[h]), caches[h]) + new_mixed[h * rows : (h + 1) * rows]
        out_ref[:, h] = (mixed * (1.0 / total[h])).astype(BF16).reshape(slots, per_head, HD)
    if groups > 1:
        pl.when(step == groups - 1)(hand_on.wait)
    else:
        hand_on.wait()


def whole(memory_space=pltpu.VMEM):
    return pl.BlockSpec(memory_space=memory_space)


def in_hbm(x):
    return pltpu.with_memory_space_constraint(x, pltpu.HBM)


def limit(mib):
    return pltpu.CompilerParams(vmem_limit_bytes=mib * 2**20)


def pack(pre_codes, pre_scales, req_dest, req_blocks, peers, tp, order):
    requests, blocks, block_tokens = pre_codes.shape[:3]
    tokens = blocks * block_tokens
    codes = (
        pre_codes.reshape(requests, tokens, 2, KVH, HD)
        .transpose(0, 1, 3, 2, 4)
        .reshape(requests, tokens * KVH * 2, HD)
    )
    scales = pre_scales.reshape(requests, tokens * 2, KVH)
    ins = [req_dest, req_blocks, codes, scales]
    return pl.pallas_call(
        functools.partial(pack_kernel, tp, order, KVH, 2 * block_tokens),
        out_shape=pltpu.VMEM((peers * tp, KVH // tp, tokens * 2, HD), BF16),
        in_specs=[whole(pltpu.SMEM)] * 2 + [whole()] * 2,
        out_specs=whole(),
        compiler_params=limit(16),
        name="pack",
    )(*[in_hbm(x) for x in ins])


def cache_rows(codes):
    slots, tokens, _, width = codes.shape
    heads = width // HD
    return (
        codes.reshape(slots, tokens, 2, heads, HD)
        .transpose(0, 1, 3, 2, 4)
        .reshape(slots, tokens * heads * 2, HD)
    )


def query_rows(query):
    slots, steps, width = query.shape
    return query.reshape(slots, steps, width // HD, HD).transpose(0, 2, 1, 3)


def new_rows_of(new):
    slots, steps, pair, width = new.shape
    heads = width // HD
    return (
        new.reshape(slots, steps, pair, heads, HD)
        .transpose(0, 1, 3, 2, 4)
        .reshape(slots * steps * heads * pair, HD)
    )


def from_rows(out, shape):
    slots, steps, width = shape
    return out.reshape(slots, width // HD, steps, HD).transpose(0, 2, 1, 3).reshape(shape)


def resident(codes, res_scales, res_len, res_query, res_new):
    slots, rows = codes.shape[:2]
    heads = res_scales.shape[-1]
    scales = res_scales.transpose(0, 2, 3, 1)
    query = query_rows(res_query).reshape(slots, heads * GROUP * STEPS, HD)
    work = query.shape[0] * query.shape[1] * rows
    return pl.pallas_call(
        resident_kernel,
        out_shape=pltpu.VMEM(query.shape, BF16),
        in_specs=[whole(pltpu.SMEM)] + [whole()] * 4,
        out_specs=whole(),
        cost_estimate=pl.CostEstimate(
            flops=4 * work * HD,
            bytes_accessed=2 * (codes.size + 2 * query.size),
            transcendentals=work,
        ),
        compiler_params=limit(16),
        name="resident",
    )(in_hbm(res_len), codes, scales, query, new_rows_of(res_new))


def arrivals(got, arr_query, arr_new, done, tp, order, block_rows):
    slots, steps, width = arr_query.shape
    heads = width // (HD * GROUP)
    query = query_rows(arr_query).reshape(slots, heads, GROUP * steps, HD)
    new = new_rows_of(arr_new)
    size = max(n for n in range(1, 7) if slots % n == 0)
    groups = slots // size
    small = got.size <= 2**18

    def part(ref, rows):
        if groups == 1:
            return whole()
        return pl.BlockSpec((rows,) + ref.shape[1:], lambda i: (i,) + (0,) * (ref.ndim - 1))

    return pl.pallas_call(
        functools.partial(arrival_kernel, tp, groups, order, block_rows),
        out_shape=[
            jax.ShapeDtypeStruct(query.shape, BF16),
            jax.ShapeDtypeStruct(done.shape, BF16),
        ],
        grid=(groups,) if groups > 1 else (),
        in_specs=[
            whole(),
            part(query, size),
            part(new, new.shape[0] // groups),
            whole(),
        ],
        out_specs=[part(query, size), whole(pltpu.HBM)],
        scratch_shapes=[pltpu.SemaphoreType.DMA],
        compiler_params=limit(16 if small else 48),
        name="arrivals",
    )(got, query, new, done)


def shards(
    pre_codes,
    pre_scales,
    req_dest,
    req_blocks,
    res_codes,
    res_scales,
    res_len,
    res_query,
    res_new,
    arr_query,
    arr_new,
):
    peers = lax.axis_size("wide")
    tp = lax.axis_size("tp")
    order = None
    if peers * tp == 16:
        order = [int(f"{p:04b}"[::-1], 2) ^ 11 for p in range(16)]
    send = pack(pre_codes, pre_scales, req_dest, req_blocks, peers, tp, order)
    got = lax.all_to_all(
        send,
        ("wide", "tp"),
        split_axis=0,
        concat_axis=0,
        tiled=True,
        axis_index_groups=[order or list(range(peers * tp))],
    )
    done = resident(cache_rows(res_codes), res_scales, res_len, res_query, res_new)
    block_rows = 2 * pre_codes.shape[2]
    arr_out, res_out = arrivals(got, arr_query, arr_new, done, tp, order, block_rows)
    return (from_rows(res_out, res_query.shape), from_rows(arr_out, arr_query.shape))


def solution(mesh):
    in_specs = (
        P(("groups", "wide"), None, "tp", None, None),
        P(("groups", "wide"), None, "tp", None, None),
        P(("groups", "wide")),
        P(("groups", "wide")),
        P(("groups", "wide"), None, None, "tp"),
        P(("groups", "wide"), None, None, "tp"),
        P(("groups", "wide")),
        P(("groups", "wide"), None, "tp"),
        P(("groups", "wide"), None, None, "tp"),
        P(("groups", "wide"), None, "tp"),
        P(("groups", "wide"), None, None, "tp"),
    )
    out_specs = (P(("groups", "wide"), None, "tp"), P(("groups", "wide"), None, "tp"))
    return jax.shard_map(shards, mesh=mesh, in_specs=in_specs, out_specs=out_specs, check_vma=False)
```

```python
import functools
import math

import jax
import jax.numpy as jnp
from jax import lax
from jax.experimental import pallas as pl
from jax.experimental.pallas import tpu as pltpu
from jax.sharding import PartitionSpec as P

KVH = 4
HD = 128
HQ = 64
GROUP = HQ // KVH
STEPS = 2

NEGATIVE = -1e30
EMPTY = 1024.0
SCORE_SCALE = 1.0 / math.sqrt(HD)

BF16 = jnp.bfloat16
F32 = jnp.float32


def iota(shape, axis):
    return lax.broadcasted_iota(jnp.int32, shape, axis)


def over(x, n):
    return jnp.right_shift(x, n.bit_length() - 1) if n & (n - 1) == 0 else x // n


def mod(x, n):
    return jnp.bitwise_and(x, n - 1) if n & (n - 1) == 0 else x % n


def dot_nt(a, b):
    return lax.dot_general(a, b, (((1,), (1,)), ((), ())), preferred_element_type=F32)


def dot_nn(a, b):
    return lax.dot_general(a, b, (((1,), (0,)), ((), ())), preferred_element_type=F32)


def top_of(*parts):
    return functools.reduce(jnp.maximum, [jnp.max(p, axis=1, keepdims=True) for p in parts])


def sum_of(*parts):
    return functools.reduce(jnp.add, [jnp.sum(p, axis=1, keepdims=True) for p in parts])


def to_values(weights):
    tiles = [pltpu.roll(weights[:, c : c + HD], 1, 1) for c in range(0, weights.shape[1], HD)]
    return jnp.concatenate(tiles, axis=1).astype(BF16)


def values_up(rows):
    return pltpu.roll(rows.astype(F32), rows.shape[0] - 1, 0).astype(BF16)


def pack_kernel(
    tp, order, heads, block_rows, dest_hbm, blocks_hbm, codes_hbm, scales_hbm, send_ref,
    dest_ref, blocks_ref, codes_ref, scales_ref, sems,
):
    requests, all_rows = codes_ref.shape[:2]
    pairs = [
        (codes_hbm.at[: requests // 2], codes_ref.at[: requests // 2]),
        (codes_hbm.at[requests // 2 :], codes_ref.at[requests // 2 :]),
        (scales_hbm, scales_ref), (dest_hbm, dest_ref), (blocks_hbm, blocks_ref),
    ]
    copies = [pltpu.make_async_copy(a, b, sems.at[i]) for i, (a, b) in enumerate(pairs)]
    for copy in copies:
        copy.start()
    rows = all_rows // heads
    per_core = heads // tp
    send_ref[...] = jnp.full(send_ref.shape, EMPTY, BF16)
    row_block = over(iota((rows, HD), 0), block_rows)
    to_row = iota((all_rows, all_rows), 0)
    from_row = iota((all_rows, all_rows), 1)
    source = over(mod(to_row, rows), 2) * (2 * heads) + over(to_row, rows) * 2 + mod(to_row, 2)
    by_head = jnp.where(from_row == source, 1.0, 0.0).astype(BF16)
    for copy in copies:
        copy.wait()

    def place(r):
        there = dest_ref[r]
        spots = [there * tp + t for t in range(tp)]
        if order is not None:
            for t in range(tp):
                at = {core // tp: p for p, core in enumerate(order) if core % tp == t}
                spots[t] = functools.reduce(
                    jnp.add, [jnp.where(there == w, p, 0) for w, p in at.items()]
                )
        held = row_block < blocks_ref[r]
        codes = dot_nn(by_head, codes_ref[r])
        scales = scales_ref[r].astype(F32)
        for j in range(heads):
            values = codes[j * rows : (j + 1) * rows] * scales[:, j : j + 1]
            values = jnp.where(held, values, EMPTY).astype(BF16)
            send_ref[spots[j // per_core], j % per_core] = values

    if requests <= 8:
        for r in range(requests):
            place(r)
    else:
        lax.fori_loop(0, requests, lambda r, c: (place(r), c)[1], 0)


def resident_kernel(
    len_ref, codes_hbm, scales_ref, query_ref, new_ref, out_ref, codes_ref, sem
):
    fetch = pltpu.make_async_copy(codes_hbm, codes_ref, sem)
    fetch.start()
    slots, rows = codes_ref.shape[:2]
    heads = scales_ref.shape[2]
    tokens = rows // (2 * heads)
    queries = query_ref.shape[1]
    new_rows = new_ref.shape[0]

    row = iota((rows, HD), 0)
    source = (mod(row, 2) * heads + mod(over(row, 2), heads)) * tokens + over(row, 2 * heads)
    lane = iota((rows, HD), 1)
    spread = jnp.concatenate(
        [jnp.where(source == lane + c, 1.0, 0.0).astype(BF16) for c in range(0, rows, HD)],
        axis=1,
    )
    flat = jnp.concatenate(
        [scales_ref[:, p, h] for p in range(2) for h in range(heads)], axis=1
    )
    columns = dot_nt(spread, flat).astype(BF16)

    col = iota((queries, rows), 1)
    row_head = over(iota((queries, rows), 0), queries // heads)
    is_key = (mod(col, 2) == 0) & (mod(over(col, 2), heads) == row_head)
    col_token = jnp.where(is_key, over(col, 2 * heads), tokens)

    new_col = iota((queries, new_rows), 1)
    new_row = iota((queries, new_rows), 0)
    new_ok = (
        (mod(new_col, 2) == 0)
        & (mod(over(new_col, 2), heads) == over(new_row, queries // heads))
        & (mod(over(new_col, 2 * heads), STEPS) <= mod(new_row, STEPS))
    )
    new_slot = jnp.where(new_ok, over(new_col, 2 * heads * STEPS), slots)

    every = range(slots)
    new = new_ref[...]
    new_all = dot_nt(query_ref[...].reshape(slots * queries, HD), new)
    fetch.wait()
    caches = [codes_ref[s] * columns[:, s : s + 1] for s in every]
    scores = [dot_nt(query_ref[s], caches[s]) for s in every]
    scores = [jnp.where(col_token < len_ref[s], scores[s] * SCORE_SCALE, NEGATIVE) for s in every]
    new_scores = [
        jnp.where(new_slot == s, new_all[s * queries : (s + 1) * queries] * SCORE_SCALE, NEGATIVE)
        for s in every
    ]
    top = [top_of(scores[s], new_scores[s]) for s in every]
    weights = [jnp.exp(scores[s] - top[s]) for s in every]
    new_weights = [jnp.exp(new_scores[s] - top[s]) for s in every]
    total = [sum_of(weights[s], new_weights[s]) for s in every]
    new_mixed = dot_nn(jnp.concatenate(new_weights, axis=0).astype(BF16), values_up(new))
    mixed = [
        dot_nn(to_values(weights[s]), caches[s]) + new_mixed[s * queries : (s + 1) * queries]
        for s in every
    ]
    for s in every:
        out_ref[s] = (mixed[s] * (1.0 / total[s])).astype(BF16)


def slots_by_rows(got_ref, tp, order, block_rows):
    chunk_rows = got_ref.shape[2]
    blocks = chunk_rows // block_rows
    rows = [got_ref[k, 0].astype(F32) for k in range(len(order))]
    here = {
        core // tp: jnp.where(x[:1] < EMPTY, 1.0, 0.0)
        for core, x in zip(order, rows)
        if core % tp == 0
    }
    ranks = {
        w: sum([here[v] for v in here if v < w], jnp.zeros((1, HD), F32)) for w in here
    }
    lane = iota((1, HD), 1)
    block = over(lane, block_rows)
    block = jnp.where(mod(lane, 2) == 0, block, -1)
    per_tile = HD // chunk_rows
    tiles = []
    for start in range(0, len(order), per_tile):
        tile = jnp.full((1, HD), -1.0, F32)
        for i in range(per_tile):
            x, rank = rows[start + i], ranks[order[start + i] // tp]
            for b in range(blocks):
                at = b * block_rows
                value = jnp.where(x[at : at + 1] < EMPTY, rank, -1.0)
                tile = jnp.where(block == i * blocks + b, value, tile)
        tiles.append(tile)
    return jnp.concatenate(tiles, axis=1)


def slots_by_matmul(got_ref, tp):
    chunks, _, chunk_rows = got_ref.shape[:3]
    columns = chunks * chunk_rows
    sender_rows = tp * chunk_rows
    piece = min(columns, 256)
    sums = dot_nt(jnp.ones((16, HD), BF16), got_ref[:, 0].reshape(columns, HD))[:8]
    col = iota((8, columns), 1)
    held = sums < EMPTY
    first = jnp.where(held & (mod(col, sender_rows) == 0), 1.0, 0.0).astype(BF16)
    row = over(iota((piece, piece), 0), sender_rows)
    before = jnp.where(row < over(iota((piece, piece), 1), sender_rows), 1.0, 0.0).astype(BF16)
    base = jnp.zeros((8, 1), F32)
    ranks = []
    for p in range(0, columns, piece):
        part = first[:, p : p + piece]
        ranks.append(dot_nn(part, before) + base)
        base = base + jnp.sum(part.astype(F32), axis=1, keepdims=True)
    rank = jnp.concatenate(ranks, axis=1)
    return jnp.where(held & (mod(col, 2) == 0), rank, -1.0)[:1]


def arrival_kernel(
    tp, groups, order, block_rows, got_ref, query_ref, new_ref, done_ref, out_ref, done_hbm, sem
):
    step = pl.program_id(0) if groups > 1 else 0
    hand_on = pltpu.make_async_copy(done_ref, done_hbm, sem)
    if groups > 1:
        pl.when(step == 0)(hand_on.start)
    else:
        hand_on.start()

    chunks, heads, chunk_rows = got_ref.shape[:3]
    slots, _, per_head = query_ref.shape[:3]
    rows = slots * per_head
    columns = chunks * chunk_rows
    every = range(heads)

    caches = [got_ref[:, h].reshape(columns, HD) for h in every]
    queries = [query_ref[:, h].reshape(rows, HD) for h in every]
    new = new_ref[...]
    scores = [dot_nt(queries[h], caches[h]) for h in every]
    new_all = dot_nt(jnp.concatenate(queries, axis=0), new)
    if order is None:
        slot_of = slots_by_matmul(got_ref, tp)
    else:
        slot_of = slots_by_rows(got_ref, tp, order, block_rows)
    first_slot = jnp.float32(step * slots)
    mine = [slot_of == first_slot + a for a in range(slots)]

    new_col = iota((rows, new.shape[0]), 1)
    new_row = iota((rows, new.shape[0]), 0)
    new_here = (
        (mod(new_col, 2) == 0)
        & (over(new_col, 2 * heads * STEPS) == over(new_row, per_head))
        & (mod(over(new_col, 2 * heads), STEPS) <= mod(new_row, STEPS))
    )
    new_head = jnp.where(new_here, mod(over(new_col, 2), heads), heads)

    scores = [
        jnp.concatenate(
            [
                jnp.where(mine[a], scores[h][a * per_head : (a + 1) * per_head] * SCORE_SCALE, NEGATIVE)
                for a in range(slots)
            ],
            axis=0,
        )
        for h in every
    ]
    new_scores = [
        jnp.where(new_head == h, new_all[h * rows : (h + 1) * rows] * SCORE_SCALE, NEGATIVE)
        for h in every
    ]
    top = [top_of(scores[h], new_scores[h]) for h in every]
    weights = [jnp.exp(scores[h] - top[h]) for h in every]
    new_weights = [jnp.exp(new_scores[h] - top[h]) for h in every]
    total = [sum_of(weights[h], new_weights[h]) for h in every]
    new_mixed = dot_nn(jnp.concatenate(new_weights, axis=0).astype(BF16), values_up(new))
    for h in every:
        mixed = dot_nn(to_values(weights[h]), caches[h]) + new_mixed[h * rows : (h + 1) * rows]
        out_ref[:, h] = (mixed * (1.0 / total[h])).astype(BF16).reshape(slots, per_head, HD)
    if groups > 1:
        pl.when(step == groups - 1)(hand_on.wait)
    else:
        hand_on.wait()


def whole(memory_space=pltpu.VMEM):
    return pl.BlockSpec(memory_space=memory_space)


def in_hbm(x):
    return pltpu.with_memory_space_constraint(x, pltpu.HBM)


def limit(mib):
    return pltpu.CompilerParams(vmem_limit_bytes=mib * 2**20)


def pack(pre_codes, pre_scales, req_dest, req_blocks, peers, tp, order):
    requests, blocks, block_tokens = pre_codes.shape[:3]
    tokens = blocks * block_tokens
    codes = (
        pre_codes.reshape(requests, tokens, 2, KVH, HD)
        .transpose(0, 1, 3, 2, 4)
        .reshape(requests, tokens * KVH * 2, HD)
    )
    scales = pre_scales.reshape(requests, tokens * 2, KVH)
    ins = [req_dest, req_blocks, codes, scales]
    return pl.pallas_call(
        functools.partial(pack_kernel, tp, order, KVH, 2 * block_tokens),
        out_shape=pltpu.VMEM((peers * tp, KVH // tp, tokens * 2, HD), BF16),
        in_specs=[whole(pltpu.HBM)] * len(ins),
        out_specs=whole(),
        scratch_shapes=[
            pltpu.SMEM(req_dest.shape, jnp.int32),
            pltpu.SMEM(req_blocks.shape, jnp.int32),
            pltpu.VMEM(codes.shape, BF16),
            pltpu.VMEM(scales.shape, BF16),
            pltpu.SemaphoreType.DMA((5,)),
        ],
        compiler_params=limit(16),
        name="pack",
    )(*[in_hbm(x) for x in ins])


def cache_rows(codes):
    slots, tokens, _, width = codes.shape
    heads = width // HD
    return (
        codes.reshape(slots, tokens, 2, heads, HD)
        .transpose(0, 1, 3, 2, 4)
        .reshape(slots, tokens * heads * 2, HD)
    )


def query_rows(query):
    slots, steps, width = query.shape
    return query.reshape(slots, steps, width // HD, HD).transpose(0, 2, 1, 3)


def new_rows_of(new):
    slots, steps, pair, width = new.shape
    heads = width // HD
    return (
        new.reshape(slots, steps, pair, heads, HD)
        .transpose(0, 1, 3, 2, 4)
        .reshape(slots * steps * heads * pair, HD)
    )


def from_rows(out, shape):
    slots, steps, width = shape
    return out.reshape(slots, width // HD, steps, HD).transpose(0, 2, 1, 3).reshape(shape)


def resident(codes, res_scales, res_len, res_query, res_new):
    slots, rows = codes.shape[:2]
    heads = res_scales.shape[-1]
    scales = res_scales.transpose(0, 2, 3, 1)
    query = query_rows(res_query).reshape(slots, heads * GROUP * STEPS, HD)
    work = query.shape[0] * query.shape[1] * rows
    return pl.pallas_call(
        resident_kernel,
        out_shape=pltpu.VMEM(query.shape, BF16),
        in_specs=[whole(pltpu.SMEM), whole(pltpu.HBM)] + [whole()] * 3,
        out_specs=whole(),
        scratch_shapes=[pltpu.VMEM(codes.shape, BF16), pltpu.SemaphoreType.DMA],
        cost_estimate=pl.CostEstimate(
            flops=4 * work * HD,
            bytes_accessed=2 * (codes.size + 2 * query.size),
            transcendentals=work,
        ),
        compiler_params=limit(16),
        name="resident",
    )(in_hbm(res_len), in_hbm(codes), scales, query, new_rows_of(res_new))


def arrivals(got, arr_query, arr_new, done, tp, order, block_rows):
    slots, steps, width = arr_query.shape
    heads = width // (HD * GROUP)
    query = query_rows(arr_query).reshape(slots, heads, GROUP * steps, HD)
    new = new_rows_of(arr_new)
    size = max(n for n in range(1, 7) if slots % n == 0)
    groups = slots // size
    small = got.size <= 2**18

    def part(ref, rows):
        if groups == 1:
            return whole()
        return pl.BlockSpec((rows,) + ref.shape[1:], lambda i: (i,) + (0,) * (ref.ndim - 1))

    return pl.pallas_call(
        functools.partial(arrival_kernel, tp, groups, order, block_rows),
        out_shape=[
            jax.ShapeDtypeStruct(query.shape, BF16),
            jax.ShapeDtypeStruct(done.shape, BF16),
        ],
        grid=(groups,) if groups > 1 else (),
        in_specs=[
            whole(),
            part(query, size),
            part(new, new.shape[0] // groups),
            whole(),
        ],
        out_specs=[part(query, size), whole(pltpu.HBM)],
        scratch_shapes=[pltpu.SemaphoreType.DMA],
        compiler_params=limit(16 if small else 48),
        name="arrivals",
    )(got, query, new, done)


def shards(
    pre_codes,
    pre_scales,
    req_dest,
    req_blocks,
    res_codes,
    res_scales,
    res_len,
    res_query,
    res_new,
    arr_query,
    arr_new,
):
    peers = lax.axis_size("wide")
    tp = lax.axis_size("tp")
    order = None
    if peers * tp == 16:
        order = [p ^ 11 for p in range(16)]
    send = pack(pre_codes, pre_scales, req_dest, req_blocks, peers, tp, order)
    got = lax.all_to_all(
        send,
        ("wide", "tp"),
        split_axis=0,
        concat_axis=0,
        tiled=True,
        axis_index_groups=[order or list(range(peers * tp))],
    )
    done = resident(cache_rows(res_codes), res_scales, res_len, res_query, res_new)
    block_rows = 2 * pre_codes.shape[2]
    arr_out, res_out = arrivals(got, arr_query, arr_new, done, tp, order, block_rows)
    return (from_rows(res_out, res_query.shape), from_rows(arr_out, arr_query.shape))


def solution(mesh):
    in_specs = (
        P(("groups", "wide"), None, "tp", None, None),
        P(("groups", "wide"), None, "tp", None, None),
        P(("groups", "wide")),
        P(("groups", "wide")),
        P(("groups", "wide"), None, None, "tp"),
        P(("groups", "wide"), None, None, "tp"),
        P(("groups", "wide")),
        P(("groups", "wide"), None, "tp"),
        P(("groups", "wide"), None, None, "tp"),
        P(("groups", "wide"), None, "tp"),
        P(("groups", "wide"), None, None, "tp"),
    )
    out_specs = (P(("groups", "wide"), None, "tp"), P(("groups", "wide"), None, "tp"))
    return jax.shard_map(shards, mesh=mesh, in_specs=in_specs, out_specs=out_specs, check_vma=False)
```

```python
import functools
import math

import jax
import jax.numpy as jnp
from jax import lax
from jax.experimental import pallas as pl
from jax.experimental.pallas import tpu as pltpu
from jax.sharding import PartitionSpec as P

KVH = 4
HD = 128
HQ = 64
GROUP = HQ // KVH
STEPS = 2

NEGATIVE = -1e30
EMPTY = 1024.0
SCORE_SCALE = 1.0 / math.sqrt(HD)

BF16 = jnp.bfloat16
F32 = jnp.float32


def iota(shape, axis):
    return lax.broadcasted_iota(jnp.int32, shape, axis)


def over(x, n):
    return jnp.right_shift(x, n.bit_length() - 1) if n & (n - 1) == 0 else x // n


def mod(x, n):
    return jnp.bitwise_and(x, n - 1) if n & (n - 1) == 0 else x % n


def dot_nt(a, b):
    return lax.dot_general(a, b, (((1,), (1,)), ((), ())), preferred_element_type=F32)


def dot_nn(a, b):
    return lax.dot_general(a, b, (((1,), (0,)), ((), ())), preferred_element_type=F32)


def top_of(*parts):
    return functools.reduce(jnp.maximum, [jnp.max(p, axis=1, keepdims=True) for p in parts])


def sum_of(*parts):
    return functools.reduce(jnp.add, [jnp.sum(p, axis=1, keepdims=True) for p in parts])


def to_values(weights):
    tiles = [pltpu.roll(weights[:, c : c + HD], 1, 1) for c in range(0, weights.shape[1], HD)]
    return jnp.concatenate(tiles, axis=1).astype(BF16)


def values_up(rows):
    return pltpu.roll(rows.astype(F32), rows.shape[0] - 1, 0).astype(BF16)


def pack_kernel(
    tp, order, heads, block_rows, dest_hbm, blocks_hbm, codes_hbm, scales_hbm, send_ref,
    dest_ref, blocks_ref, codes_ref, scales_ref, sems,
):
    requests, all_rows = codes_ref.shape[:2]
    pairs = [
        (codes_hbm.at[: requests // 2], codes_ref.at[: requests // 2]),
        (codes_hbm.at[requests // 2 :], codes_ref.at[requests // 2 :]),
        (scales_hbm, scales_ref), (dest_hbm, dest_ref), (blocks_hbm, blocks_ref),
    ]
    copies = [pltpu.make_async_copy(a, b, sems.at[i]) for i, (a, b) in enumerate(pairs)]
    for copy in copies:
        copy.start()
    rows = all_rows // heads
    per_core = heads // tp
    send_ref[...] = jnp.full(send_ref.shape, EMPTY, BF16)
    row_block = over(iota((rows, HD), 0), block_rows)
    to_row = iota((all_rows, all_rows), 0)
    from_row = iota((all_rows, all_rows), 1)
    source = over(mod(to_row, rows), 2) * (2 * heads) + over(to_row, rows) * 2 + mod(to_row, 2)
    by_head = jnp.where(from_row == source, 1.0, 0.0).astype(BF16)
    for copy in copies:
        copy.wait()

    def place(r):
        there = dest_ref[r]
        spots = [there * tp + t for t in range(tp)]
        if order is not None:
            for t in range(tp):
                at = {core // tp: p for p, core in enumerate(order) if core % tp == t}
                spots[t] = functools.reduce(
                    jnp.add, [jnp.where(there == w, p, 0) for w, p in at.items()]
                )
        held = row_block < blocks_ref[r]
        codes = dot_nn(by_head, codes_ref[r])
        scales = scales_ref[r].astype(F32)
        for j in range(heads):
            values = codes[j * rows : (j + 1) * rows] * scales[:, j : j + 1]
            values = jnp.where(held, values, EMPTY).astype(BF16)
            send_ref[spots[j // per_core], j % per_core] = values

    if requests <= 8:
        for r in range(requests):
            place(r)
    else:
        lax.fori_loop(0, requests, lambda r, c: (place(r), c)[1], 0)


def resident_kernel(
    len_ref, codes_hbm, scales_ref, query_ref, new_ref, out_ref, codes_ref, sem
):
    fetch = pltpu.make_async_copy(codes_hbm, codes_ref, sem)
    fetch.start()
    slots, rows = codes_ref.shape[:2]
    heads = scales_ref.shape[2]
    tokens = rows // (2 * heads)
    queries = query_ref.shape[1]
    new_rows = new_ref.shape[0]

    row = iota((rows, HD), 0)
    source = (mod(row, 2) * heads + mod(over(row, 2), heads)) * tokens + over(row, 2 * heads)
    lane = iota((rows, HD), 1)
    spread = jnp.concatenate(
        [jnp.where(source == lane + c, 1.0, 0.0).astype(BF16) for c in range(0, rows, HD)],
        axis=1,
    )
    flat = jnp.concatenate(
        [scales_ref[:, p, h] for p in range(2) for h in range(heads)], axis=1
    )
    columns = dot_nt(spread, flat).astype(BF16)

    col = iota((queries, rows), 1)
    row_head = over(iota((queries, rows), 0), queries // heads)
    is_key = (mod(col, 2) == 0) & (mod(over(col, 2), heads) == row_head)
    col_token = jnp.where(is_key, over(col, 2 * heads), tokens)

    new_col = iota((queries, new_rows), 1)
    new_row = iota((queries, new_rows), 0)
    new_ok = (
        (mod(new_col, 2) == 0)
        & (mod(over(new_col, 2), heads) == over(new_row, queries // heads))
        & (mod(over(new_col, 2 * heads), STEPS) <= mod(new_row, STEPS))
    )
    new_slot = jnp.where(new_ok, over(new_col, 2 * heads * STEPS), slots)

    every = range(slots)
    new = new_ref[...]
    new_all = dot_nt(query_ref[...].reshape(slots * queries, HD), new)
    fetch.wait()
    caches = [codes_ref[s] * columns[:, s : s + 1] for s in every]
    scores = [dot_nt(query_ref[s], caches[s]) for s in every]
    scores = [jnp.where(col_token < len_ref[s], scores[s] * SCORE_SCALE, NEGATIVE) for s in every]
    new_scores = [
        jnp.where(new_slot == s, new_all[s * queries : (s + 1) * queries] * SCORE_SCALE, NEGATIVE)
        for s in every
    ]
    top = [top_of(scores[s], new_scores[s]) for s in every]
    weights = [jnp.exp(scores[s] - top[s]) for s in every]
    new_weights = [jnp.exp(new_scores[s] - top[s]) for s in every]
    total = [sum_of(weights[s], new_weights[s]) for s in every]
    new_mixed = dot_nn(jnp.concatenate(new_weights, axis=0).astype(BF16), values_up(new))
    mixed = [
        dot_nn(to_values(weights[s]), caches[s]) + new_mixed[s * queries : (s + 1) * queries]
        for s in every
    ]
    for s in every:
        out_ref[s] = (mixed[s] * (1.0 / total[s])).astype(BF16)


def slots_by_rows(got_ref, tp, order, block_rows):
    chunk_rows = got_ref.shape[2]
    blocks = chunk_rows // block_rows
    rows = [got_ref[k, 0].astype(F32) for k in range(len(order))]
    here = {
        core // tp: jnp.where(x[:1] < EMPTY, 1.0, 0.0)
        for core, x in zip(order, rows)
        if core % tp == 0
    }
    ranks = {
        w: sum([here[v] for v in here if v < w], jnp.zeros((1, HD), F32)) for w in here
    }
    lane = iota((1, HD), 1)
    block = over(lane, block_rows)
    block = jnp.where(mod(lane, 2) == 0, block, -1)
    per_tile = HD // chunk_rows
    tiles = []
    for start in range(0, len(order), per_tile):
        tile = jnp.full((1, HD), -1.0, F32)
        for i in range(per_tile):
            x, rank = rows[start + i], ranks[order[start + i] // tp]
            for b in range(blocks):
                at = b * block_rows
                value = jnp.where(x[at : at + 1] < EMPTY, rank, -1.0)
                tile = jnp.where(block == i * blocks + b, value, tile)
        tiles.append(tile)
    return jnp.concatenate(tiles, axis=1)


def slots_by_matmul(got_ref, tp):
    chunks, _, chunk_rows = got_ref.shape[:3]
    columns = chunks * chunk_rows
    sender_rows = tp * chunk_rows
    piece = min(columns, 256)
    sums = dot_nt(jnp.ones((16, HD), BF16), got_ref[:, 0].reshape(columns, HD))[:8]
    col = iota((8, columns), 1)
    held = sums < EMPTY
    first = jnp.where(held & (mod(col, sender_rows) == 0), 1.0, 0.0).astype(BF16)
    row = over(iota((piece, piece), 0), sender_rows)
    before = jnp.where(row < over(iota((piece, piece), 1), sender_rows), 1.0, 0.0).astype(BF16)
    base = jnp.zeros((8, 1), F32)
    ranks = []
    for p in range(0, columns, piece):
        part = first[:, p : p + piece]
        ranks.append(dot_nn(part, before) + base)
        base = base + jnp.sum(part.astype(F32), axis=1, keepdims=True)
    rank = jnp.concatenate(ranks, axis=1)
    return jnp.where(held & (mod(col, 2) == 0), rank, -1.0)[:1]


def arrival_kernel(
    tp, groups, order, block_rows, got_ref, query_ref, new_ref, done_ref, out_ref, done_hbm, sem
):
    step = pl.program_id(0) if groups > 1 else 0
    hand_on = pltpu.make_async_copy(done_ref, done_hbm, sem)
    if groups > 1:
        pl.when(step == 0)(hand_on.start)
    else:
        hand_on.start()

    chunks, heads, chunk_rows = got_ref.shape[:3]
    slots, _, per_head = query_ref.shape[:3]
    rows = slots * per_head
    columns = chunks * chunk_rows
    every = range(heads)

    caches = [got_ref[:, h].reshape(columns, HD) for h in every]
    queries = [query_ref[:, h].reshape(rows, HD) for h in every]
    new = new_ref[...]
    scores = [dot_nt(queries[h], caches[h]) for h in every]
    new_all = dot_nt(jnp.concatenate(queries, axis=0), new)
    if order is None:
        slot_of = slots_by_matmul(got_ref, tp)
    else:
        slot_of = slots_by_rows(got_ref, tp, order, block_rows)
    first_slot = jnp.float32(step * slots)
    mine = [slot_of == first_slot + a for a in range(slots)]

    new_col = iota((rows, new.shape[0]), 1)
    new_row = iota((rows, new.shape[0]), 0)
    new_here = (
        (mod(new_col, 2) == 0)
        & (over(new_col, 2 * heads * STEPS) == over(new_row, per_head))
        & (mod(over(new_col, 2 * heads), STEPS) <= mod(new_row, STEPS))
    )
    new_head = jnp.where(new_here, mod(over(new_col, 2), heads), heads)

    scores = [
        jnp.concatenate(
            [
                jnp.where(mine[a], scores[h][a * per_head : (a + 1) * per_head] * SCORE_SCALE, NEGATIVE)
                for a in range(slots)
            ],
            axis=0,
        )
        for h in every
    ]
    new_scores = [
        jnp.where(new_head == h, new_all[h * rows : (h + 1) * rows] * SCORE_SCALE, NEGATIVE)
        for h in every
    ]
    top = [top_of(scores[h], new_scores[h]) for h in every]
    weights = [jnp.exp(scores[h] - top[h]) for h in every]
    new_weights = [jnp.exp(new_scores[h] - top[h]) for h in every]
    total = [sum_of(weights[h], new_weights[h]) for h in every]
    new_mixed = dot_nn(jnp.concatenate(new_weights, axis=0).astype(BF16), values_up(new))
    for h in every:
        mixed = dot_nn(to_values(weights[h]), caches[h]) + new_mixed[h * rows : (h + 1) * rows]
        out_ref[:, h] = (mixed * (1.0 / total[h])).astype(BF16).reshape(slots, per_head, HD)
    if groups > 1:
        pl.when(step == groups - 1)(hand_on.wait)
    else:
        hand_on.wait()


def whole(memory_space=pltpu.VMEM):
    return pl.BlockSpec(memory_space=memory_space)


def in_hbm(x):
    return pltpu.with_memory_space_constraint(x, pltpu.HBM)


def limit(mib):
    return pltpu.CompilerParams(vmem_limit_bytes=mib * 2**20)


def pack(pre_codes, pre_scales, req_dest, req_blocks, peers, tp, order):
    requests, blocks, block_tokens = pre_codes.shape[:3]
    tokens = blocks * block_tokens
    codes = (
        pre_codes.reshape(requests, tokens, 2, KVH, HD)
        .transpose(0, 1, 3, 2, 4)
        .reshape(requests, tokens * KVH * 2, HD)
    )
    scales = pre_scales.reshape(requests, tokens * 2, KVH)
    ins = [req_dest, req_blocks, codes, scales]
    return pl.pallas_call(
        functools.partial(pack_kernel, tp, order, KVH, 2 * block_tokens),
        out_shape=pltpu.VMEM((peers * tp, KVH // tp, tokens * 2, HD), BF16),
        in_specs=[whole(pltpu.HBM)] * len(ins),
        out_specs=whole(),
        scratch_shapes=[
            pltpu.SMEM(req_dest.shape, jnp.int32),
            pltpu.SMEM(req_blocks.shape, jnp.int32),
            pltpu.VMEM(codes.shape, BF16),
            pltpu.VMEM(scales.shape, BF16),
            pltpu.SemaphoreType.DMA((5,)),
        ],
        compiler_params=limit(16),
        name="pack",
    )(*[in_hbm(x) for x in ins])


def cache_rows(codes):
    slots, tokens, _, width = codes.shape
    heads = width // HD
    return (
        codes.reshape(slots, tokens, 2, heads, HD)
        .transpose(0, 1, 3, 2, 4)
        .reshape(slots, tokens * heads * 2, HD)
    )


def query_rows(query):
    slots, steps, width = query.shape
    return query.reshape(slots, steps, width // HD, HD).transpose(0, 2, 1, 3)


def new_rows_of(new):
    slots, steps, pair, width = new.shape
    heads = width // HD
    return (
        new.reshape(slots, steps, pair, heads, HD)
        .transpose(0, 1, 3, 2, 4)
        .reshape(slots * steps * heads * pair, HD)
    )


def from_rows(out, shape):
    slots, steps, width = shape
    return out.reshape(slots, width // HD, steps, HD).transpose(0, 2, 1, 3).reshape(shape)


def resident(codes, res_scales, res_len, res_query, res_new):
    slots, rows = codes.shape[:2]
    heads = res_scales.shape[-1]
    scales = res_scales.transpose(0, 2, 3, 1)
    query = query_rows(res_query).reshape(slots, heads * GROUP * STEPS, HD)
    work = query.shape[0] * query.shape[1] * rows
    return pl.pallas_call(
        resident_kernel,
        out_shape=pltpu.VMEM(query.shape, BF16),
        in_specs=[whole(pltpu.SMEM), whole(pltpu.HBM)] + [whole()] * 3,
        out_specs=whole(),
        scratch_shapes=[pltpu.VMEM(codes.shape, BF16), pltpu.SemaphoreType.DMA],
        cost_estimate=pl.CostEstimate(
            flops=4 * work * HD,
            bytes_accessed=2 * (codes.size + 2 * query.size),
            transcendentals=work,
        ),
        compiler_params=limit(16),
        name="resident",
    )(in_hbm(res_len), in_hbm(codes), scales, query, new_rows_of(res_new))


def arrivals(got, arr_query, arr_new, done, tp, order, block_rows):
    slots, steps, width = arr_query.shape
    heads = width // (HD * GROUP)
    query = query_rows(arr_query).reshape(slots, heads, GROUP * steps, HD)
    new = new_rows_of(arr_new)
    size = max(n for n in range(1, 7) if slots % n == 0)
    groups = slots // size
    small = got.size <= 2**18

    def part(ref, rows):
        if groups == 1:
            return whole()
        return pl.BlockSpec((rows,) + ref.shape[1:], lambda i: (i,) + (0,) * (ref.ndim - 1))

    return pl.pallas_call(
        functools.partial(arrival_kernel, tp, groups, order, block_rows),
        out_shape=[
            jax.ShapeDtypeStruct(query.shape, BF16),
            jax.ShapeDtypeStruct(done.shape, BF16),
        ],
        grid=(groups,) if groups > 1 else (),
        in_specs=[
            whole(),
            part(query, size),
            part(new, new.shape[0] // groups),
            whole(),
        ],
        out_specs=[part(query, size), whole(pltpu.HBM)],
        scratch_shapes=[pltpu.SemaphoreType.DMA],
        compiler_params=limit(16 if small else 48),
        name="arrivals",
    )(got, query, new, done)


def shards(
    pre_codes,
    pre_scales,
    req_dest,
    req_blocks,
    res_codes,
    res_scales,
    res_len,
    res_query,
    res_new,
    arr_query,
    arr_new,
):
    peers = lax.axis_size("wide")
    tp = lax.axis_size("tp")
    order = None
    if peers * tp == 16:
        order = [p ^ 7 for p in range(16)]
    send = pack(pre_codes, pre_scales, req_dest, req_blocks, peers, tp, order)
    got = lax.all_to_all(
        send,
        ("wide", "tp"),
        split_axis=0,
        concat_axis=0,
        tiled=True,
        axis_index_groups=[order or list(range(peers * tp))],
    )
    done = resident(cache_rows(res_codes), res_scales, res_len, res_query, res_new)
    block_rows = 2 * pre_codes.shape[2]
    arr_out, res_out = arrivals(got, arr_query, arr_new, done, tp, order, block_rows)
    return (from_rows(res_out, res_query.shape), from_rows(arr_out, arr_query.shape))


def solution(mesh):
    in_specs = (
        P(("groups", "wide"), None, "tp", None, None),
        P(("groups", "wide"), None, "tp", None, None),
        P(("groups", "wide")),
        P(("groups", "wide")),
        P(("groups", "wide"), None, None, "tp"),
        P(("groups", "wide"), None, None, "tp"),
        P(("groups", "wide")),
        P(("groups", "wide"), None, "tp"),
        P(("groups", "wide"), None, None, "tp"),
        P(("groups", "wide"), None, "tp"),
        P(("groups", "wide"), None, None, "tp"),
    )
    out_specs = (P(("groups", "wide"), None, "tp"), P(("groups", "wide"), None, "tp"))
    return jax.shard_map(shards, mesh=mesh, in_specs=in_specs, out_specs=out_specs, check_vma=False)
```

```python
import functools
import math

import jax
import jax.numpy as jnp
from jax import lax
from jax.experimental import pallas as pl
from jax.experimental.pallas import tpu as pltpu
from jax.sharding import PartitionSpec as P

KVH = 4
HD = 128
HQ = 64
GROUP = HQ // KVH
STEPS = 2

NEGATIVE = -1e30
EMPTY = 1024.0
SCORE_SCALE = 1.0 / math.sqrt(HD)

BF16 = jnp.bfloat16
F32 = jnp.float32


def iota(shape, axis):
    return lax.broadcasted_iota(jnp.int32, shape, axis)


def over(x, n):
    return jnp.right_shift(x, n.bit_length() - 1) if n & (n - 1) == 0 else x // n


def mod(x, n):
    return jnp.bitwise_and(x, n - 1) if n & (n - 1) == 0 else x % n


def dot_nt(a, b):
    return lax.dot_general(a, b, (((1,), (1,)), ((), ())), preferred_element_type=F32)


def dot_nn(a, b):
    return lax.dot_general(a, b, (((1,), (0,)), ((), ())), preferred_element_type=F32)


def top_of(*parts):
    return functools.reduce(jnp.maximum, [jnp.max(p, axis=1, keepdims=True) for p in parts])


def sum_of(*parts):
    return functools.reduce(jnp.add, [jnp.sum(p, axis=1, keepdims=True) for p in parts])


def to_values(weights):
    tiles = [pltpu.roll(weights[:, c : c + HD], 1, 1) for c in range(0, weights.shape[1], HD)]
    return jnp.concatenate(tiles, axis=1).astype(BF16)


def values_up(rows):
    return pltpu.roll(rows.astype(F32), rows.shape[0] - 1, 0).astype(BF16)


def pack_kernel(
    tp, order, heads, block_rows, dest_hbm, blocks_hbm, codes_hbm, scales_hbm, send_ref,
    dest_ref, blocks_ref, codes_ref, scales_ref, sems,
):
    requests, all_rows = codes_ref.shape[:2]
    pairs = [
        (codes_hbm.at[: requests // 2], codes_ref.at[: requests // 2]),
        (codes_hbm.at[requests // 2 :], codes_ref.at[requests // 2 :]),
        (scales_hbm, scales_ref), (dest_hbm, dest_ref), (blocks_hbm, blocks_ref),
    ]
    copies = [pltpu.make_async_copy(a, b, sems.at[i]) for i, (a, b) in enumerate(pairs)]
    for copy in copies:
        copy.start()
    rows = all_rows // heads
    per_core = heads // tp
    send_ref[...] = jnp.full(send_ref.shape, EMPTY, BF16)
    row_block = over(iota((rows, HD), 0), block_rows)
    to_row = iota((all_rows, all_rows), 0)
    from_row = iota((all_rows, all_rows), 1)
    source = over(mod(to_row, rows), 2) * (2 * heads) + over(to_row, rows) * 2 + mod(to_row, 2)
    by_head = jnp.where(from_row == source, 1.0, 0.0).astype(BF16)
    for copy in copies:
        copy.wait()

    def place(r):
        there = dest_ref[r]
        spots = [there * tp + t for t in range(tp)]
        if order is not None:
            for t in range(tp):
                at = {core // tp: p for p, core in enumerate(order) if core % tp == t}
                spots[t] = functools.reduce(
                    jnp.add, [jnp.where(there == w, p, 0) for w, p in at.items()]
                )
        held = row_block < blocks_ref[r]
        codes = dot_nn(by_head, codes_ref[r])
        scales = scales_ref[r].astype(F32)
        for j in range(heads):
            values = codes[j * rows : (j + 1) * rows] * scales[:, j : j + 1]
            values = jnp.where(held, values, EMPTY).astype(BF16)
            send_ref[spots[j // per_core], j % per_core] = values

    if requests <= 8:
        for r in range(requests):
            place(r)
    else:
        lax.fori_loop(0, requests, lambda r, c: (place(r), c)[1], 0)


def resident_kernel(
    len_ref, codes_hbm, scales_ref, query_ref, new_ref, out_ref, codes_ref, sem
):
    fetch = pltpu.make_async_copy(codes_hbm, codes_ref, sem)
    fetch.start()
    slots, rows = codes_ref.shape[:2]
    heads = scales_ref.shape[2]
    tokens = rows // (2 * heads)
    queries = query_ref.shape[1]
    new_rows = new_ref.shape[0]

    row = iota((rows, HD), 0)
    source = (mod(row, 2) * heads + mod(over(row, 2), heads)) * tokens + over(row, 2 * heads)
    lane = iota((rows, HD), 1)
    spread = jnp.concatenate(
        [jnp.where(source == lane + c, 1.0, 0.0).astype(BF16) for c in range(0, rows, HD)],
        axis=1,
    )
    flat = jnp.concatenate(
        [scales_ref[:, p, h] for p in range(2) for h in range(heads)], axis=1
    )
    columns = dot_nt(spread, flat).astype(BF16)

    col = iota((queries, rows), 1)
    row_head = over(iota((queries, rows), 0), queries // heads)
    is_key = (mod(col, 2) == 0) & (mod(over(col, 2), heads) == row_head)
    col_token = jnp.where(is_key, over(col, 2 * heads), tokens)

    new_col = iota((queries, new_rows), 1)
    new_row = iota((queries, new_rows), 0)
    new_ok = (
        (mod(new_col, 2) == 0)
        & (mod(over(new_col, 2), heads) == over(new_row, queries // heads))
        & (mod(over(new_col, 2 * heads), STEPS) <= mod(new_row, STEPS))
    )
    new_slot = jnp.where(new_ok, over(new_col, 2 * heads * STEPS), slots)

    every = range(slots)
    new = new_ref[...]
    new_all = dot_nt(query_ref[...].reshape(slots * queries, HD), new)
    fetch.wait()
    caches = [codes_ref[s] * columns[:, s : s + 1] for s in every]
    scores = [dot_nt(query_ref[s], caches[s]) for s in every]
    scores = [jnp.where(col_token < len_ref[s], scores[s] * SCORE_SCALE, NEGATIVE) for s in every]
    new_scores = [
        jnp.where(new_slot == s, new_all[s * queries : (s + 1) * queries] * SCORE_SCALE, NEGATIVE)
        for s in every
    ]
    top = [top_of(scores[s], new_scores[s]) for s in every]
    weights = [jnp.exp(scores[s] - top[s]) for s in every]
    new_weights = [jnp.exp(new_scores[s] - top[s]) for s in every]
    total = [sum_of(weights[s], new_weights[s]) for s in every]
    new_mixed = dot_nn(jnp.concatenate(new_weights, axis=0).astype(BF16), values_up(new))
    mixed = [
        dot_nn(to_values(weights[s]), caches[s]) + new_mixed[s * queries : (s + 1) * queries]
        for s in every
    ]
    for s in every:
        out_ref[s] = (mixed[s] * (1.0 / total[s])).astype(BF16)


def slots_by_rows(got_ref, tp, order, block_rows):
    chunk_rows = got_ref.shape[2]
    blocks = chunk_rows // block_rows
    rows = [got_ref[k, 0].astype(F32) for k in range(len(order))]
    here = {
        core // tp: jnp.where(x[:1] < EMPTY, 1.0, 0.0)
        for core, x in zip(order, rows)
        if core % tp == 0
    }
    ranks = {
        w: sum([here[v] for v in here if v < w], jnp.zeros((1, HD), F32)) for w in here
    }
    lane = iota((1, HD), 1)
    block = over(lane, block_rows)
    block = jnp.where(mod(lane, 2) == 0, block, -1)
    per_tile = HD // chunk_rows
    tiles = []
    for start in range(0, len(order), per_tile):
        tile = jnp.full((1, HD), -1.0, F32)
        for i in range(per_tile):
            x, rank = rows[start + i], ranks[order[start + i] // tp]
            for b in range(blocks):
                at = b * block_rows
                value = jnp.where(x[at : at + 1] < EMPTY, rank, -1.0)
                tile = jnp.where(block == i * blocks + b, value, tile)
        tiles.append(tile)
    return jnp.concatenate(tiles, axis=1)


def slots_by_matmul(got_ref, tp):
    chunks, _, chunk_rows = got_ref.shape[:3]
    columns = chunks * chunk_rows
    sender_rows = tp * chunk_rows
    piece = min(columns, 256)
    sums = dot_nt(jnp.ones((16, HD), BF16), got_ref[:, 0].reshape(columns, HD))[:8]
    col = iota((8, columns), 1)
    held = sums < EMPTY
    first = jnp.where(held & (mod(col, sender_rows) == 0), 1.0, 0.0).astype(BF16)
    row = over(iota((piece, piece), 0), sender_rows)
    before = jnp.where(row < over(iota((piece, piece), 1), sender_rows), 1.0, 0.0).astype(BF16)
    base = jnp.zeros((8, 1), F32)
    ranks = []
    for p in range(0, columns, piece):
        part = first[:, p : p + piece]
        ranks.append(dot_nn(part, before) + base)
        base = base + jnp.sum(part.astype(F32), axis=1, keepdims=True)
    rank = jnp.concatenate(ranks, axis=1)
    return jnp.where(held & (mod(col, 2) == 0), rank, -1.0)[:1]


def arrival_kernel(
    tp, groups, order, block_rows, got_ref, query_ref, new_ref, done_ref, out_ref, done_hbm, sem
):
    step = pl.program_id(0) if groups > 1 else 0
    hand_on = pltpu.make_async_copy(done_ref, done_hbm, sem)
    if groups > 1:
        pl.when(step == 0)(hand_on.start)
    else:
        hand_on.start()

    chunks, heads, chunk_rows = got_ref.shape[:3]
    slots, _, per_head = query_ref.shape[:3]
    rows = slots * per_head
    columns = chunks * chunk_rows
    every = range(heads)

    caches = [got_ref[:, h].reshape(columns, HD) for h in every]
    queries = [query_ref[:, h].reshape(rows, HD) for h in every]
    new = new_ref[...]
    scores = [dot_nt(queries[h], caches[h]) for h in every]
    new_all = dot_nt(jnp.concatenate(queries, axis=0), new)
    if order is None:
        slot_of = slots_by_matmul(got_ref, tp)
    else:
        slot_of = slots_by_rows(got_ref, tp, order, block_rows)
    first_slot = jnp.float32(step * slots)
    mine = [slot_of == first_slot + a for a in range(slots)]

    new_col = iota((rows, new.shape[0]), 1)
    new_row = iota((rows, new.shape[0]), 0)
    new_here = (
        (mod(new_col, 2) == 0)
        & (over(new_col, 2 * heads * STEPS) == over(new_row, per_head))
        & (mod(over(new_col, 2 * heads), STEPS) <= mod(new_row, STEPS))
    )
    new_head = jnp.where(new_here, mod(over(new_col, 2), heads), heads)

    scores = [
        jnp.concatenate(
            [
                jnp.where(mine[a], scores[h][a * per_head : (a + 1) * per_head] * SCORE_SCALE, NEGATIVE)
                for a in range(slots)
            ],
            axis=0,
        )
        for h in every
    ]
    new_scores = [
        jnp.where(new_head == h, new_all[h * rows : (h + 1) * rows] * SCORE_SCALE, NEGATIVE)
        for h in every
    ]
    top = [top_of(scores[h], new_scores[h]) for h in every]
    weights = [jnp.exp(scores[h] - top[h]) for h in every]
    new_weights = [jnp.exp(new_scores[h] - top[h]) for h in every]
    total = [sum_of(weights[h], new_weights[h]) for h in every]
    new_mixed = dot_nn(jnp.concatenate(new_weights, axis=0).astype(BF16), values_up(new))
    for h in every:
        mixed = dot_nn(to_values(weights[h]), caches[h]) + new_mixed[h * rows : (h + 1) * rows]
        out_ref[:, h] = (mixed * (1.0 / total[h])).astype(BF16).reshape(slots, per_head, HD)
    if groups > 1:
        pl.when(step == groups - 1)(hand_on.wait)
    else:
        hand_on.wait()


def whole(memory_space=pltpu.VMEM):
    return pl.BlockSpec(memory_space=memory_space)


def in_hbm(x):
    return pltpu.with_memory_space_constraint(x, pltpu.HBM)


def limit(mib):
    return pltpu.CompilerParams(vmem_limit_bytes=mib * 2**20)


def pack(pre_codes, pre_scales, req_dest, req_blocks, peers, tp, order):
    requests, blocks, block_tokens = pre_codes.shape[:3]
    tokens = blocks * block_tokens
    codes = (
        pre_codes.reshape(requests, tokens, 2, KVH, HD)
        .transpose(0, 1, 3, 2, 4)
        .reshape(requests, tokens * KVH * 2, HD)
    )
    scales = pre_scales.reshape(requests, tokens * 2, KVH)
    ins = [req_dest, req_blocks, codes, scales]
    return pl.pallas_call(
        functools.partial(pack_kernel, tp, order, KVH, 2 * block_tokens),
        out_shape=pltpu.VMEM((peers * tp, KVH // tp, tokens * 2, HD), BF16),
        in_specs=[whole(pltpu.HBM)] * len(ins),
        out_specs=whole(),
        scratch_shapes=[
            pltpu.SMEM(req_dest.shape, jnp.int32),
            pltpu.SMEM(req_blocks.shape, jnp.int32),
            pltpu.VMEM(codes.shape, BF16),
            pltpu.VMEM(scales.shape, BF16),
            pltpu.SemaphoreType.DMA((5,)),
        ],
        compiler_params=limit(16),
        name="pack",
    )(*[in_hbm(x) for x in ins])


def cache_rows(codes):
    slots, tokens, _, width = codes.shape
    heads = width // HD
    return (
        codes.reshape(slots, tokens, 2, heads, HD)
        .transpose(0, 1, 3, 2, 4)
        .reshape(slots, tokens * heads * 2, HD)
    )


def query_rows(query):
    slots, steps, width = query.shape
    return query.reshape(slots, steps, width // HD, HD).transpose(0, 2, 1, 3)


def new_rows_of(new):
    slots, steps, pair, width = new.shape
    heads = width // HD
    return (
        new.reshape(slots, steps, pair, heads, HD)
        .transpose(0, 1, 3, 2, 4)
        .reshape(slots * steps * heads * pair, HD)
    )


def from_rows(out, shape):
    slots, steps, width = shape
    return out.reshape(slots, width // HD, steps, HD).transpose(0, 2, 1, 3).reshape(shape)


def resident(codes, res_scales, res_len, res_query, res_new):
    slots, rows = codes.shape[:2]
    heads = res_scales.shape[-1]
    scales = res_scales.transpose(0, 2, 3, 1)
    query = query_rows(res_query).reshape(slots, heads * GROUP * STEPS, HD)
    work = query.shape[0] * query.shape[1] * rows
    return pl.pallas_call(
        resident_kernel,
        out_shape=pltpu.VMEM(query.shape, BF16),
        in_specs=[whole(pltpu.SMEM), whole(pltpu.HBM)] + [whole()] * 3,
        out_specs=whole(),
        scratch_shapes=[pltpu.VMEM(codes.shape, BF16), pltpu.SemaphoreType.DMA],
        cost_estimate=pl.CostEstimate(
            flops=4 * work * HD,
            bytes_accessed=2 * (codes.size + 2 * query.size),
            transcendentals=work,
        ),
        compiler_params=limit(16),
        name="resident",
    )(in_hbm(res_len), in_hbm(codes), scales, query, new_rows_of(res_new))


def arrivals(got, arr_query, arr_new, done, tp, order, block_rows):
    slots, steps, width = arr_query.shape
    heads = width // (HD * GROUP)
    query = query_rows(arr_query).reshape(slots, heads, GROUP * steps, HD)
    new = new_rows_of(arr_new)
    size = max(n for n in range(1, 7) if slots % n == 0)
    groups = slots // size
    small = got.size <= 2**18

    def part(ref, rows):
        if groups == 1:
            return whole()
        return pl.BlockSpec((rows,) + ref.shape[1:], lambda i: (i,) + (0,) * (ref.ndim - 1))

    return pl.pallas_call(
        functools.partial(arrival_kernel, tp, groups, order, block_rows),
        out_shape=[
            jax.ShapeDtypeStruct(query.shape, BF16),
            jax.ShapeDtypeStruct(done.shape, BF16),
        ],
        grid=(groups,) if groups > 1 else (),
        in_specs=[
            whole(),
            part(query, size),
            part(new, new.shape[0] // groups),
            whole(),
        ],
        out_specs=[part(query, size), whole(pltpu.HBM)],
        scratch_shapes=[pltpu.SemaphoreType.DMA],
        compiler_params=limit(16 if small else 48),
        name="arrivals",
    )(got, query, new, done)


def shards(
    pre_codes,
    pre_scales,
    req_dest,
    req_blocks,
    res_codes,
    res_scales,
    res_len,
    res_query,
    res_new,
    arr_query,
    arr_new,
):
    peers = lax.axis_size("wide")
    tp = lax.axis_size("tp")
    order = None
    if peers * tp == 16:
        order = [(p & 1 | p >> 2 & 2 | p << 1 & 12) ^ 11 for p in range(16)]
    send = pack(pre_codes, pre_scales, req_dest, req_blocks, peers, tp, order)
    got = lax.all_to_all(
        send,
        ("wide", "tp"),
        split_axis=0,
        concat_axis=0,
        tiled=True,
        axis_index_groups=[order or list(range(peers * tp))],
    )
    done = resident(cache_rows(res_codes), res_scales, res_len, res_query, res_new)
    block_rows = 2 * pre_codes.shape[2]
    arr_out, res_out = arrivals(got, arr_query, arr_new, done, tp, order, block_rows)
    return (from_rows(res_out, res_query.shape), from_rows(arr_out, arr_query.shape))


def solution(mesh):
    in_specs = (
        P(("groups", "wide"), None, "tp", None, None),
        P(("groups", "wide"), None, "tp", None, None),
        P(("groups", "wide")),
        P(("groups", "wide")),
        P(("groups", "wide"), None, None, "tp"),
        P(("groups", "wide"), None, None, "tp"),
        P(("groups", "wide")),
        P(("groups", "wide"), None, "tp"),
        P(("groups", "wide"), None, None, "tp"),
        P(("groups", "wide"), None, "tp"),
        P(("groups", "wide"), None, None, "tp"),
    )
    out_specs = (P(("groups", "wide"), None, "tp"), P(("groups", "wide"), None, "tp"))
    return jax.shard_map(shards, mesh=mesh, in_specs=in_specs, out_specs=out_specs, check_vma=False)
```

```python
import functools
import math

import jax
import jax.numpy as jnp
from jax import lax
from jax.experimental import pallas as pl
from jax.experimental.pallas import tpu as pltpu
from jax.sharding import PartitionSpec as P

KVH = 4
HD = 128
HQ = 64
GROUP = HQ // KVH
STEPS = 2

NEGATIVE = -1e30
EMPTY = 1024.0
SCORE_SCALE = 1.0 / math.sqrt(HD)

BF16 = jnp.bfloat16
F32 = jnp.float32


def iota(shape, axis):
    return lax.broadcasted_iota(jnp.int32, shape, axis)


def over(x, n):
    return jnp.right_shift(x, n.bit_length() - 1) if n & (n - 1) == 0 else x // n


def mod(x, n):
    return jnp.bitwise_and(x, n - 1) if n & (n - 1) == 0 else x % n


def dot_nt(a, b):
    return lax.dot_general(a, b, (((1,), (1,)), ((), ())), preferred_element_type=F32)


def dot_nn(a, b):
    return lax.dot_general(a, b, (((1,), (0,)), ((), ())), preferred_element_type=F32)


def top_of(*parts):
    return functools.reduce(jnp.maximum, [jnp.max(p, axis=1, keepdims=True) for p in parts])


def sum_of(*parts):
    return functools.reduce(jnp.add, [jnp.sum(p, axis=1, keepdims=True) for p in parts])


def to_values(weights):
    tiles = [pltpu.roll(weights[:, c : c + HD], 1, 1) for c in range(0, weights.shape[1], HD)]
    return jnp.concatenate(tiles, axis=1).astype(BF16)


def values_up(rows):
    return pltpu.roll(rows.astype(F32), rows.shape[0] - 1, 0).astype(BF16)


def pack_kernel(
    tp, order, heads, block_rows, dest_hbm, blocks_hbm, codes_hbm, scales_hbm, send_ref,
    dest_ref, blocks_ref, codes_ref, scales_ref, sems,
):
    requests, all_rows = codes_ref.shape[:2]
    pairs = [
        (codes_hbm.at[: requests // 2], codes_ref.at[: requests // 2]),
        (codes_hbm.at[requests // 2 :], codes_ref.at[requests // 2 :]),
        (scales_hbm, scales_ref), (dest_hbm, dest_ref), (blocks_hbm, blocks_ref),
    ]
    copies = [pltpu.make_async_copy(a, b, sems.at[i]) for i, (a, b) in enumerate(pairs)]
    for copy in copies:
        copy.start()
    rows = all_rows // heads
    per_core = heads // tp
    send_ref[...] = jnp.full(send_ref.shape, EMPTY, BF16)
    row_block = over(iota((rows, HD), 0), block_rows)
    to_row = iota((all_rows, all_rows), 0)
    from_row = iota((all_rows, all_rows), 1)
    source = over(mod(to_row, rows), 2) * (2 * heads) + over(to_row, rows) * 2 + mod(to_row, 2)
    by_head = jnp.where(from_row == source, 1.0, 0.0).astype(BF16)
    for copy in copies:
        copy.wait()

    def place(r):
        there = dest_ref[r]
        spots = [there * tp + t for t in range(tp)]
        if order is not None:
            for t in range(tp):
                at = {core // tp: p for p, core in enumerate(order) if core % tp == t}
                spots[t] = functools.reduce(
                    jnp.add, [jnp.where(there == w, p, 0) for w, p in at.items()]
                )
        held = row_block < blocks_ref[r]
        codes = dot_nn(by_head, codes_ref[r])
        scales = scales_ref[r].astype(F32)
        for j in range(heads):
            values = codes[j * rows : (j + 1) * rows] * scales[:, j : j + 1]
            values = jnp.where(held, values, EMPTY).astype(BF16)
            send_ref[spots[j // per_core], j % per_core] = values

    if requests <= 8:
        for r in range(requests):
            place(r)
    else:
        lax.fori_loop(0, requests, lambda r, c: (place(r), c)[1], 0)


def resident_kernel(
    len_ref, codes_hbm, scales_ref, query_ref, new_ref, out_ref, codes_ref, sem
):
    fetch = pltpu.make_async_copy(codes_hbm, codes_ref, sem)
    fetch.start()
    slots, rows = codes_ref.shape[:2]
    heads = scales_ref.shape[2]
    tokens = rows // (2 * heads)
    queries = query_ref.shape[1]
    new_rows = new_ref.shape[0]

    row = iota((rows, HD), 0)
    source = (mod(row, 2) * heads + mod(over(row, 2), heads)) * tokens + over(row, 2 * heads)
    lane = iota((rows, HD), 1)
    spread = jnp.concatenate(
        [jnp.where(source == lane + c, 1.0, 0.0).astype(BF16) for c in range(0, rows, HD)],
        axis=1,
    )
    flat = jnp.concatenate(
        [scales_ref[:, p, h] for p in range(2) for h in range(heads)], axis=1
    )
    columns = dot_nt(spread, flat).astype(BF16)

    col = iota((queries, rows), 1)
    row_head = over(iota((queries, rows), 0), queries // heads)
    is_key = (mod(col, 2) == 0) & (mod(over(col, 2), heads) == row_head)
    col_token = jnp.where(is_key, over(col, 2 * heads), tokens)

    new_col = iota((queries, new_rows), 1)
    new_row = iota((queries, new_rows), 0)
    new_ok = (
        (mod(new_col, 2) == 0)
        & (mod(over(new_col, 2), heads) == over(new_row, queries // heads))
        & (mod(over(new_col, 2 * heads), STEPS) <= mod(new_row, STEPS))
    )
    new_slot = jnp.where(new_ok, over(new_col, 2 * heads * STEPS), slots)

    every = range(slots)
    new = new_ref[...]
    new_all = dot_nt(query_ref[...].reshape(slots * queries, HD), new)
    fetch.wait()
    caches = [codes_ref[s] * columns[:, s : s + 1] for s in every]
    scores = [dot_nt(query_ref[s], caches[s]) for s in every]
    scores = [jnp.where(col_token < len_ref[s], scores[s] * SCORE_SCALE, NEGATIVE) for s in every]
    new_scores = [
        jnp.where(new_slot == s, new_all[s * queries : (s + 1) * queries] * SCORE_SCALE, NEGATIVE)
        for s in every
    ]
    top = [top_of(scores[s], new_scores[s]) for s in every]
    weights = [jnp.exp(scores[s] - top[s]) for s in every]
    new_weights = [jnp.exp(new_scores[s] - top[s]) for s in every]
    total = [sum_of(weights[s], new_weights[s]) for s in every]
    new_mixed = dot_nn(jnp.concatenate(new_weights, axis=0).astype(BF16), values_up(new))
    mixed = [
        dot_nn(to_values(weights[s]), caches[s]) + new_mixed[s * queries : (s + 1) * queries]
        for s in every
    ]
    for s in every:
        out_ref[s] = (mixed[s] * (1.0 / total[s])).astype(BF16)


def slots_by_rows(got_ref, tp, order, block_rows):
    chunk_rows = got_ref.shape[2]
    blocks = chunk_rows // block_rows
    rows = [got_ref[k, 0].astype(F32) for k in range(len(order))]
    here = {
        core // tp: jnp.where(x[:1] < EMPTY, 1.0, 0.0)
        for core, x in zip(order, rows)
        if core % tp == 0
    }
    ranks = {
        w: sum([here[v] for v in here if v < w], jnp.zeros((1, HD), F32)) for w in here
    }
    lane = iota((1, HD), 1)
    block = over(lane, block_rows)
    block = jnp.where(mod(lane, 2) == 0, block, -1)
    per_tile = HD // chunk_rows
    tiles = []
    for start in range(0, len(order), per_tile):
        tile = jnp.full((1, HD), -1.0, F32)
        for i in range(per_tile):
            x, rank = rows[start + i], ranks[order[start + i] // tp]
            for b in range(blocks):
                at = b * block_rows
                value = jnp.where(x[at : at + 1] < EMPTY, rank, -1.0)
                tile = jnp.where(block == i * blocks + b, value, tile)
        tiles.append(tile)
    return jnp.concatenate(tiles, axis=1)


def slots_by_matmul(got_ref, tp):
    chunks, _, chunk_rows = got_ref.shape[:3]
    columns = chunks * chunk_rows
    sender_rows = tp * chunk_rows
    piece = min(columns, 256)
    sums = dot_nt(jnp.ones((16, HD), BF16), got_ref[:, 0].reshape(columns, HD))[:8]
    col = iota((8, columns), 1)
    held = sums < EMPTY
    first = jnp.where(held & (mod(col, sender_rows) == 0), 1.0, 0.0).astype(BF16)
    row = over(iota((piece, piece), 0), sender_rows)
    before = jnp.where(row < over(iota((piece, piece), 1), sender_rows), 1.0, 0.0).astype(BF16)
    base = jnp.zeros((8, 1), F32)
    ranks = []
    for p in range(0, columns, piece):
        part = first[:, p : p + piece]
        ranks.append(dot_nn(part, before) + base)
        base = base + jnp.sum(part.astype(F32), axis=1, keepdims=True)
    rank = jnp.concatenate(ranks, axis=1)
    return jnp.where(held & (mod(col, 2) == 0), rank, -1.0)[:1]


def arrival_kernel(
    tp, groups, order, block_rows, got_ref, query_ref, new_ref, done_ref, out_ref, done_hbm, sem
):
    step = pl.program_id(0) if groups > 1 else 0
    hand_on = pltpu.make_async_copy(done_ref, done_hbm, sem)
    if groups > 1:
        pl.when(step == 0)(hand_on.start)
    else:
        hand_on.start()

    chunks, heads, chunk_rows = got_ref.shape[:3]
    slots, _, per_head = query_ref.shape[:3]
    rows = slots * per_head
    columns = chunks * chunk_rows
    every = range(heads)

    caches = [got_ref[:, h].reshape(columns, HD) for h in every]
    queries = [query_ref[:, h].reshape(rows, HD) for h in every]
    new = new_ref[...]
    scores = [dot_nt(queries[h], caches[h]) for h in every]
    new_all = dot_nt(jnp.concatenate(queries, axis=0), new)
    if order is None:
        slot_of = slots_by_matmul(got_ref, tp)
    else:
        slot_of = slots_by_rows(got_ref, tp, order, block_rows)
    first_slot = jnp.float32(step * slots)
    mine = [slot_of == first_slot + a for a in range(slots)]

    new_col = iota((rows, new.shape[0]), 1)
    new_row = iota((rows, new.shape[0]), 0)
    new_here = (
        (mod(new_col, 2) == 0)
        & (over(new_col, 2 * heads * STEPS) == over(new_row, per_head))
        & (mod(over(new_col, 2 * heads), STEPS) <= mod(new_row, STEPS))
    )
    new_head = jnp.where(new_here, mod(over(new_col, 2), heads), heads)

    scores = [
        jnp.concatenate(
            [
                jnp.where(mine[a], scores[h][a * per_head : (a + 1) * per_head] * SCORE_SCALE, NEGATIVE)
                for a in range(slots)
            ],
            axis=0,
        )
        for h in every
    ]
    new_scores = [
        jnp.where(new_head == h, new_all[h * rows : (h + 1) * rows] * SCORE_SCALE, NEGATIVE)
        for h in every
    ]
    top = [top_of(scores[h], new_scores[h]) for h in every]
    weights = [jnp.exp(scores[h] - top[h]) for h in every]
    new_weights = [jnp.exp(new_scores[h] - top[h]) for h in every]
    total = [sum_of(weights[h], new_weights[h]) for h in every]
    new_mixed = dot_nn(jnp.concatenate(new_weights, axis=0).astype(BF16), values_up(new))
    for h in every:
        mixed = dot_nn(to_values(weights[h]), caches[h]) + new_mixed[h * rows : (h + 1) * rows]
        out_ref[:, h] = (mixed * (1.0 / total[h])).astype(BF16).reshape(slots, per_head, HD)
    if groups > 1:
        pl.when(step == groups - 1)(hand_on.wait)
    else:
        hand_on.wait()


def whole(memory_space=pltpu.VMEM):
    return pl.BlockSpec(memory_space=memory_space)


def in_hbm(x):
    return pltpu.with_memory_space_constraint(x, pltpu.HBM)


def limit(mib):
    return pltpu.CompilerParams(vmem_limit_bytes=mib * 2**20)


def pack(pre_codes, pre_scales, req_dest, req_blocks, peers, tp, order):
    requests, blocks, block_tokens = pre_codes.shape[:3]
    tokens = blocks * block_tokens
    codes = (
        pre_codes.reshape(requests, tokens, 2, KVH, HD)
        .transpose(0, 1, 3, 2, 4)
        .reshape(requests, tokens * KVH * 2, HD)
    )
    scales = pre_scales.reshape(requests, tokens * 2, KVH)
    ins = [req_dest, req_blocks, codes, scales]
    return pl.pallas_call(
        functools.partial(pack_kernel, tp, order, KVH, 2 * block_tokens),
        out_shape=pltpu.VMEM((peers * tp, KVH // tp, tokens * 2, HD), BF16),
        in_specs=[whole(pltpu.HBM)] * len(ins),
        out_specs=whole(),
        scratch_shapes=[
            pltpu.SMEM(req_dest.shape, jnp.int32),
            pltpu.SMEM(req_blocks.shape, jnp.int32),
            pltpu.VMEM(codes.shape, BF16),
            pltpu.VMEM(scales.shape, BF16),
            pltpu.SemaphoreType.DMA((5,)),
        ],
        compiler_params=limit(16),
        name="pack",
    )(*[in_hbm(x) for x in ins])


def cache_rows(codes):
    slots, tokens, _, width = codes.shape
    heads = width // HD
    return (
        codes.reshape(slots, tokens, 2, heads, HD)
        .transpose(0, 1, 3, 2, 4)
        .reshape(slots, tokens * heads * 2, HD)
    )


def query_rows(query):
    slots, steps, width = query.shape
    return query.reshape(slots, steps, width // HD, HD).transpose(0, 2, 1, 3)


def new_rows_of(new):
    slots, steps, pair, width = new.shape
    heads = width // HD
    return (
        new.reshape(slots, steps, pair, heads, HD)
        .transpose(0, 1, 3, 2, 4)
        .reshape(slots * steps * heads * pair, HD)
    )


def from_rows(out, shape):
    slots, steps, width = shape
    return out.reshape(slots, width // HD, steps, HD).transpose(0, 2, 1, 3).reshape(shape)


def resident(codes, res_scales, res_len, res_query, res_new):
    slots, rows = codes.shape[:2]
    heads = res_scales.shape[-1]
    scales = res_scales.transpose(0, 2, 3, 1)
    query = query_rows(res_query).reshape(slots, heads * GROUP * STEPS, HD)
    work = query.shape[0] * query.shape[1] * rows
    return pl.pallas_call(
        resident_kernel,
        out_shape=pltpu.VMEM(query.shape, BF16),
        in_specs=[whole(pltpu.SMEM), whole(pltpu.HBM)] + [whole()] * 3,
        out_specs=whole(),
        scratch_shapes=[pltpu.VMEM(codes.shape, BF16), pltpu.SemaphoreType.DMA],
        cost_estimate=pl.CostEstimate(
            flops=4 * work * HD,
            bytes_accessed=2 * (codes.size + 2 * query.size),
            transcendentals=work,
        ),
        compiler_params=limit(16),
        name="resident",
    )(in_hbm(res_len), in_hbm(codes), scales, query, new_rows_of(res_new))


def arrivals(got, arr_query, arr_new, done, tp, order, block_rows):
    slots, steps, width = arr_query.shape
    heads = width // (HD * GROUP)
    query = query_rows(arr_query).reshape(slots, heads, GROUP * steps, HD)
    new = new_rows_of(arr_new)
    size = max(n for n in range(1, 7) if slots % n == 0)
    groups = slots // size
    small = got.size <= 2**18

    def part(ref, rows):
        if groups == 1:
            return whole()
        return pl.BlockSpec((rows,) + ref.shape[1:], lambda i: (i,) + (0,) * (ref.ndim - 1))

    return pl.pallas_call(
        functools.partial(arrival_kernel, tp, groups, order, block_rows),
        out_shape=[
            jax.ShapeDtypeStruct(query.shape, BF16),
            jax.ShapeDtypeStruct(done.shape, BF16),
        ],
        grid=(groups,) if groups > 1 else (),
        in_specs=[
            whole(),
            part(query, size),
            part(new, new.shape[0] // groups),
            whole(),
        ],
        out_specs=[part(query, size), whole(pltpu.HBM)],
        scratch_shapes=[pltpu.SemaphoreType.DMA],
        compiler_params=limit(16 if small else 48),
        name="arrivals",
    )(got, query, new, done)


def shards(
    pre_codes,
    pre_scales,
    req_dest,
    req_blocks,
    res_codes,
    res_scales,
    res_len,
    res_query,
    res_new,
    arr_query,
    arr_new,
):
    peers = lax.axis_size("wide")
    tp = lax.axis_size("tp")
    order = None
    if peers * tp == 16:
        order = [(11 - p) % 16 for p in range(16)]
    send = pack(pre_codes, pre_scales, req_dest, req_blocks, peers, tp, order)
    got = lax.all_to_all(
        send,
        ("wide", "tp"),
        split_axis=0,
        concat_axis=0,
        tiled=True,
        axis_index_groups=[order or list(range(peers * tp))],
    )
    done = resident(cache_rows(res_codes), res_scales, res_len, res_query, res_new)
    block_rows = 2 * pre_codes.shape[2]
    arr_out, res_out = arrivals(got, arr_query, arr_new, done, tp, order, block_rows)
    return (from_rows(res_out, res_query.shape), from_rows(arr_out, arr_query.shape))


def solution(mesh):
    in_specs = (
        P(("groups", "wide"), None, "tp", None, None),
        P(("groups", "wide"), None, "tp", None, None),
        P(("groups", "wide")),
        P(("groups", "wide")),
        P(("groups", "wide"), None, None, "tp"),
        P(("groups", "wide"), None, None, "tp"),
        P(("groups", "wide")),
        P(("groups", "wide"), None, "tp"),
        P(("groups", "wide"), None, None, "tp"),
        P(("groups", "wide"), None, "tp"),
        P(("groups", "wide"), None, None, "tp"),
    )
    out_specs = (P(("groups", "wide"), None, "tp"), P(("groups", "wide"), None, "tp"))
    return jax.shard_map(shards, mesh=mesh, in_specs=in_specs, out_specs=out_specs, check_vma=False)
```

```python
import functools
import math

import jax
import jax.numpy as jnp
from jax import lax
from jax.experimental import pallas as pl
from jax.experimental.pallas import tpu as pltpu
from jax.sharding import PartitionSpec as P

KVH = 4
HD = 128
HQ = 64
GROUP = HQ // KVH
STEPS = 2

NEGATIVE = -1e30
EMPTY = 1024.0
SCORE_SCALE = 1.0 / math.sqrt(HD)

BF16 = jnp.bfloat16
F32 = jnp.float32


def iota(shape, axis):
    return lax.broadcasted_iota(jnp.int32, shape, axis)


def over(x, n):
    return jnp.right_shift(x, n.bit_length() - 1) if n & (n - 1) == 0 else x // n


def mod(x, n):
    return jnp.bitwise_and(x, n - 1) if n & (n - 1) == 0 else x % n


def dot_nt(a, b):
    return lax.dot_general(a, b, (((1,), (1,)), ((), ())), preferred_element_type=F32)


def dot_nn(a, b):
    return lax.dot_general(a, b, (((1,), (0,)), ((), ())), preferred_element_type=F32)


def top_of(*parts):
    return functools.reduce(jnp.maximum, [jnp.max(p, axis=1, keepdims=True) for p in parts])


def sum_of(*parts):
    return functools.reduce(jnp.add, [jnp.sum(p, axis=1, keepdims=True) for p in parts])


def to_values(weights):
    tiles = [pltpu.roll(weights[:, c : c + HD], 1, 1) for c in range(0, weights.shape[1], HD)]
    return jnp.concatenate(tiles, axis=1).astype(BF16)


def values_up(rows):
    return pltpu.roll(rows.astype(F32), rows.shape[0] - 1, 0).astype(BF16)


def pack_kernel(
    tp, order, heads, block_rows, dest_hbm, blocks_hbm, codes_hbm, scales_hbm, send_ref,
    dest_ref, blocks_ref, codes_ref, scales_ref, sems,
):
    requests, all_rows = codes_ref.shape[:2]
    pairs = [
        (codes_hbm.at[: requests // 2], codes_ref.at[: requests // 2]),
        (codes_hbm.at[requests // 2 :], codes_ref.at[requests // 2 :]),
        (scales_hbm, scales_ref), (dest_hbm, dest_ref), (blocks_hbm, blocks_ref),
    ]
    copies = [pltpu.make_async_copy(a, b, sems.at[i]) for i, (a, b) in enumerate(pairs)]
    for copy in copies:
        copy.start()
    rows = all_rows // heads
    per_core = heads // tp
    send_ref[...] = jnp.full(send_ref.shape, EMPTY, BF16)
    row_block = over(iota((rows, HD), 0), block_rows)
    to_row = iota((all_rows, all_rows), 0)
    from_row = iota((all_rows, all_rows), 1)
    source = over(mod(to_row, rows), 2) * (2 * heads) + over(to_row, rows) * 2 + mod(to_row, 2)
    by_head = jnp.where(from_row == source, 1.0, 0.0).astype(BF16)
    for copy in copies:
        copy.wait()

    def place(r):
        there = dest_ref[r]
        spots = [there * tp + t for t in range(tp)]
        if order is not None:
            for t in range(tp):
                at = {core // tp: p for p, core in enumerate(order) if core % tp == t}
                spots[t] = functools.reduce(
                    jnp.add, [jnp.where(there == w, p, 0) for w, p in at.items()]
                )
        held = row_block < blocks_ref[r]
        codes = dot_nn(by_head, codes_ref[r])
        scales = scales_ref[r].astype(F32)
        for j in range(heads):
            values = codes[j * rows : (j + 1) * rows] * scales[:, j : j + 1]
            values = jnp.where(held, values, EMPTY).astype(BF16)
            send_ref[spots[j // per_core], j % per_core] = values

    if requests <= 8:
        for r in range(requests):
            place(r)
    else:
        lax.fori_loop(0, requests, lambda r, c: (place(r), c)[1], 0)


def resident_kernel(
    len_ref, codes_hbm, scales_ref, query_ref, new_ref, out_ref, codes_ref, sem
):
    fetch = pltpu.make_async_copy(codes_hbm, codes_ref, sem)
    fetch.start()
    slots, rows = codes_ref.shape[:2]
    heads = scales_ref.shape[2]
    tokens = rows // (2 * heads)
    queries = query_ref.shape[1]
    new_rows = new_ref.shape[0]

    row = iota((rows, HD), 0)
    source = (mod(row, 2) * heads + mod(over(row, 2), heads)) * tokens + over(row, 2 * heads)
    lane = iota((rows, HD), 1)
    spread = jnp.concatenate(
        [jnp.where(source == lane + c, 1.0, 0.0).astype(BF16) for c in range(0, rows, HD)],
        axis=1,
    )
    flat = jnp.concatenate(
        [scales_ref[:, p, h] for p in range(2) for h in range(heads)], axis=1
    )
    columns = dot_nt(spread, flat).astype(BF16)

    col = iota((queries, rows), 1)
    row_head = over(iota((queries, rows), 0), queries // heads)
    is_key = (mod(col, 2) == 0) & (mod(over(col, 2), heads) == row_head)
    col_token = jnp.where(is_key, over(col, 2 * heads), tokens)

    new_col = iota((queries, new_rows), 1)
    new_row = iota((queries, new_rows), 0)
    new_ok = (
        (mod(new_col, 2) == 0)
        & (mod(over(new_col, 2), heads) == over(new_row, queries // heads))
        & (mod(over(new_col, 2 * heads), STEPS) <= mod(new_row, STEPS))
    )
    new_slot = jnp.where(new_ok, over(new_col, 2 * heads * STEPS), slots)

    every = range(slots)
    new = new_ref[...]
    new_all = dot_nt(query_ref[...].reshape(slots * queries, HD), new)
    fetch.wait()
    caches = [codes_ref[s] * columns[:, s : s + 1] for s in every]
    scores = [dot_nt(query_ref[s], caches[s]) for s in every]
    scores = [jnp.where(col_token < len_ref[s], scores[s] * SCORE_SCALE, NEGATIVE) for s in every]
    new_scores = [
        jnp.where(new_slot == s, new_all[s * queries : (s + 1) * queries] * SCORE_SCALE, NEGATIVE)
        for s in every
    ]
    top = [top_of(scores[s], new_scores[s]) for s in every]
    weights = [jnp.exp(scores[s] - top[s]) for s in every]
    new_weights = [jnp.exp(new_scores[s] - top[s]) for s in every]
    total = [sum_of(weights[s], new_weights[s]) for s in every]
    new_mixed = dot_nn(jnp.concatenate(new_weights, axis=0).astype(BF16), values_up(new))
    mixed = [
        dot_nn(to_values(weights[s]), caches[s]) + new_mixed[s * queries : (s + 1) * queries]
        for s in every
    ]
    for s in every:
        out_ref[s] = (mixed[s] * (1.0 / total[s])).astype(BF16)


def slots_by_rows(got_ref, tp, order, block_rows):
    chunk_rows = got_ref.shape[2]
    blocks = chunk_rows // block_rows
    rows = [got_ref[k, 0].astype(F32) for k in range(len(order))]
    here = {
        core // tp: jnp.where(x[:1] < EMPTY, 1.0, 0.0)
        for core, x in zip(order, rows)
        if core % tp == 0
    }
    ranks = {
        w: sum([here[v] for v in here if v < w], jnp.zeros((1, HD), F32)) for w in here
    }
    lane = iota((1, HD), 1)
    block = over(lane, block_rows)
    block = jnp.where(mod(lane, 2) == 0, block, -1)
    per_tile = HD // chunk_rows
    tiles = []
    for start in range(0, len(order), per_tile):
        tile = jnp.full((1, HD), -1.0, F32)
        for i in range(per_tile):
            x, rank = rows[start + i], ranks[order[start + i] // tp]
            for b in range(blocks):
                at = b * block_rows
                value = jnp.where(x[at : at + 1] < EMPTY, rank, -1.0)
                tile = jnp.where(block == i * blocks + b, value, tile)
        tiles.append(tile)
    return jnp.concatenate(tiles, axis=1)


def slots_by_matmul(got_ref, tp):
    chunks, _, chunk_rows = got_ref.shape[:3]
    columns = chunks * chunk_rows
    sender_rows = tp * chunk_rows
    piece = min(columns, 256)
    sums = dot_nt(jnp.ones((16, HD), BF16), got_ref[:, 0].reshape(columns, HD))[:8]
    col = iota((8, columns), 1)
    held = sums < EMPTY
    first = jnp.where(held & (mod(col, sender_rows) == 0), 1.0, 0.0).astype(BF16)
    row = over(iota((piece, piece), 0), sender_rows)
    before = jnp.where(row < over(iota((piece, piece), 1), sender_rows), 1.0, 0.0).astype(BF16)
    base = jnp.zeros((8, 1), F32)
    ranks = []
    for p in range(0, columns, piece):
        part = first[:, p : p + piece]
        ranks.append(dot_nn(part, before) + base)
        base = base + jnp.sum(part.astype(F32), axis=1, keepdims=True)
    rank = jnp.concatenate(ranks, axis=1)
    return jnp.where(held & (mod(col, 2) == 0), rank, -1.0)[:1]


def arrival_kernel(
    tp, groups, order, block_rows, got_ref, query_ref, new_ref, done_ref, out_ref, done_hbm, sem
):
    step = pl.program_id(0) if groups > 1 else 0
    hand_on = pltpu.make_async_copy(done_ref, done_hbm, sem)
    if groups > 1:
        pl.when(step == 0)(hand_on.start)
    else:
        hand_on.start()

    chunks, heads, chunk_rows = got_ref.shape[:3]
    slots, _, per_head = query_ref.shape[:3]
    rows = slots * per_head
    columns = chunks * chunk_rows
    every = range(heads)

    caches = [got_ref[:, h].reshape(columns, HD) for h in every]
    queries = [query_ref[:, h].reshape(rows, HD) for h in every]
    new = new_ref[...]
    scores = [dot_nt(queries[h], caches[h]) for h in every]
    new_all = dot_nt(jnp.concatenate(queries, axis=0), new)
    if order is None:
        slot_of = slots_by_matmul(got_ref, tp)
    else:
        slot_of = slots_by_rows(got_ref, tp, order, block_rows)
    first_slot = jnp.float32(step * slots)
    mine = [slot_of == first_slot + a for a in range(slots)]

    new_col = iota((rows, new.shape[0]), 1)
    new_row = iota((rows, new.shape[0]), 0)
    new_here = (
        (mod(new_col, 2) == 0)
        & (over(new_col, 2 * heads * STEPS) == over(new_row, per_head))
        & (mod(over(new_col, 2 * heads), STEPS) <= mod(new_row, STEPS))
    )
    new_head = jnp.where(new_here, mod(over(new_col, 2), heads), heads)

    scores = [
        jnp.concatenate(
            [
                jnp.where(mine[a], scores[h][a * per_head : (a + 1) * per_head] * SCORE_SCALE, NEGATIVE)
                for a in range(slots)
            ],
            axis=0,
        )
        for h in every
    ]
    new_scores = [
        jnp.where(new_head == h, new_all[h * rows : (h + 1) * rows] * SCORE_SCALE, NEGATIVE)
        for h in every
    ]
    top = [top_of(scores[h], new_scores[h]) for h in every]
    weights = [jnp.exp(scores[h] - top[h]) for h in every]
    new_weights = [jnp.exp(new_scores[h] - top[h]) for h in every]
    total = [sum_of(weights[h], new_weights[h]) for h in every]
    new_mixed = dot_nn(jnp.concatenate(new_weights, axis=0).astype(BF16), values_up(new))
    for h in every:
        mixed = dot_nn(to_values(weights[h]), caches[h]) + new_mixed[h * rows : (h + 1) * rows]
        out_ref[:, h] = (mixed * (1.0 / total[h])).astype(BF16).reshape(slots, per_head, HD)
    if groups > 1:
        pl.when(step == groups - 1)(hand_on.wait)
    else:
        hand_on.wait()


def whole(memory_space=pltpu.VMEM):
    return pl.BlockSpec(memory_space=memory_space)


def in_hbm(x):
    return pltpu.with_memory_space_constraint(x, pltpu.HBM)


def limit(mib):
    return pltpu.CompilerParams(vmem_limit_bytes=mib * 2**20)


def pack(pre_codes, pre_scales, req_dest, req_blocks, peers, tp, order):
    requests, blocks, block_tokens = pre_codes.shape[:3]
    tokens = blocks * block_tokens
    codes = (
        pre_codes.reshape(requests, tokens, 2, KVH, HD)
        .transpose(0, 1, 3, 2, 4)
        .reshape(requests, tokens * KVH * 2, HD)
    )
    scales = pre_scales.reshape(requests, tokens * 2, KVH)
    ins = [req_dest, req_blocks, codes, scales]
    return pl.pallas_call(
        functools.partial(pack_kernel, tp, order, KVH, 2 * block_tokens),
        out_shape=pltpu.VMEM((peers * tp, KVH // tp, tokens * 2, HD), BF16),
        in_specs=[whole(pltpu.HBM)] * len(ins),
        out_specs=whole(),
        scratch_shapes=[
            pltpu.SMEM(req_dest.shape, jnp.int32),
            pltpu.SMEM(req_blocks.shape, jnp.int32),
            pltpu.VMEM(codes.shape, BF16),
            pltpu.VMEM(scales.shape, BF16),
            pltpu.SemaphoreType.DMA((5,)),
        ],
        compiler_params=limit(16),
        name="pack",
    )(*[in_hbm(x) for x in ins])


def cache_rows(codes):
    slots, tokens, _, width = codes.shape
    heads = width // HD
    return (
        codes.reshape(slots, tokens, 2, heads, HD)
        .transpose(0, 1, 3, 2, 4)
        .reshape(slots, tokens * heads * 2, HD)
    )


def query_rows(query):
    slots, steps, width = query.shape
    return query.reshape(slots, steps, width // HD, HD).transpose(0, 2, 1, 3)


def new_rows_of(new):
    slots, steps, pair, width = new.shape
    heads = width // HD
    return (
        new.reshape(slots, steps, pair, heads, HD)
        .transpose(0, 1, 3, 2, 4)
        .reshape(slots * steps * heads * pair, HD)
    )


def from_rows(out, shape):
    slots, steps, width = shape
    return out.reshape(slots, width // HD, steps, HD).transpose(0, 2, 1, 3).reshape(shape)


def resident(codes, res_scales, res_len, res_query, res_new):
    slots, rows = codes.shape[:2]
    heads = res_scales.shape[-1]
    scales = res_scales.transpose(0, 2, 3, 1)
    query = query_rows(res_query).reshape(slots, heads * GROUP * STEPS, HD)
    work = query.shape[0] * query.shape[1] * rows
    return pl.pallas_call(
        resident_kernel,
        out_shape=pltpu.VMEM(query.shape, BF16),
        in_specs=[whole(pltpu.SMEM), whole(pltpu.HBM)] + [whole()] * 3,
        out_specs=whole(),
        scratch_shapes=[pltpu.VMEM(codes.shape, BF16), pltpu.SemaphoreType.DMA],
        cost_estimate=pl.CostEstimate(
            flops=4 * work * HD,
            bytes_accessed=2 * (codes.size + 2 * query.size),
            transcendentals=work,
        ),
        compiler_params=limit(16),
        name="resident",
    )(in_hbm(res_len), in_hbm(codes), scales, query, new_rows_of(res_new))


def arrivals(got, arr_query, arr_new, done, tp, order, block_rows):
    slots, steps, width = arr_query.shape
    heads = width // (HD * GROUP)
    query = query_rows(arr_query).reshape(slots, heads, GROUP * steps, HD)
    new = new_rows_of(arr_new)
    size = max(n for n in range(1, 7) if slots % n == 0)
    groups = slots // size
    small = got.size <= 2**18

    def part(ref, rows):
        if groups == 1:
            return whole()
        return pl.BlockSpec((rows,) + ref.shape[1:], lambda i: (i,) + (0,) * (ref.ndim - 1))

    return pl.pallas_call(
        functools.partial(arrival_kernel, tp, groups, order, block_rows),
        out_shape=[
            jax.ShapeDtypeStruct(query.shape, BF16),
            jax.ShapeDtypeStruct(done.shape, BF16),
        ],
        grid=(groups,) if groups > 1 else (),
        in_specs=[
            whole(),
            part(query, size),
            part(new, new.shape[0] // groups),
            whole(),
        ],
        out_specs=[part(query, size), whole(pltpu.HBM)],
        scratch_shapes=[pltpu.SemaphoreType.DMA],
        compiler_params=limit(16 if small else 48),
        name="arrivals",
    )(got, query, new, done)


def shards(
    pre_codes,
    pre_scales,
    req_dest,
    req_blocks,
    res_codes,
    res_scales,
    res_len,
    res_query,
    res_new,
    arr_query,
    arr_new,
):
    peers = lax.axis_size("wide")
    tp = lax.axis_size("tp")
    order = None
    if peers * tp == 16:
        order = [11, 10, 13, 12, 15, 14, 3, 2, 1, 0, 5, 4, 7, 6, 9, 8]
    send = pack(pre_codes, pre_scales, req_dest, req_blocks, peers, tp, order)
    got = lax.all_to_all(
        send,
        ("wide", "tp"),
        split_axis=0,
        concat_axis=0,
        tiled=True,
        axis_index_groups=[order or list(range(peers * tp))],
    )
    done = resident(cache_rows(res_codes), res_scales, res_len, res_query, res_new)
    block_rows = 2 * pre_codes.shape[2]
    arr_out, res_out = arrivals(got, arr_query, arr_new, done, tp, order, block_rows)
    return (from_rows(res_out, res_query.shape), from_rows(arr_out, arr_query.shape))


def solution(mesh):
    in_specs = (
        P(("groups", "wide"), None, "tp", None, None),
        P(("groups", "wide"), None, "tp", None, None),
        P(("groups", "wide")),
        P(("groups", "wide")),
        P(("groups", "wide"), None, None, "tp"),
        P(("groups", "wide"), None, None, "tp"),
        P(("groups", "wide")),
        P(("groups", "wide"), None, "tp"),
        P(("groups", "wide"), None, None, "tp"),
        P(("groups", "wide"), None, "tp"),
        P(("groups", "wide"), None, None, "tp"),
    )
    out_specs = (P(("groups", "wide"), None, "tp"), P(("groups", "wide"), None, "tp"))
    return jax.shard_map(shards, mesh=mesh, in_specs=in_specs, out_specs=out_specs, check_vma=False)
```

```python
import functools
import math

import jax
import jax.numpy as jnp
from jax import lax
from jax.experimental import pallas as pl
from jax.experimental.pallas import tpu as pltpu
from jax.sharding import PartitionSpec as P

KVH = 4
HD = 128
HQ = 64
GROUP = HQ // KVH
STEPS = 2

NEGATIVE = -1e30
EMPTY = 1024.0
SCORE_SCALE = 1.0 / math.sqrt(HD)

BF16 = jnp.bfloat16
F32 = jnp.float32


def iota(shape, axis):
    return lax.broadcasted_iota(jnp.int32, shape, axis)


def over(x, n):
    return jnp.right_shift(x, n.bit_length() - 1) if n & (n - 1) == 0 else x // n


def mod(x, n):
    return jnp.bitwise_and(x, n - 1) if n & (n - 1) == 0 else x % n


def dot_nt(a, b):
    return lax.dot_general(a, b, (((1,), (1,)), ((), ())), preferred_element_type=F32)


def dot_nn(a, b):
    return lax.dot_general(a, b, (((1,), (0,)), ((), ())), preferred_element_type=F32)


def top_of(*parts):
    return functools.reduce(jnp.maximum, [jnp.max(p, axis=1, keepdims=True) for p in parts])


def sum_of(*parts):
    return functools.reduce(jnp.add, [jnp.sum(p, axis=1, keepdims=True) for p in parts])


def to_values(weights):
    tiles = [pltpu.roll(weights[:, c : c + HD], 1, 1) for c in range(0, weights.shape[1], HD)]
    return jnp.concatenate(tiles, axis=1).astype(BF16)


def values_up(rows):
    return pltpu.roll(rows.astype(F32), rows.shape[0] - 1, 0).astype(BF16)


def pack_kernel(
    tp, order, heads, block_rows, dest_hbm, blocks_hbm, codes_hbm, scales_hbm, send_ref,
    dest_ref, blocks_ref, codes_ref, scales_ref, sems,
):
    requests, all_rows = codes_ref.shape[:2]
    pairs = [
        (codes_hbm.at[: requests // 2], codes_ref.at[: requests // 2]),
        (codes_hbm.at[requests // 2 :], codes_ref.at[requests // 2 :]),
        (scales_hbm, scales_ref), (dest_hbm, dest_ref), (blocks_hbm, blocks_ref),
    ]
    copies = [pltpu.make_async_copy(a, b, sems.at[i]) for i, (a, b) in enumerate(pairs)]
    for copy in copies:
        copy.start()
    rows = all_rows // heads
    per_core = heads // tp
    send_ref[...] = jnp.full(send_ref.shape, EMPTY, BF16)
    row_block = over(iota((rows, HD), 0), block_rows)
    to_row = iota((all_rows, all_rows), 0)
    from_row = iota((all_rows, all_rows), 1)
    source = over(mod(to_row, rows), 2) * (2 * heads) + over(to_row, rows) * 2 + mod(to_row, 2)
    by_head = jnp.where(from_row == source, 1.0, 0.0).astype(BF16)
    for copy in copies:
        copy.wait()

    def place(r):
        there = dest_ref[r]
        spots = [there * tp + t for t in range(tp)]
        if order is not None:
            for t in range(tp):
                at = {core // tp: p for p, core in enumerate(order) if core % tp == t}
                spots[t] = functools.reduce(
                    jnp.add, [jnp.where(there == w, p, 0) for w, p in at.items()]
                )
        held = row_block < blocks_ref[r]
        codes = dot_nn(by_head, codes_ref[r])
        scales = scales_ref[r].astype(F32)
        for j in range(heads):
            values = codes[j * rows : (j + 1) * rows] * scales[:, j : j + 1]
            values = jnp.where(held, values, EMPTY).astype(BF16)
            send_ref[spots[j // per_core], j % per_core] = values

    if requests <= 8:
        for r in range(requests):
            place(r)
    else:
        lax.fori_loop(0, requests, lambda r, c: (place(r), c)[1], 0)


def resident_kernel(
    len_ref, codes_hbm, scales_ref, query_ref, new_ref, out_ref, codes_ref, sem
):
    fetch = pltpu.make_async_copy(codes_hbm, codes_ref, sem)
    fetch.start()
    slots, rows = codes_ref.shape[:2]
    heads = scales_ref.shape[2]
    tokens = rows // (2 * heads)
    queries = query_ref.shape[1]
    new_rows = new_ref.shape[0]

    row = iota((rows, HD), 0)
    source = (mod(row, 2) * heads + mod(over(row, 2), heads)) * tokens + over(row, 2 * heads)
    lane = iota((rows, HD), 1)
    spread = jnp.concatenate(
        [jnp.where(source == lane + c, 1.0, 0.0).astype(BF16) for c in range(0, rows, HD)],
        axis=1,
    )
    flat = jnp.concatenate(
        [scales_ref[:, p, h] for p in range(2) for h in range(heads)], axis=1
    )
    columns = dot_nt(spread, flat).astype(BF16)

    col = iota((queries, rows), 1)
    row_head = over(iota((queries, rows), 0), queries // heads)
    is_key = (mod(col, 2) == 0) & (mod(over(col, 2), heads) == row_head)
    col_token = jnp.where(is_key, over(col, 2 * heads), tokens)

    new_col = iota((queries, new_rows), 1)
    new_row = iota((queries, new_rows), 0)
    new_ok = (
        (mod(new_col, 2) == 0)
        & (mod(over(new_col, 2), heads) == over(new_row, queries // heads))
        & (mod(over(new_col, 2 * heads), STEPS) <= mod(new_row, STEPS))
    )
    new_slot = jnp.where(new_ok, over(new_col, 2 * heads * STEPS), slots)

    every = range(slots)
    new = new_ref[...]
    new_all = dot_nt(query_ref[...].reshape(slots * queries, HD), new)
    fetch.wait()
    caches = [codes_ref[s] * columns[:, s : s + 1] for s in every]
    scores = [dot_nt(query_ref[s], caches[s]) for s in every]
    scores = [jnp.where(col_token < len_ref[s], scores[s] * SCORE_SCALE, NEGATIVE) for s in every]
    new_scores = [
        jnp.where(new_slot == s, new_all[s * queries : (s + 1) * queries] * SCORE_SCALE, NEGATIVE)
        for s in every
    ]
    top = [top_of(scores[s], new_scores[s]) for s in every]
    weights = [jnp.exp(scores[s] - top[s]) for s in every]
    new_weights = [jnp.exp(new_scores[s] - top[s]) for s in every]
    total = [sum_of(weights[s], new_weights[s]) for s in every]
    new_mixed = dot_nn(jnp.concatenate(new_weights, axis=0).astype(BF16), values_up(new))
    mixed = [
        dot_nn(to_values(weights[s]), caches[s]) + new_mixed[s * queries : (s + 1) * queries]
        for s in every
    ]
    for s in every:
        out_ref[s] = (mixed[s] * (1.0 / total[s])).astype(BF16)


def slots_by_rows(got_ref, tp, order, block_rows):
    chunk_rows = got_ref.shape[2]
    blocks = chunk_rows // block_rows
    rows = [got_ref[k, 0].astype(F32) for k in range(len(order))]
    here = {
        core // tp: jnp.where(x[:1] < EMPTY, 1.0, 0.0)
        for core, x in zip(order, rows)
        if core % tp == 0
    }
    ranks = {
        w: sum([here[v] for v in here if v < w], jnp.zeros((1, HD), F32)) for w in here
    }
    lane = iota((1, HD), 1)
    block = over(lane, block_rows)
    block = jnp.where(mod(lane, 2) == 0, block, -1)
    per_tile = HD // chunk_rows
    tiles = []
    for start in range(0, len(order), per_tile):
        tile = jnp.full((1, HD), -1.0, F32)
        for i in range(per_tile):
            x, rank = rows[start + i], ranks[order[start + i] // tp]
            for b in range(blocks):
                at = b * block_rows
                value = jnp.where(x[at : at + 1] < EMPTY, rank, -1.0)
                tile = jnp.where(block == i * blocks + b, value, tile)
        tiles.append(tile)
    return jnp.concatenate(tiles, axis=1)


def slots_by_matmul(got_ref, tp):
    chunks, _, chunk_rows = got_ref.shape[:3]
    columns = chunks * chunk_rows
    sender_rows = tp * chunk_rows
    piece = min(columns, 256)
    sums = dot_nt(jnp.ones((16, HD), BF16), got_ref[:, 0].reshape(columns, HD))[:8]
    col = iota((8, columns), 1)
    held = sums < EMPTY
    first = jnp.where(held & (mod(col, sender_rows) == 0), 1.0, 0.0).astype(BF16)
    row = over(iota((piece, piece), 0), sender_rows)
    before = jnp.where(row < over(iota((piece, piece), 1), sender_rows), 1.0, 0.0).astype(BF16)
    base = jnp.zeros((8, 1), F32)
    ranks = []
    for p in range(0, columns, piece):
        part = first[:, p : p + piece]
        ranks.append(dot_nn(part, before) + base)
        base = base + jnp.sum(part.astype(F32), axis=1, keepdims=True)
    rank = jnp.concatenate(ranks, axis=1)
    return jnp.where(held & (mod(col, 2) == 0), rank, -1.0)[:1]


def arrival_kernel(
    tp, groups, order, block_rows, got_ref, query_ref, new_ref, done_ref, out_ref, done_hbm, sem
):
    step = pl.program_id(0) if groups > 1 else 0
    hand_on = pltpu.make_async_copy(done_ref, done_hbm, sem)
    if groups > 1:
        pl.when(step == 0)(hand_on.start)
    else:
        hand_on.start()

    chunks, heads, chunk_rows = got_ref.shape[:3]
    slots, _, per_head = query_ref.shape[:3]
    rows = slots * per_head
    columns = chunks * chunk_rows
    every = range(heads)

    caches = [got_ref[:, h].reshape(columns, HD) for h in every]
    queries = [query_ref[:, h].reshape(rows, HD) for h in every]
    new = new_ref[...]
    scores = [dot_nt(queries[h], caches[h]) for h in every]
    new_all = dot_nt(jnp.concatenate(queries, axis=0), new)
    if order is None:
        slot_of = slots_by_matmul(got_ref, tp)
    else:
        slot_of = slots_by_rows(got_ref, tp, order, block_rows)
    first_slot = jnp.float32(step * slots)
    mine = [slot_of == first_slot + a for a in range(slots)]

    new_col = iota((rows, new.shape[0]), 1)
    new_row = iota((rows, new.shape[0]), 0)
    new_here = (
        (mod(new_col, 2) == 0)
        & (over(new_col, 2 * heads * STEPS) == over(new_row, per_head))
        & (mod(over(new_col, 2 * heads), STEPS) <= mod(new_row, STEPS))
    )
    new_head = jnp.where(new_here, mod(over(new_col, 2), heads), heads)

    scores = [
        jnp.concatenate(
            [
                jnp.where(mine[a], scores[h][a * per_head : (a + 1) * per_head] * SCORE_SCALE, NEGATIVE)
                for a in range(slots)
            ],
            axis=0,
        )
        for h in every
    ]
    new_scores = [
        jnp.where(new_head == h, new_all[h * rows : (h + 1) * rows] * SCORE_SCALE, NEGATIVE)
        for h in every
    ]
    top = [top_of(scores[h], new_scores[h]) for h in every]
    weights = [jnp.exp(scores[h] - top[h]) for h in every]
    new_weights = [jnp.exp(new_scores[h] - top[h]) for h in every]
    total = [sum_of(weights[h], new_weights[h]) for h in every]
    new_mixed = dot_nn(jnp.concatenate(new_weights, axis=0).astype(BF16), values_up(new))
    for h in every:
        mixed = dot_nn(to_values(weights[h]), caches[h]) + new_mixed[h * rows : (h + 1) * rows]
        out_ref[:, h] = (mixed * (1.0 / total[h])).astype(BF16).reshape(slots, per_head, HD)
    if groups > 1:
        pl.when(step == groups - 1)(hand_on.wait)
    else:
        hand_on.wait()


def whole(memory_space=pltpu.VMEM):
    return pl.BlockSpec(memory_space=memory_space)


def in_hbm(x):
    return pltpu.with_memory_space_constraint(x, pltpu.HBM)


def limit(mib):
    return pltpu.CompilerParams(vmem_limit_bytes=mib * 2**20)


def pack(pre_codes, pre_scales, req_dest, req_blocks, peers, tp, order):
    requests, blocks, block_tokens = pre_codes.shape[:3]
    tokens = blocks * block_tokens
    codes = (
        pre_codes.reshape(requests, tokens, 2, KVH, HD)
        .transpose(0, 1, 3, 2, 4)
        .reshape(requests, tokens * KVH * 2, HD)
    )
    scales = pre_scales.reshape(requests, tokens * 2, KVH)
    ins = [req_dest, req_blocks, codes, scales]
    return pl.pallas_call(
        functools.partial(pack_kernel, tp, order, KVH, 2 * block_tokens),
        out_shape=pltpu.VMEM((peers * tp, KVH // tp, tokens * 2, HD), BF16),
        in_specs=[whole(pltpu.HBM)] * len(ins),
        out_specs=whole(),
        scratch_shapes=[
            pltpu.SMEM(req_dest.shape, jnp.int32),
            pltpu.SMEM(req_blocks.shape, jnp.int32),
            pltpu.VMEM(codes.shape, BF16),
            pltpu.VMEM(scales.shape, BF16),
            pltpu.SemaphoreType.DMA((5,)),
        ],
        compiler_params=limit(16),
        name="pack",
    )(*[in_hbm(x) for x in ins])


def cache_rows(codes):
    slots, tokens, _, width = codes.shape
    heads = width // HD
    return (
        codes.reshape(slots, tokens, 2, heads, HD)
        .transpose(0, 1, 3, 2, 4)
        .reshape(slots, tokens * heads * 2, HD)
    )


def query_rows(query):
    slots, steps, width = query.shape
    return query.reshape(slots, steps, width // HD, HD).transpose(0, 2, 1, 3)


def new_rows_of(new):
    slots, steps, pair, width = new.shape
    heads = width // HD
    return (
        new.reshape(slots, steps, pair, heads, HD)
        .transpose(0, 1, 3, 2, 4)
        .reshape(slots * steps * heads * pair, HD)
    )


def from_rows(out, shape):
    slots, steps, width = shape
    return out.reshape(slots, width // HD, steps, HD).transpose(0, 2, 1, 3).reshape(shape)


def resident(codes, res_scales, res_len, res_query, res_new):
    slots, rows = codes.shape[:2]
    heads = res_scales.shape[-1]
    scales = res_scales.transpose(0, 2, 3, 1)
    query = query_rows(res_query).reshape(slots, heads * GROUP * STEPS, HD)
    work = query.shape[0] * query.shape[1] * rows
    return pl.pallas_call(
        resident_kernel,
        out_shape=pltpu.VMEM(query.shape, BF16),
        in_specs=[whole(pltpu.SMEM), whole(pltpu.HBM)] + [whole()] * 3,
        out_specs=whole(),
        scratch_shapes=[pltpu.VMEM(codes.shape, BF16), pltpu.SemaphoreType.DMA],
        cost_estimate=pl.CostEstimate(
            flops=4 * work * HD,
            bytes_accessed=2 * (codes.size + 2 * query.size),
            transcendentals=work,
        ),
        compiler_params=limit(16),
        name="resident",
    )(in_hbm(res_len), in_hbm(codes), scales, query, new_rows_of(res_new))


def arrivals(got, arr_query, arr_new, done, tp, order, block_rows):
    slots, steps, width = arr_query.shape
    heads = width // (HD * GROUP)
    query = query_rows(arr_query).reshape(slots, heads, GROUP * steps, HD)
    new = new_rows_of(arr_new)
    size = max(n for n in range(1, 7) if slots % n == 0)
    groups = slots // size
    small = got.size <= 2**18

    def part(ref, rows):
        if groups == 1:
            return whole()
        return pl.BlockSpec((rows,) + ref.shape[1:], lambda i: (i,) + (0,) * (ref.ndim - 1))

    return pl.pallas_call(
        functools.partial(arrival_kernel, tp, groups, order, block_rows),
        out_shape=[
            jax.ShapeDtypeStruct(query.shape, BF16),
            jax.ShapeDtypeStruct(done.shape, BF16),
        ],
        grid=(groups,) if groups > 1 else (),
        in_specs=[
            whole(),
            part(query, size),
            part(new, new.shape[0] // groups),
            whole(),
        ],
        out_specs=[part(query, size), whole(pltpu.HBM)],
        scratch_shapes=[pltpu.SemaphoreType.DMA],
        compiler_params=limit(16 if small else 48),
        name="arrivals",
    )(got, query, new, done)


def shards(
    pre_codes,
    pre_scales,
    req_dest,
    req_blocks,
    res_codes,
    res_scales,
    res_len,
    res_query,
    res_new,
    arr_query,
    arr_new,
):
    peers = lax.axis_size("wide")
    tp = lax.axis_size("tp")
    order = None
    if peers * tp == 16:
        order = [11, 10, 15, 14, 3, 2, 1, 0, 5, 4, 9, 8, 13, 12, 7, 6]
    send = pack(pre_codes, pre_scales, req_dest, req_blocks, peers, tp, order)
    got = lax.all_to_all(
        send,
        ("wide", "tp"),
        split_axis=0,
        concat_axis=0,
        tiled=True,
        axis_index_groups=[order or list(range(peers * tp))],
    )
    done = resident(cache_rows(res_codes), res_scales, res_len, res_query, res_new)
    block_rows = 2 * pre_codes.shape[2]
    arr_out, res_out = arrivals(got, arr_query, arr_new, done, tp, order, block_rows)
    return (from_rows(res_out, res_query.shape), from_rows(arr_out, arr_query.shape))


def solution(mesh):
    in_specs = (
        P(("groups", "wide"), None, "tp", None, None),
        P(("groups", "wide"), None, "tp", None, None),
        P(("groups", "wide")),
        P(("groups", "wide")),
        P(("groups", "wide"), None, None, "tp"),
        P(("groups", "wide"), None, None, "tp"),
        P(("groups", "wide")),
        P(("groups", "wide"), None, "tp"),
        P(("groups", "wide"), None, None, "tp"),
        P(("groups", "wide"), None, "tp"),
        P(("groups", "wide"), None, None, "tp"),
    )
    out_specs = (P(("groups", "wide"), None, "tp"), P(("groups", "wide"), None, "tp"))
    return jax.shard_map(shards, mesh=mesh, in_specs=in_specs, out_specs=out_specs, check_vma=False)
```

```python
import functools
import math

import jax
import jax.numpy as jnp
from jax import lax
from jax.experimental import pallas as pl
from jax.experimental.pallas import tpu as pltpu
from jax.sharding import PartitionSpec as P

KVH = 4
HD = 128
HQ = 64
GROUP = HQ // KVH
STEPS = 2

NEGATIVE = -1e30
EMPTY = 1024.0
SCORE_SCALE = 1.0 / math.sqrt(HD)

BF16 = jnp.bfloat16
F32 = jnp.float32


def iota(shape, axis):
    return lax.broadcasted_iota(jnp.int32, shape, axis)


def over(x, n):
    return jnp.right_shift(x, n.bit_length() - 1) if n & (n - 1) == 0 else x // n


def mod(x, n):
    return jnp.bitwise_and(x, n - 1) if n & (n - 1) == 0 else x % n


def dot_nt(a, b):
    return lax.dot_general(a, b, (((1,), (1,)), ((), ())), preferred_element_type=F32)


def dot_nn(a, b):
    return lax.dot_general(a, b, (((1,), (0,)), ((), ())), preferred_element_type=F32)


def dot_tn(a, b):
    return lax.dot_general(a, b, (((0,), (0,)), ((), ())), preferred_element_type=F32)


def top_of(*parts):
    return functools.reduce(jnp.maximum, [jnp.max(p, axis=1, keepdims=True) for p in parts])


def sum_of(*parts):
    return functools.reduce(jnp.add, [jnp.sum(p, axis=1, keepdims=True) for p in parts])


def to_values(weights):
    tiles = [pltpu.roll(weights[:, c : c + HD], 1, 1) for c in range(0, weights.shape[1], HD)]
    return jnp.concatenate(tiles, axis=1).astype(BF16)


def values_up(rows):
    return pltpu.roll(rows.astype(F32), rows.shape[0] - 1, 0).astype(BF16)


def pack_kernel(
    tp, order, heads, block_rows, dest_hbm, blocks_hbm, codes_hbm, scales_hbm, send_ref,
    dest_ref, blocks_ref, codes_ref, scales_ref, sems,
):
    requests, all_rows = codes_ref.shape[:2]
    pairs = [
        (codes_hbm.at[: requests // 2], codes_ref.at[: requests // 2]),
        (codes_hbm.at[requests // 2 :], codes_ref.at[requests // 2 :]),
        (scales_hbm, scales_ref), (dest_hbm, dest_ref), (blocks_hbm, blocks_ref),
    ]
    copies = [pltpu.make_async_copy(a, b, sems.at[i]) for i, (a, b) in enumerate(pairs)]
    for copy in copies:
        copy.start()
    rows = all_rows // heads
    per_core = heads // tp
    send_ref[...] = jnp.full(send_ref.shape, EMPTY, BF16)
    row_block = over(iota((rows, HD), 0), block_rows)
    to_row = iota((all_rows, all_rows), 0)
    from_row = iota((all_rows, all_rows), 1)
    source = over(mod(to_row, rows), 2) * (2 * heads) + over(to_row, rows) * 2 + mod(to_row, 2)
    by_head = jnp.where(from_row == source, 1.0, 0.0).astype(BF16)
    for copy in copies:
        copy.wait()

    def place(r):
        there = dest_ref[r]
        spots = [there * tp + t for t in range(tp)]
        if order is not None:
            for t in range(tp):
                at = {core // tp: p for p, core in enumerate(order) if core % tp == t}
                spots[t] = functools.reduce(
                    jnp.add, [jnp.where(there == w, p, 0) for w, p in at.items()]
                )
        held = row_block < blocks_ref[r]
        codes = dot_nn(by_head, codes_ref[r])
        scales = scales_ref[r].astype(F32)
        for j in range(heads):
            values = codes[j * rows : (j + 1) * rows] * scales[:, j : j + 1]
            values = jnp.where(held, values, EMPTY).astype(BF16)
            send_ref[spots[j // per_core], j % per_core] = values

    if requests <= 8:
        for r in range(requests):
            place(r)
    else:
        lax.fori_loop(0, requests, lambda r, c: (place(r), c)[1], 0)


def turn_queries(query_ref, new_ref, turned_ref, scores_ref, values_ref):
    slots, heads, per_head = query_ref.shape[:3]
    rows = slots * per_head
    new = new_ref[...]
    values_ref[...] = values_up(new)
    shape = scores_ref.shape[1:]
    row = iota(shape, 0)
    col = iota(shape, 1)
    ok = (
        (mod(row, 2) == 0)
        & (over(row, 2 * heads * STEPS) == over(col, per_head))
        & (mod(over(row, 2 * heads), STEPS) <= mod(col, STEPS))
    )
    for h in range(heads):
        query = query_ref[:, h].reshape(rows, HD)
        if shape[1] > rows:
            query = jnp.concatenate([query, jnp.zeros((shape[1] - rows, HD), BF16)], axis=0)
        turned_ref[h] = query.astype(F32).T.astype(BF16)
        scores = dot_nt(new, query) * SCORE_SCALE
        scores_ref[h] = jnp.where(ok & (mod(over(row, 2), heads) == h), scores, NEGATIVE)


def resident_kernel(len_ref, codes_hbm, scales_ref, query_ref, new_ref, *refs):
    *refs, codes_ref, sem = refs
    fetch = pltpu.make_async_copy(codes_hbm, codes_ref, sem)
    fetch.start()
    out_ref = refs[0]
    if len(refs) > 1:
        arr_query_ref, arr_new_ref, out_ref, *turned_refs = refs
        turn_queries(arr_query_ref, arr_new_ref, *turned_refs)
    slots, rows = codes_ref.shape[:2]
    heads = scales_ref.shape[2]
    tokens = rows // (2 * heads)
    queries = query_ref.shape[1]
    new_rows = new_ref.shape[0]

    row = iota((rows, HD), 0)
    source = (mod(row, 2) * heads + mod(over(row, 2), heads)) * tokens + over(row, 2 * heads)
    lane = iota((rows, HD), 1)
    spread = jnp.concatenate(
        [jnp.where(source == lane + c, 1.0, 0.0).astype(BF16) for c in range(0, rows, HD)],
        axis=1,
    )
    flat = jnp.concatenate(
        [scales_ref[:, p, h] for p in range(2) for h in range(heads)], axis=1
    )
    columns = dot_nt(spread, flat).astype(BF16)

    col = iota((queries, rows), 1)
    row_head = over(iota((queries, rows), 0), queries // heads)
    is_key = (mod(col, 2) == 0) & (mod(over(col, 2), heads) == row_head)
    col_token = jnp.where(is_key, over(col, 2 * heads), tokens)

    new_col = iota((queries, new_rows), 1)
    new_row = iota((queries, new_rows), 0)
    new_ok = (
        (mod(new_col, 2) == 0)
        & (mod(over(new_col, 2), heads) == over(new_row, queries // heads))
        & (mod(over(new_col, 2 * heads), STEPS) <= mod(new_row, STEPS))
    )
    new_slot = jnp.where(new_ok, over(new_col, 2 * heads * STEPS), slots)

    every = range(slots)
    new = new_ref[...]
    new_all = dot_nt(query_ref[...].reshape(slots * queries, HD), new)
    fetch.wait()
    caches = [codes_ref[s] * columns[:, s : s + 1] for s in every]
    scores = [dot_nt(query_ref[s], caches[s]) for s in every]
    scores = [jnp.where(col_token < len_ref[s], scores[s] * SCORE_SCALE, NEGATIVE) for s in every]
    new_scores = [
        jnp.where(new_slot == s, new_all[s * queries : (s + 1) * queries] * SCORE_SCALE, NEGATIVE)
        for s in every
    ]
    top = [top_of(scores[s], new_scores[s]) for s in every]
    weights = [jnp.exp(scores[s] - top[s]) for s in every]
    new_weights = [jnp.exp(new_scores[s] - top[s]) for s in every]
    total = [sum_of(weights[s], new_weights[s]) for s in every]
    new_mixed = dot_nn(jnp.concatenate(new_weights, axis=0).astype(BF16), values_up(new))
    mixed = [
        dot_nn(to_values(weights[s]), caches[s]) + new_mixed[s * queries : (s + 1) * queries]
        for s in every
    ]
    for s in every:
        out_ref[s] = (mixed[s] * (1.0 / total[s])).astype(BF16)


def slots_by_matmul(got_ref, tp):
    chunks, _, chunk_rows = got_ref.shape[:3]
    columns = chunks * chunk_rows
    sender_rows = tp * chunk_rows
    piece = min(columns, 256)
    sums = dot_nt(jnp.ones((16, HD), BF16), got_ref[:, 0].reshape(columns, HD))[:8]
    col = iota((8, columns), 1)
    held = sums < EMPTY
    first = jnp.where(held & (mod(col, sender_rows) == 0), 1.0, 0.0).astype(BF16)
    row = over(iota((piece, piece), 0), sender_rows)
    before = jnp.where(row < over(iota((piece, piece), 1), sender_rows), 1.0, 0.0).astype(BF16)
    base = jnp.zeros((8, 1), F32)
    ranks = []
    for p in range(0, columns, piece):
        part = first[:, p : p + piece]
        ranks.append(dot_nn(part, before) + base)
        base = base + jnp.sum(part.astype(F32), axis=1, keepdims=True)
    rank = jnp.concatenate(ranks, axis=1)
    return jnp.where(held & (mod(col, 2) == 0), rank, -1.0)[:1]


def turned_kernel(
    tp, order, got_ref, turned_ref, new_scores_ref, new_values_ref, done_ref, out_ref, done_hbm, sem
):
    hand_on = pltpu.make_async_copy(done_ref, done_hbm, sem)
    hand_on.start()
    chunks, heads, chunk_rows = got_ref.shape[:3]
    slots, _, per_head = out_ref.shape[:3]
    columns = turned_ref.shape[2]
    rows = chunks * chunk_rows
    arrived = [got_ref[:, h].reshape(rows, HD) for h in range(heads)]
    scores = [dot_nn(arrived[h], turned_ref[h]) for h in range(heads)]

    plain = arrived[0].astype(F32)
    firsts = [plain[k * chunk_rows : k * chunk_rows + 1] for k in range(chunks)]
    here = {
        core // tp: jnp.where(first < EMPTY, 1.0, 0.0)
        for core, first in zip(order, firsts)
        if core % tp == 0
    }
    ranks = {w: sum([here[v] for v in here if v < w], jnp.zeros((1, HD), F32)) for w in here}
    rank = jnp.concatenate(
        [jnp.broadcast_to(ranks[core // tp], (chunk_rows, HD)) for core in order], axis=0
    )
    key = (plain < EMPTY) & (mod(iota((rows, HD), 0), 2) == 0)
    slot_of = jnp.where(key, rank, -1.0)
    mine = [
        slot_of == over(iota((1, HD), 1) + c, per_head).astype(F32) for c in range(0, columns, HD)
    ]
    for h in range(heads):
        score = jnp.concatenate(
            [
                jnp.where(mine[i], scores[h][:, c : c + HD] * SCORE_SCALE, NEGATIVE)
                for i, c in enumerate(range(0, columns, HD))
            ],
            axis=1,
        )
        new_score = new_scores_ref[h]
        top = jnp.maximum(
            jnp.max(score, axis=0, keepdims=True), jnp.max(new_score, axis=0, keepdims=True)
        )
        weights = jnp.exp(score - top)
        new_weights = jnp.exp(new_score - top)
        total = jnp.sum(weights, axis=0, keepdims=True) + jnp.sum(
            new_weights, axis=0, keepdims=True
        )
        mixed = dot_tn(values_up(arrived[h]), weights.astype(BF16))
        mixed = mixed + dot_tn(new_values_ref[...], new_weights.astype(BF16))
        out = (mixed * (1.0 / total)).T[: slots * per_head]
        out_ref[:, h] = out.astype(BF16).reshape(slots, per_head, HD)
    hand_on.wait()


def arrival_kernel(
    tp, groups, got_ref, query_ref, new_ref, done_ref, out_ref, done_hbm, sem
):
    step = pl.program_id(0) if groups > 1 else 0
    hand_on = pltpu.make_async_copy(done_ref, done_hbm, sem)
    if groups > 1:
        pl.when(step == 0)(hand_on.start)
    else:
        hand_on.start()

    chunks, heads, chunk_rows = got_ref.shape[:3]
    slots, _, per_head = query_ref.shape[:3]
    rows = slots * per_head
    columns = chunks * chunk_rows
    every = range(heads)

    caches = [got_ref[:, h].reshape(columns, HD) for h in every]
    queries = [query_ref[:, h].reshape(rows, HD) for h in every]
    new = new_ref[...]
    scores = [dot_nt(queries[h], caches[h]) for h in every]
    new_all = dot_nt(jnp.concatenate(queries, axis=0), new)
    slot_of = slots_by_matmul(got_ref, tp)
    first_slot = jnp.float32(step * slots)
    mine = [slot_of == first_slot + a for a in range(slots)]

    new_col = iota((rows, new.shape[0]), 1)
    new_row = iota((rows, new.shape[0]), 0)
    new_here = (
        (mod(new_col, 2) == 0)
        & (over(new_col, 2 * heads * STEPS) == over(new_row, per_head))
        & (mod(over(new_col, 2 * heads), STEPS) <= mod(new_row, STEPS))
    )
    new_head = jnp.where(new_here, mod(over(new_col, 2), heads), heads)

    scores = [
        jnp.concatenate(
            [
                jnp.where(mine[a], scores[h][a * per_head : (a + 1) * per_head] * SCORE_SCALE, NEGATIVE)
                for a in range(slots)
            ],
            axis=0,
        )
        for h in every
    ]
    new_scores = [
        jnp.where(new_head == h, new_all[h * rows : (h + 1) * rows] * SCORE_SCALE, NEGATIVE)
        for h in every
    ]
    top = [top_of(scores[h], new_scores[h]) for h in every]
    weights = [jnp.exp(scores[h] - top[h]) for h in every]
    new_weights = [jnp.exp(new_scores[h] - top[h]) for h in every]
    total = [sum_of(weights[h], new_weights[h]) for h in every]
    new_mixed = dot_nn(jnp.concatenate(new_weights, axis=0).astype(BF16), values_up(new))
    for h in every:
        mixed = dot_nn(to_values(weights[h]), caches[h]) + new_mixed[h * rows : (h + 1) * rows]
        out_ref[:, h] = (mixed * (1.0 / total[h])).astype(BF16).reshape(slots, per_head, HD)
    if groups > 1:
        pl.when(step == groups - 1)(hand_on.wait)
    else:
        hand_on.wait()


def whole(memory_space=pltpu.VMEM):
    return pl.BlockSpec(memory_space=memory_space)


def in_hbm(x):
    return pltpu.with_memory_space_constraint(x, pltpu.HBM)


def limit(mib):
    return pltpu.CompilerParams(vmem_limit_bytes=mib * 2**20)


def pack(pre_codes, pre_scales, req_dest, req_blocks, peers, tp, order):
    requests, blocks, block_tokens = pre_codes.shape[:3]
    tokens = blocks * block_tokens
    codes = (
        pre_codes.reshape(requests, tokens, 2, KVH, HD)
        .transpose(0, 1, 3, 2, 4)
        .reshape(requests, tokens * KVH * 2, HD)
    )
    scales = pre_scales.reshape(requests, tokens * 2, KVH)
    ins = [req_dest, req_blocks, codes, scales]
    return pl.pallas_call(
        functools.partial(pack_kernel, tp, order, KVH, 2 * block_tokens),
        out_shape=pltpu.VMEM((peers * tp, KVH // tp, tokens * 2, HD), BF16),
        in_specs=[whole(pltpu.HBM)] * len(ins),
        out_specs=whole(),
        scratch_shapes=[
            pltpu.SMEM(req_dest.shape, jnp.int32),
            pltpu.SMEM(req_blocks.shape, jnp.int32),
            pltpu.VMEM(codes.shape, BF16),
            pltpu.VMEM(scales.shape, BF16),
            pltpu.SemaphoreType.DMA((5,)),
        ],
        compiler_params=limit(16),
        name="pack",
    )(*[in_hbm(x) for x in ins])


def cache_rows(codes):
    slots, tokens, _, width = codes.shape
    heads = width // HD
    return (
        codes.reshape(slots, tokens, 2, heads, HD)
        .transpose(0, 1, 3, 2, 4)
        .reshape(slots, tokens * heads * 2, HD)
    )


def query_rows(query):
    slots, steps, width = query.shape
    return query.reshape(slots, steps, width // HD, HD).transpose(0, 2, 1, 3)


def new_rows_of(new):
    slots, steps, pair, width = new.shape
    heads = width // HD
    return (
        new.reshape(slots, steps, pair, heads, HD)
        .transpose(0, 1, 3, 2, 4)
        .reshape(slots * steps * heads * pair, HD)
    )


def from_rows(out, shape):
    slots, steps, width = shape
    return out.reshape(slots, width // HD, steps, HD).transpose(0, 2, 1, 3).reshape(shape)


def resident(codes, res_scales, res_len, res_query, res_new, arr_query, arr_new, turn):
    slots, rows = codes.shape[:2]
    heads = res_scales.shape[-1]
    scales = res_scales.transpose(0, 2, 3, 1)
    query = query_rows(res_query).reshape(slots, heads * GROUP * STEPS, HD)
    ins = [in_hbm(res_len), in_hbm(codes), scales, query, new_rows_of(res_new)]
    outs = [pltpu.VMEM(query.shape, BF16)]
    if turn:
        arr_rows = query_rows(arr_query).reshape(-1, heads, GROUP * STEPS, HD)
        arr_new = new_rows_of(arr_new)
        columns = pl.cdiv(arr_rows.shape[0] * GROUP * STEPS, HD) * HD
        ins += [arr_rows, arr_new]
        outs += [
            pltpu.VMEM((heads, HD, columns), BF16),
            pltpu.VMEM((heads, arr_new.shape[0], columns), F32),
            pltpu.VMEM(arr_new.shape, BF16),
        ]
    work = query.shape[0] * query.shape[1] * rows
    return pl.pallas_call(
        resident_kernel,
        out_shape=outs,
        in_specs=[whole(pltpu.SMEM), whole(pltpu.HBM)] + [whole()] * (len(ins) - 2),
        out_specs=[whole()] * len(outs),
        scratch_shapes=[pltpu.VMEM(codes.shape, BF16), pltpu.SemaphoreType.DMA],
        cost_estimate=pl.CostEstimate(
            flops=4 * work * HD,
            bytes_accessed=2 * (codes.size + 2 * query.size),
            transcendentals=work,
        ),
        compiler_params=limit(24),
        name="resident",
    )(*ins)


def turned(got, prepared, done, shape, tp, order):
    return pl.pallas_call(
        functools.partial(turned_kernel, tp, order),
        out_shape=[jax.ShapeDtypeStruct(shape, BF16), jax.ShapeDtypeStruct(done.shape, BF16)],
        in_specs=[whole()] * (2 + len(prepared)),
        out_specs=[whole(), whole(pltpu.HBM)],
        scratch_shapes=[pltpu.SemaphoreType.DMA],
        compiler_params=limit(16),
        name="arrivals",
    )(got, *prepared, done)


def arrivals(got, arr_query, arr_new, done, tp):
    slots, steps, width = arr_query.shape
    heads = width // (HD * GROUP)
    query = query_rows(arr_query).reshape(slots, heads, GROUP * steps, HD)
    new = new_rows_of(arr_new)
    size = max(n for n in range(1, 7) if slots % n == 0)
    groups = slots // size
    small = got.size <= 2**18

    def part(ref, rows):
        if groups == 1:
            return whole()
        return pl.BlockSpec((rows,) + ref.shape[1:], lambda i: (i,) + (0,) * (ref.ndim - 1))

    return pl.pallas_call(
        functools.partial(arrival_kernel, tp, groups),
        out_shape=[
            jax.ShapeDtypeStruct(query.shape, BF16),
            jax.ShapeDtypeStruct(done.shape, BF16),
        ],
        grid=(groups,) if groups > 1 else (),
        in_specs=[
            whole(),
            part(query, size),
            part(new, new.shape[0] // groups),
            whole(),
        ],
        out_specs=[part(query, size), whole(pltpu.HBM)],
        scratch_shapes=[pltpu.SemaphoreType.DMA],
        compiler_params=limit(16 if small else 48),
        name="arrivals",
    )(got, query, new, done)


def shards(
    pre_codes,
    pre_scales,
    req_dest,
    req_blocks,
    res_codes,
    res_scales,
    res_len,
    res_query,
    res_new,
    arr_query,
    arr_new,
):
    peers = lax.axis_size("wide")
    tp = lax.axis_size("tp")
    order = None
    if peers * tp == 16:
        order = [11, 10, 13, 12, 15, 14, 3, 2, 1, 0, 5, 4, 7, 6, 9, 8]
    send = pack(pre_codes, pre_scales, req_dest, req_blocks, peers, tp, order)
    got = lax.all_to_all(
        send,
        ("wide", "tp"),
        split_axis=0,
        concat_axis=0,
        tiled=True,
        axis_index_groups=[order or list(range(peers * tp))],
    )
    done, *prepared = resident(
        cache_rows(res_codes), res_scales, res_len, res_query, res_new, arr_query, arr_new,
        order is not None,
    )
    if order is None:
        arr_out, res_out = arrivals(got, arr_query, arr_new, done, tp)
    else:
        shape = (arr_query.shape[0], KVH // tp, GROUP * STEPS, HD)
        arr_out, res_out = turned(got, prepared, done, shape, tp, order)
    return (from_rows(res_out, res_query.shape), from_rows(arr_out, arr_query.shape))


def solution(mesh):
    in_specs = (
        P(("groups", "wide"), None, "tp", None, None),
        P(("groups", "wide"), None, "tp", None, None),
        P(("groups", "wide")),
        P(("groups", "wide")),
        P(("groups", "wide"), None, None, "tp"),
        P(("groups", "wide"), None, None, "tp"),
        P(("groups", "wide")),
        P(("groups", "wide"), None, "tp"),
        P(("groups", "wide"), None, None, "tp"),
        P(("groups", "wide"), None, "tp"),
        P(("groups", "wide"), None, None, "tp"),
    )
    out_specs = (P(("groups", "wide"), None, "tp"), P(("groups", "wide"), None, "tp"))
    return jax.shard_map(shards, mesh=mesh, in_specs=in_specs, out_specs=out_specs, check_vma=False)
```

```python
import functools
import math

import jax
import jax.numpy as jnp
from jax import lax
from jax.experimental import pallas as pl
from jax.experimental.pallas import tpu as pltpu
from jax.sharding import PartitionSpec as P

KVH = 4
HD = 128
HQ = 64
GROUP = HQ // KVH
STEPS = 2

NEGATIVE = -1e30
EMPTY = 1024.0
SCORE_SCALE = 1.0 / math.sqrt(HD)

BF16 = jnp.bfloat16
F32 = jnp.float32


def iota(shape, axis):
    return lax.broadcasted_iota(jnp.int32, shape, axis)


def over(x, n):
    return jnp.right_shift(x, n.bit_length() - 1) if n & (n - 1) == 0 else x // n


def mod(x, n):
    return jnp.bitwise_and(x, n - 1) if n & (n - 1) == 0 else x % n


def dot_nt(a, b):
    return lax.dot_general(a, b, (((1,), (1,)), ((), ())), preferred_element_type=F32)


def dot_nn(a, b):
    return lax.dot_general(a, b, (((1,), (0,)), ((), ())), preferred_element_type=F32)


def top_of(*parts):
    return functools.reduce(jnp.maximum, [jnp.max(p, axis=1, keepdims=True) for p in parts])


def sum_of(*parts):
    return functools.reduce(jnp.add, [jnp.sum(p, axis=1, keepdims=True) for p in parts])


def to_values(weights):
    tiles = [pltpu.roll(weights[:, c : c + HD], 1, 1) for c in range(0, weights.shape[1], HD)]
    return jnp.concatenate(tiles, axis=1).astype(BF16)


def values_up(rows):
    return pltpu.roll(rows.astype(F32), rows.shape[0] - 1, 0).astype(BF16)


def pack_kernel(
    tp, chips, heads, block_rows, dest_hbm, blocks_hbm, codes_hbm, scales_hbm, send_hbm,
    dest_ref, blocks_ref, codes_ref, scales_ref, empty_ref, values_ref, sems, out_sems,
):
    requests, all_rows = codes_ref.shape[:2]
    pairs = [
        (codes_hbm, codes_ref), (scales_hbm, scales_ref),
        (dest_hbm, dest_ref), (blocks_hbm, blocks_ref), (empty_ref, send_hbm),
    ]
    copies = [pltpu.make_async_copy(a, b, sems.at[i]) for i, (a, b) in enumerate(pairs)]
    for copy in copies[:-1]:
        copy.start()
    empty_ref[...] = jnp.full(empty_ref.shape, EMPTY, BF16)
    copies[-1].start()
    rows = all_rows // heads
    per_core = heads // tp
    row_block = over(iota((rows, HD), 0), block_rows)
    to_row = iota((all_rows, all_rows), 0)
    from_row = iota((all_rows, all_rows), 1)
    source = over(mod(to_row, rows), 2) * (2 * heads) + over(to_row, rows) * 2 + mod(to_row, 2)
    by_head = jnp.where(from_row == source, 1.0, 0.0).astype(BF16)
    for copy in copies:
        copy.wait()

    def hand_out(r):
        there = dest_ref[r]
        if chips is not None:
            there = functools.reduce(
                jnp.add, [jnp.where(there == w, p, 0) for p, w in enumerate(chips)]
            )
        target = send_hbm.at[pl.ds(there * tp, tp)]
        return pltpu.make_async_copy(values_ref.at[r], target, out_sems.at[r])

    def place(r):
        held = row_block < blocks_ref[r]
        codes = dot_nn(by_head, codes_ref[r])
        scales = scales_ref[r].astype(F32)
        for j in range(heads):
            values = codes[j * rows : (j + 1) * rows] * scales[:, j : j + 1]
            values = jnp.where(held, values, EMPTY).astype(BF16)
            values_ref[r, tp - 1 - j // per_core, j % per_core] = values

    if requests <= 8:
        for r in range(requests):
            place(r)
        outs = [hand_out(r) for r in range(requests)]
        for out in outs:
            out.start()
        for out in outs:
            out.wait()
    else:
        pl.loop(0, requests)(place)
        pl.loop(0, requests)(lambda r: hand_out(r).start())
        pl.loop(0, requests)(lambda r: hand_out(r).wait())


def resident_kernel(
    len_hbm, codes_hbm, scales_hbm, query_hbm, new_hbm, out_ref,
    len_ref, codes_ref, scales_ref, query_ref, new_ref, sems,
):
    pairs = [
        (query_hbm, query_ref), (new_hbm, new_ref), (scales_hbm, scales_ref),
        (len_hbm, len_ref), (codes_hbm, codes_ref),
    ]
    copies = [pltpu.make_async_copy(a, b, sems.at[i]) for i, (a, b) in enumerate(pairs)]
    for copy in copies:
        copy.start()
    slots, rows = codes_ref.shape[:2]
    heads = scales_ref.shape[2]
    tokens = rows // (2 * heads)
    queries = query_ref.shape[1]
    new_rows = new_ref.shape[0]

    row = iota((rows, HD), 0)
    source = (mod(row, 2) * heads + mod(over(row, 2), heads)) * tokens + over(row, 2 * heads)
    lane = iota((rows, HD), 1)
    spread = jnp.concatenate(
        [jnp.where(source == lane + c, 1.0, 0.0).astype(BF16) for c in range(0, rows, HD)],
        axis=1,
    )
    for copy in copies[:-1]:
        copy.wait()
    flat = jnp.concatenate(
        [scales_ref[:, p, h] for p in range(2) for h in range(heads)], axis=1
    )
    columns = dot_nt(spread, flat).astype(BF16)

    col = iota((queries, rows), 1)
    row_head = over(iota((queries, rows), 0), queries // heads)
    is_key = (mod(col, 2) == 0) & (mod(over(col, 2), heads) == row_head)
    col_token = jnp.where(is_key, over(col, 2 * heads), tokens)

    new_col = iota((queries, new_rows), 1)
    new_row = iota((queries, new_rows), 0)
    new_ok = (
        (mod(new_col, 2) == 0)
        & (mod(over(new_col, 2), heads) == over(new_row, queries // heads))
        & (mod(over(new_col, 2 * heads), STEPS) <= mod(new_row, STEPS))
    )
    new_slot = jnp.where(new_ok, over(new_col, 2 * heads * STEPS), slots)

    every = range(slots)
    new = new_ref[...]
    new_all = dot_nt(query_ref[...].reshape(slots * queries, HD), new)
    copies[-1].wait()
    caches = [codes_ref[s] * columns[:, s : s + 1] for s in every]
    scores = [dot_nt(query_ref[s], caches[s]) for s in every]
    scores = [jnp.where(col_token < len_ref[s], scores[s] * SCORE_SCALE, NEGATIVE) for s in every]
    new_scores = [
        jnp.where(new_slot == s, new_all[s * queries : (s + 1) * queries] * SCORE_SCALE, NEGATIVE)
        for s in every
    ]
    top = [top_of(scores[s], new_scores[s]) for s in every]
    weights = [jnp.exp(scores[s] - top[s]) for s in every]
    new_weights = [jnp.exp(new_scores[s] - top[s]) for s in every]
    total = [sum_of(weights[s], new_weights[s]) for s in every]
    new_mixed = dot_nn(jnp.concatenate(new_weights, axis=0).astype(BF16), values_up(new))
    mixed = [
        dot_nn(to_values(weights[s]), caches[s]) + new_mixed[s * queries : (s + 1) * queries]
        for s in every
    ]
    for s in every:
        out_ref[s] = (mixed[s] * (1.0 / total[s])).astype(BF16)


def slots_by_rows(got_ref, tp, order, block_rows):
    chunk_rows = got_ref.shape[2]
    blocks = chunk_rows // block_rows
    rows = [got_ref[k, 0].astype(F32) for k in range(len(order))]
    here = {
        core // tp: jnp.where(x[:1] < EMPTY, 1.0, 0.0)
        for core, x in zip(order, rows)
        if core % tp == 0
    }
    ranks = {
        w: sum([here[v] for v in here if v < w], jnp.zeros((1, HD), F32)) for w in here
    }
    lane = iota((1, HD), 1)
    block = over(lane, block_rows)
    block = jnp.where(mod(lane, 2) == 0, block, -1)
    per_tile = HD // chunk_rows
    tiles = []
    for start in range(0, len(order), per_tile):
        tile = jnp.full((1, HD), -1.0, F32)
        for i in range(per_tile):
            x, rank = rows[start + i], ranks[order[start + i] // tp]
            for b in range(blocks):
                at = b * block_rows
                value = jnp.where(x[at : at + 1] < EMPTY, rank, -1.0)
                tile = jnp.where(block == i * blocks + b, value, tile)
        tiles.append(tile)
    return jnp.concatenate(tiles, axis=1)


def slots_by_matmul(got_ref, tp):
    chunks, _, chunk_rows = got_ref.shape[:3]
    columns = chunks * chunk_rows
    sender_rows = tp * chunk_rows
    piece = min(columns, 256)
    sums = dot_nt(jnp.ones((16, HD), BF16), got_ref[:, 0].reshape(columns, HD))[:8]
    col = iota((8, columns), 1)
    held = sums < EMPTY
    first = jnp.where(held & (mod(col, sender_rows) == 0), 1.0, 0.0).astype(BF16)
    row = over(iota((piece, piece), 0), sender_rows)
    before = jnp.where(row < over(iota((piece, piece), 1), sender_rows), 1.0, 0.0).astype(BF16)
    base = jnp.zeros((8, 1), F32)
    ranks = []
    for p in range(0, columns, piece):
        part = first[:, p : p + piece]
        ranks.append(dot_nn(part, before) + base)
        base = base + jnp.sum(part.astype(F32), axis=1, keepdims=True)
    rank = jnp.concatenate(ranks, axis=1)
    return jnp.where(held & (mod(col, 2) == 0), rank, -1.0)[:1]


def arrival_kernel(
    tp, groups, order, block_rows, got_ref, query_ref, new_ref, out_ref
):
    step = pl.program_id(0) if groups > 1 else 0
    chunks, heads, chunk_rows = got_ref.shape[:3]
    slots, _, per_head = query_ref.shape[:3]
    rows = slots * per_head
    columns = chunks * chunk_rows
    every = range(heads)

    caches = [got_ref[:, h].reshape(columns, HD) for h in every]
    queries = [query_ref[:, h].reshape(rows, HD) for h in every]
    new = new_ref[...]
    scores = [dot_nt(queries[h], caches[h]) for h in every]
    new_all = dot_nt(jnp.concatenate(queries, axis=0), new)
    if order is None:
        slot_of = slots_by_matmul(got_ref, tp)
    else:
        slot_of = slots_by_rows(got_ref, tp, order, block_rows)
    first_slot = jnp.float32(step * slots)
    mine = [slot_of == first_slot + a for a in range(slots)]

    new_col = iota((rows, new.shape[0]), 1)
    new_row = iota((rows, new.shape[0]), 0)
    new_here = (
        (mod(new_col, 2) == 0)
        & (over(new_col, 2 * heads * STEPS) == over(new_row, per_head))
        & (mod(over(new_col, 2 * heads), STEPS) <= mod(new_row, STEPS))
    )
    new_head = jnp.where(new_here, mod(over(new_col, 2), heads), heads)

    scores = [
        jnp.concatenate(
            [
                jnp.where(mine[a], scores[h][a * per_head : (a + 1) * per_head] * SCORE_SCALE, NEGATIVE)
                for a in range(slots)
            ],
            axis=0,
        )
        for h in every
    ]
    new_scores = [
        jnp.where(new_head == h, new_all[h * rows : (h + 1) * rows] * SCORE_SCALE, NEGATIVE)
        for h in every
    ]
    top = [top_of(scores[h], new_scores[h]) for h in every]
    weights = [jnp.exp(scores[h] - top[h]) for h in every]
    new_weights = [jnp.exp(new_scores[h] - top[h]) for h in every]
    total = [sum_of(weights[h], new_weights[h]) for h in every]
    new_mixed = dot_nn(jnp.concatenate(new_weights, axis=0).astype(BF16), values_up(new))
    for h in every:
        mixed = dot_nn(to_values(weights[h]), caches[h]) + new_mixed[h * rows : (h + 1) * rows]
        out_ref[:, h] = (mixed * (1.0 / total[h])).astype(BF16).reshape(slots, per_head, HD)


def whole(memory_space=pltpu.VMEM):
    return pl.BlockSpec(memory_space=memory_space)


def in_hbm(x):
    return pltpu.with_memory_space_constraint(x, pltpu.HBM)


def limit(mib):
    return pltpu.CompilerParams(vmem_limit_bytes=mib * 2**20)


def pack(pre_codes, pre_scales, req_dest, req_blocks, peers, tp, chips):
    requests, blocks, block_tokens = pre_codes.shape[:3]
    tokens = blocks * block_tokens
    codes = (
        pre_codes.reshape(requests, tokens, 2, KVH, HD)
        .transpose(0, 1, 3, 2, 4)
        .reshape(requests, tokens * KVH * 2, HD)
    )
    scales = pre_scales.reshape(requests, tokens * 2, KVH)
    ins = [req_dest, req_blocks, codes, scales]
    chunk = (KVH // tp, tokens * 2, HD)
    return pl.pallas_call(
        functools.partial(pack_kernel, tp, chips, KVH, 2 * block_tokens),
        out_shape=jax.ShapeDtypeStruct((peers * tp,) + chunk, BF16),
        in_specs=[whole(pltpu.HBM)] * len(ins),
        out_specs=whole(pltpu.HBM),
        scratch_shapes=[
            pltpu.SMEM(req_dest.shape, jnp.int32),
            pltpu.SMEM(req_blocks.shape, jnp.int32),
            pltpu.VMEM(codes.shape, BF16),
            pltpu.VMEM(scales.shape, BF16),
            pltpu.VMEM((peers * tp,) + chunk, BF16),
            pltpu.VMEM((requests, tp) + chunk, BF16),
            pltpu.SemaphoreType.DMA((5,)),
            pltpu.SemaphoreType.DMA((requests,)),
        ],
        compiler_params=limit(24),
        name="pack",
    )(*[in_hbm(x) for x in ins])


def cache_rows(codes):
    slots, tokens, _, width = codes.shape
    heads = width // HD
    return (
        codes.reshape(slots, tokens, 2, heads, HD)
        .transpose(0, 1, 3, 2, 4)
        .reshape(slots, tokens * heads * 2, HD)
    )


def query_rows(query):
    slots, steps, width = query.shape
    return query.reshape(slots, steps, width // HD, HD).transpose(0, 2, 1, 3)


def new_rows_of(new):
    slots, steps, pair, width = new.shape
    heads = width // HD
    return (
        new.reshape(slots, steps, pair, heads, HD)
        .transpose(0, 1, 3, 2, 4)
        .reshape(slots * steps * heads * pair, HD)
    )


def from_rows(out, shape):
    slots, steps, width = shape
    return out.reshape(slots, width // HD, steps, HD).transpose(0, 2, 1, 3).reshape(shape)


def resident(codes, res_scales, res_len, res_query, res_new):
    slots, rows = codes.shape[:2]
    heads = res_scales.shape[-1]
    scales = res_scales.transpose(0, 2, 3, 1)
    query = query_rows(res_query).reshape(slots, heads * GROUP * STEPS, HD)
    ins = [res_len, codes, scales, query, new_rows_of(res_new)]
    work = query.shape[0] * query.shape[1] * rows
    return pl.pallas_call(
        resident_kernel,
        out_shape=jax.ShapeDtypeStruct(query.shape, BF16),
        in_specs=[whole(pltpu.HBM)] * len(ins),
        out_specs=whole(),
        scratch_shapes=[
            pltpu.SMEM(res_len.shape, jnp.int32),
            *[pltpu.VMEM(x.shape, BF16) for x in ins[1:]],
            pltpu.SemaphoreType.DMA((len(ins),)),
        ],
        cost_estimate=pl.CostEstimate(
            flops=4 * work * HD,
            bytes_accessed=2 * (codes.size + 2 * query.size),
            transcendentals=work,
        ),
        compiler_params=limit(16),
        name="resident",
    )(*[in_hbm(x) for x in ins])


def arrivals(got, arr_query, arr_new, tp, order, block_rows):
    slots, steps, width = arr_query.shape
    heads = width // (HD * GROUP)
    query = query_rows(arr_query).reshape(slots, heads, GROUP * steps, HD)
    new = new_rows_of(arr_new)
    size = max(n for n in range(1, 7) if slots % n == 0)
    groups = slots // size
    small = got.size <= 2**18

    def part(ref, rows):
        if groups == 1:
            return whole()
        return pl.BlockSpec((rows,) + ref.shape[1:], lambda i: (i,) + (0,) * (ref.ndim - 1))

    return pl.pallas_call(
        functools.partial(arrival_kernel, tp, groups, order, block_rows),
        out_shape=jax.ShapeDtypeStruct(query.shape, BF16),
        grid=(groups,) if groups > 1 else (),
        in_specs=[whole(), part(query, size), part(new, new.shape[0] // groups)],
        out_specs=part(query, size),
        compiler_params=limit(16 if small else 48),
        name="arrivals",
    )(got, query, new)


def shards(
    pre_codes,
    pre_scales,
    req_dest,
    req_blocks,
    res_codes,
    res_scales,
    res_len,
    res_query,
    res_new,
    arr_query,
    arr_new,
):
    peers = lax.axis_size("wide")
    tp = lax.axis_size("tp")
    chips = [5, 6, 7, 1, 0, 2, 3, 4] if peers == 8 else None
    cores = [w * tp + t for w in chips or range(peers) for t in reversed(range(tp))]
    order = chips and cores
    send = pack(pre_codes, pre_scales, req_dest, req_blocks, peers, tp, chips)
    got = lax.all_to_all(
        send,
        ("wide", "tp"),
        split_axis=0,
        concat_axis=0,
        tiled=True,
        axis_index_groups=[cores],
    )
    res_out = resident(cache_rows(res_codes), res_scales, res_len, res_query, res_new)
    block_rows = 2 * pre_codes.shape[2]
    arr_out = arrivals(got, arr_query, arr_new, tp, order, block_rows)
    return (from_rows(res_out, res_query.shape), from_rows(arr_out, arr_query.shape))


def solution(mesh):
    in_specs = (
        P(("groups", "wide"), None, "tp", None, None),
        P(("groups", "wide"), None, "tp", None, None),
        P(("groups", "wide")),
        P(("groups", "wide")),
        P(("groups", "wide"), None, None, "tp"),
        P(("groups", "wide"), None, None, "tp"),
        P(("groups", "wide")),
        P(("groups", "wide"), None, "tp"),
        P(("groups", "wide"), None, None, "tp"),
        P(("groups", "wide"), None, "tp"),
        P(("groups", "wide"), None, None, "tp"),
    )
    out_specs = (P(("groups", "wide"), None, "tp"), P(("groups", "wide"), None, "tp"))
    return jax.shard_map(shards, mesh=mesh, in_specs=in_specs, out_specs=out_specs, check_vma=False)
```

```python
import functools
import math

import jax
import jax.numpy as jnp
from jax import lax
from jax.experimental import pallas as pl
from jax.experimental.pallas import tpu as pltpu
from jax.sharding import PartitionSpec as P

KVH = 4
HD = 128
HQ = 64
GROUP = HQ // KVH
STEPS = 2

NEGATIVE = -1e30
EMPTY = 1024.0
SCORE_SCALE = 1.0 / math.sqrt(HD)

BF16 = jnp.bfloat16
F32 = jnp.float32


def iota(shape, axis):
    return lax.broadcasted_iota(jnp.int32, shape, axis)


def over(x, n):
    return jnp.right_shift(x, n.bit_length() - 1) if n & (n - 1) == 0 else x // n


def mod(x, n):
    return jnp.bitwise_and(x, n - 1) if n & (n - 1) == 0 else x % n


def dot_nt(a, b):
    return lax.dot_general(a, b, (((1,), (1,)), ((), ())), preferred_element_type=F32)


def dot_nn(a, b):
    return lax.dot_general(a, b, (((1,), (0,)), ((), ())), preferred_element_type=F32)


def dot_tn(a, b):
    return lax.dot_general(a, b, (((0,), (0,)), ((), ())), preferred_element_type=F32)


def top_of(*parts):
    return functools.reduce(jnp.maximum, [jnp.max(p, axis=1, keepdims=True) for p in parts])


def sum_of(*parts):
    return functools.reduce(jnp.add, [jnp.sum(p, axis=1, keepdims=True) for p in parts])


def to_values(weights):
    tiles = [pltpu.roll(weights[:, c : c + HD], 1, 1) for c in range(0, weights.shape[1], HD)]
    return jnp.concatenate(tiles, axis=1).astype(BF16)


def values_up(rows):
    return pltpu.roll(rows.astype(F32), rows.shape[0] - 1, 0).astype(BF16)


def pack_kernel(
    tp, chips, heads, block_rows, dest_hbm, blocks_hbm, codes_hbm, scales_hbm, send_ref,
    dest_ref, blocks_ref, codes_ref, scales_ref, sems,
):
    requests, all_rows = codes_ref.shape[:2]
    pairs = [
        (codes_hbm, codes_ref), (scales_hbm, scales_ref),
        (dest_hbm, dest_ref), (blocks_hbm, blocks_ref),
    ]
    copies = [pltpu.make_async_copy(a, b, sems.at[i]) for i, (a, b) in enumerate(pairs)]
    for copy in copies:
        copy.start()
    send_ref[...] = jnp.full(send_ref.shape, EMPTY, BF16)
    rows = all_rows // heads
    per_core = heads // tp
    row_block = over(iota((rows, HD), 0), block_rows)
    to_row = iota((all_rows, all_rows), 0)
    from_row = iota((all_rows, all_rows), 1)
    source = over(mod(to_row, rows), 2) * (2 * heads) + over(to_row, rows) * 2 + mod(to_row, 2)
    by_head = jnp.where(from_row == source, 1.0, 0.0).astype(BF16)
    for copy in copies:
        copy.wait()

    def place(r):
        there = dest_ref[r]
        if chips is not None:
            there = functools.reduce(
                jnp.add, [jnp.where(there == w, p, 0) for p, w in enumerate(chips)]
            )
        last = there * tp + tp - 1
        held = row_block < blocks_ref[r]
        codes = dot_nn(by_head, codes_ref[r])
        scales = scales_ref[r].astype(F32)
        for j in range(heads):
            values = codes[j * rows : (j + 1) * rows] * scales[:, j : j + 1]
            values = jnp.where(held, values, EMPTY).astype(BF16)
            send_ref[last - j // per_core, j % per_core] = values

    if requests <= 8:
        for r in range(requests):
            place(r)
    else:
        pl.loop(0, requests)(place)


def turn_queries(query_ref, new_ref, turned_ref, scores_ref, values_ref):
    slots, heads, per_head = query_ref.shape[:3]
    rows = slots * per_head
    new = new_ref[...]
    values_ref[...] = values_up(new)
    shape = scores_ref.shape[1:]
    row = iota(shape, 0)
    col = iota(shape, 1)
    ok = (
        (mod(row, 2) == 0)
        & (over(row, 2 * heads * STEPS) == over(col, per_head))
        & (mod(over(row, 2 * heads), STEPS) <= mod(col, STEPS))
    )
    for h in range(heads):
        query = query_ref[:, h].reshape(rows, HD)
        if shape[1] > rows:
            query = jnp.concatenate([query, jnp.zeros((shape[1] - rows, HD), BF16)], axis=0)
        turned_ref[h] = query.astype(F32).T.astype(BF16)
        scores = dot_nt(new, query) * SCORE_SCALE
        scores_ref[h] = jnp.where(ok & (mod(over(row, 2), heads) == h), scores, NEGATIVE)


def resident_kernel(turn, *refs):
    count = 7 if turn else 5
    hbm, outs, rest = refs[:count], refs[count:-count - 1], refs[-count - 1 :]
    copies = [
        pltpu.make_async_copy(a, b, rest[-1].at[i]) for i, (a, b) in enumerate(zip(hbm, rest))
    ]
    for copy in copies:
        copy.start()
    len_ref, query_ref, new_ref, scales_ref, codes_ref = rest[:5]
    out_ref = outs[0]
    slots, rows = codes_ref.shape[:2]
    heads = scales_ref.shape[2]
    tokens = rows // (2 * heads)
    queries = query_ref.shape[1]
    new_rows = new_ref.shape[0]

    row = iota((rows, HD), 0)
    source = (mod(row, 2) * heads + mod(over(row, 2), heads)) * tokens + over(row, 2 * heads)
    lane = iota((rows, HD), 1)
    spread = jnp.concatenate(
        [jnp.where(source == lane + c, 1.0, 0.0).astype(BF16) for c in range(0, rows, HD)],
        axis=1,
    )
    for copy in copies[:4]:
        copy.wait()
    flat = jnp.concatenate(
        [scales_ref[:, p, h] for p in range(2) for h in range(heads)], axis=1
    )
    columns = dot_nt(spread, flat).astype(BF16)

    col = iota((queries, rows), 1)
    row_head = over(iota((queries, rows), 0), queries // heads)
    is_key = (mod(col, 2) == 0) & (mod(over(col, 2), heads) == row_head)
    col_token = jnp.where(is_key, over(col, 2 * heads), tokens)

    new_col = iota((queries, new_rows), 1)
    new_row = iota((queries, new_rows), 0)
    new_ok = (
        (mod(new_col, 2) == 0)
        & (mod(over(new_col, 2), heads) == over(new_row, queries // heads))
        & (mod(over(new_col, 2 * heads), STEPS) <= mod(new_row, STEPS))
    )
    new_slot = jnp.where(new_ok, over(new_col, 2 * heads * STEPS), slots)

    every = range(slots)
    new = new_ref[...]
    new_all = dot_nt(query_ref[...].reshape(slots * queries, HD), new)
    for copy in copies[4:]:
        copy.wait()
    if turn:
        turn_queries(*rest[5:7], *outs[1:])
    caches = [codes_ref[s] * columns[:, s : s + 1] for s in every]
    scores = [dot_nt(query_ref[s], caches[s]) for s in every]
    scores = [jnp.where(col_token < len_ref[s], scores[s] * SCORE_SCALE, NEGATIVE) for s in every]
    new_scores = [
        jnp.where(new_slot == s, new_all[s * queries : (s + 1) * queries] * SCORE_SCALE, NEGATIVE)
        for s in every
    ]
    top = [top_of(scores[s], new_scores[s]) for s in every]
    weights = [jnp.exp(scores[s] - top[s]) for s in every]
    new_weights = [jnp.exp(new_scores[s] - top[s]) for s in every]
    total = [sum_of(weights[s], new_weights[s]) for s in every]
    new_mixed = dot_nn(jnp.concatenate(new_weights, axis=0).astype(BF16), values_up(new))
    mixed = [
        dot_nn(to_values(weights[s]), caches[s]) + new_mixed[s * queries : (s + 1) * queries]
        for s in every
    ]
    for s in every:
        out_ref[s] = (mixed[s] * (1.0 / total[s])).astype(BF16)


def slots_by_matmul(got_ref, tp):
    chunks, _, chunk_rows = got_ref.shape[:3]
    columns = chunks * chunk_rows
    sender_rows = tp * chunk_rows
    piece = min(columns, 256)
    sums = dot_nt(jnp.ones((16, HD), BF16), got_ref[:, 0].reshape(columns, HD))[:8]
    col = iota((8, columns), 1)
    held = sums < EMPTY
    first = jnp.where(held & (mod(col, sender_rows) == 0), 1.0, 0.0).astype(BF16)
    row = over(iota((piece, piece), 0), sender_rows)
    before = jnp.where(row < over(iota((piece, piece), 1), sender_rows), 1.0, 0.0).astype(BF16)
    base = jnp.zeros((8, 1), F32)
    ranks = []
    for p in range(0, columns, piece):
        part = first[:, p : p + piece]
        ranks.append(dot_nn(part, before) + base)
        base = base + jnp.sum(part.astype(F32), axis=1, keepdims=True)
    rank = jnp.concatenate(ranks, axis=1)
    return jnp.where(held & (mod(col, 2) == 0), rank, -1.0)[:1]


def turned_kernel(
    tp, order, got_ref, turned_ref, new_scores_ref, new_values_ref, out_ref
):
    chunks, heads, chunk_rows = got_ref.shape[:3]
    slots, _, per_head = out_ref.shape[:3]
    columns = turned_ref.shape[2]
    rows = chunks * chunk_rows
    arrived = [got_ref[:, h].reshape(rows, HD) for h in range(heads)]
    scores = [dot_nn(arrived[h], turned_ref[h]) for h in range(heads)]

    plain = arrived[0].astype(F32)
    firsts = [plain[k * chunk_rows : k * chunk_rows + 1] for k in range(chunks)]
    here = {
        core // tp: jnp.where(first < EMPTY, 1.0, 0.0)
        for core, first in zip(order, firsts)
        if core % tp == 0
    }
    ranks = {w: sum([here[v] for v in here if v < w], jnp.zeros((1, HD), F32)) for w in here}
    rank = jnp.concatenate(
        [jnp.broadcast_to(ranks[core // tp], (chunk_rows, HD)) for core in order], axis=0
    )
    key = (plain < EMPTY) & (mod(iota((rows, HD), 0), 2) == 0)
    slot_of = jnp.where(key, rank, -1.0)
    mine = [
        slot_of == over(iota((1, HD), 1) + c, per_head).astype(F32) for c in range(0, columns, HD)
    ]
    for h in range(heads):
        score = jnp.concatenate(
            [
                jnp.where(mine[i], scores[h][:, c : c + HD] * SCORE_SCALE, NEGATIVE)
                for i, c in enumerate(range(0, columns, HD))
            ],
            axis=1,
        )
        new_score = new_scores_ref[h]
        top = jnp.maximum(
            jnp.max(score, axis=0, keepdims=True), jnp.max(new_score, axis=0, keepdims=True)
        )
        weights = jnp.exp(score - top)
        new_weights = jnp.exp(new_score - top)
        total = jnp.sum(weights, axis=0, keepdims=True) + jnp.sum(
            new_weights, axis=0, keepdims=True
        )
        mixed = dot_tn(values_up(arrived[h]), weights.astype(BF16))
        mixed = mixed + dot_tn(new_values_ref[...], new_weights.astype(BF16))
        out = (mixed * (1.0 / total)).T[: slots * per_head]
        out_ref[:, h] = out.astype(BF16).reshape(slots, per_head, HD)


def arrival_kernel(
    tp, groups, got_ref, query_ref, new_ref, out_ref
):
    step = pl.program_id(0) if groups > 1 else 0
    chunks, heads, chunk_rows = got_ref.shape[:3]
    slots, _, per_head = query_ref.shape[:3]
    rows = slots * per_head
    columns = chunks * chunk_rows
    every = range(heads)

    caches = [got_ref[:, h].reshape(columns, HD) for h in every]
    queries = [query_ref[:, h].reshape(rows, HD) for h in every]
    new = new_ref[...]
    scores = [dot_nt(queries[h], caches[h]) for h in every]
    new_all = dot_nt(jnp.concatenate(queries, axis=0), new)
    slot_of = slots_by_matmul(got_ref, tp)
    first_slot = jnp.float32(step * slots)
    mine = [slot_of == first_slot + a for a in range(slots)]

    new_col = iota((rows, new.shape[0]), 1)
    new_row = iota((rows, new.shape[0]), 0)
    new_here = (
        (mod(new_col, 2) == 0)
        & (over(new_col, 2 * heads * STEPS) == over(new_row, per_head))
        & (mod(over(new_col, 2 * heads), STEPS) <= mod(new_row, STEPS))
    )
    new_head = jnp.where(new_here, mod(over(new_col, 2), heads), heads)

    scores = [
        jnp.concatenate(
            [
                jnp.where(mine[a], scores[h][a * per_head : (a + 1) * per_head] * SCORE_SCALE, NEGATIVE)
                for a in range(slots)
            ],
            axis=0,
        )
        for h in every
    ]
    new_scores = [
        jnp.where(new_head == h, new_all[h * rows : (h + 1) * rows] * SCORE_SCALE, NEGATIVE)
        for h in every
    ]
    top = [top_of(scores[h], new_scores[h]) for h in every]
    weights = [jnp.exp(scores[h] - top[h]) for h in every]
    new_weights = [jnp.exp(new_scores[h] - top[h]) for h in every]
    total = [sum_of(weights[h], new_weights[h]) for h in every]
    new_mixed = dot_nn(jnp.concatenate(new_weights, axis=0).astype(BF16), values_up(new))
    for h in every:
        mixed = dot_nn(to_values(weights[h]), caches[h]) + new_mixed[h * rows : (h + 1) * rows]
        out_ref[:, h] = (mixed * (1.0 / total[h])).astype(BF16).reshape(slots, per_head, HD)


def whole(memory_space=pltpu.VMEM):
    return pl.BlockSpec(memory_space=memory_space)


def in_hbm(x):
    return pltpu.with_memory_space_constraint(x, pltpu.HBM)


def limit(mib):
    return pltpu.CompilerParams(vmem_limit_bytes=mib * 2**20)


def pack(pre_codes, pre_scales, req_dest, req_blocks, peers, tp, chips):
    requests, blocks, block_tokens = pre_codes.shape[:3]
    tokens = blocks * block_tokens
    codes = (
        pre_codes.reshape(requests, tokens, 2, KVH, HD)
        .transpose(0, 1, 3, 2, 4)
        .reshape(requests, tokens * KVH * 2, HD)
    )
    scales = pre_scales.reshape(requests, tokens * 2, KVH)
    ins = [req_dest, req_blocks, codes, scales]
    chunk = (KVH // tp, tokens * 2, HD)
    return pl.pallas_call(
        functools.partial(pack_kernel, tp, chips, KVH, 2 * block_tokens),
        out_shape=jax.ShapeDtypeStruct((peers * tp,) + chunk, BF16),
        in_specs=[whole(pltpu.HBM)] * len(ins),
        out_specs=whole(),
        scratch_shapes=[
            pltpu.SMEM(req_dest.shape, jnp.int32),
            pltpu.SMEM(req_blocks.shape, jnp.int32),
            pltpu.VMEM(codes.shape, BF16),
            pltpu.VMEM(scales.shape, BF16),
            pltpu.SemaphoreType.DMA((len(ins),)),
        ],
        compiler_params=limit(24),
        name="pack",
    )(*[in_hbm(x) for x in ins])


def cache_rows(codes):
    slots, tokens, _, width = codes.shape
    heads = width // HD
    return (
        codes.reshape(slots, tokens, 2, heads, HD)
        .transpose(0, 1, 3, 2, 4)
        .reshape(slots, tokens * heads * 2, HD)
    )


def query_rows(query):
    slots, steps, width = query.shape
    return query.reshape(slots, steps, width // HD, HD).transpose(0, 2, 1, 3)


def new_rows_of(new):
    slots, steps, pair, width = new.shape
    heads = width // HD
    return (
        new.reshape(slots, steps, pair, heads, HD)
        .transpose(0, 1, 3, 2, 4)
        .reshape(slots * steps * heads * pair, HD)
    )


def from_rows(out, shape):
    slots, steps, width = shape
    return out.reshape(slots, width // HD, steps, HD).transpose(0, 2, 1, 3).reshape(shape)


def resident(codes, res_scales, res_len, res_query, res_new, arr_query, arr_new, turn):
    slots, rows = codes.shape[:2]
    heads = res_scales.shape[-1]
    scales = res_scales.transpose(0, 2, 3, 1)
    query = query_rows(res_query).reshape(slots, heads * GROUP * STEPS, HD)
    ins = [res_len, query, new_rows_of(res_new), scales, codes]
    outs = [jax.ShapeDtypeStruct(query.shape, BF16)]
    if turn:
        arr_rows = query_rows(arr_query).reshape(-1, heads, GROUP * STEPS, HD)
        arr_new = new_rows_of(arr_new)
        columns = pl.cdiv(arr_rows.shape[0] * GROUP * STEPS, HD) * HD
        ins += [arr_rows, arr_new]
        outs += [
            pltpu.VMEM((heads, HD, columns), BF16),
            pltpu.VMEM((heads, arr_new.shape[0], columns), F32),
            pltpu.VMEM(arr_new.shape, BF16),
        ]
    work = query.shape[0] * query.shape[1] * rows
    return pl.pallas_call(
        functools.partial(resident_kernel, turn),
        out_shape=outs,
        in_specs=[whole(pltpu.HBM)] * len(ins),
        out_specs=[whole()] * len(outs),
        scratch_shapes=[
            pltpu.SMEM(res_len.shape, jnp.int32),
            *[pltpu.VMEM(x.shape, BF16) for x in ins[1:]],
            pltpu.SemaphoreType.DMA((len(ins),)),
        ],
        cost_estimate=pl.CostEstimate(
            flops=4 * work * HD,
            bytes_accessed=2 * (codes.size + 2 * query.size),
            transcendentals=work,
        ),
        compiler_params=limit(24),
        name="resident",
    )(*[in_hbm(x) for x in ins])


def turned(got, prepared, shape, tp, order):
    return pl.pallas_call(
        functools.partial(turned_kernel, tp, order),
        out_shape=jax.ShapeDtypeStruct(shape, BF16),
        in_specs=[whole()] * (1 + len(prepared)),
        out_specs=whole(),
        compiler_params=limit(16),
        name="arrivals",
    )(got, *prepared)


def arrivals(got, arr_query, arr_new, tp):
    slots, steps, width = arr_query.shape
    heads = width // (HD * GROUP)
    query = query_rows(arr_query).reshape(slots, heads, GROUP * steps, HD)
    new = new_rows_of(arr_new)
    size = max(n for n in range(1, 7) if slots % n == 0)
    groups = slots // size
    small = got.size <= 2**18

    def part(ref, rows):
        if groups == 1:
            return whole()
        return pl.BlockSpec((rows,) + ref.shape[1:], lambda i: (i,) + (0,) * (ref.ndim - 1))

    return pl.pallas_call(
        functools.partial(arrival_kernel, tp, groups),
        out_shape=jax.ShapeDtypeStruct(query.shape, BF16),
        grid=(groups,) if groups > 1 else (),
        in_specs=[whole(), part(query, size), part(new, new.shape[0] // groups)],
        out_specs=part(query, size),
        compiler_params=limit(16 if small else 48),
        name="arrivals",
    )(got, query, new)


def shards(
    pre_codes,
    pre_scales,
    req_dest,
    req_blocks,
    res_codes,
    res_scales,
    res_len,
    res_query,
    res_new,
    arr_query,
    arr_new,
):
    peers = lax.axis_size("wide")
    tp = lax.axis_size("tp")
    chips = [5, 6, 7, 1, 0, 2, 3, 4] if peers == 8 else None
    cores = [w * tp + t for w in chips or range(peers) for t in reversed(range(tp))]
    order = chips and cores
    send = pack(pre_codes, pre_scales, req_dest, req_blocks, peers, tp, chips)
    got = lax.all_to_all(
        send,
        ("wide", "tp"),
        split_axis=0,
        concat_axis=0,
        tiled=True,
        axis_index_groups=[cores],
    )
    res_out, *prepared = resident(
        cache_rows(res_codes), res_scales, res_len, res_query, res_new, arr_query, arr_new,
        order is not None,
    )
    if order is None:
        arr_out = arrivals(got, arr_query, arr_new, tp)
    else:
        shape = (arr_query.shape[0], KVH // tp, GROUP * STEPS, HD)
        arr_out = turned(got, prepared, shape, tp, order)
    return (from_rows(res_out, res_query.shape), from_rows(arr_out, arr_query.shape))


def solution(mesh):
    in_specs = (
        P(("groups", "wide"), None, "tp", None, None),
        P(("groups", "wide"), None, "tp", None, None),
        P(("groups", "wide")),
        P(("groups", "wide")),
        P(("groups", "wide"), None, None, "tp"),
        P(("groups", "wide"), None, None, "tp"),
        P(("groups", "wide")),
        P(("groups", "wide"), None, "tp"),
        P(("groups", "wide"), None, None, "tp"),
        P(("groups", "wide"), None, "tp"),
        P(("groups", "wide"), None, None, "tp"),
    )
    out_specs = (P(("groups", "wide"), None, "tp"), P(("groups", "wide"), None, "tp"))
    return jax.shard_map(shards, mesh=mesh, in_specs=in_specs, out_specs=out_specs, check_vma=False)
```

```python
import functools
import math

import jax
import jax.numpy as jnp
from jax import lax
from jax.experimental import pallas as pl
from jax.experimental.pallas import tpu as pltpu
from jax.sharding import PartitionSpec as P

KVH = 4
HD = 128
HQ = 64
GROUP = HQ // KVH
STEPS = 2

NEGATIVE = -1e30
EMPTY = 1024.0
SCORE_SCALE = 1.0 / math.sqrt(HD)

BF16 = jnp.bfloat16
F32 = jnp.float32


def iota(shape, axis):
    return lax.broadcasted_iota(jnp.int32, shape, axis)


def over(x, n):
    return jnp.right_shift(x, n.bit_length() - 1) if n & (n - 1) == 0 else x // n


def mod(x, n):
    return jnp.bitwise_and(x, n - 1) if n & (n - 1) == 0 else x % n


def dot_nt(a, b):
    return lax.dot_general(a, b, (((1,), (1,)), ((), ())), preferred_element_type=F32)


def dot_nn(a, b):
    return lax.dot_general(a, b, (((1,), (0,)), ((), ())), preferred_element_type=F32)


def top_of(*parts):
    return functools.reduce(jnp.maximum, [jnp.max(p, axis=1, keepdims=True) for p in parts])


def sum_of(*parts):
    return functools.reduce(jnp.add, [jnp.sum(p, axis=1, keepdims=True) for p in parts])


def to_values(weights):
    tiles = [pltpu.roll(weights[:, c : c + HD], 1, 1) for c in range(0, weights.shape[1], HD)]
    return jnp.concatenate(tiles, axis=1).astype(BF16)


def values_up(rows):
    return pltpu.roll(rows.astype(F32), rows.shape[0] - 1, 0).astype(BF16)


def pack_kernel(
    tp, chips, heads, block_rows, dest_hbm, blocks_hbm, codes_hbm, scales_hbm, send_ref,
    dest_ref, blocks_ref, codes_ref, scales_ref, sems,
):
    requests, all_rows = codes_ref.shape[:2]
    pairs = [
        (codes_hbm, codes_ref), (scales_hbm, scales_ref),
        (dest_hbm, dest_ref), (blocks_hbm, blocks_ref),
    ]
    copies = [pltpu.make_async_copy(a, b, sems.at[i]) for i, (a, b) in enumerate(pairs)]
    for copy in copies:
        copy.start()
    send_ref[...] = jnp.full(send_ref.shape, EMPTY, BF16)
    rows = all_rows // heads
    per_core = heads // tp
    row_block = over(iota((rows, HD), 0), block_rows)
    to_row = iota((all_rows, all_rows), 0)
    from_row = iota((all_rows, all_rows), 1)
    source = over(mod(to_row, rows), 2) * (2 * heads) + over(to_row, rows) * 2 + mod(to_row, 2)
    by_head = jnp.where(from_row == source, 1.0, 0.0).astype(BF16)
    for copy in copies:
        copy.wait()

    def place(r):
        there = dest_ref[r]
        if chips is not None:
            there = functools.reduce(
                jnp.add, [jnp.where(there == w, p, 0) for p, w in enumerate(chips)]
            )
        last = there * tp + tp - 1
        held = row_block < blocks_ref[r]
        codes = dot_nn(by_head, codes_ref[r])
        scales = scales_ref[r].astype(F32)
        for j in range(heads):
            values = codes[j * rows : (j + 1) * rows] * scales[:, j : j + 1]
            values = jnp.where(held, values, EMPTY).astype(BF16)
            send_ref[last - j // per_core, j % per_core] = values

    if requests <= 8:
        for r in range(requests):
            place(r)
    else:
        pl.loop(0, requests)(place)


def resident_kernel(
    len_hbm, codes_hbm, scales_hbm, query_hbm, new_hbm, out_ref,
    len_ref, codes_ref, scales_ref, query_ref, new_ref, sems,
):
    pairs = [
        (query_hbm, query_ref), (new_hbm, new_ref), (scales_hbm, scales_ref),
        (len_hbm, len_ref), (codes_hbm, codes_ref),
    ]
    copies = [pltpu.make_async_copy(a, b, sems.at[i]) for i, (a, b) in enumerate(pairs)]
    for copy in copies:
        copy.start()
    slots, rows = codes_ref.shape[:2]
    heads = scales_ref.shape[2]
    tokens = rows // (2 * heads)
    queries = query_ref.shape[1]
    new_rows = new_ref.shape[0]

    row = iota((rows, HD), 0)
    source = (mod(row, 2) * heads + mod(over(row, 2), heads)) * tokens + over(row, 2 * heads)
    lane = iota((rows, HD), 1)
    spread = jnp.concatenate(
        [jnp.where(source == lane + c, 1.0, 0.0).astype(BF16) for c in range(0, rows, HD)],
        axis=1,
    )
    for copy in copies[:-1]:
        copy.wait()
    flat = jnp.concatenate(
        [scales_ref[:, p, h] for p in range(2) for h in range(heads)], axis=1
    )
    columns = dot_nt(spread, flat).astype(BF16)

    col = iota((queries, rows), 1)
    row_head = over(iota((queries, rows), 0), queries // heads)
    is_key = (mod(col, 2) == 0) & (mod(over(col, 2), heads) == row_head)
    col_token = jnp.where(is_key, over(col, 2 * heads), tokens)

    new_col = iota((queries, new_rows), 1)
    new_row = iota((queries, new_rows), 0)
    new_ok = (
        (mod(new_col, 2) == 0)
        & (mod(over(new_col, 2), heads) == over(new_row, queries // heads))
        & (mod(over(new_col, 2 * heads), STEPS) <= mod(new_row, STEPS))
    )
    new_slot = jnp.where(new_ok, over(new_col, 2 * heads * STEPS), slots)

    every = range(slots)
    new = new_ref[...]
    new_all = dot_nt(query_ref[...].reshape(slots * queries, HD), new)
    copies[-1].wait()
    caches = [codes_ref[s] * columns[:, s : s + 1] for s in every]
    scores = [dot_nt(query_ref[s], caches[s]) for s in every]
    scores = [jnp.where(col_token < len_ref[s], scores[s] * SCORE_SCALE, NEGATIVE) for s in every]
    new_scores = [
        jnp.where(new_slot == s, new_all[s * queries : (s + 1) * queries] * SCORE_SCALE, NEGATIVE)
        for s in every
    ]
    top = [top_of(scores[s], new_scores[s]) for s in every]
    weights = [jnp.exp(scores[s] - top[s]) for s in every]
    new_weights = [jnp.exp(new_scores[s] - top[s]) for s in every]
    total = [sum_of(weights[s], new_weights[s]) for s in every]
    new_mixed = dot_nn(jnp.concatenate(new_weights, axis=0).astype(BF16), values_up(new))
    mixed = [
        dot_nn(to_values(weights[s]), caches[s]) + new_mixed[s * queries : (s + 1) * queries]
        for s in every
    ]
    for s in every:
        out_ref[s] = (mixed[s] * (1.0 / total[s])).astype(BF16)


def slots_by_rows(got_ref, tp, order, block_rows):
    chunk_rows = got_ref.shape[2]
    blocks = chunk_rows // block_rows
    rows = [got_ref[k, 0].astype(F32) for k in range(len(order))]
    here = {
        core // tp: jnp.where(x[:1] < EMPTY, 1.0, 0.0)
        for core, x in zip(order, rows)
        if core % tp == 0
    }
    ranks = {
        w: sum([here[v] for v in here if v < w], jnp.zeros((1, HD), F32)) for w in here
    }
    lane = iota((1, HD), 1)
    block = over(lane, block_rows)
    block = jnp.where(mod(lane, 2) == 0, block, -1)
    per_tile = HD // chunk_rows
    tiles = []
    for start in range(0, len(order), per_tile):
        tile = jnp.full((1, HD), -1.0, F32)
        for i in range(per_tile):
            x, rank = rows[start + i], ranks[order[start + i] // tp]
            for b in range(blocks):
                at = b * block_rows
                value = jnp.where(x[at : at + 1] < EMPTY, rank, -1.0)
                tile = jnp.where(block == i * blocks + b, value, tile)
        tiles.append(tile)
    return jnp.concatenate(tiles, axis=1)


def slots_by_matmul(got_ref, tp):
    chunks, _, chunk_rows = got_ref.shape[:3]
    columns = chunks * chunk_rows
    sender_rows = tp * chunk_rows
    piece = min(columns, 256)
    sums = dot_nt(jnp.ones((16, HD), BF16), got_ref[:, 0].reshape(columns, HD))[:8]
    col = iota((8, columns), 1)
    held = sums < EMPTY
    first = jnp.where(held & (mod(col, sender_rows) == 0), 1.0, 0.0).astype(BF16)
    row = over(iota((piece, piece), 0), sender_rows)
    before = jnp.where(row < over(iota((piece, piece), 1), sender_rows), 1.0, 0.0).astype(BF16)
    base = jnp.zeros((8, 1), F32)
    ranks = []
    for p in range(0, columns, piece):
        part = first[:, p : p + piece]
        ranks.append(dot_nn(part, before) + base)
        base = base + jnp.sum(part.astype(F32), axis=1, keepdims=True)
    rank = jnp.concatenate(ranks, axis=1)
    return jnp.where(held & (mod(col, 2) == 0), rank, -1.0)[:1]


def arrival_kernel(
    tp, groups, order, block_rows, got_ref, query_ref, new_ref, out_hbm, out_ref, sems
):
    step = pl.program_id(0) if groups > 1 else 0
    chunks, heads, chunk_rows = got_ref.shape[:3]
    slots, _, per_head = query_ref.shape[:3]
    rows = slots * per_head
    columns = chunks * chunk_rows
    every = range(heads)

    caches = [got_ref[:, h].reshape(columns, HD) for h in every]
    queries = [query_ref[:, h].reshape(rows, HD) for h in every]
    new = new_ref[...]
    new_values = values_up(new)
    scores = [dot_nt(queries[h], caches[h]) for h in every]
    new_all = [dot_nt(queries[h], new) for h in every]
    if order is None:
        slot_of = slots_by_matmul(got_ref, tp)
    else:
        slot_of = slots_by_rows(got_ref, tp, order, block_rows)
    first_slot = jnp.float32(step * slots)
    mine = [slot_of == first_slot + a for a in range(slots)]

    new_col = iota((rows, new.shape[0]), 1)
    new_row = iota((rows, new.shape[0]), 0)
    new_here = (
        (mod(new_col, 2) == 0)
        & (over(new_col, 2 * heads * STEPS) == over(new_row, per_head))
        & (mod(over(new_col, 2 * heads), STEPS) <= mod(new_row, STEPS))
    )
    new_head = jnp.where(new_here, mod(over(new_col, 2), heads), heads)

    copies = []
    for h in every:
        score = jnp.concatenate(
            [
                jnp.where(mine[a], scores[h][a * per_head : (a + 1) * per_head] * SCORE_SCALE, NEGATIVE)
                for a in range(slots)
            ],
            axis=0,
        )
        new_score = jnp.where(new_head == h, new_all[h] * SCORE_SCALE, NEGATIVE)
        top = top_of(score, new_score)
        weights = jnp.exp(score - top)
        new_weights = jnp.exp(new_score - top)
        total = sum_of(weights, new_weights)
        mixed = dot_nn(to_values(weights), caches[h]) + dot_nn(new_weights.astype(BF16), new_values)
        out_ref[h] = (mixed * (1.0 / total)).astype(BF16).reshape(slots, per_head, HD)
        target = out_hbm.at[pl.ds(step * slots, slots), h]
        copies.append(pltpu.make_async_copy(out_ref.at[h], target, sems.at[h]))
        copies[-1].start()
    for copy in copies:
        copy.wait()


def whole(memory_space=pltpu.VMEM):
    return pl.BlockSpec(memory_space=memory_space)


def in_hbm(x):
    return pltpu.with_memory_space_constraint(x, pltpu.HBM)


def limit(mib):
    return pltpu.CompilerParams(vmem_limit_bytes=mib * 2**20)


def pack(pre_codes, pre_scales, req_dest, req_blocks, peers, tp, chips):
    requests, blocks, block_tokens = pre_codes.shape[:3]
    tokens = blocks * block_tokens
    codes = (
        pre_codes.reshape(requests, tokens, 2, KVH, HD)
        .transpose(0, 1, 3, 2, 4)
        .reshape(requests, tokens * KVH * 2, HD)
    )
    scales = pre_scales.reshape(requests, tokens * 2, KVH)
    ins = [req_dest, req_blocks, codes, scales]
    chunk = (KVH // tp, tokens * 2, HD)
    return pl.pallas_call(
        functools.partial(pack_kernel, tp, chips, KVH, 2 * block_tokens),
        out_shape=jax.ShapeDtypeStruct((peers * tp,) + chunk, BF16),
        in_specs=[whole(pltpu.HBM)] * len(ins),
        out_specs=whole(),
        scratch_shapes=[
            pltpu.SMEM(req_dest.shape, jnp.int32),
            pltpu.SMEM(req_blocks.shape, jnp.int32),
            pltpu.VMEM(codes.shape, BF16),
            pltpu.VMEM(scales.shape, BF16),
            pltpu.SemaphoreType.DMA((len(ins),)),
        ],
        compiler_params=limit(24),
        name="pack",
    )(*[in_hbm(x) for x in ins])


def cache_rows(codes):
    slots, tokens, _, width = codes.shape
    heads = width // HD
    return (
        codes.reshape(slots, tokens, 2, heads, HD)
        .transpose(0, 1, 3, 2, 4)
        .reshape(slots, tokens * heads * 2, HD)
    )


def query_rows(query):
    slots, steps, width = query.shape
    return query.reshape(slots, steps, width // HD, HD).transpose(0, 2, 1, 3)


def new_rows_of(new):
    slots, steps, pair, width = new.shape
    heads = width // HD
    return (
        new.reshape(slots, steps, pair, heads, HD)
        .transpose(0, 1, 3, 2, 4)
        .reshape(slots * steps * heads * pair, HD)
    )


def from_rows(out, shape):
    slots, steps, width = shape
    return out.reshape(slots, width // HD, steps, HD).transpose(0, 2, 1, 3).reshape(shape)


def resident(codes, res_scales, res_len, res_query, res_new):
    slots, rows = codes.shape[:2]
    heads = res_scales.shape[-1]
    scales = res_scales.transpose(0, 2, 3, 1)
    query = query_rows(res_query).reshape(slots, heads * GROUP * STEPS, HD)
    ins = [res_len, codes, scales, query, new_rows_of(res_new)]
    work = query.shape[0] * query.shape[1] * rows
    return pl.pallas_call(
        resident_kernel,
        out_shape=jax.ShapeDtypeStruct(query.shape, BF16),
        in_specs=[whole(pltpu.HBM)] * len(ins),
        out_specs=whole(),
        scratch_shapes=[
            pltpu.SMEM(res_len.shape, jnp.int32),
            *[pltpu.VMEM(x.shape, BF16) for x in ins[1:]],
            pltpu.SemaphoreType.DMA((len(ins),)),
        ],
        cost_estimate=pl.CostEstimate(
            flops=4 * work * HD,
            bytes_accessed=2 * (codes.size + 2 * query.size),
            transcendentals=work,
        ),
        compiler_params=limit(16),
        name="resident",
    )(*[in_hbm(x) for x in ins])


def arrivals(got, arr_query, arr_new, tp, order, block_rows):
    slots, steps, width = arr_query.shape
    heads = width // (HD * GROUP)
    query = query_rows(arr_query).reshape(slots, heads, GROUP * steps, HD)
    new = new_rows_of(arr_new)
    size = max(n for n in range(1, 7) if slots % n == 0)
    groups = slots // size
    small = got.size <= 2**18

    def part(ref, rows):
        if groups == 1:
            return whole()
        return pl.BlockSpec((rows,) + ref.shape[1:], lambda i: (i,) + (0,) * (ref.ndim - 1))

    return pl.pallas_call(
        functools.partial(arrival_kernel, tp, groups, order, block_rows),
        out_shape=jax.ShapeDtypeStruct(query.shape, BF16),
        grid=(groups,) if groups > 1 else (),
        in_specs=[whole(), part(query, size), part(new, new.shape[0] // groups)],
        out_specs=whole(pltpu.HBM),
        scratch_shapes=[
            pltpu.VMEM((heads, size) + query.shape[2:], BF16),
            pltpu.SemaphoreType.DMA((heads,)),
        ],
        compiler_params=limit(16 if small else 48),
        name="arrivals",
    )(got, query, new)


def shards(
    pre_codes,
    pre_scales,
    req_dest,
    req_blocks,
    res_codes,
    res_scales,
    res_len,
    res_query,
    res_new,
    arr_query,
    arr_new,
):
    peers = lax.axis_size("wide")
    tp = lax.axis_size("tp")
    chips = [5, 6, 7, 1, 0, 2, 3, 4] if peers == 8 else None
    cores = [w * tp + t for w in chips or range(peers) for t in reversed(range(tp))]
    order = chips and cores
    send = pack(pre_codes, pre_scales, req_dest, req_blocks, peers, tp, chips)
    got = lax.all_to_all(
        send,
        ("wide", "tp"),
        split_axis=0,
        concat_axis=0,
        tiled=True,
        axis_index_groups=[cores],
    )
    res_out = resident(cache_rows(res_codes), res_scales, res_len, res_query, res_new)
    block_rows = 2 * pre_codes.shape[2]
    arr_out = arrivals(got, arr_query, arr_new, tp, order, block_rows)
    return (from_rows(res_out, res_query.shape), from_rows(arr_out, arr_query.shape))


def solution(mesh):
    in_specs = (
        P(("groups", "wide"), None, "tp", None, None),
        P(("groups", "wide"), None, "tp", None, None),
        P(("groups", "wide")),
        P(("groups", "wide")),
        P(("groups", "wide"), None, None, "tp"),
        P(("groups", "wide"), None, None, "tp"),
        P(("groups", "wide")),
        P(("groups", "wide"), None, "tp"),
        P(("groups", "wide"), None, None, "tp"),
        P(("groups", "wide"), None, "tp"),
        P(("groups", "wide"), None, None, "tp"),
    )
    out_specs = (P(("groups", "wide"), None, "tp"), P(("groups", "wide"), None, "tp"))
    return jax.shard_map(shards, mesh=mesh, in_specs=in_specs, out_specs=out_specs, check_vma=False)
```

```python
import functools
import math

import jax
import jax.numpy as jnp
from jax import lax
from jax.experimental import pallas as pl
from jax.experimental.pallas import tpu as pltpu
from jax.sharding import PartitionSpec as P

KVH = 4
HD = 128
HQ = 64
GROUP = HQ // KVH
STEPS = 2

NEGATIVE = -1e30
EMPTY = 1024.0
SCORE_SCALE = 1.0 / math.sqrt(HD)

BF16 = jnp.bfloat16
F32 = jnp.float32


def iota(shape, axis):
    return lax.broadcasted_iota(jnp.int32, shape, axis)


def over(x, n):
    return jnp.right_shift(x, n.bit_length() - 1) if n & (n - 1) == 0 else x // n


def mod(x, n):
    return jnp.bitwise_and(x, n - 1) if n & (n - 1) == 0 else x % n


def dot_nt(a, b):
    return lax.dot_general(a, b, (((1,), (1,)), ((), ())), preferred_element_type=F32)


def dot_nn(a, b):
    return lax.dot_general(a, b, (((1,), (0,)), ((), ())), preferred_element_type=F32)


def top_of(*parts):
    return functools.reduce(jnp.maximum, [jnp.max(p, axis=1, keepdims=True) for p in parts])


def sum_of(*parts):
    return functools.reduce(jnp.add, [jnp.sum(p, axis=1, keepdims=True) for p in parts])


def to_values(weights):
    tiles = [pltpu.roll(weights[:, c : c + HD], 1, 1) for c in range(0, weights.shape[1], HD)]
    return jnp.concatenate(tiles, axis=1).astype(BF16)


def values_up(rows):
    return pltpu.roll(rows.astype(F32), rows.shape[0] - 1, 0).astype(BF16)


def pack_kernel(
    tp, order, heads, block_rows, dest_hbm, blocks_hbm, codes_hbm, scales_hbm, send_ref,
    dest_ref, blocks_ref, codes_ref, scales_ref, sems,
):
    requests, all_rows = codes_ref.shape[:2]
    pairs = [
        (codes_hbm, codes_ref), (scales_hbm, scales_ref),
        (dest_hbm, dest_ref), (blocks_hbm, blocks_ref),
    ]
    copies = [pltpu.make_async_copy(a, b, sems.at[i]) for i, (a, b) in enumerate(pairs)]
    for copy in copies:
        copy.start()
    send_ref[...] = jnp.full(send_ref.shape, EMPTY, BF16)
    rows = all_rows // heads
    per_core = heads // tp
    row_block = over(iota((rows, HD), 0), block_rows)
    to_row = iota((all_rows, all_rows), 0)
    from_row = iota((all_rows, all_rows), 1)
    source = over(mod(to_row, rows), 2) * (2 * heads) + over(to_row, rows) * 2 + mod(to_row, 2)
    by_head = jnp.where(from_row == source, 1.0, 0.0).astype(BF16)
    for copy in copies:
        copy.wait()

    def place(r):
        there = dest_ref[r]
        spots = [there * tp + t for t in range(tp)]
        if order is not None:
            for t in range(tp):
                at = {core // tp: p for p, core in enumerate(order) if core % tp == t}
                spots[t] = functools.reduce(
                    jnp.add, [jnp.where(there == w, p, 0) for w, p in at.items()]
                )
        held = row_block < blocks_ref[r]
        codes = dot_nn(by_head, codes_ref[r])
        scales = scales_ref[r].astype(F32)
        for j in range(heads):
            values = codes[j * rows : (j + 1) * rows] * scales[:, j : j + 1]
            values = jnp.where(held, values, EMPTY).astype(BF16)
            send_ref[spots[j // per_core], j % per_core] = values

    if requests <= 8:
        for r in range(requests):
            place(r)
    else:
        pl.loop(0, requests)(place)


def resident_kernel(
    len_hbm, codes_hbm, scales_hbm, query_hbm, new_hbm, out_ref,
    len_ref, codes_ref, scales_ref, query_ref, new_ref, sems,
):
    pairs = [
        (query_hbm, query_ref), (new_hbm, new_ref), (scales_hbm, scales_ref),
        (len_hbm, len_ref), (codes_hbm, codes_ref),
    ]
    copies = [pltpu.make_async_copy(a, b, sems.at[i]) for i, (a, b) in enumerate(pairs)]
    for copy in copies:
        copy.start()
    slots, rows = codes_ref.shape[:2]
    heads = scales_ref.shape[2]
    tokens = rows // (2 * heads)
    queries = query_ref.shape[1]
    new_rows = new_ref.shape[0]

    row = iota((rows, HD), 0)
    source = (mod(row, 2) * heads + mod(over(row, 2), heads)) * tokens + over(row, 2 * heads)
    lane = iota((rows, HD), 1)
    spread = jnp.concatenate(
        [jnp.where(source == lane + c, 1.0, 0.0).astype(BF16) for c in range(0, rows, HD)],
        axis=1,
    )
    for copy in copies[:-1]:
        copy.wait()
    flat = jnp.concatenate(
        [scales_ref[:, p, h] for p in range(2) for h in range(heads)], axis=1
    )
    columns = dot_nt(spread, flat).astype(BF16)

    col = iota((queries, rows), 1)
    row_head = over(iota((queries, rows), 0), queries // heads)
    is_key = (mod(col, 2) == 0) & (mod(over(col, 2), heads) == row_head)
    col_token = jnp.where(is_key, over(col, 2 * heads), tokens)

    new_col = iota((queries, new_rows), 1)
    new_row = iota((queries, new_rows), 0)
    new_ok = (
        (mod(new_col, 2) == 0)
        & (mod(over(new_col, 2), heads) == over(new_row, queries // heads))
        & (mod(over(new_col, 2 * heads), STEPS) <= mod(new_row, STEPS))
    )
    new_slot = jnp.where(new_ok, over(new_col, 2 * heads * STEPS), slots)

    every = range(slots)
    new = new_ref[...]
    new_all = dot_nt(query_ref[...].reshape(slots * queries, HD), new)
    copies[-1].wait()
    caches = [codes_ref[s] * columns[:, s : s + 1] for s in every]
    scores = [dot_nt(query_ref[s], caches[s]) for s in every]
    scores = [jnp.where(col_token < len_ref[s], scores[s] * SCORE_SCALE, NEGATIVE) for s in every]
    new_scores = [
        jnp.where(new_slot == s, new_all[s * queries : (s + 1) * queries] * SCORE_SCALE, NEGATIVE)
        for s in every
    ]
    top = [top_of(scores[s], new_scores[s]) for s in every]
    weights = [jnp.exp(scores[s] - top[s]) for s in every]
    new_weights = [jnp.exp(new_scores[s] - top[s]) for s in every]
    total = [sum_of(weights[s], new_weights[s]) for s in every]
    new_mixed = dot_nn(jnp.concatenate(new_weights, axis=0).astype(BF16), values_up(new))
    mixed = [
        dot_nn(to_values(weights[s]), caches[s]) + new_mixed[s * queries : (s + 1) * queries]
        for s in every
    ]
    for s in every:
        out_ref[s] = (mixed[s] * (1.0 / total[s])).astype(BF16)


def slots_by_rows(got_ref, tp, order, block_rows):
    chunk_rows = got_ref.shape[2]
    blocks = chunk_rows // block_rows
    rows = [got_ref[k, 0].astype(F32) for k in range(len(order))]
    here = {
        core // tp: jnp.where(x[:1] < EMPTY, 1.0, 0.0)
        for core, x in zip(order, rows)
        if core % tp == 0
    }
    ranks = {
        w: sum([here[v] for v in here if v < w], jnp.zeros((1, HD), F32)) for w in here
    }
    lane = iota((1, HD), 1)
    block = over(lane, block_rows)
    block = jnp.where(mod(lane, 2) == 0, block, -1)
    per_tile = HD // chunk_rows
    tiles = []
    for start in range(0, len(order), per_tile):
        tile = jnp.full((1, HD), -1.0, F32)
        for i in range(per_tile):
            x, rank = rows[start + i], ranks[order[start + i] // tp]
            for b in range(blocks):
                at = b * block_rows
                value = jnp.where(x[at : at + 1] < EMPTY, rank, -1.0)
                tile = jnp.where(block == i * blocks + b, value, tile)
        tiles.append(tile)
    return jnp.concatenate(tiles, axis=1)


def slots_by_matmul(got_ref, tp):
    chunks, _, chunk_rows = got_ref.shape[:3]
    columns = chunks * chunk_rows
    sender_rows = tp * chunk_rows
    piece = min(columns, 256)
    sums = dot_nt(jnp.ones((16, HD), BF16), got_ref[:, 0].reshape(columns, HD))[:8]
    col = iota((8, columns), 1)
    held = sums < EMPTY
    first = jnp.where(held & (mod(col, sender_rows) == 0), 1.0, 0.0).astype(BF16)
    row = over(iota((piece, piece), 0), sender_rows)
    before = jnp.where(row < over(iota((piece, piece), 1), sender_rows), 1.0, 0.0).astype(BF16)
    base = jnp.zeros((8, 1), F32)
    ranks = []
    for p in range(0, columns, piece):
        part = first[:, p : p + piece]
        ranks.append(dot_nn(part, before) + base)
        base = base + jnp.sum(part.astype(F32), axis=1, keepdims=True)
    rank = jnp.concatenate(ranks, axis=1)
    return jnp.where(held & (mod(col, 2) == 0), rank, -1.0)[:1]


def arrival_kernel(
    tp, groups, order, block_rows, got_ref, query_ref, new_ref, out_ref
):
    step = pl.program_id(0) if groups > 1 else 0
    chunks, heads, chunk_rows = got_ref.shape[:3]
    slots, _, per_head = query_ref.shape[:3]
    rows = slots * per_head
    columns = chunks * chunk_rows
    every = range(heads)

    caches = [got_ref[:, h].reshape(columns, HD) for h in every]
    queries = [query_ref[:, h].reshape(rows, HD) for h in every]
    new = new_ref[...]
    scores = [dot_nt(queries[h], caches[h]) for h in every]
    new_all = dot_nt(jnp.concatenate(queries, axis=0), new)
    if order is None:
        slot_of = slots_by_matmul(got_ref, tp)
    else:
        slot_of = slots_by_rows(got_ref, tp, order, block_rows)
    first_slot = jnp.float32(step * slots)
    mine = [slot_of == first_slot + a for a in range(slots)]

    new_col = iota((rows, new.shape[0]), 1)
    new_row = iota((rows, new.shape[0]), 0)
    new_here = (
        (mod(new_col, 2) == 0)
        & (over(new_col, 2 * heads * STEPS) == over(new_row, per_head))
        & (mod(over(new_col, 2 * heads), STEPS) <= mod(new_row, STEPS))
    )
    new_head = jnp.where(new_here, mod(over(new_col, 2), heads), heads)

    scores = [
        jnp.concatenate(
            [
                jnp.where(mine[a], scores[h][a * per_head : (a + 1) * per_head] * SCORE_SCALE, NEGATIVE)
                for a in range(slots)
            ],
            axis=0,
        )
        for h in every
    ]
    new_scores = [
        jnp.where(new_head == h, new_all[h * rows : (h + 1) * rows] * SCORE_SCALE, NEGATIVE)
        for h in every
    ]
    top = [top_of(scores[h], new_scores[h]) for h in every]
    weights = [jnp.exp(scores[h] - top[h]) for h in every]
    new_weights = [jnp.exp(new_scores[h] - top[h]) for h in every]
    total = [sum_of(weights[h], new_weights[h]) for h in every]
    new_mixed = dot_nn(jnp.concatenate(new_weights, axis=0).astype(BF16), values_up(new))
    for h in every:
        mixed = dot_nn(to_values(weights[h]), caches[h]) + new_mixed[h * rows : (h + 1) * rows]
        out_ref[:, h] = (mixed * (1.0 / total[h])).astype(BF16).reshape(slots, per_head, HD)


def whole(memory_space=pltpu.VMEM):
    return pl.BlockSpec(memory_space=memory_space)


def in_hbm(x):
    return pltpu.with_memory_space_constraint(x, pltpu.HBM)


def limit(mib):
    return pltpu.CompilerParams(vmem_limit_bytes=mib * 2**20)


def pack(pre_codes, pre_scales, req_dest, req_blocks, peers, tp, order):
    requests, blocks, block_tokens = pre_codes.shape[:3]
    tokens = blocks * block_tokens
    codes = (
        pre_codes.reshape(requests, tokens, 2, KVH, HD)
        .transpose(0, 1, 3, 2, 4)
        .reshape(requests, tokens * KVH * 2, HD)
    )
    scales = pre_scales.reshape(requests, tokens * 2, KVH)
    ins = [req_dest, req_blocks, codes, scales]
    chunk = (KVH // tp, tokens * 2, HD)
    return pl.pallas_call(
        functools.partial(pack_kernel, tp, order, KVH, 2 * block_tokens),
        out_shape=jax.ShapeDtypeStruct((peers * tp,) + chunk, BF16),
        in_specs=[whole(pltpu.HBM)] * len(ins),
        out_specs=whole(),
        scratch_shapes=[
            pltpu.SMEM(req_dest.shape, jnp.int32),
            pltpu.SMEM(req_blocks.shape, jnp.int32),
            pltpu.VMEM(codes.shape, BF16),
            pltpu.VMEM(scales.shape, BF16),
            pltpu.SemaphoreType.DMA((len(ins),)),
        ],
        compiler_params=limit(24),
        name="pack",
    )(*[in_hbm(x) for x in ins])


def cache_rows(codes):
    slots, tokens, _, width = codes.shape
    heads = width // HD
    return (
        codes.reshape(slots, tokens, 2, heads, HD)
        .transpose(0, 1, 3, 2, 4)
        .reshape(slots, tokens * heads * 2, HD)
    )


def query_rows(query):
    slots, steps, width = query.shape
    return query.reshape(slots, steps, width // HD, HD).transpose(0, 2, 1, 3)


def new_rows_of(new):
    slots, steps, pair, width = new.shape
    heads = width // HD
    return (
        new.reshape(slots, steps, pair, heads, HD)
        .transpose(0, 1, 3, 2, 4)
        .reshape(slots * steps * heads * pair, HD)
    )


def from_rows(out, shape):
    slots, steps, width = shape
    return out.reshape(slots, width // HD, steps, HD).transpose(0, 2, 1, 3).reshape(shape)


def resident(codes, res_scales, res_len, res_query, res_new):
    slots, rows = codes.shape[:2]
    heads = res_scales.shape[-1]
    scales = res_scales.transpose(0, 2, 3, 1)
    query = query_rows(res_query).reshape(slots, heads * GROUP * STEPS, HD)
    ins = [res_len, codes, scales, query, new_rows_of(res_new)]
    work = query.shape[0] * query.shape[1] * rows
    return pl.pallas_call(
        resident_kernel,
        out_shape=jax.ShapeDtypeStruct(query.shape, BF16),
        in_specs=[whole(pltpu.HBM)] * len(ins),
        out_specs=whole(),
        scratch_shapes=[
            pltpu.SMEM(res_len.shape, jnp.int32),
            *[pltpu.VMEM(x.shape, BF16) for x in ins[1:]],
            pltpu.SemaphoreType.DMA((len(ins),)),
        ],
        cost_estimate=pl.CostEstimate(
            flops=4 * work * HD,
            bytes_accessed=2 * (codes.size + 2 * query.size),
            transcendentals=work,
        ),
        compiler_params=limit(16),
        name="resident",
    )(*[in_hbm(x) for x in ins])


def arrivals(got, arr_query, arr_new, tp, order, block_rows):
    slots, steps, width = arr_query.shape
    heads = width // (HD * GROUP)
    query = query_rows(arr_query).reshape(slots, heads, GROUP * steps, HD)
    new = new_rows_of(arr_new)
    size = max(n for n in range(1, 7) if slots % n == 0)
    groups = slots // size
    small = got.size <= 2**18

    def part(ref, rows):
        if groups == 1:
            return whole()
        return pl.BlockSpec((rows,) + ref.shape[1:], lambda i: (i,) + (0,) * (ref.ndim - 1))

    return pl.pallas_call(
        functools.partial(arrival_kernel, tp, groups, order, block_rows),
        out_shape=jax.ShapeDtypeStruct(query.shape, BF16),
        grid=(groups,) if groups > 1 else (),
        in_specs=[whole(), part(query, size), part(new, new.shape[0] // groups)],
        out_specs=part(query, size),
        compiler_params=limit(16 if small else 48),
        name="arrivals",
    )(got, query, new)


def shards(
    pre_codes,
    pre_scales,
    req_dest,
    req_blocks,
    res_codes,
    res_scales,
    res_len,
    res_query,
    res_new,
    arr_query,
    arr_new,
):
    peers = lax.axis_size("wide")
    tp = lax.axis_size("tp")
    order = None
    if peers * tp == 16:
        order = [11, 13, 15, 3, 1, 5, 7, 9, 10, 12, 14, 2, 0, 4, 6, 8]
    send = pack(pre_codes, pre_scales, req_dest, req_blocks, peers, tp, order)
    got = lax.all_to_all(
        send,
        ("wide", "tp"),
        split_axis=0,
        concat_axis=0,
        tiled=True,
        axis_index_groups=[order or list(range(peers * tp))],
    )
    res_out = resident(cache_rows(res_codes), res_scales, res_len, res_query, res_new)
    block_rows = 2 * pre_codes.shape[2]
    arr_out = arrivals(got, arr_query, arr_new, tp, order, block_rows)
    return (from_rows(res_out, res_query.shape), from_rows(arr_out, arr_query.shape))


def solution(mesh):
    in_specs = (
        P(("groups", "wide"), None, "tp", None, None),
        P(("groups", "wide"), None, "tp", None, None),
        P(("groups", "wide")),
        P(("groups", "wide")),
        P(("groups", "wide"), None, None, "tp"),
        P(("groups", "wide"), None, None, "tp"),
        P(("groups", "wide")),
        P(("groups", "wide"), None, "tp"),
        P(("groups", "wide"), None, None, "tp"),
        P(("groups", "wide"), None, "tp"),
        P(("groups", "wide"), None, None, "tp"),
    )
    out_specs = (P(("groups", "wide"), None, "tp"), P(("groups", "wide"), None, "tp"))
    return jax.shard_map(shards, mesh=mesh, in_specs=in_specs, out_specs=out_specs, check_vma=False)
```

```python
import functools
import math

import jax
import jax.numpy as jnp
from jax import lax
from jax.experimental import pallas as pl
from jax.experimental.pallas import tpu as pltpu
from jax.sharding import PartitionSpec as P

KVH = 4
HD = 128
HQ = 64
GROUP = HQ // KVH
STEPS = 2

NEGATIVE = -1e30
EMPTY = 1024.0
SCORE_SCALE = 1.0 / math.sqrt(HD)

BF16 = jnp.bfloat16
F32 = jnp.float32


def iota(shape, axis):
    return lax.broadcasted_iota(jnp.int32, shape, axis)


def over(x, n):
    return jnp.right_shift(x, n.bit_length() - 1) if n & (n - 1) == 0 else x // n


def mod(x, n):
    return jnp.bitwise_and(x, n - 1) if n & (n - 1) == 0 else x % n


def dot_nt(a, b):
    return lax.dot_general(a, b, (((1,), (1,)), ((), ())), preferred_element_type=F32)


def dot_nn(a, b):
    return lax.dot_general(a, b, (((1,), (0,)), ((), ())), preferred_element_type=F32)


def top_of(*parts):
    return functools.reduce(jnp.maximum, [jnp.max(p, axis=1, keepdims=True) for p in parts])


def sum_of(*parts):
    return functools.reduce(jnp.add, [jnp.sum(p, axis=1, keepdims=True) for p in parts])


def to_values(weights):
    tiles = [pltpu.roll(weights[:, c : c + HD], 1, 1) for c in range(0, weights.shape[1], HD)]
    return jnp.concatenate(tiles, axis=1).astype(BF16)


def values_up(rows):
    return pltpu.roll(rows.astype(F32), rows.shape[0] - 1, 0).astype(BF16)


def pack_kernel(
    tp, order, heads, block_rows, dest_hbm, blocks_hbm, codes_hbm, scales_hbm, send_ref,
    dest_ref, blocks_ref, codes_ref, scales_ref, sems,
):
    requests, all_rows = codes_ref.shape[:2]
    pairs = [
        (codes_hbm, codes_ref), (scales_hbm, scales_ref),
        (dest_hbm, dest_ref), (blocks_hbm, blocks_ref),
    ]
    copies = [pltpu.make_async_copy(a, b, sems.at[i]) for i, (a, b) in enumerate(pairs)]
    for copy in copies:
        copy.start()
    send_ref[...] = jnp.full(send_ref.shape, EMPTY, BF16)
    rows = all_rows // heads
    per_core = heads // tp
    row_block = over(iota((rows, HD), 0), block_rows)
    to_row = iota((all_rows, all_rows), 0)
    from_row = iota((all_rows, all_rows), 1)
    source = over(mod(to_row, rows), 2) * (2 * heads) + over(to_row, rows) * 2 + mod(to_row, 2)
    by_head = jnp.where(from_row == source, 1.0, 0.0).astype(BF16)
    for copy in copies:
        copy.wait()

    def place(r):
        there = dest_ref[r]
        spots = [there * tp + t for t in range(tp)]
        if order is not None:
            for t in range(tp):
                at = {core // tp: p for p, core in enumerate(order) if core % tp == t}
                spots[t] = functools.reduce(
                    jnp.add, [jnp.where(there == w, p, 0) for w, p in at.items()]
                )
        held = row_block < blocks_ref[r]
        codes = dot_nn(by_head, codes_ref[r])
        scales = scales_ref[r].astype(F32)
        for j in range(heads):
            values = codes[j * rows : (j + 1) * rows] * scales[:, j : j + 1]
            values = jnp.where(held, values, EMPTY).astype(BF16)
            send_ref[spots[j // per_core], j % per_core] = values

    if requests <= 8:
        for r in range(requests):
            place(r)
    else:
        pl.loop(0, requests)(place)


def resident_kernel(
    len_hbm, codes_hbm, scales_hbm, query_hbm, new_hbm, out_ref,
    len_ref, codes_ref, scales_ref, query_ref, new_ref, sems,
):
    pairs = [
        (query_hbm, query_ref), (new_hbm, new_ref), (scales_hbm, scales_ref),
        (len_hbm, len_ref), (codes_hbm, codes_ref),
    ]
    copies = [pltpu.make_async_copy(a, b, sems.at[i]) for i, (a, b) in enumerate(pairs)]
    for copy in copies:
        copy.start()
    slots, rows = codes_ref.shape[:2]
    heads = scales_ref.shape[2]
    tokens = rows // (2 * heads)
    queries = query_ref.shape[1]
    new_rows = new_ref.shape[0]

    row = iota((rows, HD), 0)
    source = (mod(row, 2) * heads + mod(over(row, 2), heads)) * tokens + over(row, 2 * heads)
    lane = iota((rows, HD), 1)
    spread = jnp.concatenate(
        [jnp.where(source == lane + c, 1.0, 0.0).astype(BF16) for c in range(0, rows, HD)],
        axis=1,
    )
    for copy in copies[:-1]:
        copy.wait()
    flat = jnp.concatenate(
        [scales_ref[:, p, h] for p in range(2) for h in range(heads)], axis=1
    )
    columns = dot_nt(spread, flat).astype(BF16)

    col = iota((queries, rows), 1)
    row_head = over(iota((queries, rows), 0), queries // heads)
    is_key = (mod(col, 2) == 0) & (mod(over(col, 2), heads) == row_head)
    col_token = jnp.where(is_key, over(col, 2 * heads), tokens)

    new_col = iota((queries, new_rows), 1)
    new_row = iota((queries, new_rows), 0)
    new_ok = (
        (mod(new_col, 2) == 0)
        & (mod(over(new_col, 2), heads) == over(new_row, queries // heads))
        & (mod(over(new_col, 2 * heads), STEPS) <= mod(new_row, STEPS))
    )
    new_slot = jnp.where(new_ok, over(new_col, 2 * heads * STEPS), slots)

    every = range(slots)
    new = new_ref[...]
    new_all = dot_nt(query_ref[...].reshape(slots * queries, HD), new)
    copies[-1].wait()
    caches = [codes_ref[s] * columns[:, s : s + 1] for s in every]
    scores = [dot_nt(query_ref[s], caches[s]) for s in every]
    scores = [jnp.where(col_token < len_ref[s], scores[s] * SCORE_SCALE, NEGATIVE) for s in every]
    new_scores = [
        jnp.where(new_slot == s, new_all[s * queries : (s + 1) * queries] * SCORE_SCALE, NEGATIVE)
        for s in every
    ]
    top = [top_of(scores[s], new_scores[s]) for s in every]
    weights = [jnp.exp(scores[s] - top[s]) for s in every]
    new_weights = [jnp.exp(new_scores[s] - top[s]) for s in every]
    total = [sum_of(weights[s], new_weights[s]) for s in every]
    new_mixed = dot_nn(jnp.concatenate(new_weights, axis=0).astype(BF16), values_up(new))
    mixed = [
        dot_nn(to_values(weights[s]), caches[s]) + new_mixed[s * queries : (s + 1) * queries]
        for s in every
    ]
    for s in every:
        out_ref[s] = (mixed[s] * (1.0 / total[s])).astype(BF16)


def slots_by_rows(got_ref, tp, order, block_rows):
    chunk_rows = got_ref.shape[2]
    blocks = chunk_rows // block_rows
    rows = [got_ref[k, 0].astype(F32) for k in range(len(order))]
    here = {
        core // tp: jnp.where(x[:1] < EMPTY, 1.0, 0.0)
        for core, x in zip(order, rows)
        if core % tp == 0
    }
    ranks = {
        w: sum([here[v] for v in here if v < w], jnp.zeros((1, HD), F32)) for w in here
    }
    lane = iota((1, HD), 1)
    block = over(lane, block_rows)
    block = jnp.where(mod(lane, 2) == 0, block, -1)
    per_tile = HD // chunk_rows
    tiles = []
    for start in range(0, len(order), per_tile):
        tile = jnp.full((1, HD), -1.0, F32)
        for i in range(per_tile):
            x, rank = rows[start + i], ranks[order[start + i] // tp]
            for b in range(blocks):
                at = b * block_rows
                value = jnp.where(x[at : at + 1] < EMPTY, rank, -1.0)
                tile = jnp.where(block == i * blocks + b, value, tile)
        tiles.append(tile)
    return jnp.concatenate(tiles, axis=1)


def slots_by_matmul(got_ref, tp):
    chunks, _, chunk_rows = got_ref.shape[:3]
    columns = chunks * chunk_rows
    sender_rows = tp * chunk_rows
    piece = min(columns, 256)
    sums = dot_nt(jnp.ones((16, HD), BF16), got_ref[:, 0].reshape(columns, HD))[:8]
    col = iota((8, columns), 1)
    held = sums < EMPTY
    first = jnp.where(held & (mod(col, sender_rows) == 0), 1.0, 0.0).astype(BF16)
    row = over(iota((piece, piece), 0), sender_rows)
    before = jnp.where(row < over(iota((piece, piece), 1), sender_rows), 1.0, 0.0).astype(BF16)
    base = jnp.zeros((8, 1), F32)
    ranks = []
    for p in range(0, columns, piece):
        part = first[:, p : p + piece]
        ranks.append(dot_nn(part, before) + base)
        base = base + jnp.sum(part.astype(F32), axis=1, keepdims=True)
    rank = jnp.concatenate(ranks, axis=1)
    return jnp.where(held & (mod(col, 2) == 0), rank, -1.0)[:1]


def arrival_kernel(
    tp, groups, order, block_rows, got_ref, query_ref, new_ref, out_ref
):
    step = pl.program_id(0) if groups > 1 else 0
    chunks, heads, chunk_rows = got_ref.shape[:3]
    slots, _, per_head = query_ref.shape[:3]
    rows = slots * per_head
    columns = chunks * chunk_rows
    every = range(heads)

    caches = [got_ref[:, h].reshape(columns, HD) for h in every]
    queries = [query_ref[:, h].reshape(rows, HD) for h in every]
    new = new_ref[...]
    scores = [dot_nt(queries[h], caches[h]) for h in every]
    new_all = dot_nt(jnp.concatenate(queries, axis=0), new)
    if order is None:
        slot_of = slots_by_matmul(got_ref, tp)
    else:
        slot_of = slots_by_rows(got_ref, tp, order, block_rows)
    first_slot = jnp.float32(step * slots)
    mine = [slot_of == first_slot + a for a in range(slots)]

    new_col = iota((rows, new.shape[0]), 1)
    new_row = iota((rows, new.shape[0]), 0)
    new_here = (
        (mod(new_col, 2) == 0)
        & (over(new_col, 2 * heads * STEPS) == over(new_row, per_head))
        & (mod(over(new_col, 2 * heads), STEPS) <= mod(new_row, STEPS))
    )
    new_head = jnp.where(new_here, mod(over(new_col, 2), heads), heads)

    scores = [
        jnp.concatenate(
            [
                jnp.where(mine[a], scores[h][a * per_head : (a + 1) * per_head] * SCORE_SCALE, NEGATIVE)
                for a in range(slots)
            ],
            axis=0,
        )
        for h in every
    ]
    new_scores = [
        jnp.where(new_head == h, new_all[h * rows : (h + 1) * rows] * SCORE_SCALE, NEGATIVE)
        for h in every
    ]
    top = [top_of(scores[h], new_scores[h]) for h in every]
    weights = [jnp.exp(scores[h] - top[h]) for h in every]
    new_weights = [jnp.exp(new_scores[h] - top[h]) for h in every]
    total = [sum_of(weights[h], new_weights[h]) for h in every]
    new_mixed = dot_nn(jnp.concatenate(new_weights, axis=0).astype(BF16), values_up(new))
    for h in every:
        mixed = dot_nn(to_values(weights[h]), caches[h]) + new_mixed[h * rows : (h + 1) * rows]
        out_ref[:, h] = (mixed * (1.0 / total[h])).astype(BF16).reshape(slots, per_head, HD)


def whole(memory_space=pltpu.VMEM):
    return pl.BlockSpec(memory_space=memory_space)


def in_hbm(x):
    return pltpu.with_memory_space_constraint(x, pltpu.HBM)


def limit(mib):
    return pltpu.CompilerParams(vmem_limit_bytes=mib * 2**20)


def pack(pre_codes, pre_scales, req_dest, req_blocks, peers, tp, order):
    requests, blocks, block_tokens = pre_codes.shape[:3]
    tokens = blocks * block_tokens
    codes = (
        pre_codes.reshape(requests, tokens, 2, KVH, HD)
        .transpose(0, 1, 3, 2, 4)
        .reshape(requests, tokens * KVH * 2, HD)
    )
    scales = pre_scales.reshape(requests, tokens * 2, KVH)
    ins = [req_dest, req_blocks, codes, scales]
    chunk = (KVH // tp, tokens * 2, HD)
    return pl.pallas_call(
        functools.partial(pack_kernel, tp, order, KVH, 2 * block_tokens),
        out_shape=jax.ShapeDtypeStruct((peers * tp,) + chunk, BF16),
        in_specs=[whole(pltpu.HBM)] * len(ins),
        out_specs=whole(),
        scratch_shapes=[
            pltpu.SMEM(req_dest.shape, jnp.int32),
            pltpu.SMEM(req_blocks.shape, jnp.int32),
            pltpu.VMEM(codes.shape, BF16),
            pltpu.VMEM(scales.shape, BF16),
            pltpu.SemaphoreType.DMA((len(ins),)),
        ],
        compiler_params=limit(24),
        name="pack",
    )(*[in_hbm(x) for x in ins])


def cache_rows(codes):
    slots, tokens, _, width = codes.shape
    heads = width // HD
    return (
        codes.reshape(slots, tokens, 2, heads, HD)
        .transpose(0, 1, 3, 2, 4)
        .reshape(slots, tokens * heads * 2, HD)
    )


def query_rows(query):
    slots, steps, width = query.shape
    return query.reshape(slots, steps, width // HD, HD).transpose(0, 2, 1, 3)


def new_rows_of(new):
    slots, steps, pair, width = new.shape
    heads = width // HD
    return (
        new.reshape(slots, steps, pair, heads, HD)
        .transpose(0, 1, 3, 2, 4)
        .reshape(slots * steps * heads * pair, HD)
    )


def from_rows(out, shape):
    slots, steps, width = shape
    return out.reshape(slots, width // HD, steps, HD).transpose(0, 2, 1, 3).reshape(shape)


def resident(codes, res_scales, res_len, res_query, res_new):
    slots, rows = codes.shape[:2]
    heads = res_scales.shape[-1]
    scales = res_scales.transpose(0, 2, 3, 1)
    query = query_rows(res_query).reshape(slots, heads * GROUP * STEPS, HD)
    ins = [res_len, codes, scales, query, new_rows_of(res_new)]
    work = query.shape[0] * query.shape[1] * rows
    return pl.pallas_call(
        resident_kernel,
        out_shape=jax.ShapeDtypeStruct(query.shape, BF16),
        in_specs=[whole(pltpu.HBM)] * len(ins),
        out_specs=whole(),
        scratch_shapes=[
            pltpu.SMEM(res_len.shape, jnp.int32),
            *[pltpu.VMEM(x.shape, BF16) for x in ins[1:]],
            pltpu.SemaphoreType.DMA((len(ins),)),
        ],
        cost_estimate=pl.CostEstimate(
            flops=4 * work * HD,
            bytes_accessed=2 * (codes.size + 2 * query.size),
            transcendentals=work,
        ),
        compiler_params=limit(16),
        name="resident",
    )(*[in_hbm(x) for x in ins])


def arrivals(got, arr_query, arr_new, tp, order, block_rows):
    slots, steps, width = arr_query.shape
    heads = width // (HD * GROUP)
    query = query_rows(arr_query).reshape(slots, heads, GROUP * steps, HD)
    new = new_rows_of(arr_new)
    size = max(n for n in range(1, 7) if slots % n == 0)
    groups = slots // size
    small = got.size <= 2**18

    def part(ref, rows):
        if groups == 1:
            return whole()
        return pl.BlockSpec((rows,) + ref.shape[1:], lambda i: (i,) + (0,) * (ref.ndim - 1))

    return pl.pallas_call(
        functools.partial(arrival_kernel, tp, groups, order, block_rows),
        out_shape=jax.ShapeDtypeStruct(query.shape, BF16),
        grid=(groups,) if groups > 1 else (),
        in_specs=[whole(), part(query, size), part(new, new.shape[0] // groups)],
        out_specs=part(query, size),
        compiler_params=limit(16 if small else 48),
        name="arrivals",
    )(got, query, new)


def shards(
    pre_codes,
    pre_scales,
    req_dest,
    req_blocks,
    res_codes,
    res_scales,
    res_len,
    res_query,
    res_new,
    arr_query,
    arr_new,
):
    peers = lax.axis_size("wide")
    tp = lax.axis_size("tp")
    order = None
    if peers * tp == 16:
        order = [10, 11, 12, 13, 14, 15, 3, 2, 1, 0, 4, 5, 6, 7, 8, 9]
    send = pack(pre_codes, pre_scales, req_dest, req_blocks, peers, tp, order)
    got = lax.all_to_all(
        send,
        ("wide", "tp"),
        split_axis=0,
        concat_axis=0,
        tiled=True,
        axis_index_groups=[order or list(range(peers * tp))],
    )
    res_out = resident(cache_rows(res_codes), res_scales, res_len, res_query, res_new)
    block_rows = 2 * pre_codes.shape[2]
    arr_out = arrivals(got, arr_query, arr_new, tp, order, block_rows)
    return (from_rows(res_out, res_query.shape), from_rows(arr_out, arr_query.shape))


def solution(mesh):
    in_specs = (
        P(("groups", "wide"), None, "tp", None, None),
        P(("groups", "wide"), None, "tp", None, None),
        P(("groups", "wide")),
        P(("groups", "wide")),
        P(("groups", "wide"), None, None, "tp"),
        P(("groups", "wide"), None, None, "tp"),
        P(("groups", "wide")),
        P(("groups", "wide"), None, "tp"),
        P(("groups", "wide"), None, None, "tp"),
        P(("groups", "wide"), None, "tp"),
        P(("groups", "wide"), None, None, "tp"),
    )
    out_specs = (P(("groups", "wide"), None, "tp"), P(("groups", "wide"), None, "tp"))
    return jax.shard_map(shards, mesh=mesh, in_specs=in_specs, out_specs=out_specs, check_vma=False)
```

```python
import functools
import math

import jax
import jax.numpy as jnp
from jax import lax
from jax.experimental import pallas as pl
from jax.experimental.pallas import tpu as pltpu
from jax.sharding import PartitionSpec as P

KVH = 4
HD = 128
HQ = 64
GROUP = HQ // KVH
STEPS = 2

NEGATIVE = -1e30
EMPTY = 1024.0
SCORE_SCALE = 1.0 / math.sqrt(HD)

BF16 = jnp.bfloat16
F32 = jnp.float32


def iota(shape, axis):
    return lax.broadcasted_iota(jnp.int32, shape, axis)


def over(x, n):
    return jnp.right_shift(x, n.bit_length() - 1) if n & (n - 1) == 0 else x // n


def mod(x, n):
    return jnp.bitwise_and(x, n - 1) if n & (n - 1) == 0 else x % n


def dot_nt(a, b):
    return lax.dot_general(a, b, (((1,), (1,)), ((), ())), preferred_element_type=F32)


def dot_nn(a, b):
    return lax.dot_general(a, b, (((1,), (0,)), ((), ())), preferred_element_type=F32)


def top_of(*parts):
    return functools.reduce(jnp.maximum, [jnp.max(p, axis=1, keepdims=True) for p in parts])


def sum_of(*parts):
    return functools.reduce(jnp.add, [jnp.sum(p, axis=1, keepdims=True) for p in parts])


def to_values(weights):
    tiles = [pltpu.roll(weights[:, c : c + HD], 1, 1) for c in range(0, weights.shape[1], HD)]
    return jnp.concatenate(tiles, axis=1).astype(BF16)


def values_up(rows):
    return pltpu.roll(rows.astype(F32), rows.shape[0] - 1, 0).astype(BF16)


def pack_kernel(
    tp, order, heads, block_rows, dest_hbm, blocks_hbm, codes_hbm, scales_hbm, send_ref,
    dest_ref, blocks_ref, codes_ref, scales_ref, sems,
):
    requests, all_rows = codes_ref.shape[:2]
    pairs = [
        (codes_hbm, codes_ref), (scales_hbm, scales_ref),
        (dest_hbm, dest_ref), (blocks_hbm, blocks_ref),
    ]
    copies = [pltpu.make_async_copy(a, b, sems.at[i]) for i, (a, b) in enumerate(pairs)]
    for copy in copies:
        copy.start()
    send_ref[...] = jnp.full(send_ref.shape, EMPTY, BF16)
    rows = all_rows // heads
    per_core = heads // tp
    row_block = over(iota((rows, HD), 0), block_rows)
    to_row = iota((all_rows, all_rows), 0)
    from_row = iota((all_rows, all_rows), 1)
    source = over(mod(to_row, rows), 2) * (2 * heads) + over(to_row, rows) * 2 + mod(to_row, 2)
    by_head = jnp.where(from_row == source, 1.0, 0.0).astype(BF16)
    for copy in copies:
        copy.wait()

    def place(r):
        there = dest_ref[r]
        spots = [there * tp + t for t in range(tp)]
        if order is not None:
            for t in range(tp):
                at = {core // tp: p for p, core in enumerate(order) if core % tp == t}
                spots[t] = functools.reduce(
                    jnp.add, [jnp.where(there == w, p, 0) for w, p in at.items()]
                )
        held = row_block < blocks_ref[r]
        codes = dot_nn(by_head, codes_ref[r])
        scales = scales_ref[r].astype(F32)
        for j in range(heads):
            values = codes[j * rows : (j + 1) * rows] * scales[:, j : j + 1]
            values = jnp.where(held, values, EMPTY).astype(BF16)
            send_ref[spots[j // per_core], j % per_core] = values

    if requests <= 8:
        for r in range(requests):
            place(r)
    else:
        pl.loop(0, requests)(place)


def resident_kernel(
    len_hbm, codes_hbm, scales_hbm, query_hbm, new_hbm, out_ref,
    len_ref, codes_ref, scales_ref, query_ref, new_ref, sems,
):
    pairs = [
        (query_hbm, query_ref), (new_hbm, new_ref), (scales_hbm, scales_ref),
        (len_hbm, len_ref), (codes_hbm, codes_ref),
    ]
    copies = [pltpu.make_async_copy(a, b, sems.at[i]) for i, (a, b) in enumerate(pairs)]
    for copy in copies:
        copy.start()
    slots, rows = codes_ref.shape[:2]
    heads = scales_ref.shape[2]
    tokens = rows // (2 * heads)
    queries = query_ref.shape[1]
    new_rows = new_ref.shape[0]

    row = iota((rows, HD), 0)
    source = (mod(row, 2) * heads + mod(over(row, 2), heads)) * tokens + over(row, 2 * heads)
    lane = iota((rows, HD), 1)
    spread = jnp.concatenate(
        [jnp.where(source == lane + c, 1.0, 0.0).astype(BF16) for c in range(0, rows, HD)],
        axis=1,
    )
    for copy in copies[:-1]:
        copy.wait()
    flat = jnp.concatenate(
        [scales_ref[:, p, h] for p in range(2) for h in range(heads)], axis=1
    )
    columns = dot_nt(spread, flat).astype(BF16)

    col = iota((queries, rows), 1)
    row_head = over(iota((queries, rows), 0), queries // heads)
    is_key = (mod(col, 2) == 0) & (mod(over(col, 2), heads) == row_head)
    col_token = jnp.where(is_key, over(col, 2 * heads), tokens)

    new_col = iota((queries, new_rows), 1)
    new_row = iota((queries, new_rows), 0)
    new_ok = (
        (mod(new_col, 2) == 0)
        & (mod(over(new_col, 2), heads) == over(new_row, queries // heads))
        & (mod(over(new_col, 2 * heads), STEPS) <= mod(new_row, STEPS))
    )
    new_slot = jnp.where(new_ok, over(new_col, 2 * heads * STEPS), slots)

    every = range(slots)
    new = new_ref[...]
    new_all = dot_nt(query_ref[...].reshape(slots * queries, HD), new)
    copies[-1].wait()
    caches = [codes_ref[s] * columns[:, s : s + 1] for s in every]
    scores = [dot_nt(query_ref[s], caches[s]) for s in every]
    scores = [jnp.where(col_token < len_ref[s], scores[s] * SCORE_SCALE, NEGATIVE) for s in every]
    new_scores = [
        jnp.where(new_slot == s, new_all[s * queries : (s + 1) * queries] * SCORE_SCALE, NEGATIVE)
        for s in every
    ]
    top = [top_of(scores[s], new_scores[s]) for s in every]
    weights = [jnp.exp(scores[s] - top[s]) for s in every]
    new_weights = [jnp.exp(new_scores[s] - top[s]) for s in every]
    total = [sum_of(weights[s], new_weights[s]) for s in every]
    new_mixed = dot_nn(jnp.concatenate(new_weights, axis=0).astype(BF16), values_up(new))
    mixed = [
        dot_nn(to_values(weights[s]), caches[s]) + new_mixed[s * queries : (s + 1) * queries]
        for s in every
    ]
    for s in every:
        out_ref[s] = (mixed[s] * (1.0 / total[s])).astype(BF16)


def slots_by_rows(got_ref, tp, order, block_rows):
    chunk_rows = got_ref.shape[2]
    blocks = chunk_rows // block_rows
    rows = [got_ref[k, 0].astype(F32) for k in range(len(order))]
    here = {
        core // tp: jnp.where(x[:1] < EMPTY, 1.0, 0.0)
        for core, x in zip(order, rows)
        if core % tp == 0
    }
    ranks = {
        w: sum([here[v] for v in here if v < w], jnp.zeros((1, HD), F32)) for w in here
    }
    lane = iota((1, HD), 1)
    block = over(lane, block_rows)
    block = jnp.where(mod(lane, 2) == 0, block, -1)
    per_tile = HD // chunk_rows
    tiles = []
    for start in range(0, len(order), per_tile):
        tile = jnp.full((1, HD), -1.0, F32)
        for i in range(per_tile):
            x, rank = rows[start + i], ranks[order[start + i] // tp]
            for b in range(blocks):
                at = b * block_rows
                value = jnp.where(x[at : at + 1] < EMPTY, rank, -1.0)
                tile = jnp.where(block == i * blocks + b, value, tile)
        tiles.append(tile)
    return jnp.concatenate(tiles, axis=1)


def slots_by_matmul(got_ref, tp):
    chunks, _, chunk_rows = got_ref.shape[:3]
    columns = chunks * chunk_rows
    sender_rows = tp * chunk_rows
    piece = min(columns, 256)
    sums = dot_nt(jnp.ones((16, HD), BF16), got_ref[:, 0].reshape(columns, HD))[:8]
    col = iota((8, columns), 1)
    held = sums < EMPTY
    first = jnp.where(held & (mod(col, sender_rows) == 0), 1.0, 0.0).astype(BF16)
    row = over(iota((piece, piece), 0), sender_rows)
    before = jnp.where(row < over(iota((piece, piece), 1), sender_rows), 1.0, 0.0).astype(BF16)
    base = jnp.zeros((8, 1), F32)
    ranks = []
    for p in range(0, columns, piece):
        part = first[:, p : p + piece]
        ranks.append(dot_nn(part, before) + base)
        base = base + jnp.sum(part.astype(F32), axis=1, keepdims=True)
    rank = jnp.concatenate(ranks, axis=1)
    return jnp.where(held & (mod(col, 2) == 0), rank, -1.0)[:1]


def arrival_kernel(
    tp, groups, order, block_rows, got_ref, query_ref, new_ref, out_ref
):
    step = pl.program_id(0) if groups > 1 else 0
    chunks, heads, chunk_rows = got_ref.shape[:3]
    slots, _, per_head = query_ref.shape[:3]
    rows = slots * per_head
    columns = chunks * chunk_rows
    every = range(heads)

    caches = [got_ref[:, h].reshape(columns, HD) for h in every]
    queries = [query_ref[:, h].reshape(rows, HD) for h in every]
    new = new_ref[...]
    scores = [dot_nt(queries[h], caches[h]) for h in every]
    new_all = dot_nt(jnp.concatenate(queries, axis=0), new)
    if order is None:
        slot_of = slots_by_matmul(got_ref, tp)
    else:
        slot_of = slots_by_rows(got_ref, tp, order, block_rows)
    first_slot = jnp.float32(step * slots)
    mine = [slot_of == first_slot + a for a in range(slots)]

    new_col = iota((rows, new.shape[0]), 1)
    new_row = iota((rows, new.shape[0]), 0)
    new_here = (
        (mod(new_col, 2) == 0)
        & (over(new_col, 2 * heads * STEPS) == over(new_row, per_head))
        & (mod(over(new_col, 2 * heads), STEPS) <= mod(new_row, STEPS))
    )
    new_head = jnp.where(new_here, mod(over(new_col, 2), heads), heads)

    scores = [
        jnp.concatenate(
            [
                jnp.where(mine[a], scores[h][a * per_head : (a + 1) * per_head] * SCORE_SCALE, NEGATIVE)
                for a in range(slots)
            ],
            axis=0,
        )
        for h in every
    ]
    new_scores = [
        jnp.where(new_head == h, new_all[h * rows : (h + 1) * rows] * SCORE_SCALE, NEGATIVE)
        for h in every
    ]
    top = [top_of(scores[h], new_scores[h]) for h in every]
    weights = [jnp.exp(scores[h] - top[h]) for h in every]
    new_weights = [jnp.exp(new_scores[h] - top[h]) for h in every]
    total = [sum_of(weights[h], new_weights[h]) for h in every]
    new_mixed = dot_nn(jnp.concatenate(new_weights, axis=0).astype(BF16), values_up(new))
    for h in every:
        mixed = dot_nn(to_values(weights[h]), caches[h]) + new_mixed[h * rows : (h + 1) * rows]
        out_ref[:, h] = (mixed * (1.0 / total[h])).astype(BF16).reshape(slots, per_head, HD)


def whole(memory_space=pltpu.VMEM):
    return pl.BlockSpec(memory_space=memory_space)


def in_hbm(x):
    return pltpu.with_memory_space_constraint(x, pltpu.HBM)


def limit(mib):
    return pltpu.CompilerParams(vmem_limit_bytes=mib * 2**20)


def pack(pre_codes, pre_scales, req_dest, req_blocks, peers, tp, order):
    requests, blocks, block_tokens = pre_codes.shape[:3]
    tokens = blocks * block_tokens
    codes = (
        pre_codes.reshape(requests, tokens, 2, KVH, HD)
        .transpose(0, 1, 3, 2, 4)
        .reshape(requests, tokens * KVH * 2, HD)
    )
    scales = pre_scales.reshape(requests, tokens * 2, KVH)
    ins = [req_dest, req_blocks, codes, scales]
    chunk = (KVH // tp, tokens * 2, HD)
    return pl.pallas_call(
        functools.partial(pack_kernel, tp, order, KVH, 2 * block_tokens),
        out_shape=jax.ShapeDtypeStruct((peers * tp,) + chunk, BF16),
        in_specs=[whole(pltpu.HBM)] * len(ins),
        out_specs=whole(),
        scratch_shapes=[
            pltpu.SMEM(req_dest.shape, jnp.int32),
            pltpu.SMEM(req_blocks.shape, jnp.int32),
            pltpu.VMEM(codes.shape, BF16),
            pltpu.VMEM(scales.shape, BF16),
            pltpu.SemaphoreType.DMA((len(ins),)),
        ],
        compiler_params=limit(24),
        name="pack",
    )(*[in_hbm(x) for x in ins])


def cache_rows(codes):
    slots, tokens, _, width = codes.shape
    heads = width // HD
    return (
        codes.reshape(slots, tokens, 2, heads, HD)
        .transpose(0, 1, 3, 2, 4)
        .reshape(slots, tokens * heads * 2, HD)
    )


def query_rows(query):
    slots, steps, width = query.shape
    return query.reshape(slots, steps, width // HD, HD).transpose(0, 2, 1, 3)


def new_rows_of(new):
    slots, steps, pair, width = new.shape
    heads = width // HD
    return (
        new.reshape(slots, steps, pair, heads, HD)
        .transpose(0, 1, 3, 2, 4)
        .reshape(slots * steps * heads * pair, HD)
    )


def from_rows(out, shape):
    slots, steps, width = shape
    return out.reshape(slots, width // HD, steps, HD).transpose(0, 2, 1, 3).reshape(shape)


def resident(codes, res_scales, res_len, res_query, res_new):
    slots, rows = codes.shape[:2]
    heads = res_scales.shape[-1]
    scales = res_scales.transpose(0, 2, 3, 1)
    query = query_rows(res_query).reshape(slots, heads * GROUP * STEPS, HD)
    ins = [res_len, codes, scales, query, new_rows_of(res_new)]
    work = query.shape[0] * query.shape[1] * rows
    return pl.pallas_call(
        resident_kernel,
        out_shape=jax.ShapeDtypeStruct(query.shape, BF16),
        in_specs=[whole(pltpu.HBM)] * len(ins),
        out_specs=whole(),
        scratch_shapes=[
            pltpu.SMEM(res_len.shape, jnp.int32),
            *[pltpu.VMEM(x.shape, BF16) for x in ins[1:]],
            pltpu.SemaphoreType.DMA((len(ins),)),
        ],
        cost_estimate=pl.CostEstimate(
            flops=4 * work * HD,
            bytes_accessed=2 * (codes.size + 2 * query.size),
            transcendentals=work,
        ),
        compiler_params=limit(16),
        name="resident",
    )(*[in_hbm(x) for x in ins])


def arrivals(got, arr_query, arr_new, tp, order, block_rows):
    slots, steps, width = arr_query.shape
    heads = width // (HD * GROUP)
    query = query_rows(arr_query).reshape(slots, heads, GROUP * steps, HD)
    new = new_rows_of(arr_new)
    size = max(n for n in range(1, 7) if slots % n == 0)
    groups = slots // size
    small = got.size <= 2**18

    def part(ref, rows):
        if groups == 1:
            return whole()
        return pl.BlockSpec((rows,) + ref.shape[1:], lambda i: (i,) + (0,) * (ref.ndim - 1))

    return pl.pallas_call(
        functools.partial(arrival_kernel, tp, groups, order, block_rows),
        out_shape=jax.ShapeDtypeStruct(query.shape, BF16),
        grid=(groups,) if groups > 1 else (),
        in_specs=[whole(), part(query, size), part(new, new.shape[0] // groups)],
        out_specs=part(query, size),
        compiler_params=limit(16 if small else 48),
        name="arrivals",
    )(got, query, new)


def shards(
    pre_codes,
    pre_scales,
    req_dest,
    req_blocks,
    res_codes,
    res_scales,
    res_len,
    res_query,
    res_new,
    arr_query,
    arr_new,
):
    peers = lax.axis_size("wide")
    tp = lax.axis_size("tp")
    order = None
    if peers * tp == 16:
        order = [11, 10, 13, 12, 15, 14, 3, 2, 1, 0, 4, 5, 6, 7, 9, 8]
    send = pack(pre_codes, pre_scales, req_dest, req_blocks, peers, tp, order)
    got = lax.all_to_all(
        send,
        ("wide", "tp"),
        split_axis=0,
        concat_axis=0,
        tiled=True,
        axis_index_groups=[order or list(range(peers * tp))],
    )
    res_out = resident(cache_rows(res_codes), res_scales, res_len, res_query, res_new)
    block_rows = 2 * pre_codes.shape[2]
    arr_out = arrivals(got, arr_query, arr_new, tp, order, block_rows)
    return (from_rows(res_out, res_query.shape), from_rows(arr_out, arr_query.shape))


def solution(mesh):
    in_specs = (
        P(("groups", "wide"), None, "tp", None, None),
        P(("groups", "wide"), None, "tp", None, None),
        P(("groups", "wide")),
        P(("groups", "wide")),
        P(("groups", "wide"), None, None, "tp"),
        P(("groups", "wide"), None, None, "tp"),
        P(("groups", "wide")),
        P(("groups", "wide"), None, "tp"),
        P(("groups", "wide"), None, None, "tp"),
        P(("groups", "wide"), None, "tp"),
        P(("groups", "wide"), None, None, "tp"),
    )
    out_specs = (P(("groups", "wide"), None, "tp"), P(("groups", "wide"), None, "tp"))
    return jax.shard_map(shards, mesh=mesh, in_specs=in_specs, out_specs=out_specs, check_vma=False)
```

```python
import functools
import math

import jax
import jax.numpy as jnp
from jax import lax
from jax.experimental import pallas as pl
from jax.experimental.pallas import tpu as pltpu
from jax.sharding import PartitionSpec as P

KVH = 4
HD = 128
HQ = 64
GROUP = HQ // KVH
STEPS = 2

NEGATIVE = -1e30
EMPTY = 1024.0
SCORE_SCALE = 1.0 / math.sqrt(HD)

BF16 = jnp.bfloat16
F32 = jnp.float32


def iota(shape, axis):
    return lax.broadcasted_iota(jnp.int32, shape, axis)


def over(x, n):
    return jnp.right_shift(x, n.bit_length() - 1) if n & (n - 1) == 0 else x // n


def mod(x, n):
    return jnp.bitwise_and(x, n - 1) if n & (n - 1) == 0 else x % n


def dot_nt(a, b):
    return lax.dot_general(a, b, (((1,), (1,)), ((), ())), preferred_element_type=F32)


def dot_nn(a, b):
    return lax.dot_general(a, b, (((1,), (0,)), ((), ())), preferred_element_type=F32)


def top_of(*parts):
    return functools.reduce(jnp.maximum, [jnp.max(p, axis=1, keepdims=True) for p in parts])


def sum_of(*parts):
    return functools.reduce(jnp.add, [jnp.sum(p, axis=1, keepdims=True) for p in parts])


def to_values(weights):
    tiles = [pltpu.roll(weights[:, c : c + HD], 1, 1) for c in range(0, weights.shape[1], HD)]
    return jnp.concatenate(tiles, axis=1).astype(BF16)


def values_up(rows):
    return pltpu.roll(rows.astype(F32), rows.shape[0] - 1, 0).astype(BF16)


def pack_kernel(
    tp, order, heads, block_rows, dest_hbm, blocks_hbm, codes_hbm, scales_hbm, send_ref,
    dest_ref, blocks_ref, codes_ref, scales_ref, sems,
):
    requests, all_rows = codes_ref.shape[:2]
    pairs = [
        (codes_hbm, codes_ref), (scales_hbm, scales_ref),
        (dest_hbm, dest_ref), (blocks_hbm, blocks_ref),
    ]
    copies = [pltpu.make_async_copy(a, b, sems.at[i]) for i, (a, b) in enumerate(pairs)]
    for copy in copies:
        copy.start()
    send_ref[...] = jnp.full(send_ref.shape, EMPTY, BF16)
    rows = all_rows // heads
    per_core = heads // tp
    row_block = over(iota((rows, HD), 0), block_rows)
    to_row = iota((all_rows, all_rows), 0)
    from_row = iota((all_rows, all_rows), 1)
    source = over(mod(to_row, rows), 2) * (2 * heads) + over(to_row, rows) * 2 + mod(to_row, 2)
    by_head = jnp.where(from_row == source, 1.0, 0.0).astype(BF16)
    for copy in copies:
        copy.wait()

    def place(r):
        there = dest_ref[r]
        spots = [there * tp + t for t in range(tp)]
        if order is not None:
            for t in range(tp):
                at = {core // tp: p for p, core in enumerate(order) if core % tp == t}
                spots[t] = functools.reduce(
                    jnp.add, [jnp.where(there == w, p, 0) for w, p in at.items()]
                )
        held = row_block < blocks_ref[r]
        codes = dot_nn(by_head, codes_ref[r])
        scales = scales_ref[r].astype(F32)
        for j in range(heads):
            values = codes[j * rows : (j + 1) * rows] * scales[:, j : j + 1]
            values = jnp.where(held, values, EMPTY).astype(BF16)
            send_ref[spots[j // per_core], j % per_core] = values

    if requests <= 8:
        for r in range(requests):
            place(r)
    else:
        pl.loop(0, requests)(place)


def resident_kernel(
    len_hbm, codes_hbm, scales_hbm, query_hbm, new_hbm, out_ref,
    len_ref, codes_ref, scales_ref, query_ref, new_ref, sems,
):
    pairs = [
        (query_hbm, query_ref), (new_hbm, new_ref), (scales_hbm, scales_ref),
        (len_hbm, len_ref), (codes_hbm, codes_ref),
    ]
    copies = [pltpu.make_async_copy(a, b, sems.at[i]) for i, (a, b) in enumerate(pairs)]
    for copy in copies:
        copy.start()
    slots, rows = codes_ref.shape[:2]
    heads = scales_ref.shape[2]
    tokens = rows // (2 * heads)
    queries = query_ref.shape[1]
    new_rows = new_ref.shape[0]

    row = iota((rows, HD), 0)
    source = (mod(row, 2) * heads + mod(over(row, 2), heads)) * tokens + over(row, 2 * heads)
    lane = iota((rows, HD), 1)
    spread = jnp.concatenate(
        [jnp.where(source == lane + c, 1.0, 0.0).astype(BF16) for c in range(0, rows, HD)],
        axis=1,
    )
    for copy in copies[:-1]:
        copy.wait()
    flat = jnp.concatenate(
        [scales_ref[:, p, h] for p in range(2) for h in range(heads)], axis=1
    )
    columns = dot_nt(spread, flat).astype(BF16)

    col = iota((queries, rows), 1)
    row_head = over(iota((queries, rows), 0), queries // heads)
    is_key = (mod(col, 2) == 0) & (mod(over(col, 2), heads) == row_head)
    col_token = jnp.where(is_key, over(col, 2 * heads), tokens)

    new_col = iota((queries, new_rows), 1)
    new_row = iota((queries, new_rows), 0)
    new_ok = (
        (mod(new_col, 2) == 0)
        & (mod(over(new_col, 2), heads) == over(new_row, queries // heads))
        & (mod(over(new_col, 2 * heads), STEPS) <= mod(new_row, STEPS))
    )
    new_slot = jnp.where(new_ok, over(new_col, 2 * heads * STEPS), slots)

    every = range(slots)
    new = new_ref[...]
    new_all = dot_nt(query_ref[...].reshape(slots * queries, HD), new)
    copies[-1].wait()
    caches = [codes_ref[s] * columns[:, s : s + 1] for s in every]
    scores = [dot_nt(query_ref[s], caches[s]) for s in every]
    scores = [jnp.where(col_token < len_ref[s], scores[s] * SCORE_SCALE, NEGATIVE) for s in every]
    new_scores = [
        jnp.where(new_slot == s, new_all[s * queries : (s + 1) * queries] * SCORE_SCALE, NEGATIVE)
        for s in every
    ]
    top = [top_of(scores[s], new_scores[s]) for s in every]
    weights = [jnp.exp(scores[s] - top[s]) for s in every]
    new_weights = [jnp.exp(new_scores[s] - top[s]) for s in every]
    total = [sum_of(weights[s], new_weights[s]) for s in every]
    new_mixed = dot_nn(jnp.concatenate(new_weights, axis=0).astype(BF16), values_up(new))
    mixed = [
        dot_nn(to_values(weights[s]), caches[s]) + new_mixed[s * queries : (s + 1) * queries]
        for s in every
    ]
    for s in every:
        out_ref[s] = (mixed[s] * (1.0 / total[s])).astype(BF16)


def slots_by_rows(got_ref, tp, order, block_rows):
    chunk_rows = got_ref.shape[2]
    blocks = chunk_rows // block_rows
    rows = [got_ref[k, 0].astype(F32) for k in range(len(order))]
    here = {
        core // tp: jnp.where(x[:1] < EMPTY, 1.0, 0.0)
        for core, x in zip(order, rows)
        if core % tp == 0
    }
    ranks = {
        w: sum([here[v] for v in here if v < w], jnp.zeros((1, HD), F32)) for w in here
    }
    lane = iota((1, HD), 1)
    block = over(lane, block_rows)
    block = jnp.where(mod(lane, 2) == 0, block, -1)
    per_tile = HD // chunk_rows
    tiles = []
    for start in range(0, len(order), per_tile):
        tile = jnp.full((1, HD), -1.0, F32)
        for i in range(per_tile):
            x, rank = rows[start + i], ranks[order[start + i] // tp]
            for b in range(blocks):
                at = b * block_rows
                value = jnp.where(x[at : at + 1] < EMPTY, rank, -1.0)
                tile = jnp.where(block == i * blocks + b, value, tile)
        tiles.append(tile)
    return jnp.concatenate(tiles, axis=1)


def slots_by_matmul(got_ref, tp):
    chunks, _, chunk_rows = got_ref.shape[:3]
    columns = chunks * chunk_rows
    sender_rows = tp * chunk_rows
    piece = min(columns, 256)
    sums = dot_nt(jnp.ones((16, HD), BF16), got_ref[:, 0].reshape(columns, HD))[:8]
    col = iota((8, columns), 1)
    held = sums < EMPTY
    first = jnp.where(held & (mod(col, sender_rows) == 0), 1.0, 0.0).astype(BF16)
    row = over(iota((piece, piece), 0), sender_rows)
    before = jnp.where(row < over(iota((piece, piece), 1), sender_rows), 1.0, 0.0).astype(BF16)
    base = jnp.zeros((8, 1), F32)
    ranks = []
    for p in range(0, columns, piece):
        part = first[:, p : p + piece]
        ranks.append(dot_nn(part, before) + base)
        base = base + jnp.sum(part.astype(F32), axis=1, keepdims=True)
    rank = jnp.concatenate(ranks, axis=1)
    return jnp.where(held & (mod(col, 2) == 0), rank, -1.0)[:1]


def arrival_kernel(
    tp, groups, order, block_rows, got_ref, query_ref, new_ref, out_ref
):
    step = pl.program_id(0) if groups > 1 else 0
    chunks, heads, chunk_rows = got_ref.shape[:3]
    slots, _, per_head = query_ref.shape[:3]
    rows = slots * per_head
    columns = chunks * chunk_rows
    every = range(heads)

    caches = [got_ref[:, h].reshape(columns, HD) for h in every]
    queries = [query_ref[:, h].reshape(rows, HD) for h in every]
    new = new_ref[...]
    scores = [dot_nt(queries[h], caches[h]) for h in every]
    new_all = dot_nt(jnp.concatenate(queries, axis=0), new)
    if order is None:
        slot_of = slots_by_matmul(got_ref, tp)
    else:
        slot_of = slots_by_rows(got_ref, tp, order, block_rows)
    first_slot = jnp.float32(step * slots)
    mine = [slot_of == first_slot + a for a in range(slots)]

    new_col = iota((rows, new.shape[0]), 1)
    new_row = iota((rows, new.shape[0]), 0)
    new_here = (
        (mod(new_col, 2) == 0)
        & (over(new_col, 2 * heads * STEPS) == over(new_row, per_head))
        & (mod(over(new_col, 2 * heads), STEPS) <= mod(new_row, STEPS))
    )
    new_head = jnp.where(new_here, mod(over(new_col, 2), heads), heads)

    scores = [
        jnp.concatenate(
            [
                jnp.where(mine[a], scores[h][a * per_head : (a + 1) * per_head] * SCORE_SCALE, NEGATIVE)
                for a in range(slots)
            ],
            axis=0,
        )
        for h in every
    ]
    new_scores = [
        jnp.where(new_head == h, new_all[h * rows : (h + 1) * rows] * SCORE_SCALE, NEGATIVE)
        for h in every
    ]
    top = [top_of(scores[h], new_scores[h]) for h in every]
    weights = [jnp.exp(scores[h] - top[h]) for h in every]
    new_weights = [jnp.exp(new_scores[h] - top[h]) for h in every]
    total = [sum_of(weights[h], new_weights[h]) for h in every]
    new_mixed = dot_nn(jnp.concatenate(new_weights, axis=0).astype(BF16), values_up(new))
    for h in every:
        mixed = dot_nn(to_values(weights[h]), caches[h]) + new_mixed[h * rows : (h + 1) * rows]
        out_ref[:, h] = (mixed * (1.0 / total[h])).astype(BF16).reshape(slots, per_head, HD)


def whole(memory_space=pltpu.VMEM):
    return pl.BlockSpec(memory_space=memory_space)


def in_hbm(x):
    return pltpu.with_memory_space_constraint(x, pltpu.HBM)


def limit(mib):
    return pltpu.CompilerParams(vmem_limit_bytes=mib * 2**20)


def pack(pre_codes, pre_scales, req_dest, req_blocks, peers, tp, order):
    requests, blocks, block_tokens = pre_codes.shape[:3]
    tokens = blocks * block_tokens
    codes = (
        pre_codes.reshape(requests, tokens, 2, KVH, HD)
        .transpose(0, 1, 3, 2, 4)
        .reshape(requests, tokens * KVH * 2, HD)
    )
    scales = pre_scales.reshape(requests, tokens * 2, KVH)
    ins = [req_dest, req_blocks, codes, scales]
    chunk = (KVH // tp, tokens * 2, HD)
    return pl.pallas_call(
        functools.partial(pack_kernel, tp, order, KVH, 2 * block_tokens),
        out_shape=jax.ShapeDtypeStruct((peers * tp,) + chunk, BF16),
        in_specs=[whole(pltpu.HBM)] * len(ins),
        out_specs=whole(),
        scratch_shapes=[
            pltpu.SMEM(req_dest.shape, jnp.int32),
            pltpu.SMEM(req_blocks.shape, jnp.int32),
            pltpu.VMEM(codes.shape, BF16),
            pltpu.VMEM(scales.shape, BF16),
            pltpu.SemaphoreType.DMA((len(ins),)),
        ],
        compiler_params=limit(24),
        name="pack",
    )(*[in_hbm(x) for x in ins])


def cache_rows(codes):
    slots, tokens, _, width = codes.shape
    heads = width // HD
    return (
        codes.reshape(slots, tokens, 2, heads, HD)
        .transpose(0, 1, 3, 2, 4)
        .reshape(slots, tokens * heads * 2, HD)
    )


def query_rows(query):
    slots, steps, width = query.shape
    return query.reshape(slots, steps, width // HD, HD).transpose(0, 2, 1, 3)


def new_rows_of(new):
    slots, steps, pair, width = new.shape
    heads = width // HD
    return (
        new.reshape(slots, steps, pair, heads, HD)
        .transpose(0, 1, 3, 2, 4)
        .reshape(slots * steps * heads * pair, HD)
    )


def from_rows(out, shape):
    slots, steps, width = shape
    return out.reshape(slots, width // HD, steps, HD).transpose(0, 2, 1, 3).reshape(shape)


def resident(codes, res_scales, res_len, res_query, res_new):
    slots, rows = codes.shape[:2]
    heads = res_scales.shape[-1]
    scales = res_scales.transpose(0, 2, 3, 1)
    query = query_rows(res_query).reshape(slots, heads * GROUP * STEPS, HD)
    ins = [res_len, codes, scales, query, new_rows_of(res_new)]
    work = query.shape[0] * query.shape[1] * rows
    return pl.pallas_call(
        resident_kernel,
        out_shape=jax.ShapeDtypeStruct(query.shape, BF16),
        in_specs=[whole(pltpu.HBM)] * len(ins),
        out_specs=whole(),
        scratch_shapes=[
            pltpu.SMEM(res_len.shape, jnp.int32),
            *[pltpu.VMEM(x.shape, BF16) for x in ins[1:]],
            pltpu.SemaphoreType.DMA((len(ins),)),
        ],
        cost_estimate=pl.CostEstimate(
            flops=4 * work * HD,
            bytes_accessed=2 * (codes.size + 2 * query.size),
            transcendentals=work,
        ),
        compiler_params=limit(16),
        name="resident",
    )(*[in_hbm(x) for x in ins])


def arrivals(got, arr_query, arr_new, tp, order, block_rows):
    slots, steps, width = arr_query.shape
    heads = width // (HD * GROUP)
    query = query_rows(arr_query).reshape(slots, heads, GROUP * steps, HD)
    new = new_rows_of(arr_new)
    size = max(n for n in range(1, 7) if slots % n == 0)
    groups = slots // size
    small = got.size <= 2**18

    def part(ref, rows):
        if groups == 1:
            return whole()
        return pl.BlockSpec((rows,) + ref.shape[1:], lambda i: (i,) + (0,) * (ref.ndim - 1))

    return pl.pallas_call(
        functools.partial(arrival_kernel, tp, groups, order, block_rows),
        out_shape=jax.ShapeDtypeStruct(query.shape, BF16),
        grid=(groups,) if groups > 1 else (),
        in_specs=[whole(), part(query, size), part(new, new.shape[0] // groups)],
        out_specs=part(query, size),
        compiler_params=limit(16 if small else 48),
        name="arrivals",
    )(got, query, new)


def shards(
    pre_codes,
    pre_scales,
    req_dest,
    req_blocks,
    res_codes,
    res_scales,
    res_len,
    res_query,
    res_new,
    arr_query,
    arr_new,
):
    peers = lax.axis_size("wide")
    tp = lax.axis_size("tp")
    order = None
    if peers * tp == 16:
        order = [11, 10, 12, 13, 14, 15, 3, 2, 1, 0, 5, 4, 7, 6, 9, 8]
    send = pack(pre_codes, pre_scales, req_dest, req_blocks, peers, tp, order)
    got = lax.all_to_all(
        send,
        ("wide", "tp"),
        split_axis=0,
        concat_axis=0,
        tiled=True,
        axis_index_groups=[order or list(range(peers * tp))],
    )
    res_out = resident(cache_rows(res_codes), res_scales, res_len, res_query, res_new)
    block_rows = 2 * pre_codes.shape[2]
    arr_out = arrivals(got, arr_query, arr_new, tp, order, block_rows)
    return (from_rows(res_out, res_query.shape), from_rows(arr_out, arr_query.shape))


def solution(mesh):
    in_specs = (
        P(("groups", "wide"), None, "tp", None, None),
        P(("groups", "wide"), None, "tp", None, None),
        P(("groups", "wide")),
        P(("groups", "wide")),
        P(("groups", "wide"), None, None, "tp"),
        P(("groups", "wide"), None, None, "tp"),
        P(("groups", "wide")),
        P(("groups", "wide"), None, "tp"),
        P(("groups", "wide"), None, None, "tp"),
        P(("groups", "wide"), None, "tp"),
        P(("groups", "wide"), None, None, "tp"),
    )
    out_specs = (P(("groups", "wide"), None, "tp"), P(("groups", "wide"), None, "tp"))
    return jax.shard_map(shards, mesh=mesh, in_specs=in_specs, out_specs=out_specs, check_vma=False)
```

```python
import functools
import math

import jax
import jax.numpy as jnp
from jax import lax
from jax.experimental import pallas as pl
from jax.experimental.pallas import tpu as pltpu
from jax.sharding import PartitionSpec as P

KVH = 4
HD = 128
HQ = 64
GROUP = HQ // KVH
STEPS = 2

NEGATIVE = -1e30
EMPTY = 1024.0
SCORE_SCALE = 1.0 / math.sqrt(HD)

BF16 = jnp.bfloat16
F32 = jnp.float32


def iota(shape, axis):
    return lax.broadcasted_iota(jnp.int32, shape, axis)


def over(x, n):
    return jnp.right_shift(x, n.bit_length() - 1) if n & (n - 1) == 0 else x // n


def mod(x, n):
    return jnp.bitwise_and(x, n - 1) if n & (n - 1) == 0 else x % n


def dot_nt(a, b):
    return lax.dot_general(a, b, (((1,), (1,)), ((), ())), preferred_element_type=F32)


def dot_nn(a, b):
    return lax.dot_general(a, b, (((1,), (0,)), ((), ())), preferred_element_type=F32)


def top_of(*parts):
    return functools.reduce(jnp.maximum, [jnp.max(p, axis=1, keepdims=True) for p in parts])


def sum_of(*parts):
    return functools.reduce(jnp.add, [jnp.sum(p, axis=1, keepdims=True) for p in parts])


def to_values(weights):
    tiles = [pltpu.roll(weights[:, c : c + HD], 1, 1) for c in range(0, weights.shape[1], HD)]
    return jnp.concatenate(tiles, axis=1).astype(BF16)


def values_up(rows):
    return pltpu.roll(rows.astype(F32), rows.shape[0] - 1, 0).astype(BF16)


def pack_kernel(
    tp, order, heads, block_rows, dest_hbm, blocks_hbm, codes_hbm, scales_hbm, send_ref,
    dest_ref, blocks_ref, codes_ref, scales_ref, sems,
):
    requests, all_rows = codes_ref.shape[:2]
    pairs = [
        (codes_hbm, codes_ref), (scales_hbm, scales_ref),
        (dest_hbm, dest_ref), (blocks_hbm, blocks_ref),
    ]
    copies = [pltpu.make_async_copy(a, b, sems.at[i]) for i, (a, b) in enumerate(pairs)]
    for copy in copies:
        copy.start()
    send_ref[...] = jnp.full(send_ref.shape, EMPTY, BF16)
    rows = all_rows // heads
    per_core = heads // tp
    row_block = over(iota((rows, HD), 0), block_rows)
    to_row = iota((all_rows, all_rows), 0)
    from_row = iota((all_rows, all_rows), 1)
    source = over(mod(to_row, rows), 2) * (2 * heads) + over(to_row, rows) * 2 + mod(to_row, 2)
    by_head = jnp.where(from_row == source, 1.0, 0.0).astype(BF16)
    for copy in copies:
        copy.wait()

    def place(r):
        there = dest_ref[r]
        spots = [there * tp + t for t in range(tp)]
        if order is not None:
            for t in range(tp):
                at = {core // tp: p for p, core in enumerate(order) if core % tp == t}
                spots[t] = functools.reduce(
                    jnp.add, [jnp.where(there == w, p, 0) for w, p in at.items()]
                )
        held = row_block < blocks_ref[r]
        codes = dot_nn(by_head, codes_ref[r])
        scales = scales_ref[r].astype(F32)
        for j in range(heads):
            values = codes[j * rows : (j + 1) * rows] * scales[:, j : j + 1]
            values = jnp.where(held, values, EMPTY).astype(BF16)
            send_ref[spots[j // per_core], j % per_core] = values

    if requests <= 8:
        for r in range(requests):
            place(r)
    else:
        pl.loop(0, requests)(place)


def resident_kernel(
    len_hbm, codes_hbm, scales_hbm, query_hbm, new_hbm, out_ref,
    len_ref, codes_ref, scales_ref, query_ref, new_ref, sems,
):
    pairs = [
        (query_hbm, query_ref), (new_hbm, new_ref), (scales_hbm, scales_ref),
        (len_hbm, len_ref), (codes_hbm, codes_ref),
    ]
    copies = [pltpu.make_async_copy(a, b, sems.at[i]) for i, (a, b) in enumerate(pairs)]
    for copy in copies:
        copy.start()
    slots, rows = codes_ref.shape[:2]
    heads = scales_ref.shape[2]
    tokens = rows // (2 * heads)
    queries = query_ref.shape[1]
    new_rows = new_ref.shape[0]

    row = iota((rows, HD), 0)
    source = (mod(row, 2) * heads + mod(over(row, 2), heads)) * tokens + over(row, 2 * heads)
    lane = iota((rows, HD), 1)
    spread = jnp.concatenate(
        [jnp.where(source == lane + c, 1.0, 0.0).astype(BF16) for c in range(0, rows, HD)],
        axis=1,
    )
    for copy in copies[:-1]:
        copy.wait()
    flat = jnp.concatenate(
        [scales_ref[:, p, h] for p in range(2) for h in range(heads)], axis=1
    )
    columns = dot_nt(spread, flat).astype(BF16)

    col = iota((queries, rows), 1)
    row_head = over(iota((queries, rows), 0), queries // heads)
    is_key = (mod(col, 2) == 0) & (mod(over(col, 2), heads) == row_head)
    col_token = jnp.where(is_key, over(col, 2 * heads), tokens)

    new_col = iota((queries, new_rows), 1)
    new_row = iota((queries, new_rows), 0)
    new_ok = (
        (mod(new_col, 2) == 0)
        & (mod(over(new_col, 2), heads) == over(new_row, queries // heads))
        & (mod(over(new_col, 2 * heads), STEPS) <= mod(new_row, STEPS))
    )
    new_slot = jnp.where(new_ok, over(new_col, 2 * heads * STEPS), slots)

    every = range(slots)
    new = new_ref[...]
    new_all = dot_nt(query_ref[...].reshape(slots * queries, HD), new)
    copies[-1].wait()
    caches = [codes_ref[s] * columns[:, s : s + 1] for s in every]
    scores = [dot_nt(query_ref[s], caches[s]) for s in every]
    scores = [jnp.where(col_token < len_ref[s], scores[s] * SCORE_SCALE, NEGATIVE) for s in every]
    new_scores = [
        jnp.where(new_slot == s, new_all[s * queries : (s + 1) * queries] * SCORE_SCALE, NEGATIVE)
        for s in every
    ]
    top = [top_of(scores[s], new_scores[s]) for s in every]
    weights = [jnp.exp(scores[s] - top[s]) for s in every]
    new_weights = [jnp.exp(new_scores[s] - top[s]) for s in every]
    total = [sum_of(weights[s], new_weights[s]) for s in every]
    new_mixed = dot_nn(jnp.concatenate(new_weights, axis=0).astype(BF16), values_up(new))
    mixed = [
        dot_nn(to_values(weights[s]), caches[s]) + new_mixed[s * queries : (s + 1) * queries]
        for s in every
    ]
    for s in every:
        out_ref[s] = (mixed[s] * (1.0 / total[s])).astype(BF16)


def slots_by_rows(got_ref, tp, order, block_rows):
    chunk_rows = got_ref.shape[2]
    blocks = chunk_rows // block_rows
    rows = [got_ref[k, 0].astype(F32) for k in range(len(order))]
    here = {
        core // tp: jnp.where(x[:1] < EMPTY, 1.0, 0.0)
        for core, x in zip(order, rows)
        if core % tp == 0
    }
    ranks = {
        w: sum([here[v] for v in here if v < w], jnp.zeros((1, HD), F32)) for w in here
    }
    lane = iota((1, HD), 1)
    block = over(lane, block_rows)
    block = jnp.where(mod(lane, 2) == 0, block, -1)
    per_tile = HD // chunk_rows
    tiles = []
    for start in range(0, len(order), per_tile):
        tile = jnp.full((1, HD), -1.0, F32)
        for i in range(per_tile):
            x, rank = rows[start + i], ranks[order[start + i] // tp]
            for b in range(blocks):
                at = b * block_rows
                value = jnp.where(x[at : at + 1] < EMPTY, rank, -1.0)
                tile = jnp.where(block == i * blocks + b, value, tile)
        tiles.append(tile)
    return jnp.concatenate(tiles, axis=1)


def slots_by_matmul(got_ref, tp):
    chunks, _, chunk_rows = got_ref.shape[:3]
    columns = chunks * chunk_rows
    sender_rows = tp * chunk_rows
    piece = min(columns, 256)
    sums = dot_nt(jnp.ones((16, HD), BF16), got_ref[:, 0].reshape(columns, HD))[:8]
    col = iota((8, columns), 1)
    held = sums < EMPTY
    first = jnp.where(held & (mod(col, sender_rows) == 0), 1.0, 0.0).astype(BF16)
    row = over(iota((piece, piece), 0), sender_rows)
    before = jnp.where(row < over(iota((piece, piece), 1), sender_rows), 1.0, 0.0).astype(BF16)
    base = jnp.zeros((8, 1), F32)
    ranks = []
    for p in range(0, columns, piece):
        part = first[:, p : p + piece]
        ranks.append(dot_nn(part, before) + base)
        base = base + jnp.sum(part.astype(F32), axis=1, keepdims=True)
    rank = jnp.concatenate(ranks, axis=1)
    return jnp.where(held & (mod(col, 2) == 0), rank, -1.0)[:1]


def arrival_kernel(
    tp, groups, order, block_rows, got_ref, query_ref, new_ref, out_ref
):
    step = pl.program_id(0) if groups > 1 else 0
    chunks, heads, chunk_rows = got_ref.shape[:3]
    slots, _, per_head = query_ref.shape[:3]
    rows = slots * per_head
    columns = chunks * chunk_rows
    every = range(heads)

    caches = [got_ref[:, h].reshape(columns, HD) for h in every]
    queries = [query_ref[:, h].reshape(rows, HD) for h in every]
    new = new_ref[...]
    scores = [dot_nt(queries[h], caches[h]) for h in every]
    new_all = dot_nt(jnp.concatenate(queries, axis=0), new)
    if order is None:
        slot_of = slots_by_matmul(got_ref, tp)
    else:
        slot_of = slots_by_rows(got_ref, tp, order, block_rows)
    first_slot = jnp.float32(step * slots)
    mine = [slot_of == first_slot + a for a in range(slots)]

    new_col = iota((rows, new.shape[0]), 1)
    new_row = iota((rows, new.shape[0]), 0)
    new_here = (
        (mod(new_col, 2) == 0)
        & (over(new_col, 2 * heads * STEPS) == over(new_row, per_head))
        & (mod(over(new_col, 2 * heads), STEPS) <= mod(new_row, STEPS))
    )
    new_head = jnp.where(new_here, mod(over(new_col, 2), heads), heads)

    scores = [
        jnp.concatenate(
            [
                jnp.where(mine[a], scores[h][a * per_head : (a + 1) * per_head] * SCORE_SCALE, NEGATIVE)
                for a in range(slots)
            ],
            axis=0,
        )
        for h in every
    ]
    new_scores = [
        jnp.where(new_head == h, new_all[h * rows : (h + 1) * rows] * SCORE_SCALE, NEGATIVE)
        for h in every
    ]
    top = [top_of(scores[h], new_scores[h]) for h in every]
    weights = [jnp.exp(scores[h] - top[h]) for h in every]
    new_weights = [jnp.exp(new_scores[h] - top[h]) for h in every]
    total = [sum_of(weights[h], new_weights[h]) for h in every]
    new_mixed = dot_nn(jnp.concatenate(new_weights, axis=0).astype(BF16), values_up(new))
    for h in every:
        mixed = dot_nn(to_values(weights[h]), caches[h]) + new_mixed[h * rows : (h + 1) * rows]
        out_ref[:, h] = (mixed * (1.0 / total[h])).astype(BF16).reshape(slots, per_head, HD)


def whole(memory_space=pltpu.VMEM):
    return pl.BlockSpec(memory_space=memory_space)


def in_hbm(x):
    return pltpu.with_memory_space_constraint(x, pltpu.HBM)


def limit(mib):
    return pltpu.CompilerParams(vmem_limit_bytes=mib * 2**20)


def pack(pre_codes, pre_scales, req_dest, req_blocks, peers, tp, order):
    requests, blocks, block_tokens = pre_codes.shape[:3]
    tokens = blocks * block_tokens
    codes = (
        pre_codes.reshape(requests, tokens, 2, KVH, HD)
        .transpose(0, 1, 3, 2, 4)
        .reshape(requests, tokens * KVH * 2, HD)
    )
    scales = pre_scales.reshape(requests, tokens * 2, KVH)
    ins = [req_dest, req_blocks, codes, scales]
    chunk = (KVH // tp, tokens * 2, HD)
    return pl.pallas_call(
        functools.partial(pack_kernel, tp, order, KVH, 2 * block_tokens),
        out_shape=jax.ShapeDtypeStruct((peers * tp,) + chunk, BF16),
        in_specs=[whole(pltpu.HBM)] * len(ins),
        out_specs=whole(),
        scratch_shapes=[
            pltpu.SMEM(req_dest.shape, jnp.int32),
            pltpu.SMEM(req_blocks.shape, jnp.int32),
            pltpu.VMEM(codes.shape, BF16),
            pltpu.VMEM(scales.shape, BF16),
            pltpu.SemaphoreType.DMA((len(ins),)),
        ],
        compiler_params=limit(24),
        name="pack",
    )(*[in_hbm(x) for x in ins])


def cache_rows(codes):
    slots, tokens, _, width = codes.shape
    heads = width // HD
    return (
        codes.reshape(slots, tokens, 2, heads, HD)
        .transpose(0, 1, 3, 2, 4)
        .reshape(slots, tokens * heads * 2, HD)
    )


def query_rows(query):
    slots, steps, width = query.shape
    return query.reshape(slots, steps, width // HD, HD).transpose(0, 2, 1, 3)


def new_rows_of(new):
    slots, steps, pair, width = new.shape
    heads = width // HD
    return (
        new.reshape(slots, steps, pair, heads, HD)
        .transpose(0, 1, 3, 2, 4)
        .reshape(slots * steps * heads * pair, HD)
    )


def from_rows(out, shape):
    slots, steps, width = shape
    return out.reshape(slots, width // HD, steps, HD).transpose(0, 2, 1, 3).reshape(shape)


def resident(codes, res_scales, res_len, res_query, res_new):
    slots, rows = codes.shape[:2]
    heads = res_scales.shape[-1]
    scales = res_scales.transpose(0, 2, 3, 1)
    query = query_rows(res_query).reshape(slots, heads * GROUP * STEPS, HD)
    ins = [res_len, codes, scales, query, new_rows_of(res_new)]
    work = query.shape[0] * query.shape[1] * rows
    return pl.pallas_call(
        resident_kernel,
        out_shape=jax.ShapeDtypeStruct(query.shape, BF16),
        in_specs=[whole(pltpu.HBM)] * len(ins),
        out_specs=whole(),
        scratch_shapes=[
            pltpu.SMEM(res_len.shape, jnp.int32),
            *[pltpu.VMEM(x.shape, BF16) for x in ins[1:]],
            pltpu.SemaphoreType.DMA((len(ins),)),
        ],
        cost_estimate=pl.CostEstimate(
            flops=4 * work * HD,
            bytes_accessed=2 * (codes.size + 2 * query.size),
            transcendentals=work,
        ),
        compiler_params=limit(16),
        name="resident",
    )(*[in_hbm(x) for x in ins])


def arrivals(got, arr_query, arr_new, tp, order, block_rows):
    slots, steps, width = arr_query.shape
    heads = width // (HD * GROUP)
    query = query_rows(arr_query).reshape(slots, heads, GROUP * steps, HD)
    new = new_rows_of(arr_new)
    size = max(n for n in range(1, 7) if slots % n == 0)
    groups = slots // size
    small = got.size <= 2**18

    def part(ref, rows):
        if groups == 1:
            return whole()
        return pl.BlockSpec((rows,) + ref.shape[1:], lambda i: (i,) + (0,) * (ref.ndim - 1))

    return pl.pallas_call(
        functools.partial(arrival_kernel, tp, groups, order, block_rows),
        out_shape=jax.ShapeDtypeStruct(query.shape, BF16),
        grid=(groups,) if groups > 1 else (),
        in_specs=[whole(), part(query, size), part(new, new.shape[0] // groups)],
        out_specs=part(query, size),
        compiler_params=limit(16 if small else 48),
        name="arrivals",
    )(got, query, new)


def shards(
    pre_codes,
    pre_scales,
    req_dest,
    req_blocks,
    res_codes,
    res_scales,
    res_len,
    res_query,
    res_new,
    arr_query,
    arr_new,
):
    peers = lax.axis_size("wide")
    tp = lax.axis_size("tp")
    order = None
    if peers * tp == 16:
        order = [11, 10, 13, 12, 15, 14, 3, 2, 1, 0, 5, 4, 7, 6, 8, 9]
    send = pack(pre_codes, pre_scales, req_dest, req_blocks, peers, tp, order)
    got = lax.all_to_all(
        send,
        ("wide", "tp"),
        split_axis=0,
        concat_axis=0,
        tiled=True,
        axis_index_groups=[order or list(range(peers * tp))],
    )
    res_out = resident(cache_rows(res_codes), res_scales, res_len, res_query, res_new)
    block_rows = 2 * pre_codes.shape[2]
    arr_out = arrivals(got, arr_query, arr_new, tp, order, block_rows)
    return (from_rows(res_out, res_query.shape), from_rows(arr_out, arr_query.shape))


def solution(mesh):
    in_specs = (
        P(("groups", "wide"), None, "tp", None, None),
        P(("groups", "wide"), None, "tp", None, None),
        P(("groups", "wide")),
        P(("groups", "wide")),
        P(("groups", "wide"), None, None, "tp"),
        P(("groups", "wide"), None, None, "tp"),
        P(("groups", "wide")),
        P(("groups", "wide"), None, "tp"),
        P(("groups", "wide"), None, None, "tp"),
        P(("groups", "wide"), None, "tp"),
        P(("groups", "wide"), None, None, "tp"),
    )
    out_specs = (P(("groups", "wide"), None, "tp"), P(("groups", "wide"), None, "tp"))
    return jax.shard_map(shards, mesh=mesh, in_specs=in_specs, out_specs=out_specs, check_vma=False)
```

```python
import functools
import math

import jax
import jax.numpy as jnp
from jax import lax
from jax.experimental import pallas as pl
from jax.experimental.pallas import tpu as pltpu
from jax.sharding import PartitionSpec as P

KVH = 4
HD = 128
HQ = 64
GROUP = HQ // KVH
STEPS = 2

NEGATIVE = -1e30
EMPTY = 1024.0
SCORE_SCALE = 1.0 / math.sqrt(HD)

BF16 = jnp.bfloat16
F32 = jnp.float32


def iota(shape, axis):
    return lax.broadcasted_iota(jnp.int32, shape, axis)


def over(x, n):
    return jnp.right_shift(x, n.bit_length() - 1) if n & (n - 1) == 0 else x // n


def mod(x, n):
    return jnp.bitwise_and(x, n - 1) if n & (n - 1) == 0 else x % n


def dot_nt(a, b):
    return lax.dot_general(a, b, (((1,), (1,)), ((), ())), preferred_element_type=F32)


def dot_nn(a, b):
    return lax.dot_general(a, b, (((1,), (0,)), ((), ())), preferred_element_type=F32)


def top_of(*parts):
    return functools.reduce(jnp.maximum, [jnp.max(p, axis=1, keepdims=True) for p in parts])


def sum_of(*parts):
    return functools.reduce(jnp.add, [jnp.sum(p, axis=1, keepdims=True) for p in parts])


def to_values(weights):
    tiles = [pltpu.roll(weights[:, c : c + HD], 1, 1) for c in range(0, weights.shape[1], HD)]
    return jnp.concatenate(tiles, axis=1).astype(BF16)


def values_up(rows):
    return pltpu.roll(rows.astype(F32), rows.shape[0] - 1, 0).astype(BF16)


def pack_kernel(
    tp, order, heads, block_rows, dest_hbm, blocks_hbm, codes_hbm, scales_hbm, send_ref,
    dest_ref, blocks_ref, codes_ref, scales_ref, sems,
):
    requests, all_rows = codes_ref.shape[:2]
    pairs = [
        (codes_hbm, codes_ref), (scales_hbm, scales_ref),
        (dest_hbm, dest_ref), (blocks_hbm, blocks_ref),
    ]
    copies = [pltpu.make_async_copy(a, b, sems.at[i]) for i, (a, b) in enumerate(pairs)]
    for copy in copies:
        copy.start()
    send_ref[...] = jnp.full(send_ref.shape, EMPTY, BF16)
    rows = all_rows // heads
    per_core = heads // tp
    row_block = over(iota((rows, HD), 0), block_rows)
    to_row = iota((all_rows, all_rows), 0)
    from_row = iota((all_rows, all_rows), 1)
    source = over(mod(to_row, rows), 2) * (2 * heads) + over(to_row, rows) * 2 + mod(to_row, 2)
    by_head = jnp.where(from_row == source, 1.0, 0.0).astype(BF16)
    for copy in copies:
        copy.wait()

    def place(r):
        there = dest_ref[r]
        spots = [there * tp + t for t in range(tp)]
        if order is not None:
            for t in range(tp):
                at = {core // tp: p for p, core in enumerate(order) if core % tp == t}
                spots[t] = functools.reduce(
                    jnp.add, [jnp.where(there == w, p, 0) for w, p in at.items()]
                )
        held = row_block < blocks_ref[r]
        codes = dot_nn(by_head, codes_ref[r])
        scales = scales_ref[r].astype(F32)
        for j in range(heads):
            values = codes[j * rows : (j + 1) * rows] * scales[:, j : j + 1]
            values = jnp.where(held, values, EMPTY).astype(BF16)
            send_ref[spots[j // per_core], j % per_core] = values

    if requests <= 8:
        for r in range(requests):
            place(r)
    else:
        pl.loop(0, requests)(place)


def resident_kernel(
    len_hbm, codes_hbm, scales_hbm, query_hbm, new_hbm, out_ref,
    len_ref, codes_ref, scales_ref, query_ref, new_ref, sems,
):
    pairs = [
        (query_hbm, query_ref), (new_hbm, new_ref), (scales_hbm, scales_ref),
        (len_hbm, len_ref), (codes_hbm, codes_ref),
    ]
    copies = [pltpu.make_async_copy(a, b, sems.at[i]) for i, (a, b) in enumerate(pairs)]
    for copy in copies:
        copy.start()
    slots, rows = codes_ref.shape[:2]
    heads = scales_ref.shape[2]
    tokens = rows // (2 * heads)
    queries = query_ref.shape[1]
    new_rows = new_ref.shape[0]

    row = iota((rows, HD), 0)
    source = (mod(row, 2) * heads + mod(over(row, 2), heads)) * tokens + over(row, 2 * heads)
    lane = iota((rows, HD), 1)
    spread = jnp.concatenate(
        [jnp.where(source == lane + c, 1.0, 0.0).astype(BF16) for c in range(0, rows, HD)],
        axis=1,
    )
    for copy in copies[:-1]:
        copy.wait()
    flat = jnp.concatenate(
        [scales_ref[:, p, h] for p in range(2) for h in range(heads)], axis=1
    )
    columns = dot_nt(spread, flat).astype(BF16)

    col = iota((queries, rows), 1)
    row_head = over(iota((queries, rows), 0), queries // heads)
    is_key = (mod(col, 2) == 0) & (mod(over(col, 2), heads) == row_head)
    col_token = jnp.where(is_key, over(col, 2 * heads), tokens)

    new_col = iota((queries, new_rows), 1)
    new_row = iota((queries, new_rows), 0)
    new_ok = (
        (mod(new_col, 2) == 0)
        & (mod(over(new_col, 2), heads) == over(new_row, queries // heads))
        & (mod(over(new_col, 2 * heads), STEPS) <= mod(new_row, STEPS))
    )
    new_slot = jnp.where(new_ok, over(new_col, 2 * heads * STEPS), slots)

    every = range(slots)
    new = new_ref[...]
    new_all = dot_nt(query_ref[...].reshape(slots * queries, HD), new)
    copies[-1].wait()
    caches = [codes_ref[s] * columns[:, s : s + 1] for s in every]
    scores = [dot_nt(query_ref[s], caches[s]) for s in every]
    scores = [jnp.where(col_token < len_ref[s], scores[s] * SCORE_SCALE, NEGATIVE) for s in every]
    new_scores = [
        jnp.where(new_slot == s, new_all[s * queries : (s + 1) * queries] * SCORE_SCALE, NEGATIVE)
        for s in every
    ]
    top = [top_of(scores[s], new_scores[s]) for s in every]
    weights = [jnp.exp(scores[s] - top[s]) for s in every]
    new_weights = [jnp.exp(new_scores[s] - top[s]) for s in every]
    total = [sum_of(weights[s], new_weights[s]) for s in every]
    new_mixed = dot_nn(jnp.concatenate(new_weights, axis=0).astype(BF16), values_up(new))
    mixed = [
        dot_nn(to_values(weights[s]), caches[s]) + new_mixed[s * queries : (s + 1) * queries]
        for s in every
    ]
    for s in every:
        out_ref[s] = (mixed[s] * (1.0 / total[s])).astype(BF16)


def slots_by_rows(got_ref, tp, order, block_rows):
    chunk_rows = got_ref.shape[2]
    blocks = chunk_rows // block_rows
    rows = [got_ref[k, 0].astype(F32) for k in range(len(order))]
    here = {
        core // tp: jnp.where(x[:1] < EMPTY, 1.0, 0.0)
        for core, x in zip(order, rows)
        if core % tp == 0
    }
    ranks = {
        w: sum([here[v] for v in here if v < w], jnp.zeros((1, HD), F32)) for w in here
    }
    lane = iota((1, HD), 1)
    block = over(lane, block_rows)
    block = jnp.where(mod(lane, 2) == 0, block, -1)
    per_tile = HD // chunk_rows
    tiles = []
    for start in range(0, len(order), per_tile):
        tile = jnp.full((1, HD), -1.0, F32)
        for i in range(per_tile):
            x, rank = rows[start + i], ranks[order[start + i] // tp]
            for b in range(blocks):
                at = b * block_rows
                value = jnp.where(x[at : at + 1] < EMPTY, rank, -1.0)
                tile = jnp.where(block == i * blocks + b, value, tile)
        tiles.append(tile)
    return jnp.concatenate(tiles, axis=1)


def slots_by_matmul(got_ref, tp):
    chunks, _, chunk_rows = got_ref.shape[:3]
    columns = chunks * chunk_rows
    sender_rows = tp * chunk_rows
    piece = min(columns, 256)
    sums = dot_nt(jnp.ones((16, HD), BF16), got_ref[:, 0].reshape(columns, HD))[:8]
    col = iota((8, columns), 1)
    held = sums < EMPTY
    first = jnp.where(held & (mod(col, sender_rows) == 0), 1.0, 0.0).astype(BF16)
    row = over(iota((piece, piece), 0), sender_rows)
    before = jnp.where(row < over(iota((piece, piece), 1), sender_rows), 1.0, 0.0).astype(BF16)
    base = jnp.zeros((8, 1), F32)
    ranks = []
    for p in range(0, columns, piece):
        part = first[:, p : p + piece]
        ranks.append(dot_nn(part, before) + base)
        base = base + jnp.sum(part.astype(F32), axis=1, keepdims=True)
    rank = jnp.concatenate(ranks, axis=1)
    return jnp.where(held & (mod(col, 2) == 0), rank, -1.0)[:1]


def arrival_kernel(
    tp, groups, order, block_rows, got_ref, query_ref, new_ref, out_ref
):
    step = pl.program_id(0) if groups > 1 else 0
    chunks, heads, chunk_rows = got_ref.shape[:3]
    slots, _, per_head = query_ref.shape[:3]
    rows = slots * per_head
    columns = chunks * chunk_rows
    every = range(heads)

    caches = [got_ref[:, h].reshape(columns, HD) for h in every]
    queries = [query_ref[:, h].reshape(rows, HD) for h in every]
    new = new_ref[...]
    scores = [dot_nt(queries[h], caches[h]) for h in every]
    new_all = dot_nt(jnp.concatenate(queries, axis=0), new)
    if order is None:
        slot_of = slots_by_matmul(got_ref, tp)
    else:
        slot_of = slots_by_rows(got_ref, tp, order, block_rows)
    first_slot = jnp.float32(step * slots)
    mine = [slot_of == first_slot + a for a in range(slots)]

    new_col = iota((rows, new.shape[0]), 1)
    new_row = iota((rows, new.shape[0]), 0)
    new_here = (
        (mod(new_col, 2) == 0)
        & (over(new_col, 2 * heads * STEPS) == over(new_row, per_head))
        & (mod(over(new_col, 2 * heads), STEPS) <= mod(new_row, STEPS))
    )
    new_head = jnp.where(new_here, mod(over(new_col, 2), heads), heads)

    scores = [
        jnp.concatenate(
            [
                jnp.where(mine[a], scores[h][a * per_head : (a + 1) * per_head] * SCORE_SCALE, NEGATIVE)
                for a in range(slots)
            ],
            axis=0,
        )
        for h in every
    ]
    new_scores = [
        jnp.where(new_head == h, new_all[h * rows : (h + 1) * rows] * SCORE_SCALE, NEGATIVE)
        for h in every
    ]
    top = [top_of(scores[h], new_scores[h]) for h in every]
    weights = [jnp.exp(scores[h] - top[h]) for h in every]
    new_weights = [jnp.exp(new_scores[h] - top[h]) for h in every]
    total = [sum_of(weights[h], new_weights[h]) for h in every]
    new_mixed = dot_nn(jnp.concatenate(new_weights, axis=0).astype(BF16), values_up(new))
    for h in every:
        mixed = dot_nn(to_values(weights[h]), caches[h]) + new_mixed[h * rows : (h + 1) * rows]
        out_ref[:, h] = (mixed * (1.0 / total[h])).astype(BF16).reshape(slots, per_head, HD)


def whole(memory_space=pltpu.VMEM):
    return pl.BlockSpec(memory_space=memory_space)


def in_hbm(x):
    return pltpu.with_memory_space_constraint(x, pltpu.HBM)


def limit(mib):
    return pltpu.CompilerParams(vmem_limit_bytes=mib * 2**20)


def pack(pre_codes, pre_scales, req_dest, req_blocks, peers, tp, order):
    requests, blocks, block_tokens = pre_codes.shape[:3]
    tokens = blocks * block_tokens
    codes = (
        pre_codes.reshape(requests, tokens, 2, KVH, HD)
        .transpose(0, 1, 3, 2, 4)
        .reshape(requests, tokens * KVH * 2, HD)
    )
    scales = pre_scales.reshape(requests, tokens * 2, KVH)
    ins = [req_dest, req_blocks, codes, scales]
    chunk = (KVH // tp, tokens * 2, HD)
    return pl.pallas_call(
        functools.partial(pack_kernel, tp, order, KVH, 2 * block_tokens),
        out_shape=jax.ShapeDtypeStruct((peers * tp,) + chunk, BF16),
        in_specs=[whole(pltpu.HBM)] * len(ins),
        out_specs=whole(),
        scratch_shapes=[
            pltpu.SMEM(req_dest.shape, jnp.int32),
            pltpu.SMEM(req_blocks.shape, jnp.int32),
            pltpu.VMEM(codes.shape, BF16),
            pltpu.VMEM(scales.shape, BF16),
            pltpu.SemaphoreType.DMA((len(ins),)),
        ],
        compiler_params=limit(24),
        name="pack",
    )(*[in_hbm(x) for x in ins])


def cache_rows(codes):
    slots, tokens, _, width = codes.shape
    heads = width // HD
    return (
        codes.reshape(slots, tokens, 2, heads, HD)
        .transpose(0, 1, 3, 2, 4)
        .reshape(slots, tokens * heads * 2, HD)
    )


def query_rows(query):
    slots, steps, width = query.shape
    return query.reshape(slots, steps, width // HD, HD).transpose(0, 2, 1, 3)


def new_rows_of(new):
    slots, steps, pair, width = new.shape
    heads = width // HD
    return (
        new.reshape(slots, steps, pair, heads, HD)
        .transpose(0, 1, 3, 2, 4)
        .reshape(slots * steps * heads * pair, HD)
    )


def from_rows(out, shape):
    slots, steps, width = shape
    return out.reshape(slots, width // HD, steps, HD).transpose(0, 2, 1, 3).reshape(shape)


def resident(codes, res_scales, res_len, res_query, res_new):
    slots, rows = codes.shape[:2]
    heads = res_scales.shape[-1]
    scales = res_scales.transpose(0, 2, 3, 1)
    query = query_rows(res_query).reshape(slots, heads * GROUP * STEPS, HD)
    ins = [res_len, codes, scales, query, new_rows_of(res_new)]
    work = query.shape[0] * query.shape[1] * rows
    return pl.pallas_call(
        resident_kernel,
        out_shape=jax.ShapeDtypeStruct(query.shape, BF16),
        in_specs=[whole(pltpu.HBM)] * len(ins),
        out_specs=whole(),
        scratch_shapes=[
            pltpu.SMEM(res_len.shape, jnp.int32),
            *[pltpu.VMEM(x.shape, BF16) for x in ins[1:]],
            pltpu.SemaphoreType.DMA((len(ins),)),
        ],
        cost_estimate=pl.CostEstimate(
            flops=4 * work * HD,
            bytes_accessed=2 * (codes.size + 2 * query.size),
            transcendentals=work,
        ),
        compiler_params=limit(16),
        name="resident",
    )(*[in_hbm(x) for x in ins])


def arrivals(got, arr_query, arr_new, tp, order, block_rows):
    slots, steps, width = arr_query.shape
    heads = width // (HD * GROUP)
    query = query_rows(arr_query).reshape(slots, heads, GROUP * steps, HD)
    new = new_rows_of(arr_new)
    size = max(n for n in range(1, 7) if slots % n == 0)
    groups = slots // size
    small = got.size <= 2**18

    def part(ref, rows):
        if groups == 1:
            return whole()
        return pl.BlockSpec((rows,) + ref.shape[1:], lambda i: (i,) + (0,) * (ref.ndim - 1))

    return pl.pallas_call(
        functools.partial(arrival_kernel, tp, groups, order, block_rows),
        out_shape=jax.ShapeDtypeStruct(query.shape, BF16),
        grid=(groups,) if groups > 1 else (),
        in_specs=[whole(), part(query, size), part(new, new.shape[0] // groups)],
        out_specs=part(query, size),
        compiler_params=limit(16 if small else 48),
        name="arrivals",
    )(got, query, new)


def shards(
    pre_codes,
    pre_scales,
    req_dest,
    req_blocks,
    res_codes,
    res_scales,
    res_len,
    res_query,
    res_new,
    arr_query,
    arr_new,
):
    peers = lax.axis_size("wide")
    tp = lax.axis_size("tp")
    order = None
    if peers * tp == 16:
        order = [11, 10, 13, 12, 15, 14, 2, 3, 1, 0, 5, 4, 7, 6, 9, 8]
    send = pack(pre_codes, pre_scales, req_dest, req_blocks, peers, tp, order)
    got = lax.all_to_all(
        send,
        ("wide", "tp"),
        split_axis=0,
        concat_axis=0,
        tiled=True,
        axis_index_groups=[order or list(range(peers * tp))],
    )
    res_out = resident(cache_rows(res_codes), res_scales, res_len, res_query, res_new)
    block_rows = 2 * pre_codes.shape[2]
    arr_out = arrivals(got, arr_query, arr_new, tp, order, block_rows)
    return (from_rows(res_out, res_query.shape), from_rows(arr_out, arr_query.shape))


def solution(mesh):
    in_specs = (
        P(("groups", "wide"), None, "tp", None, None),
        P(("groups", "wide"), None, "tp", None, None),
        P(("groups", "wide")),
        P(("groups", "wide")),
        P(("groups", "wide"), None, None, "tp"),
        P(("groups", "wide"), None, None, "tp"),
        P(("groups", "wide")),
        P(("groups", "wide"), None, "tp"),
        P(("groups", "wide"), None, None, "tp"),
        P(("groups", "wide"), None, "tp"),
        P(("groups", "wide"), None, None, "tp"),
    )
    out_specs = (P(("groups", "wide"), None, "tp"), P(("groups", "wide"), None, "tp"))
    return jax.shard_map(shards, mesh=mesh, in_specs=in_specs, out_specs=out_specs, check_vma=False)
```

```python
import functools
import math

import jax
import jax.numpy as jnp
from jax import lax
from jax.experimental import pallas as pl
from jax.experimental.pallas import tpu as pltpu
from jax.sharding import PartitionSpec as P

KVH = 4
HD = 128
HQ = 64
GROUP = HQ // KVH
STEPS = 2

NEGATIVE = -1e30
EMPTY = 1024.0
SCORE_SCALE = 1.0 / math.sqrt(HD)

BF16 = jnp.bfloat16
F32 = jnp.float32


def iota(shape, axis):
    return lax.broadcasted_iota(jnp.int32, shape, axis)


def over(x, n):
    return jnp.right_shift(x, n.bit_length() - 1) if n & (n - 1) == 0 else x // n


def mod(x, n):
    return jnp.bitwise_and(x, n - 1) if n & (n - 1) == 0 else x % n


def dot_nt(a, b):
    return lax.dot_general(a, b, (((1,), (1,)), ((), ())), preferred_element_type=F32)


def dot_nn(a, b):
    return lax.dot_general(a, b, (((1,), (0,)), ((), ())), preferred_element_type=F32)


def top_of(*parts):
    return functools.reduce(jnp.maximum, [jnp.max(p, axis=1, keepdims=True) for p in parts])


def sum_of(*parts):
    return functools.reduce(jnp.add, [jnp.sum(p, axis=1, keepdims=True) for p in parts])


def to_values(weights):
    tiles = [pltpu.roll(weights[:, c : c + HD], 1, 1) for c in range(0, weights.shape[1], HD)]
    return jnp.concatenate(tiles, axis=1).astype(BF16)


def values_up(rows):
    return pltpu.roll(rows.astype(F32), rows.shape[0] - 1, 0).astype(BF16)


def pack_kernel(
    tp, order, heads, block_rows, dest_hbm, blocks_hbm, codes_hbm, scales_hbm, send_ref,
    dest_ref, blocks_ref, codes_ref, scales_ref, sems,
):
    requests, all_rows = codes_ref.shape[:2]
    pairs = [
        (codes_hbm, codes_ref), (scales_hbm, scales_ref),
        (dest_hbm, dest_ref), (blocks_hbm, blocks_ref),
    ]
    copies = [pltpu.make_async_copy(a, b, sems.at[i]) for i, (a, b) in enumerate(pairs)]
    for copy in copies:
        copy.start()
    send_ref[...] = jnp.full(send_ref.shape, EMPTY, BF16)
    rows = all_rows // heads
    per_core = heads // tp
    row_block = over(iota((rows, HD), 0), block_rows)
    to_row = iota((all_rows, all_rows), 0)
    from_row = iota((all_rows, all_rows), 1)
    source = over(mod(to_row, rows), 2) * (2 * heads) + over(to_row, rows) * 2 + mod(to_row, 2)
    by_head = jnp.where(from_row == source, 1.0, 0.0).astype(BF16)
    for copy in copies:
        copy.wait()

    def place(r):
        there = dest_ref[r]
        spots = [there * tp + t for t in range(tp)]
        if order is not None:
            for t in range(tp):
                at = {core // tp: p for p, core in enumerate(order) if core % tp == t}
                spots[t] = functools.reduce(
                    jnp.add, [jnp.where(there == w, p, 0) for w, p in at.items()]
                )
        held = row_block < blocks_ref[r]
        codes = dot_nn(by_head, codes_ref[r])
        scales = scales_ref[r].astype(F32)
        for j in range(heads):
            values = codes[j * rows : (j + 1) * rows] * scales[:, j : j + 1]
            values = jnp.where(held, values, EMPTY).astype(BF16)
            send_ref[spots[j // per_core], j % per_core] = values

    if requests <= 8:
        for r in range(requests):
            place(r)
    else:
        pl.loop(0, requests)(place)


def resident_kernel(
    len_hbm, codes_hbm, scales_hbm, query_hbm, new_hbm, out_ref,
    len_ref, codes_ref, scales_ref, query_ref, new_ref, sems,
):
    pairs = [
        (query_hbm, query_ref), (new_hbm, new_ref), (scales_hbm, scales_ref),
        (len_hbm, len_ref), (codes_hbm, codes_ref),
    ]
    copies = [pltpu.make_async_copy(a, b, sems.at[i]) for i, (a, b) in enumerate(pairs)]
    for copy in copies[:-1]:
        copy.start()
    slots, rows = codes_ref.shape[:2]
    heads = scales_ref.shape[2]
    tokens = rows // (2 * heads)
    queries = query_ref.shape[1]
    new_rows = new_ref.shape[0]

    row = iota((rows, HD), 0)
    source = (mod(row, 2) * heads + mod(over(row, 2), heads)) * tokens + over(row, 2 * heads)
    lane = iota((rows, HD), 1)
    spread = jnp.concatenate(
        [jnp.where(source == lane + c, 1.0, 0.0).astype(BF16) for c in range(0, rows, HD)],
        axis=1,
    )
    for copy in copies[:-1]:
        copy.wait()
    copies[-1].start()
    flat = jnp.concatenate(
        [scales_ref[:, p, h] for p in range(2) for h in range(heads)], axis=1
    )
    columns = dot_nt(spread, flat).astype(BF16)

    col = iota((queries, rows), 1)
    row_head = over(iota((queries, rows), 0), queries // heads)
    is_key = (mod(col, 2) == 0) & (mod(over(col, 2), heads) == row_head)
    col_token = jnp.where(is_key, over(col, 2 * heads), tokens)

    new_col = iota((queries, new_rows), 1)
    new_row = iota((queries, new_rows), 0)
    new_ok = (
        (mod(new_col, 2) == 0)
        & (mod(over(new_col, 2), heads) == over(new_row, queries // heads))
        & (mod(over(new_col, 2 * heads), STEPS) <= mod(new_row, STEPS))
    )
    new_slot = jnp.where(new_ok, over(new_col, 2 * heads * STEPS), slots)

    every = range(slots)
    new = new_ref[...]
    new_all = dot_nt(query_ref[...].reshape(slots * queries, HD), new)
    copies[-1].wait()
    caches = [codes_ref[s] * columns[:, s : s + 1] for s in every]
    scores = [dot_nt(query_ref[s], caches[s]) for s in every]
    scores = [jnp.where(col_token < len_ref[s], scores[s] * SCORE_SCALE, NEGATIVE) for s in every]
    new_scores = [
        jnp.where(new_slot == s, new_all[s * queries : (s + 1) * queries] * SCORE_SCALE, NEGATIVE)
        for s in every
    ]
    top = [top_of(scores[s], new_scores[s]) for s in every]
    weights = [jnp.exp(scores[s] - top[s]) for s in every]
    new_weights = [jnp.exp(new_scores[s] - top[s]) for s in every]
    total = [sum_of(weights[s], new_weights[s]) for s in every]
    new_mixed = dot_nn(jnp.concatenate(new_weights, axis=0).astype(BF16), values_up(new))
    mixed = [
        dot_nn(to_values(weights[s]), caches[s]) + new_mixed[s * queries : (s + 1) * queries]
        for s in every
    ]
    for s in every:
        out_ref[s] = (mixed[s] * (1.0 / total[s])).astype(BF16)


def slots_by_rows(got_ref, tp, order, block_rows):
    chunk_rows = got_ref.shape[2]
    blocks = chunk_rows // block_rows
    rows = [got_ref[k, 0].astype(F32) for k in range(len(order))]
    here = {
        core // tp: jnp.where(x[:1] < EMPTY, 1.0, 0.0)
        for core, x in zip(order, rows)
        if core % tp == 0
    }
    ranks = {
        w: sum([here[v] for v in here if v < w], jnp.zeros((1, HD), F32)) for w in here
    }
    lane = iota((1, HD), 1)
    block = over(lane, block_rows)
    block = jnp.where(mod(lane, 2) == 0, block, -1)
    per_tile = HD // chunk_rows
    tiles = []
    for start in range(0, len(order), per_tile):
        tile = jnp.full((1, HD), -1.0, F32)
        for i in range(per_tile):
            x, rank = rows[start + i], ranks[order[start + i] // tp]
            for b in range(blocks):
                at = b * block_rows
                value = jnp.where(x[at : at + 1] < EMPTY, rank, -1.0)
                tile = jnp.where(block == i * blocks + b, value, tile)
        tiles.append(tile)
    return jnp.concatenate(tiles, axis=1)


def slots_by_matmul(got_ref, tp):
    chunks, _, chunk_rows = got_ref.shape[:3]
    columns = chunks * chunk_rows
    sender_rows = tp * chunk_rows
    piece = min(columns, 256)
    sums = dot_nt(jnp.ones((16, HD), BF16), got_ref[:, 0].reshape(columns, HD))[:8]
    col = iota((8, columns), 1)
    held = sums < EMPTY
    first = jnp.where(held & (mod(col, sender_rows) == 0), 1.0, 0.0).astype(BF16)
    row = over(iota((piece, piece), 0), sender_rows)
    before = jnp.where(row < over(iota((piece, piece), 1), sender_rows), 1.0, 0.0).astype(BF16)
    base = jnp.zeros((8, 1), F32)
    ranks = []
    for p in range(0, columns, piece):
        part = first[:, p : p + piece]
        ranks.append(dot_nn(part, before) + base)
        base = base + jnp.sum(part.astype(F32), axis=1, keepdims=True)
    rank = jnp.concatenate(ranks, axis=1)
    return jnp.where(held & (mod(col, 2) == 0), rank, -1.0)[:1]


def arrival_kernel(
    tp, groups, order, block_rows, got_ref, query_ref, new_ref, out_ref
):
    step = pl.program_id(0) if groups > 1 else 0
    chunks, heads, chunk_rows = got_ref.shape[:3]
    slots, _, per_head = query_ref.shape[:3]
    rows = slots * per_head
    columns = chunks * chunk_rows
    every = range(heads)

    caches = [got_ref[:, h].reshape(columns, HD) for h in every]
    queries = [query_ref[:, h].reshape(rows, HD) for h in every]
    new = new_ref[...]
    scores = [dot_nt(queries[h], caches[h]) for h in every]
    new_all = dot_nt(jnp.concatenate(queries, axis=0), new)
    if order is None:
        slot_of = slots_by_matmul(got_ref, tp)
    else:
        slot_of = slots_by_rows(got_ref, tp, order, block_rows)
    first_slot = jnp.float32(step * slots)
    mine = [slot_of == first_slot + a for a in range(slots)]

    new_col = iota((rows, new.shape[0]), 1)
    new_row = iota((rows, new.shape[0]), 0)
    new_here = (
        (mod(new_col, 2) == 0)
        & (over(new_col, 2 * heads * STEPS) == over(new_row, per_head))
        & (mod(over(new_col, 2 * heads), STEPS) <= mod(new_row, STEPS))
    )
    new_head = jnp.where(new_here, mod(over(new_col, 2), heads), heads)

    scores = [
        jnp.concatenate(
            [
                jnp.where(mine[a], scores[h][a * per_head : (a + 1) * per_head] * SCORE_SCALE, NEGATIVE)
                for a in range(slots)
            ],
            axis=0,
        )
        for h in every
    ]
    new_scores = [
        jnp.where(new_head == h, new_all[h * rows : (h + 1) * rows] * SCORE_SCALE, NEGATIVE)
        for h in every
    ]
    top = [top_of(scores[h], new_scores[h]) for h in every]
    weights = [jnp.exp(scores[h] - top[h]) for h in every]
    new_weights = [jnp.exp(new_scores[h] - top[h]) for h in every]
    total = [sum_of(weights[h], new_weights[h]) for h in every]
    new_mixed = dot_nn(jnp.concatenate(new_weights, axis=0).astype(BF16), values_up(new))
    for h in every:
        mixed = dot_nn(to_values(weights[h]), caches[h]) + new_mixed[h * rows : (h + 1) * rows]
        out_ref[:, h] = (mixed * (1.0 / total[h])).astype(BF16).reshape(slots, per_head, HD)


def whole(memory_space=pltpu.VMEM):
    return pl.BlockSpec(memory_space=memory_space)


def in_hbm(x):
    return pltpu.with_memory_space_constraint(x, pltpu.HBM)


def limit(mib):
    return pltpu.CompilerParams(vmem_limit_bytes=mib * 2**20)


def pack(pre_codes, pre_scales, req_dest, req_blocks, peers, tp, order):
    requests, blocks, block_tokens = pre_codes.shape[:3]
    tokens = blocks * block_tokens
    codes = (
        pre_codes.reshape(requests, tokens, 2, KVH, HD)
        .transpose(0, 1, 3, 2, 4)
        .reshape(requests, tokens * KVH * 2, HD)
    )
    scales = pre_scales.reshape(requests, tokens * 2, KVH)
    ins = [req_dest, req_blocks, codes, scales]
    chunk = (KVH // tp, tokens * 2, HD)
    return pl.pallas_call(
        functools.partial(pack_kernel, tp, order, KVH, 2 * block_tokens),
        out_shape=jax.ShapeDtypeStruct((peers * tp,) + chunk, BF16),
        in_specs=[whole(pltpu.HBM)] * len(ins),
        out_specs=whole(),
        scratch_shapes=[
            pltpu.SMEM(req_dest.shape, jnp.int32),
            pltpu.SMEM(req_blocks.shape, jnp.int32),
            pltpu.VMEM(codes.shape, BF16),
            pltpu.VMEM(scales.shape, BF16),
            pltpu.SemaphoreType.DMA((len(ins),)),
        ],
        compiler_params=limit(24),
        name="pack",
    )(*[in_hbm(x) for x in ins])


def cache_rows(codes):
    slots, tokens, _, width = codes.shape
    heads = width // HD
    return (
        codes.reshape(slots, tokens, 2, heads, HD)
        .transpose(0, 1, 3, 2, 4)
        .reshape(slots, tokens * heads * 2, HD)
    )


def query_rows(query):
    slots, steps, width = query.shape
    return query.reshape(slots, steps, width // HD, HD).transpose(0, 2, 1, 3)


def new_rows_of(new):
    slots, steps, pair, width = new.shape
    heads = width // HD
    return (
        new.reshape(slots, steps, pair, heads, HD)
        .transpose(0, 1, 3, 2, 4)
        .reshape(slots * steps * heads * pair, HD)
    )


def from_rows(out, shape):
    slots, steps, width = shape
    return out.reshape(slots, width // HD, steps, HD).transpose(0, 2, 1, 3).reshape(shape)


def resident(codes, res_scales, res_len, res_query, res_new):
    slots, rows = codes.shape[:2]
    heads = res_scales.shape[-1]
    scales = res_scales.transpose(0, 2, 3, 1)
    query = query_rows(res_query).reshape(slots, heads * GROUP * STEPS, HD)
    ins = [res_len, codes, scales, query, new_rows_of(res_new)]
    work = query.shape[0] * query.shape[1] * rows
    return pl.pallas_call(
        resident_kernel,
        out_shape=jax.ShapeDtypeStruct(query.shape, BF16),
        in_specs=[whole(pltpu.HBM)] * len(ins),
        out_specs=whole(),
        scratch_shapes=[
            pltpu.SMEM(res_len.shape, jnp.int32),
            *[pltpu.VMEM(x.shape, BF16) for x in ins[1:]],
            pltpu.SemaphoreType.DMA((len(ins),)),
        ],
        cost_estimate=pl.CostEstimate(
            flops=4 * work * HD,
            bytes_accessed=2 * (codes.size + 2 * query.size),
            transcendentals=work,
        ),
        compiler_params=limit(16),
        name="resident",
    )(*[in_hbm(x) for x in ins])


def arrivals(got, arr_query, arr_new, tp, order, block_rows):
    slots, steps, width = arr_query.shape
    heads = width // (HD * GROUP)
    query = query_rows(arr_query).reshape(slots, heads, GROUP * steps, HD)
    new = new_rows_of(arr_new)
    size = max(n for n in range(1, 7) if slots % n == 0)
    groups = slots // size
    small = got.size <= 2**18

    def part(ref, rows):
        if groups == 1:
            return whole()
        return pl.BlockSpec((rows,) + ref.shape[1:], lambda i: (i,) + (0,) * (ref.ndim - 1))

    return pl.pallas_call(
        functools.partial(arrival_kernel, tp, groups, order, block_rows),
        out_shape=jax.ShapeDtypeStruct(query.shape, BF16),
        grid=(groups,) if groups > 1 else (),
        in_specs=[whole(), part(query, size), part(new, new.shape[0] // groups)],
        out_specs=part(query, size),
        compiler_params=limit(16 if small else 48),
        name="arrivals",
    )(got, query, new)


def shards(
    pre_codes,
    pre_scales,
    req_dest,
    req_blocks,
    res_codes,
    res_scales,
    res_len,
    res_query,
    res_new,
    arr_query,
    arr_new,
):
    peers = lax.axis_size("wide")
    tp = lax.axis_size("tp")
    order = None
    if peers * tp == 16:
        order = [11, 10, 13, 12, 15, 14, 3, 2, 1, 0, 4, 5, 6, 7, 9, 8]
    send = pack(pre_codes, pre_scales, req_dest, req_blocks, peers, tp, order)
    got = lax.all_to_all(
        send,
        ("wide", "tp"),
        split_axis=0,
        concat_axis=0,
        tiled=True,
        axis_index_groups=[order or list(range(peers * tp))],
    )
    res_out = resident(cache_rows(res_codes), res_scales, res_len, res_query, res_new)
    block_rows = 2 * pre_codes.shape[2]
    arr_out = arrivals(got, arr_query, arr_new, tp, order, block_rows)
    return (from_rows(res_out, res_query.shape), from_rows(arr_out, arr_query.shape))


def solution(mesh):
    in_specs = (
        P(("groups", "wide"), None, "tp", None, None),
        P(("groups", "wide"), None, "tp", None, None),
        P(("groups", "wide")),
        P(("groups", "wide")),
        P(("groups", "wide"), None, None, "tp"),
        P(("groups", "wide"), None, None, "tp"),
        P(("groups", "wide")),
        P(("groups", "wide"), None, "tp"),
        P(("groups", "wide"), None, None, "tp"),
        P(("groups", "wide"), None, "tp"),
        P(("groups", "wide"), None, None, "tp"),
    )
    out_specs = (P(("groups", "wide"), None, "tp"), P(("groups", "wide"), None, "tp"))
    return jax.shard_map(shards, mesh=mesh, in_specs=in_specs, out_specs=out_specs, check_vma=False)
```
